128 devices in a mesh: ctx: 32 (over x, y, z_hi), fsdp: 4 (over z_lo, core).
Axes of the slice: x: 4, y: 4, z: 4 (z_hi: 2, z_lo: 2; z = z_hi * 2 + z_lo), core: 2. Of those that a mesh axis runs over, the one named last changes fastest.
Arguments:
- hidden_in: bfloat16 [4, 4096, 1024], P('fsdp', 'ctx'), may hold values from -6 to 6
- cotangent: bfloat16 [4, 4096, 1024], P('fsdp', 'ctx'), may hold values from -6 to 6
- pair_table: int32 [32], replicated, may hold values from 0 to 31, each once
- norm_gain: bfloat16 [2, 2, 1024], P(None, None, 'fsdp'), may hold values from 0.5 to 1.5
- norm_bias: bfloat16 [2, 2, 1024], P(None, None, 'fsdp'), may hold values from -1.75 to 1.75
- qkv_weight: bfloat16 [2, 1024, 3072], P(None, 'fsdp'), may hold values from -0.1875 to 0.1875
- qkv_bias: bfloat16 [2, 3072], P(None, 'fsdp'), may hold values from -3 to 3
- out_weight: bfloat16 [2, 1024, 1024], P(None, 'fsdp'), may hold values from -4 to 4
- out_bias: bfloat16 [2, 1024], P(None, 'fsdp'), may hold values from -3 to 3
- up_weight: bfloat16 [2, 1024, 4096], P(None, 'fsdp'), may hold values from -0.1875 to 0.1875
- up_bias: bfloat16 [2, 4096], P(None, 'fsdp'), may hold values from -3 to 3
- down_weight: bfloat16 [2, 4096, 1024], P(None, 'fsdp'), may hold values from -0.09375 to 0.09375
- down_bias: bfloat16 [2, 1024], P(None, 'fsdp'), may hold values from -3 to 3
Outputs:
- hidden_out: bfloat16 [4, 4096, 1024], P('fsdp', 'ctx')
- input_grad: float32 [4, 4096, 1024], P('fsdp', 'ctx')
- norm_gain_grad: float32 [2, 2, 1024], P(None, None, 'fsdp')
- norm_bias_grad: float32 [2, 2, 1024], P(None, None, 'fsdp')
- qkv_weight_grad: float32 [2, 1024, 3072], P(None, 'fsdp')
- qkv_bias_grad: float32 [2, 3072], P(None, 'fsdp')
- out_weight_grad: float32 [2, 1024, 1024], P(None, 'fsdp')
- out_bias_grad: float32 [2, 1024], P(None, 'fsdp')
- up_weight_grad: float32 [2, 1024, 4096], P(None, 'fsdp')
- up_bias_grad: float32 [2, 4096], P(None, 'fsdp')
- down_weight_grad: float32 [2, 4096, 1024], P(None, 'fsdp')
- down_bias_grad: float32 [2, 1024], P(None, 'fsdp')
The draws below stay inside these ranges and needn't reach their ends.
Inputs may be any that keep to these rules, and one draw needn't show every extreme that they name: pair_table is a permutation of the 32 block pairs; slot c holds pair pair_table[c].
All inputs are finite; a program needn't handle non-finite values.
Results may differ from the reference program's by a relative error of at most 0.025.
Values may be sent and summed in bfloat16 or wider, within the bound.
A program may use at most 384 MiB of HBM per device.

```python
import math
import jax
import jax.numpy as jnp
from jax import lax

D = 1024
HEADS = 16
FF = 4096
LAYERS = 2
HEAD_DIM = 64
ROT = 16
BLK = 64
SEQ = 4096
SEQS = 4
N_CTX = 32


def levels(own_key, dims, split, low, top_value):
    factor_of, own = 1.0, jax.random.fold_in(own_key, 6)
    for dim, blocks in split:
        heights = jnp.exp(jax.random.uniform(jax.random.fold_in(own, dim), (blocks,), jnp.float32, low / len(split), top_value / len(split)))
        factor_of = factor_of * jnp.repeat(heights, dims[dim] // blocks).reshape([-1 if axis == dim else 1 for axis in range(len(dims))])
    return factor_of


def normal_values(rng, extent, deviation, limit, split=(), held_as=jnp.bfloat16):
    values = deviation * jax.random.normal(rng, extent, jnp.float32)
    if split:
        values = values * levels(rng, extent, split, -0.22, 0.18)
    return jnp.clip(values, -limit, limit).astype(held_as)


def setup_inputs(seed: int = 0) -> dict:
    seeds = jax.random.split(jax.random.key(seed), 14)
    return {
        "hidden_in": normal_values(seeds[0], (SEQS, SEQ, D), 1.0, 6.0, ((0, 4), (1, 32))),
        "cotangent": normal_values(seeds[1], (SEQS, SEQ, D), 1.0, 6.0, ((0, 4), (1, 32))),
        "pair_table": jax.random.permutation(seeds[2], N_CTX).astype(jnp.int32),
        "norm_gain": jnp.clip(1.0 + 0.1 * jax.random.normal(seeds[3], (LAYERS, 2, D), jnp.float32), 0.5, 1.5).astype(jnp.bfloat16),
        "norm_bias": normal_values(seeds[4], (LAYERS, 2, D), 0.3, 1.75, ((2, 4),)),
        "qkv_weight": normal_values(seeds[5], (LAYERS, D, 3 * D), D ** -0.5, 0.1875, ((1, 4),)),
        "qkv_bias": normal_values(seeds[6], (LAYERS, 3 * D), 0.5, 3.0, ((1, 4),)),
        "out_weight": normal_values(seeds[7], (LAYERS, D, D), (max(1, D * 8 // SEQ)) ** -0.5, 4.0, ((1, 4),)),
        "out_bias": normal_values(seeds[8], (LAYERS, D), 0.5, 3.0, ((1, 4),)),
        "up_weight": normal_values(seeds[9], (LAYERS, D, FF), D ** -0.5, 0.1875, ((1, 4),)),
        "up_bias": normal_values(seeds[10], (LAYERS, FF), 0.5, 3.0, ((1, 4),)),
        "down_weight": normal_values(seeds[11], (LAYERS, FF, D), FF ** -0.5, 0.09375, ((1, 4),)),
        "down_bias": normal_values(seeds[12], (LAYERS, D), 0.5, 3.0, ((1, 4),)),
    }


EPS = 1e-05
HIGH = lax.Precision.HIGHEST
NEGATIVE = -1e+30

@jax.custom_vjp
def low(v):
    return lax.optimization_barrier(v.astype(jnp.bfloat16)).astype(jnp.float32)

@jax.custom_vjp
def low_back(v):
    return v

def low_keep(v):
    return (low(v), None)

def low_pass(kept, grad):
    return (grad,)

def back_keep(v):
    return (v, None)

def back_low(kept, grad):
    return (low(grad),)
low.defvjp(low_keep, low_pass)
low_back.defvjp(back_keep, back_low)

def pair_positions(pair_table, block_len):
    slots = pair_table.shape[0]
    blocks = jnp.stack([pair_table, 2 * slots - 1 - pair_table], 1)
    within = jnp.arange(block_len, dtype=jnp.int32)
    return (blocks[:, :, None] * block_len + within[None, None, :]).reshape(-1).astype(jnp.int32)

def rotation(positions, rot_dims):
    freqs = 10000.0 ** (-jnp.arange(0, rot_dims, 2, dtype=jnp.float32) / rot_dims)
    angles = positions.astype(jnp.float32)[:, None] * freqs[None, :]
    return (jnp.concatenate([jnp.cos(angles)] * 2, -1), jnp.concatenate([jnp.sin(angles)] * 2, -1))

def rope(inputs, cosines, sines):
    rot_dims = cosines.shape[-1]
    half_dims = rot_dims // 2
    turning = inputs[..., :rot_dims]
    turned = jnp.concatenate([-turning[..., half_dims:], turning[..., :half_dims]], -1)
    rotated = turning * cosines[:, None, :] + turned * sines[:, None, :]
    return jnp.concatenate([rotated, inputs[..., rot_dims:]], -1)

def attend_block(queries, query_pos, keys_all, values_all, key_pos):
    scores = jnp.einsum('qhe,khe->hqk', queries, keys_all, precision=HIGH) * HEAD_DIM ** (-0.5)
    scores = low_back(scores)
    allowed = key_pos[None, None, :] <= query_pos[None, :, None]
    scores = jnp.where(allowed, scores, NEGATIVE)
    probs = low(jax.nn.softmax(scores, axis=-1))
    return jnp.einsum('hqk,khe->qhe', probs, values_all, precision=HIGH)

def attend(queries, keys_all, values_all, positions):
    block_rows = math.gcd(SEQ, 512)
    block_count = SEQ // block_rows

    def one_block(pieces):
        return attend_block(pieces[0], pieces[1], keys_all, values_all, positions)
    blocks = (queries.reshape(block_count, block_rows, HEADS, HEAD_DIM), positions.reshape(block_count, block_rows))
    result = lax.map(jax.checkpoint(one_block), blocks)
    return result.reshape(SEQ, HEADS, HEAD_DIM)

def layer(stream, params, cosines, sines, positions):
    gain, shift, w_qkv, b_qkv, w_out, b_out, w_up, b_up, w_down, b_down = params
    row_mean = lax.optimization_barrier(jnp.mean(stream, -1, keepdims=True))
    centered = stream - row_mean
    spread = lax.optimization_barrier(jnp.mean(centered * centered, -1, keepdims=True))
    normed = centered * lax.rsqrt(spread + EPS)
    first = low(normed * gain[0] + shift[0])
    second = low(normed * gain[1] + shift[1])
    mixed = low_back(jnp.dot(first, w_qkv, precision=HIGH) + b_qkv)
    token_count = stream.shape[0]
    queries = mixed[:, :D].reshape(SEQS, SEQ, HEADS, HEAD_DIM)
    keys_all = mixed[:, D:2 * D].reshape(SEQS, SEQ, HEADS, HEAD_DIM)
    values_all = low(mixed[:, 2 * D:]).reshape(SEQS, SEQ, HEADS, HEAD_DIM)
    queries = low(rope(queries, cosines, sines))
    keys_all = low(rope(keys_all, cosines, sines))
    context = lax.map(lambda triple: attend(triple[0], triple[1], triple[2], positions), (queries, keys_all, values_all))
    context = low(low_back(context.reshape(token_count, D)))
    attn_out = low_back(jnp.dot(context, w_out, precision=HIGH) + b_out)
    hidden = low_back(jnp.dot(second, w_up, precision=HIGH) + b_up)
    active = low(jax.nn.gelu(hidden, approximate=False))
    mlp_out = low_back(jnp.dot(active, w_down, precision=HIGH) + b_down)
    return stream + attn_out + mlp_out

def reference(hidden_in, cotangent, pair_table, norm_gain, norm_bias, qkv_weight, qkv_bias, out_weight, out_bias, up_weight, up_bias, down_weight, down_bias):
    positions = pair_positions(pair_table, BLK)
    cosines, sines = rotation(positions, ROT)
    weights = tuple((param.astype(jnp.float32) for param in (norm_gain, norm_bias, qkv_weight, qkv_bias, out_weight, out_bias, up_weight, up_bias, down_weight, down_bias)))
    start = hidden_in.astype(jnp.float32).reshape(SEQS * SEQ, D)

    def forward(stream, params):
        for layer_index in range(LAYERS):
            stream = layer(stream, tuple((param[layer_index] for param in params)), cosines, sines, positions)
        return stream
    result, pull = jax.vjp(forward, start, weights)
    grad_in, grads = pull(cotangent.astype(jnp.float32).reshape(SEQS * SEQ, D))
    return (result.astype(jnp.bfloat16).reshape(SEQS, SEQ, D), grad_in.reshape(SEQS, SEQ, D), grads[0], grads[1], grads[2], grads[3], grads[4], grads[5], grads[6], grads[7], grads[8], grads[9])
```

```python
import functools

import jax
import jax.numpy as jnp
from jax import lax
from jax.experimental import pallas as pl
from jax.experimental.pallas import tpu as pltpu
from jax.sharding import PartitionSpec as P

HEADS = 16
HEAD = 64
ROT = 16
BLK = 64
SIDE = 4
EPS = 1e-05
NEGATIVE = -1e30
MESH = pl.DeviceIdType.MESH
F32 = jnp.float32
BF16 = jnp.bfloat16
TILE = 256
KEYS = 512


def place():
    slot = lax.axis_index("ctx")
    return slot // 8, (slot // 2) % SIDE, slot % 2


def device(x, y, z):
    return {"ctx": ((x % SIDE) * SIDE + (y % SIDE)) * 2 + z}


class Grid:
    def __init__(self):
        self.x, self.y, self.z = place()

    def spot(self, half, dp, dq):
        dx, dy = (dp, dq) if half == 0 else (dq, dp)
        return (self.x + dx + SIDE) % SIDE, (self.y + dy + SIDE) % SIDE

    def rank(self, half, dp, dq):
        x, y = self.spot(half, dp, dq)
        return x * SIDE + y

    def device(self, half, dp, dq):
        x, y = self.spot(half, dp, dq)
        return device(x, y, self.z)

    def barrier(self):
        gate = pltpu.get_barrier_semaphore()
        for step in ((1, 0), (-1, 0), (0, 1), (0, -1)):
            pl.semaphore_signal(
                gate, inc=1, device_id=self.device(0, *step), device_id_type=MESH
            )
        pl.semaphore_wait(gate, 4)


def gather_plane(grid, own_ref, all_ref, send_sem, recv_sem, ready=None):
    rows = own_ref.shape[0]
    half_rows, quarter = rows // 2, rows // 4
    sends = []

    def view(half, dp, dq, low, count):
        return all_ref.at[grid.rank(half, dp, dq), pl.ds(half * half_rows + low, count)]

    def start(half, event, to, block, low, count, own=False):
        source = (
            own_ref.at[pl.ds(half * half_rows + low, count)]
            if own
            else view(half, *block, low, count)
        )
        copy = pltpu.make_async_remote_copy(
            src_ref=source,
            dst_ref=view(half, *block, low, count),
            send_sem=send_sem.at[half, event],
            recv_sem=recv_sem.at[half, event],
            device_id=grid.device(half, *to),
            device_id_type=MESH,
        )
        copy.start()
        sends.append(copy)

    def arrive(half, event, block, low, count):
        there = view(half, *block, low, count)
        pltpu.make_async_remote_copy(
            src_ref=there,
            dst_ref=there,
            send_sem=send_sem.at[half, event],
            recv_sem=recv_sem.at[half, event],
            device_id=grid.device(half, 1, 0),
            device_id_type=MESH,
        ).wait_recv()

    def spread(half, column, dp, own=False):
        start(half, 4 + 4 * column, (0, 1), (dp, 0), 0, half_rows, own)
        start(half, 5 + 4 * column, (0, -1), (dp, 0), 0, half_rows, own)

    for half in (0, 1):
        start(half, 0, (1, 0), (0, 0), 0, half_rows, True)
        start(half, 1, (-1, 0), (0, 0), 0, half_rows, True)
    for half in (0, 1):
        spread(half, 0, 0, True)
    for half in (0, 1):
        arrive(half, 0, (-1, 0), 0, half_rows)
        start(half, 2, (1, 0), (-1, 0), 0, quarter)
        spread(half, 1, -1)
    for half in (0, 1):
        arrive(half, 1, (1, 0), 0, half_rows)
        start(half, 3, (-1, 0), (1, 0), quarter, quarter)
        spread(half, 2, 1)
    for half in (0, 1):
        arrive(half, 2, (2, 0), 0, quarter)
        arrive(half, 3, (2, 0), quarter, quarter)
        spread(half, 3, 2)
    steps = (0, -1, 1, 2)
    for column in range(4):
        for half in (0, 1):
            arrive(half, 4 + 4 * column, (steps[column], -1), 0, half_rows)
            start(half, 6 + 4 * column, (0, 1), (steps[column], -1), 0, quarter)
            arrive(half, 5 + 4 * column, (steps[column], 1), 0, half_rows)
            start(half, 7 + 4 * column, (0, -1), (steps[column], 1), quarter, quarter)
    for column in range(4):
        for half in (0, 1):
            arrive(half, 6 + 4 * column, (steps[column], 2), 0, quarter)
            arrive(half, 7 + 4 * column, (steps[column], 2), quarter, quarter)
    for copy in sends:
        copy.wait_send()


def gather_kernel(own_ref, all_ref, local_sem, send_sem, recv_sem):
    grid = Grid()
    grid.barrier()
    keep = pltpu.make_async_copy(own_ref, all_ref.at[grid.rank(0, 0, 0)], local_sem)
    keep.start()
    gather_plane(grid, own_ref, all_ref, send_sem, recv_sem)
    keep.wait()


def plane_all_gather(own, name, number):
    return pl.pallas_call(
        gather_kernel,
        out_shape=jax.ShapeDtypeStruct((16,) + own.shape, own.dtype),
        in_specs=[pl.BlockSpec(memory_space=pl.ANY)],
        out_specs=pl.BlockSpec(memory_space=pl.ANY),
        scratch_shapes=[
            pltpu.SemaphoreType.DMA,
            pltpu.SemaphoreType.DMA((2, 20)),
            pltpu.SemaphoreType.DMA((2, 20)),
        ],
        name=name,
        compiler_params=pltpu.CompilerParams(collective_id=number, has_side_effects=True),
    )(own)


def scatter_plane(grid, part_ref, out_ref, land_half, land_full, stage, total, send_sem, recv_sem):
    rows = part_ref.shape[1]
    half_rows, quarter = rows // 2, rows // 4
    sends = []
    steps = (2, -1, 1, 0)

    def start(half, event, source, target, to):
        copy = pltpu.make_async_remote_copy(
            src_ref=source,
            dst_ref=target,
            send_sem=send_sem.at[half, event],
            recv_sem=recv_sem.at[half, event],
            device_id=grid.device(half, *to),
            device_id_type=MESH,
        )
        copy.start()
        sends.append(copy)

    def arrive(half, event, target):
        pltpu.make_async_remote_copy(
            src_ref=target,
            dst_ref=target,
            send_sem=send_sem.at[half, event],
            recv_sem=recv_sem.at[half, event],
            device_id=grid.device(half, 1, 0),
            device_id_type=MESH,
        ).wait_recv()

    def part(half, dp, dq, low=0, count=None):
        return part_ref.at[
            grid.rank(half, dp, dq),
            pl.ds(half * half_rows + low, half_rows if count is None else count),
        ]

    def move(phase):
        return (lambda s: (0, s)) if phase == 0 else (lambda s: (s, 0))

    def opposite(half, column, pieces, step):
        start(
            half, 4 * column, pieces(2, 0, quarter), land_half.at[half, column, 0], step(1)
        )
        start(
            half,
            4 * column + 1,
            pieces(2, quarter, quarter),
            land_half.at[half, column, 1],
            step(-1),
        )

    def neighbours(half, column, pieces, step):
        arrive(half, 4 * column, land_half.at[half, column, 0])
        stage[half, column, 0, 0:quarter] = (
            pieces(1, 0, quarter)[...].astype(F32)
            + land_half[half, column, 0].astype(F32)
        ).astype(BF16)
        stage[half, column, 0, quarter:half_rows] = pieces(1, quarter, quarter)[...]
        start(
            half, 4 * column + 2, stage.at[half, column, 0], land_full.at[half, column, 0], step(1)
        )
        arrive(half, 4 * column + 1, land_half.at[half, column, 1])
        stage[half, column, 1, 0:quarter] = pieces(-1, 0, quarter)[...]
        stage[half, column, 1, quarter:half_rows] = (
            pieces(-1, quarter, quarter)[...].astype(F32)
            + land_half[half, column, 1].astype(F32)
        ).astype(BF16)
        start(
            half, 4 * column + 3, stage.at[half, column, 1], land_full.at[half, column, 1], step(-1)
        )

    def settle(half, column, own):
        arrive(half, 4 * column + 2, land_full.at[half, column, 0])
        arrive(half, 4 * column + 3, land_full.at[half, column, 1])
        return (
            own[...].astype(F32)
            + land_full[half, column, 0].astype(F32)
            + land_full[half, column, 1].astype(F32)
        )

    def first(column):
        dp = steps[column]
        return lambda half: (
            lambda dq, low, count: part(half, dp, dq, low, count)
        )

    second_index = {2: 0, -1: 1, 1: 2, 0: 3}

    def second(half):
        return lambda dp, low, count: total.at[half, second_index[dp], pl.ds(low, count)]

    along, across = move(0), move(1)
    for column in range(4):
        for half in (0, 1):
            opposite(half, column, first(column)(half), along)
    for column in range(4):
        for half in (0, 1):
            neighbours(half, column, first(column)(half), along)
    for column in range(4):
        for half in (0, 1):
            total[half, column] = settle(half, column, part(half, steps[column], 0)).astype(BF16)
            if column == 0:
                opposite(half, 4, second(half), across)
            if column == 2:
                neighbours(half, 4, second(half), across)
    for half in (0, 1):
        out_ref[pl.ds(half * half_rows, half_rows)] = settle(half, 4, total.at[half, 3])
    for copy in sends:
        copy.wait_send()


def scatter_kernel(part_ref, out_ref, land_half, land_full, stage, total, send_sem, recv_sem):
    grid = Grid()
    grid.barrier()
    scatter_plane(
        grid, part_ref, out_ref, land_half, land_full, stage, total, send_sem, recv_sem
    )


def plane_reduce_scatter(part, name, number):
    ranks, rows, width = part.shape
    half_rows, quarter = rows // 2, rows // 4
    return pl.pallas_call(
        scatter_kernel,
        out_shape=jax.ShapeDtypeStruct((rows, width), F32),
        in_specs=[pl.BlockSpec(memory_space=pltpu.VMEM)],
        out_specs=pl.BlockSpec(memory_space=pltpu.VMEM),
        scratch_shapes=[
            pltpu.VMEM((2, 5, 2, quarter, width), BF16),
            pltpu.VMEM((2, 5, 2, half_rows, width), BF16),
            pltpu.VMEM((2, 5, 2, half_rows, width), BF16),
            pltpu.VMEM((2, 4, half_rows, width), BF16),
            pltpu.SemaphoreType.DMA((2, 20)),
            pltpu.SemaphoreType.DMA((2, 20)),
        ],
        name=name,
        compiler_params=pltpu.CompilerParams(
            collective_id=number, has_side_effects=True, vmem_limit_bytes=40 << 20
        ),
    )(part)


def dots(a, b, da, db):
    return lax.dot_general(a, b, (((da,), (db,)), ((), ())), preferred_element_type=F32)


def sort_in(source_ref, order_ref, target_ref, count):
    def body(i, unused):
        start = pl.multiple_of(order_ref[i] * BLK, BLK)
        target_ref[pl.ds(pl.multiple_of(i * BLK, BLK), BLK), :] = source_ref[
            pl.ds(start, BLK), :
        ]
        return unused

    lax.fori_loop(0, count, body, 0)


def tile_positions(number_ref, tile, axis):
    per = TILE // BLK
    shape = (TILE, 1) if axis == 0 else (1, TILE)
    row = lax.broadcasted_iota(jnp.int32, shape, axis)
    base = jnp.zeros(shape, jnp.int32)
    for i in range(per):
        base = jnp.where(row // BLK == i, number_ref[tile * per + i] * BLK, base)
    return base + row % BLK


def attend_kernel(
    source_ref, order_ref, number_ref, q_ref, kv_ref, context_ref, log_ref, qs, kvs
):
    sort_in(kv_ref, source_ref, kvs, 64)
    sort_in(q_ref, order_ref, qs, 32)
    per = TILE // BLK

    def one_tile(tile, unused):
        queries = qs[pl.ds(pl.multiple_of(tile * TILE, TILE), TILE), :]
        low = number_ref[tile * per] * BLK
        high = (number_ref[tile * per + per - 1] + 1) * BLK
        positions = tile_positions(number_ref, tile, 0)

        def step(masked):
            def body(index, carry):
                row_max, row_sum, weighted = carry
                keys = kvs[pl.ds(pl.multiple_of(index * KEYS, KEYS), KEYS), :]
                scores = dots(queries, keys, 1, 1)
                if masked:
                    spots = index * KEYS + lax.broadcasted_iota(jnp.int32, (1, KEYS), 1)
                    scores = jnp.where(spots <= positions, scores, NEGATIVE)
                new_max = jnp.maximum(row_max, jnp.max(scores, 1, keepdims=True))
                weights = jnp.exp(scores - new_max)
                rescale = jnp.exp(row_max - new_max)
                row_sum = row_sum * rescale + jnp.sum(weights, 1, keepdims=True)
                weighted = weighted * rescale + dots(weights.astype(BF16), keys, 1, 0)
                return new_max, row_sum, weighted

            return body

        carry = (
            jnp.full((TILE, 1), NEGATIVE, F32),
            jnp.zeros((TILE, 1), F32),
            jnp.zeros((TILE, 2 * HEAD), F32),
        )
        clear = (low + 1) // KEYS
        carry = lax.fori_loop(0, clear, step(False), carry)
        row_max, row_sum, weighted = lax.fori_loop(
            clear, (high + KEYS - 1) // KEYS, step(True), carry
        )
        result = weighted / row_sum
        logs = jnp.broadcast_to(row_max + jnp.log(row_sum), (TILE, 2 * HEAD))
        for i in range(per):
            start = pl.multiple_of(order_ref[tile * per + i] * BLK, BLK)
            context_ref[pl.ds(start, BLK), :] = result[i * BLK : (i + 1) * BLK]
            log_ref[pl.ds(start, BLK), :] = logs[i * BLK : (i + 1) * BLK]
        return unused

    lax.fori_loop(0, 2048 // TILE, one_tile, 0)


def attend(source, order, number, queries, pairs):
    rows = queries.shape[0]
    smem, vmem = pl.BlockSpec(memory_space=pltpu.SMEM), pl.BlockSpec(memory_space=pltpu.VMEM)
    return pl.pallas_call(
        attend_kernel,
        out_shape=[
            jax.ShapeDtypeStruct((rows, 2 * HEAD), F32),
            jax.ShapeDtypeStruct((rows, 2 * HEAD), F32),
        ],
        in_specs=[smem, smem, smem, vmem, vmem],
        out_specs=[vmem, vmem],
        scratch_shapes=[
            pltpu.VMEM((rows, 2 * HEAD), BF16),
            pltpu.VMEM(pairs.shape, BF16),
        ],
        name="attend",
        compiler_params=pltpu.CompilerParams(vmem_limit_bytes=40 << 20),
    )(source, order, number, queries, pairs)


def attend_back_kernel(
    source_ref,
    order_ref,
    number_ref,
    q_ref,
    kv_ref,
    pull_ref,
    stat_ref,
    query_grad_ref,
    pair_grad_ref,
    qs,
    kvs,
    pulls,
    stats,
    sums,
):
    sort_in(kv_ref, source_ref, kvs, 64)
    sort_in(q_ref, order_ref, qs, 32)
    sort_in(pull_ref, order_ref, pulls, 32)
    sort_in(stat_ref, order_ref, stats, 32)
    sums[...] = jnp.zeros_like(sums)
    per = TILE // BLK

    def one_tile(tile, unused):
        rows = pl.ds(pl.multiple_of(tile * TILE, TILE), TILE)
        queries, pull = qs[rows, :], pulls[rows, :]
        turned = jnp.transpose(stats[rows, :])
        log_total, offset = turned[0:1, :], turned[1:2, :]
        low = number_ref[tile * per] * BLK
        high = (number_ref[tile * per + per - 1] + 1) * BLK
        positions = tile_positions(number_ref, tile, 1)

        def step(masked):
            def body(index, query_grad):
                spot = pl.ds(pl.multiple_of(index * KEYS, KEYS), KEYS)
                keys = kvs[spot, :]
                scores = dots(keys, queries, 1, 1)
                if masked:
                    spots = index * KEYS + lax.broadcasted_iota(jnp.int32, (KEYS, 1), 0)
                    scores = jnp.where(spots <= positions, scores, NEGATIVE)
                probs = jnp.exp(scores - log_total)
                prob_grad = dots(keys, pull, 1, 1)
                score_grad = (probs * (prob_grad - offset)).astype(BF16)
                sums[spot, :] += dots(score_grad, queries, 1, 0) + dots(
                    probs.astype(BF16), pull, 1, 0
                )
                return query_grad + dots(score_grad, keys, 0, 0)

            return body

        clear = (low + 1) // KEYS
        carry = jnp.zeros((TILE, 2 * HEAD), F32)
        carry = lax.fori_loop(0, clear, step(False), carry)
        carry = lax.fori_loop(clear, (high + KEYS - 1) // KEYS, step(True), carry)
        for i in range(per):
            start = pl.multiple_of(order_ref[tile * per + i] * BLK, BLK)
            query_grad_ref[pl.ds(start, BLK), :] = carry[i * BLK : (i + 1) * BLK]
        return unused

    lax.fori_loop(0, 2048 // TILE, one_tile, 0)

    def put(i, unused):
        start = pl.multiple_of(source_ref[i] * BLK, BLK)
        pair_grad_ref[pl.ds(start, BLK), :] = sums[
            pl.ds(pl.multiple_of(i * BLK, BLK), BLK), :
        ].astype(BF16)
        return unused

    lax.fori_loop(0, 64, put, 0)


def attend_back(source, order, number, queries, pairs, pull, stats):
    rows = queries.shape[0]
    smem, vmem = pl.BlockSpec(memory_space=pltpu.SMEM), pl.BlockSpec(memory_space=pltpu.VMEM)
    return pl.pallas_call(
        attend_back_kernel,
        out_shape=[
            jax.ShapeDtypeStruct((rows, 2 * HEAD), F32),
            jax.ShapeDtypeStruct(pairs.shape, BF16),
        ],
        in_specs=[smem, smem, smem, vmem, vmem, vmem, vmem],
        out_specs=[vmem, vmem],
        scratch_shapes=[
            pltpu.VMEM((rows, 2 * HEAD), BF16),
            pltpu.VMEM(pairs.shape, BF16),
            pltpu.VMEM((rows, 2 * HEAD), BF16),
            pltpu.VMEM((rows, 2 * HEAD), F32),
            pltpu.VMEM(pairs.shape, F32),
        ],
        name="attend_back",
        compiler_params=pltpu.CompilerParams(vmem_limit_bytes=48 << 20),
    )(source, order, number, queries, pairs, pull, stats)


def block_tables(pair_table, z):
    slots = pair_table.shape[0]
    ranks = slots // 2
    own = lax.dynamic_slice_in_dim(pair_table.reshape(ranks, 2), z, 1, 1)
    numbers = jnp.concatenate([own, 2 * slots - 1 - own], 1).reshape(-1)
    index = jnp.arange(slots, dtype=jnp.int32)
    standing = jnp.sum((numbers[None, :] < numbers[:, None]).astype(jnp.int32), 1)
    chosen = (standing[None, :] == index[:, None]).astype(jnp.int32)
    order = jnp.sum(chosen * index[None, :], 1)
    sorted_numbers = jnp.sum(chosen * numbers[None, :], 1)
    slot_of = jnp.sum(
        (pair_table[None, :] == index[:, None]).astype(jnp.int32) * index[None, :], 1
    )
    lies = jnp.where(slot_of % 2 == z, 0, slots) + (slot_of // 2) * 2
    source = jnp.concatenate([lies, lies[::-1] + 1])
    return numbers, order, sorted_numbers, source


def rotation(positions):
    freqs = 10000.0 ** (-jnp.arange(0, ROT, 2, dtype=F32) / ROT)
    angles = positions.astype(F32)[:, None] * freqs[None, :]
    return (jnp.concatenate([jnp.cos(angles)] * 2, -1), jnp.concatenate([jnp.sin(angles)] * 2, -1))


def rope(inputs, cosines, sines):
    half_dims = ROT // 2
    turning = inputs[..., :ROT]
    turned = jnp.concatenate([-turning[..., half_dims:], turning[..., :half_dims]], -1)
    return jnp.concatenate([turning * cosines + turned * sines, inputs[..., ROT:]], -1)


def standardize(stream):
    row_mean = jnp.mean(stream, -1, keepdims=True)
    centered = stream - row_mean
    spread = jnp.mean(centered * centered, -1, keepdims=True)
    inverse = lax.rsqrt(spread + EPS)
    return (centered * inverse, inverse)


def gelu_exact(inputs):
    return jax.nn.gelu(inputs, approximate=False)


def swap(value):
    pairs = [(i, i ^ 1) for i in range(lax.axis_size("ctx"))]
    return lax.ppermute(value, "ctx", pairs)


def on_device(
    hidden_in,
    cotangent,
    pair_table,
    norm_gain,
    norm_bias,
    qkv_weight,
    qkv_bias,
    out_weight,
    out_bias,
    up_weight,
    up_bias,
    down_weight,
    down_bias,
):
    layers = norm_gain.shape[0]
    slot = lax.axis_index("ctx")
    shard = lax.axis_index("fsdp")
    rank, z = slot // 2, slot % 2
    width = hidden_in.shape[2]
    quarter = width // 4

    numbers, order, sorted_numbers, source = block_tables(pair_table, z)
    positions = (
        numbers[:, None] * BLK + jnp.arange(BLK, dtype=jnp.int32)[None, :]
    ).reshape(-1)
    cosines, sines = rotation(positions)

    pieces = [
        lax.dynamic_slice_in_dim(qkv_weight, part * width + rank * HEAD, HEAD, 2)
        for part in range(3)
    ] + [
        lax.dynamic_slice_in_dim(up_weight, part * width + rank * HEAD, HEAD, 2)
        for part in range(4)
    ]
    wide = lax.all_gather(jnp.concatenate(pieces, 2), "fsdp", axis=1, tiled=True)
    tall = lax.all_gather(
        jnp.concatenate(
            [
                lax.dynamic_slice_in_dim(down_weight, rank * HEAD, HEAD, 1),
                lax.dynamic_slice_in_dim(out_weight, (rank % 4) * HEAD, HEAD, 1),
            ],
            1,
        ),
        "fsdp",
        axis=0,
    )
    vectors = lax.all_gather(
        jnp.concatenate(
            [
                norm_gain.reshape(layers, -1),
                norm_bias.reshape(layers, -1),
                qkv_bias,
                out_bias,
                up_bias,
                down_bias,
            ],
            1,
        ),
        "fsdp",
        axis=0,
    ).astype(F32)
    out_all = lax.dynamic_slice_in_dim(tall, rank // 4, 1, 0)[0, :, HEAD:]

    weights = []
    for layer in range(layers):
        vector = vectors[:, layer]
        gain = jnp.transpose(vector[:, 0:512].reshape(4, 2, 256), (1, 0, 2)).reshape(2, width)
        shift = jnp.transpose(vector[:, 512:1024].reshape(4, 2, 256), (1, 0, 2)).reshape(2, width)
        b_qkv = lax.dynamic_slice_in_dim(
            vector[:, 1024:1792].reshape(3, 16, HEAD), rank, 1, 1
        ).reshape(3 * HEAD)
        b_out = vector[:, 1792:2048].reshape(width)
        b_up = lax.dynamic_slice_in_dim(
            vector[:, 2048:3072].reshape(4, 16, HEAD), rank, 1, 1
        ).reshape(4 * HEAD)
        b_down = vector[:, 3072:3328].reshape(width)
        weights.append(
            (
                gain,
                shift,
                wide[layer, :, : 3 * HEAD],
                b_qkv,
                out_all[layer],
                wide[layer, :, 3 * HEAD :],
                b_up,
                tall[:, layer, :HEAD].reshape(4 * HEAD, width),
                b_out + b_down,
            )
        )

    number = 1
    stream = hidden_in[0].astype(F32)
    saved = []
    for layer in range(layers):
        gain, shift, w_qkv, b_qkv, w_out, w_up, b_up, w_down, b_last = weights[layer]
        normed, inverse = standardize(stream)
        normed_all = plane_all_gather(normed.astype(BF16), "gather_normed", number).reshape(
            -1, width
        )
        number += 1
        plain = normed_all.astype(F32)
        first = (plain * gain[0] + shift[0]).astype(BF16)
        second = (plain * gain[1] + shift[1]).astype(BF16)
        mixed = jnp.dot(first, w_qkv, preferred_element_type=F32) + b_qkv
        q = rope(mixed[:, :HEAD], cosines, sines).astype(BF16)
        k = rope(mixed[:, HEAD : 2 * HEAD], cosines, sines).astype(BF16)
        v = mixed[:, 2 * HEAD :].astype(BF16)
        queries = jnp.concatenate([q * jnp.asarray(0.125, BF16), jnp.zeros_like(q)], 1)
        pairs = jnp.concatenate([k, v], 1)
        pairs = jnp.concatenate([pairs, swap(pairs)], 0)
        context, logs = attend(source, order, sorted_numbers, queries, pairs)
        context_low = context[:, HEAD:].astype(BF16)
        hidden = jnp.dot(second, w_up, preferred_element_type=F32) + b_up
        active = gelu_exact(hidden).astype(BF16)
        partial = (
            jnp.dot(context_low, w_out, preferred_element_type=F32)
            + jnp.dot(active, w_down, preferred_element_type=F32)
        ).astype(BF16)
        summed = plane_reduce_scatter(partial.reshape(16, -1, width), "scatter_out", number)
        number += 1
        stream = stream + summed + b_last
        saved.append(
            (normed, inverse, normed_all, queries, pairs, context, logs, context_low, hidden, active)
        )
    output = stream.astype(BF16)[None]

    grad = cotangent[0].astype(F32)
    grads = [None] * layers
    for layer in reversed(range(layers)):
        gain, shift, w_qkv, b_qkv, w_out, w_up, b_up, w_down, b_last = weights[layer]
        normed, inverse, normed_all, queries, pairs, context, logs, context_low, hidden, active = (
            saved[layer]
        )
        branch = grad.astype(BF16)
        branch_bias = jnp.sum(branch.astype(F32), 0)
        branch_all = plane_all_gather(branch, "gather_branch", number).reshape(-1, width)
        number += 1
        out_grad = dots(context_low, branch_all, 0, 0)
        down_grad = dots(active, branch_all, 0, 0)
        context_grad = dots(branch_all, w_out, 1, 1).astype(BF16)
        active_grad = dots(branch_all, w_down, 1, 1)
        unused, gelu_pull = jax.vjp(gelu_exact, hidden)
        hidden_grad = gelu_pull(active_grad)[0].astype(BF16)
        up_raw = dots(normed_all, hidden_grad, 0, 0)
        up_bias_grad = jnp.sum(hidden_grad.astype(F32), 0)
        offsets = jnp.sum(context_grad.astype(F32) * context[:, HEAD:], 1, keepdims=True)
        lane = lax.broadcasted_iota(jnp.int32, (1, 2 * HEAD), 1)
        stats = jnp.where(lane == 0, logs, offsets)
        pull = jnp.concatenate([jnp.zeros_like(context_grad), context_grad], 1)
        query_grad, pair_grads = attend_back(
            source, order, sorted_numbers, queries, pairs, pull, stats
        )
        own_rows = queries.shape[0]
        pair_grad = pair_grads[:own_rows].astype(F32) + swap(pair_grads[own_rows:]).astype(F32)
        mixed_grad = jnp.concatenate(
            [
                rope(query_grad[:, :HEAD] * 0.125, cosines, -sines),
                rope(pair_grad[:, :HEAD], cosines, -sines),
                pair_grad[:, HEAD:],
            ],
            1,
        ).astype(BF16)
        qkv_raw = dots(normed_all, mixed_grad, 0, 0)
        qkv_bias_grad = jnp.sum(mixed_grad.astype(F32), 0)
        first_grad = dots(mixed_grad, w_qkv, 1, 1)
        second_grad = dots(hidden_grad, w_up, 1, 1)
        partial = (first_grad * gain[0] + second_grad * gain[1]).astype(BF16)
        normed_grad = plane_reduce_scatter(
            partial.reshape(16, -1, width), "scatter_normed", number
        )
        number += 1
        grad = grad + inverse * (
            normed_grad
            - jnp.mean(normed_grad, -1, keepdims=True)
            - normed * jnp.mean(normed_grad * normed, -1, keepdims=True)
        )
        full_qkv, full_up = w_qkv.astype(F32), w_up.astype(F32)
        vector_parts = jnp.stack(
            [
                jnp.sum(full_qkv * qkv_raw, 1),
                jnp.sum(full_up * up_raw, 1),
                jnp.sum(full_qkv * qkv_bias_grad, 1),
                jnp.sum(full_up * up_bias_grad, 1),
                branch_bias,
            ]
        )
        qkv_grad = qkv_raw * gain[0][:, None] + shift[0][:, None] * qkv_bias_grad
        up_grad = up_raw * gain[1][:, None] + shift[1][:, None] * up_bias_grad
        grads[layer] = (
            jnp.concatenate([qkv_grad, up_grad], 1),
            down_grad,
            out_grad,
            vector_parts,
            qkv_bias_grad,
            up_bias_grad,
        )

    wide_grad, down_grad, out_grad, vector_grad, qkv_bias_grad, up_bias_grad = (
        jnp.stack([grads[layer][i] for layer in range(layers)]) for i in range(6)
    )
    wide_grad = lax.psum_scatter(
        wide_grad.astype(BF16), "fsdp", scatter_dimension=1, tiled=True
    )
    down_grad = lax.psum_scatter(
        down_grad.astype(BF16), "fsdp", scatter_dimension=1, tiled=True
    )
    out_grad = lax.psum(out_grad.astype(BF16), "fsdp")
    tall_grad = jnp.concatenate([down_grad, out_grad], 1)
    wide_grad = (wide_grad.astype(F32) + swap(wide_grad).astype(F32)).astype(BF16)
    tall_grad = (tall_grad.astype(F32) + swap(tall_grad).astype(F32)).astype(BF16)
    wide_all = plane_all_gather(wide_grad.reshape(-1, 7 * HEAD), "gather_wide", number)
    number += 1
    tall_all = plane_all_gather(tall_grad.reshape(-1, width), "gather_tall", number)
    number += 1
    wide_all = wide_all.reshape(16, layers, quarter, 7, HEAD)
    wide_all = jnp.transpose(wide_all, (1, 2, 3, 0, 4)).reshape(layers, quarter, 7 * width)
    qkv_out = wide_all[:, :, : 3 * width].astype(F32)
    up_out = wide_all[:, :, 3 * width :].astype(F32)
    tall_all = tall_all.reshape(16, layers, 2, HEAD, width)
    tall_all = tall_all.astype(F32)
    down_out = jnp.transpose(tall_all[:, :, 0], (1, 0, 2, 3)).reshape(layers, width, width)
    out_out = jnp.transpose(
        lax.dynamic_slice_in_dim(tall_all[:, :, 1], shard * 4, 4, 0), (1, 0, 2, 3)
    ).reshape(layers, quarter, width)

    zeros = jnp.zeros((layers, 7, 16, HEAD), F32)
    biases = jnp.concatenate([qkv_bias_grad, up_bias_grad], 1).reshape(layers, 7, 1, HEAD)
    biases = lax.dynamic_update_slice_in_dim(zeros, biases, rank, 2).reshape(layers, -1)
    small = lax.psum(
        jnp.concatenate([vector_grad.reshape(layers, -1), biases], 1), ("ctx", "fsdp")
    )

    def mine(start, total):
        share = total // 4
        return lax.dynamic_slice_in_dim(small, start + shard * share, share, 1)

    gain_out = jnp.stack([mine(0, width), mine(width, width)], 1)
    shift_out = jnp.stack([mine(2 * width, width), mine(3 * width, width)], 1)
    branch_out = mine(4 * width, width)
    qkv_bias_out = mine(5 * width, 3 * width)
    up_bias_out = mine(8 * width, 4 * width)
    return (
        output,
        grad[None],
        gain_out,
        shift_out,
        qkv_out,
        qkv_bias_out,
        out_out,
        branch_out,
        up_out,
        up_bias_out,
        down_out,
        branch_out,
    )


def solution(mesh):
    rows = P("fsdp", "ctx", None)
    vector, matrix = P(None, "fsdp"), P(None, "fsdp", None)
    gains = P(None, None, "fsdp")
    params = (gains, gains) + (matrix, vector) * 4
    return jax.shard_map(
        on_device,
        mesh=mesh,
        in_specs=(rows, rows, P()) + params,
        out_specs=(rows, rows) + params,
        check_vma=False,
    )
```

```python
import functools

import jax
import jax.numpy as jnp
from jax import lax
from jax.experimental import pallas as pl
from jax.experimental.pallas import tpu as pltpu
from jax.sharding import PartitionSpec as P

HEADS = 16
HEAD = 64
ROT = 16
BLK = 64
SIDE = 4
EPS = 1e-05
NEGATIVE = -1e30
MESH = pl.DeviceIdType.MESH
F32 = jnp.float32
BF16 = jnp.bfloat16
TILE = 256
KEYS = 512
PART = 64
PARTS = 13
LANES = 256
OUT_PART = 11


def place():
    slot = lax.axis_index("ctx")
    return slot // 8, (slot // 2) % SIDE, slot % 2


def device(x, y, z):
    return {"ctx": ((x % SIDE) * SIDE + (y % SIDE)) * 2 + z}


class Grid:
    def __init__(self):
        self.x, self.y, self.z = place()

    def spot(self, half, dp, dq):
        dx, dy = (dp, dq) if half == 0 else (dq, dp)
        return (self.x + dx + SIDE) % SIDE, (self.y + dy + SIDE) % SIDE

    def rank(self, half, dp, dq):
        x, y = self.spot(half, dp, dq)
        return x * SIDE + y

    def device(self, half, dp, dq):
        x, y = self.spot(half, dp, dq)
        return device(x, y, self.z)

    def barrier(self, others=()):
        gate = pltpu.get_barrier_semaphore()
        partners = [self.device(0, *step) for step in ((1, 0), (-1, 0), (0, 1), (0, -1))]
        partners += others
        for partner in partners:
            pl.semaphore_signal(gate, inc=1, device_id=partner, device_id_type=MESH)
        pl.semaphore_wait(gate, len(partners))


def gather_half(grid, half, own_ref, all_ref, send_sem, recv_sem):
    rows = own_ref.shape[0]
    half_rows, quarter = rows // 2, rows // 4
    sends = []

    def view(dp, dq, low, count):
        return all_ref.at[grid.rank(half, dp, dq), pl.ds(half * half_rows + low, count)]

    def start(event, to, block, low, count, own=False):
        source = (
            own_ref.at[pl.ds(half * half_rows + low, count)]
            if own
            else view(*block, low, count)
        )
        copy = pltpu.make_async_remote_copy(
            src_ref=source,
            dst_ref=view(*block, low, count),
            send_sem=send_sem.at[half, event],
            recv_sem=recv_sem.at[half, event],
            device_id=grid.device(half, *to),
            device_id_type=MESH,
        )
        copy.start()
        sends.append(copy)

    def arrive(event, block, low, count):
        there = view(*block, low, count)
        pltpu.make_async_remote_copy(
            src_ref=there,
            dst_ref=there,
            send_sem=send_sem.at[half, event],
            recv_sem=recv_sem.at[half, event],
            device_id=grid.device(half, 1, 0),
            device_id_type=MESH,
        ).wait_recv()

    def spread(column, dp, own=False):
        start(4 + 4 * column, (0, 1), (dp, 0), 0, half_rows, own)
        start(5 + 4 * column, (0, -1), (dp, 0), 0, half_rows, own)

    start(0, (1, 0), (0, 0), 0, half_rows, True)
    start(1, (-1, 0), (0, 0), 0, half_rows, True)
    spread(0, 0, True)
    yield
    arrive(0, (-1, 0), 0, half_rows)
    start(2, (1, 0), (-1, 0), 0, quarter)
    spread(1, -1)
    arrive(1, (1, 0), 0, half_rows)
    start(3, (-1, 0), (1, 0), quarter, quarter)
    spread(2, 1)
    yield
    arrive(2, (2, 0), 0, quarter)
    arrive(3, (2, 0), quarter, quarter)
    spread(3, 2)
    yield
    steps = (0, -1, 1, 2)
    for column in range(4):
        arrive(4 + 4 * column, (steps[column], -1), 0, half_rows)
        start(6 + 4 * column, (0, 1), (steps[column], -1), 0, quarter)
        arrive(5 + 4 * column, (steps[column], 1), 0, half_rows)
        start(7 + 4 * column, (0, -1), (steps[column], 1), quarter, quarter)
        yield
    for column in range(4):
        arrive(6 + 4 * column, (steps[column], 2), 0, quarter)
        arrive(7 + 4 * column, (steps[column], 2), quarter, quarter)
        if column % 2 == 0:
            yield
    for copy in sends:
        copy.wait_send()


GATHER_STEPS = 10


def gather_steps(grid, own_ref, all_ref, send_sem, recv_sem):
    halves = [
        gather_half(grid, half, own_ref, all_ref, send_sem, recv_sem) for half in (0, 1)
    ]
    for step in range(GATHER_STEPS):
        for half in halves:
            next(half, None)
        if step < GATHER_STEPS - 1:
            yield


def run(steps, count=None):
    while count is None or count > 0:
        if next(steps, StopIteration) is StopIteration:
            return
        count = None if count is None else count - 1


def scatter_steps(grid, part_ref, out_ref, land_half, land_full, stage, total, send_sem, recv_sem):
    rows = part_ref.shape[1]
    half_rows, quarter = rows // 2, rows // 4
    sends = []
    steps = (2, -1, 1, 0)

    def start(half, event, source, target, to):
        copy = pltpu.make_async_remote_copy(
            src_ref=source,
            dst_ref=target,
            send_sem=send_sem.at[half, event],
            recv_sem=recv_sem.at[half, event],
            device_id=grid.device(half, *to),
            device_id_type=MESH,
        )
        copy.start()
        sends.append(copy)

    def arrive(half, event, target):
        pltpu.make_async_remote_copy(
            src_ref=target,
            dst_ref=target,
            send_sem=send_sem.at[half, event],
            recv_sem=recv_sem.at[half, event],
            device_id=grid.device(half, 1, 0),
            device_id_type=MESH,
        ).wait_recv()

    def first(half, column):
        def piece(dq, low, count):
            return part_ref.at[
                grid.rank(half, steps[column], dq), pl.ds(half * half_rows + low, count)
            ]

        return piece

    def second(half):
        return lambda dp, low, count: total.at[half, steps.index(dp), pl.ds(low, count)]

    def along(step):
        return (0, step)

    def across(step):
        return (step, 0)

    def opposite(half, column, piece, step):
        for side, low in ((0, 0), (1, quarter)):
            start(
                half,
                4 * column + side,
                piece(2, low, quarter),
                land_half.at[half, column, side],
                step(1 - 2 * side),
            )

    def neighbours(half, column, piece, step):
        for side in (0, 1):
            land = land_half.at[half, column, side]
            arrive(half, 4 * column + side, land)
            low, other = side * quarter, (1 - side) * quarter
            toward = 1 - 2 * side
            stage[half, column, side, low : low + quarter] = (
                piece(toward, low, quarter)[...].astype(F32) + land[...].astype(F32)
            ).astype(BF16)
            stage[half, column, side, other : other + quarter] = piece(toward, other, quarter)[...]
            start(
                half,
                4 * column + 2 + side,
                stage.at[half, column, side],
                land_full.at[half, column, side],
                step(toward),
            )

    def settle(half, column, own):
        for side in (0, 1):
            arrive(half, 4 * column + 2 + side, land_full.at[half, column, side])
        return (
            own[...].astype(F32)
            + land_full[half, column, 0].astype(F32)
            + land_full[half, column, 1].astype(F32)
        )

    for column in range(4):
        for half in (0, 1):
            opposite(half, column, first(half, column), along)
    yield
    for column in range(4):
        for half in (0, 1):
            neighbours(half, column, first(half, column), along)
        if column % 2:
            yield
    for column in range(4):
        for half in (0, 1):
            total[half, column] = settle(
                half, column, first(half, column)(0, 0, half_rows)
            ).astype(BF16)
            if column == 0:
                opposite(half, 4, second(half), across)
            if column == 2:
                neighbours(half, 4, second(half), across)
        yield
    for half in (0, 1):
        out_ref[pl.ds(half * half_rows, half_rows)] = settle(half, 4, total.at[half, 3])
    for copy in sends:
        copy.wait_send()


SCATTER_STEPS = 8


def scatter_scratch(rows, width):
    half_rows, quarter = rows // 2, rows // 4
    return [
        pltpu.VMEM((2, 5, 2, quarter, width), BF16),
        pltpu.VMEM((2, 5, 2, half_rows, width), BF16),
        pltpu.VMEM((2, 5, 2, half_rows, width), BF16),
        pltpu.VMEM((2, 4, half_rows, width), BF16),
        pltpu.SemaphoreType.DMA((2, 20)),
        pltpu.SemaphoreType.DMA((2, 20)),
    ]


def skip_two(index):
    return index + index // 2


def far_spot(index):
    inside = index < 4
    return jnp.where(inside, index, 2), jnp.where(inside, 2, skip_two(jnp.maximum(index - 4, 0)))


def near_spot(index):
    return skip_two(index // 3), skip_two(index % 3)


def over_places(grid, spot, count, body):
    def one(index, unused):
        dx, dy = spot(index)
        body(((grid.x + dx) % SIDE) * SIDE + (grid.y + dy) % SIDE)
        return unused

    lax.fori_loop(0, count, one, 0)


def follow(grid, gather, block, ready=None):
    def places(*steps):
        def spot(index):
            dx, dy = jnp.int32(steps[0][0]), jnp.int32(steps[0][1])
            for i in range(1, len(steps)):
                dx = jnp.where(index == i, steps[i][0], dx)
                dy = jnp.where(index == i, steps[i][1], dy)
            return dx, dy

        over_places(grid, spot, len(steps), block)

    run(gather, 2)
    if ready is not None:
        ready()
    places((0, 0))
    next(gather)
    places((0, 1), (0, 3), (1, 0), (3, 0))
    next(gather)
    next(gather)
    places((1, 1), (1, 3), (3, 1), (3, 3))
    next(gather)
    next(gather)
    places((0, 2), (2, 0))
    next(gather)
    places((1, 2), (3, 2), (2, 1), (2, 3))
    run(gather)
    places((2, 2))


SQRT_HALF = 0.7071067811865476
DENSITY = 0.3989422804014327


def standardize(stream):
    row_mean = jnp.mean(stream, -1, keepdims=True)
    centered = stream - row_mean
    spread = jnp.mean(centered * centered, -1, keepdims=True)
    inverse = lax.rsqrt(spread + EPS)
    return (centered * inverse, inverse)


def dots(a, b, da, db):
    return lax.dot_general(a, b, (((da,), (db,)), ((), ())), preferred_element_type=F32)


def rotate(values, cosines, sines):
    lane = lax.broadcasted_iota(jnp.int32, values.shape, 1)
    half_dims = ROT // 2
    up = pltpu.roll(values, 2 * HEAD - half_dims, 1)
    down = pltpu.roll(values, half_dims, 1)
    return values * cosines + jnp.where(lane < half_dims, -up, down) * sines


def block_rows(rank, rows):
    return pl.ds(pl.multiple_of(rank * rows, rows), rows)


def share_partners():
    shard = lax.axis_index("fsdp")
    return [{"fsdp": shard + 1 - 2 * (shard % 2)}, {"fsdp": (shard + 2) % 4}]


def share_steps(items, send_sem, recv_sem):
    shard = lax.axis_index("fsdp")
    sibling = shard + 1 - 2 * (shard % 2)
    mate = (shard + 2) % 4
    third = (sibling + 2) % 4
    sends = []

    def copy(item, source, target, event, to):
        return pltpu.make_async_remote_copy(
            src_ref=source,
            dst_ref=target,
            send_sem=send_sem.at[item, event],
            recv_sem=recv_sem.at[item, event],
            device_id={"fsdp": to},
            device_id_type=MESH,
        )

    def start(*args):
        made = copy(*args)
        made.start()
        sends.append(made)

    for item, (own, every) in enumerate(items):
        start(item, own, every.at[shard], 0, mate)
        start(item, own, every.at[shard], 1, sibling)
        every[shard] = own[...]
    yield
    for item, (own, every) in enumerate(items):
        copy(item, own, every.at[mate], 0, mate).wait_recv()
        start(item, every.at[mate], every.at[mate], 2, sibling)
        yield
    for item, (own, every) in enumerate(items):
        copy(item, own, every.at[sibling], 1, sibling).wait_recv()
        copy(item, own, every.at[third], 2, sibling).wait_recv()
        yield
    for made in sends:
        made.wait_send()


def share_sems(items):
    return [pltpu.SemaphoreType.DMA((items, 3)), pltpu.SemaphoreType.DMA((items, 3))]


def stack_tall(tall_all, tall_ref):
    for part in range(4):
        tall_ref[part * HEAD : (part + 1) * HEAD] = tall_all[part, :HEAD]
    tall_ref[4 * HEAD : 5 * HEAD] = jnp.zeros((HEAD, tall_ref.shape[1]), BF16)
    tall_ref[5 * HEAD :] = tall_all[place()[0], HEAD:]


def enter_kernel(shares, *refs):
    (stream_ref, scale_ref, bias_ref, cos_ref, sin_ref, given_ref), refs = refs[:6], refs[6:]
    (normed_ref, q_ref, kv_ref, active_ref, slope_ref), refs = refs[:5], refs[5:]
    if shares:
        (wide_ref, own, send_sem, recv_sem), share_refs = refs[:4], refs[4:]
    else:
        own, send_sem, recv_sem = refs
        wide_ref = given_ref
    grid = Grid()
    rows, width = stream_ref.shape
    own[...] = standardize(stream_ref[...])[0].astype(BF16)
    normed_ref[grid.rank(0, 0, 0)] = own[...]
    grid.barrier(share_partners() if shares else ())
    sharing = None
    if shares:
        sharing = share_steps([(given_ref, wide_ref)], *share_refs)
        next(sharing)
    gather = gather_steps(grid, own, normed_ref, send_sem, recv_sem)
    next(gather)

    def block(rank):
        place_rows = block_rows(rank, rows)
        plain = normed_ref[rank].astype(F32)
        first = (plain * scale_ref[0:1] + scale_ref[2:3]).astype(BF16)
        second = (plain * scale_ref[1:2] + scale_ref[3:4]).astype(BF16)
        weight = wide_ref[...].reshape(width, 8 * HEAD)
        mixed = dots(first, weight[:, : 4 * HEAD], 1, 0) + bias_ref[:, : 4 * HEAD]
        hidden = dots(second, weight[:, 4 * HEAD :], 1, 0) + bias_ref[:, 4 * HEAD :]
        cosines, sines = cos_ref[place_rows, :], sin_ref[place_rows, :]
        kv_ref[place_rows, :] = rotate(mixed[:, : 2 * HEAD], cosines, sines).astype(BF16)
        q_ref[place_rows, :] = (rotate(mixed[:, 2 * HEAD :], cosines, sines) * 0.125).astype(BF16)
        share = 0.5 * (1.0 + lax.erf(hidden * SQRT_HALF))
        active_ref[place_rows, :] = (hidden * share).astype(BF16)
        slope_ref[place_rows, :] = share + hidden * (DENSITY * jnp.exp(-0.5 * hidden * hidden))

    def ready():
        if shares:
            run(sharing)

    follow(grid, gather, block, ready)


def enter(stream, scale, bias, cosines, sines, wide, shares, number):
    rows, width = stream.shape
    total = 16 * rows
    shapes = [
        jax.ShapeDtypeStruct((16, rows, width), BF16),
        jax.ShapeDtypeStruct((total, 2 * HEAD), BF16),
        jax.ShapeDtypeStruct((total, 2 * HEAD), BF16),
        jax.ShapeDtypeStruct((total, 4 * HEAD), BF16),
        jax.ShapeDtypeStruct((total, 4 * HEAD), F32),
    ]
    scratch = [
        pltpu.VMEM((rows, width), BF16),
        pltpu.SemaphoreType.DMA((2, 20)),
        pltpu.SemaphoreType.DMA((2, 20)),
    ]
    if shares:
        shapes.append(jax.ShapeDtypeStruct((4,) + wide.shape, BF16))
        scratch += share_sems(1)
    return pl.pallas_call(
        functools.partial(enter_kernel, shares),
        out_shape=shapes,
        in_specs=[pl.BlockSpec(memory_space=pltpu.VMEM)] * 6,
        out_specs=[pl.BlockSpec(memory_space=pltpu.VMEM)] * len(shapes),
        scratch_shapes=scratch,
        name="enter",
        compiler_params=pltpu.CompilerParams(
            collective_id=number, has_side_effects=True, vmem_limit_bytes=48 << 20
        ),
    )(stream, scale, bias, cosines, sines, wide)


def leave_steps(
    grid, active_ref, context_ref, tall_ref, stream_ref, bias_ref, out_ref, parts, total_rows, scratch
):
    rows = stream_ref.shape[0]

    def block(rank):
        place_rows = block_rows(rank, rows)
        both = jnp.concatenate(
            [active_ref[place_rows, :], context_ref[place_rows, :].astype(BF16)], 1
        )
        parts[rank] = dots(both, tall_ref[...], 1, 0).astype(BF16)

    scatter = scatter_steps(grid, parts, total_rows, *scratch)
    over_places(grid, far_spot, 7, block)
    next(scatter)
    over_places(grid, near_spot, 9, block)
    yield
    yield from scatter
    out_ref[...] = (stream_ref[...] + total_rows[...] + bias_ref[...]).astype(out_ref.dtype)


def leave_kernel(*refs):
    given, (wide_own, tall_own), made = refs[:5], refs[5:7], refs[7:10]
    out_ref, wide_ref, tall_ref = made
    (parts, total_rows, tall_all), refs = refs[10:13], refs[13:]
    grid = Grid()
    grid.barrier(share_partners())
    sharing = share_steps([(wide_own, wide_ref), (tall_own, tall_all)], *refs[:2])
    next(sharing)
    steps = leave_steps(grid, *given, out_ref, parts, total_rows, refs[2:])
    run(steps, 4)
    run(sharing, 1)
    run(steps, 2)
    run(sharing, 1)
    run(steps)
    run(sharing)
    stack_tall(tall_all, tall_ref)


def leave(active, context, tall, stream, bias, wide_own, tall_own, number):
    rows, width = stream.shape
    vmem = pl.BlockSpec(memory_space=pltpu.VMEM)
    return pl.pallas_call(
        leave_kernel,
        out_shape=[
            jax.ShapeDtypeStruct((rows, width), F32),
            jax.ShapeDtypeStruct((4,) + wide_own.shape, BF16),
            jax.ShapeDtypeStruct((6 * HEAD, width), BF16),
        ],
        in_specs=[vmem] * 7,
        out_specs=[vmem] * 3,
        scratch_shapes=[
            pltpu.VMEM((16, rows, width), BF16),
            pltpu.VMEM((rows, width), F32),
            pltpu.VMEM((4,) + tall_own.shape, BF16),
        ]
        + share_sems(2)
        + scatter_scratch(rows, width),
        name="leave",
        compiler_params=pltpu.CompilerParams(
            collective_id=number, has_side_effects=True, vmem_limit_bytes=48 << 20
        ),
    )(active, context, tall, stream, bias, wide_own, tall_own)


def back_enter_kernel(gathers, folds, *refs):
    grad_ref, active_ref, context_ref, slope_ref, normed_ref, tall_ref = refs[:6]
    refs = refs[6:]
    if folds:
        (in_ref, quarter_ref), refs = refs[:2], refs[2:]
    pull_ref, offset_ref, hidden_ref, down_ref, out_ref, up_ref, up_bias_ref = refs[:7]
    refs = refs[7:]
    if folds:
        (folded_ref,), refs = refs[:1], refs[1:]
    tall_sum, refs = refs[0], refs[1:]
    grid = Grid()
    tall_sum[...] = jnp.zeros_like(tall_sum)
    up_ref[...] = jnp.zeros_like(up_ref)
    up_bias_ref[...] = jnp.zeros_like(up_bias_ref)
    rows = grad_ref.shape[-2]

    if gathers:
        own, all_rows, send_sem, recv_sem = refs[:4]
        refs = refs[4:]
        own[...] = grad_ref[...].astype(BF16)
        all_rows[grid.rank(0, 0, 0)] = own[...]
        if folds:
            fold_barrier(grid)
        else:
            grid.barrier()
        gather = gather_steps(grid, own, all_rows, send_sem, recv_sem)
        next(gather)
    else:
        all_rows = grad_ref

    def block(rank):
        place_rows = block_rows(rank, rows)
        branch = all_rows[rank]
        back = dots(branch, tall_ref[...], 1, 1)
        hidden_grad = (back[:, : 4 * HEAD] * slope_ref[place_rows, :]).astype(BF16)
        pull = back[:, 4 * HEAD :].astype(BF16)
        hidden_ref[place_rows, :] = hidden_grad
        pull_ref[place_rows, :] = pull
        context = context_ref[place_rows, :]
        offset = jnp.sum(pull.astype(F32) * context, 1, keepdims=True)
        offset_ref[place_rows, :] = jnp.broadcast_to(offset, (rows, 2 * HEAD))
        both = jnp.concatenate([active_ref[place_rows, :], context.astype(BF16)], 1)
        ones = jnp.ones((rows, 2 * HEAD), BF16)
        tall_sum[...] += dots(both, branch, 0, 0)
        up_ref[...] += dots(hidden_grad, normed_ref[rank], 0, 0)
        up_bias_ref[...] += dots(hidden_grad, ones, 0, 0)

    if gathers:
        if folds:
            fold = fold_steps(grid, in_ref, quarter_ref, folded_ref, refs)
            next(fold)

            def together():
                for step in range(1, GATHER_STEPS):
                    run(gather, 1)
                    if step in (1, 4, 6, 8, 9):
                        run(fold, 1)
                    yield
                run(gather)
                run(fold)

            follow(grid, together(), block)
        else:
            follow(grid, gather, block)
    else:

        def one(rank, unused):
            block(rank)
            return unused

        lax.fori_loop(0, 16, one, 0)
    for shard in range(4):
        for lanes in range(4):
            down_ref[shard, lanes * HEAD : (lanes + 1) * HEAD] = tall_sum[
                shard * HEAD : (shard + 1) * HEAD, lanes * LANES : (lanes + 1) * LANES
            ].astype(BF16)
            low = 5 * HEAD + shard * 16
            out_ref[shard, lanes * 16 : (lanes + 1) * 16] = tall_sum[
                low : low + 16, lanes * LANES : (lanes + 1) * LANES
            ].astype(BF16)


def back_enter(grad, active, context, slope, normed, tall, number=None, folding=None):
    rows, width = grad.shape[-2:]
    total = 16 * rows
    vmem = pl.BlockSpec(memory_space=pltpu.VMEM)
    given = [grad, active, context, slope, normed, tall]
    shapes = [
        jax.ShapeDtypeStruct((total, 2 * HEAD), BF16),
        jax.ShapeDtypeStruct((total, 2 * HEAD), F32),
        jax.ShapeDtypeStruct((total, 4 * HEAD), BF16),
        jax.ShapeDtypeStruct((4, 4 * HEAD, LANES), BF16),
        jax.ShapeDtypeStruct((4, HEAD, LANES), BF16),
        jax.ShapeDtypeStruct((4 * HEAD, width), F32),
        jax.ShapeDtypeStruct((4 * HEAD, 2 * HEAD), F32),
    ]
    scratch = [pltpu.VMEM((6 * HEAD, width), F32)]
    params = dict(vmem_limit_bytes=48 << 20)
    if number is not None:
        params.update(collective_id=number, has_side_effects=True)
        scratch += [
            pltpu.VMEM((rows, width), BF16),
            pltpu.VMEM((16, rows, width), BF16),
            pltpu.SemaphoreType.DMA((2, 20)),
            pltpu.SemaphoreType.DMA((2, 20)),
        ]
    if folding is not None:
        given += list(folding)
        shapes.append(jax.ShapeDtypeStruct(folding[0].shape[1:], BF16))
        scratch += fold_scratch(folding[0].shape[1])
    return pl.pallas_call(
        functools.partial(back_enter_kernel, number is not None, folding is not None),
        out_shape=shapes,
        in_specs=[vmem] * len(given),
        out_specs=[vmem] * len(shapes),
        scratch_shapes=scratch,
        name="back_enter",
        compiler_params=pltpu.CompilerParams(**params),
    )(*given)


def back_leave_kernel(
    query_grad_ref,
    pair_grad_ref,
    hidden_ref,
    normed_ref,
    wide_ref,
    scale_ref,
    cos_ref,
    sin_ref,
    stream_ref,
    grad_ref,
    up_ref,
    up_bias_ref,
    down_ref,
    new_ref,
    addend_ref,
    mixed,
    raw,
    raw_bias,
    parts,
    total_rows,
    *scratch,
):
    grid = Grid()
    rows, width = stream_ref.shape
    grid.barrier()
    lane = lax.broadcasted_iota(jnp.int32, (rows, 2 * HEAD), 1)
    ones = jnp.ones((rows, 2 * HEAD), BF16)

    def block(rank):
        place_rows = block_rows(rank, rows)
        cosines, sines = cos_ref[place_rows, :], -sin_ref[place_rows, :]
        pair = pair_grad_ref[place_rows, :]
        query = jnp.where(lane < HEAD, query_grad_ref[place_rows, :] * 0.125, 0.0)
        both = jnp.concatenate(
            [rotate(pair, cosines, sines), rotate(query, cosines, sines)], 1
        ).astype(BF16)
        mixed[place_rows, :] = both
        first = dots(both, wide_ref[:, : 4 * HEAD], 1, 1)
        second = dots(hidden_ref[place_rows, :], wide_ref[:, 4 * HEAD :], 1, 1)
        parts[rank] = (first * scale_ref[0:1] + second * scale_ref[1:2]).astype(BF16)

    scatter = scatter_steps(grid, parts, total_rows, *scratch)
    over_places(grid, far_spot, 7, block)
    next(scatter)
    over_places(grid, near_spot, 9, block)
    next(scatter)
    raw[...] = jnp.zeros_like(raw)
    raw_bias[...] = jnp.zeros_like(raw_bias)

    def sums(first, count):
        def one(rank, unused):
            place_rows = block_rows(rank, rows)
            both = mixed[place_rows, :]
            raw[...] += dots(both, normed_ref[rank], 0, 0)
            raw_bias[...] += dots(both, ones, 0, 0)
            return unused

        lax.fori_loop(first, first + count, one, 0)

    sums(0, 4)
    next(scatter)
    sums(4, 4)
    next(scatter)
    sums(8, 4)
    next(scatter)
    sums(12, 4)
    next(scatter)

    wide_t = jnp.transpose(wide_ref[:, : 4 * HEAD].astype(F32))
    up_t = jnp.transpose(wide_ref[:, 4 * HEAD :].astype(F32))
    mixed_bias, up_bias = raw_bias[:, 0:1], up_bias_ref[:, 0:1]
    first_raw, second_raw = raw[...], up_ref[...]
    vectors = [
        jnp.sum(wide_t * first_raw, 0, keepdims=True),
        jnp.sum(up_t * second_raw, 0, keepdims=True),
        jnp.sum(wide_t * mixed_bias, 0, keepdims=True),
        jnp.sum(up_t * up_bias, 0, keepdims=True),
        jnp.sum(grad_ref[...].astype(BF16).astype(F32), 0, keepdims=True),
    ]
    first_grad = (first_raw * scale_ref[0:1] + mixed_bias * scale_ref[2:3]).astype(BF16)
    second_grad = (second_raw * scale_ref[1:2] + up_bias * scale_ref[3:4]).astype(BF16)
    biases = [
        jnp.transpose(raw_bias[...])[0:1],
        jnp.transpose(up_bias_ref[...])[0:1],
    ]
    for shard in range(4):
        lanes = slice(shard * LANES, (shard + 1) * LANES)
        addend_ref[shard, : 3 * PART] = first_grad[: 3 * PART, lanes]
        addend_ref[shard, 3 * PART : 7 * PART] = second_grad[:, lanes]
        addend_ref[shard, 7 * PART : OUT_PART * PART] = down_ref[shard]
        tail = jnp.concatenate(
            [jnp.zeros((PART, LANES), F32)]
            + [vector[:, lanes] for vector in vectors]
            + biases
            + [jnp.zeros((PART - 7, LANES), F32)],
            0,
        )
        addend_ref[shard, OUT_PART * PART :] = tail.astype(BF16)
    next(scatter)
    run(scatter)
    normed, inverse = standardize(stream_ref[...])
    normed_grad = total_rows[...]
    new_ref[...] = grad_ref[...] + inverse * (
        normed_grad
        - jnp.mean(normed_grad, -1, keepdims=True)
        - normed * jnp.mean(normed_grad * normed, -1, keepdims=True)
    )


def back_leave(given, rows, width, number):
    vmem = pl.BlockSpec(memory_space=pltpu.VMEM)
    total = 16 * rows
    return pl.pallas_call(
        back_leave_kernel,
        out_shape=[
            jax.ShapeDtypeStruct((rows, width), F32),
            jax.ShapeDtypeStruct((4, PARTS * PART, LANES), BF16),
        ],
        in_specs=[vmem] * len(given),
        out_specs=[vmem] * 2,
        scratch_shapes=[
            pltpu.VMEM((total, 4 * HEAD), BF16),
            pltpu.VMEM((4 * HEAD, width), F32),
            pltpu.VMEM((4 * HEAD, 2 * HEAD), F32),
            pltpu.VMEM((16, rows, width), BF16),
            pltpu.VMEM((rows, width), F32),
        ]
        + scatter_scratch(rows, width),
        name="back_leave",
        compiler_params=pltpu.CompilerParams(
            collective_id=number, has_side_effects=True, vmem_limit_bytes=56 << 20
        ),
    )(*given)


def fold_partners(grid):
    shard = lax.axis_index("fsdp")
    return [
        {"fsdp": shard + 1 - 2 * (shard % 2)},
        {"fsdp": (shard + 2) % 4},
        {"ctx": lax.axis_index("ctx") + 1 - 2 * grid.z},
    ]


def fold_barrier(grid):
    shard = lax.axis_index("fsdp")
    at_home = grid.x == shard
    gate = pltpu.get_barrier_semaphore()
    partners = [grid.device(0, *step) for step in ((1, 0), (-1, 0), (0, 1), (0, -1))]
    partners += fold_partners(grid)
    for partner in partners:
        pl.semaphore_signal(gate, inc=1, device_id=partner, device_id_type=MESH)
    for other in range(4):

        @pl.when(jnp.logical_not(at_home & (shard == other)))
        def greet():
            pl.semaphore_signal(
                gate,
                inc=1,
                device_id={"ctx": (shard * SIDE + grid.y) * 2 + grid.z, "fsdp": other},
                device_id_type=MESH,
            )

    pl.semaphore_wait(gate, len(partners) + 4 - at_home.astype(jnp.int32))


def fold_steps(grid, in_ref, quarter_ref, own, scratch):
    land_core, sums, land_low, pair, land_high, land_out = scratch[:6]
    core_sem, low_sem, high_sem, out_send, out_recv = scratch[6:]
    x, y, z = grid.x, grid.y, grid.z
    shard = lax.axis_index("fsdp")
    low, core = shard // 2, shard % 2
    away = 1 - low
    sibling, mate, far = fold_partners(grid)
    at_home = x == shard
    half_rows = in_ref.shape[1] // 2

    def remote(source, target, send, recv, to):
        return pltpu.make_async_remote_copy(
            src_ref=source,
            dst_ref=target,
            send_sem=send,
            recv_sem=recv,
            device_id=to,
            device_id_type=MESH,
        )

    def added(a, b):
        return (a.astype(F32) + b.astype(F32)).astype(BF16)

    def out_copy(column):
        return remote(
            quarter_ref.at[column],
            land_out.at[shard],
            out_send.at[column],
            out_recv.at[shard],
            {"ctx": (column * SIDE + y) * 2 + z, "fsdp": x},
        )

    spans = [pl.ds(half * half_rows, half_rows) for half in (0, 1)]
    core_copies, low_copies, high_copies = {}, [], []
    for half, span in enumerate(spans):
        for part in (0, 1):
            core_copies[half, part] = remote(
                in_ref.at[part * 2 + 1 - core, span],
                land_core.at[part, span],
                core_sem.at[0, half, part],
                core_sem.at[1, half, part],
                sibling,
            )
            core_copies[half, part].start()
    for column in range(4):

        @pl.when(jnp.logical_not(at_home & (x == column)))
        def give():
            out_copy(column).start()

        @pl.when(at_home & (x == column))
        def keep():
            land_out[shard] = quarter_ref[column]

    yield
    for half, span in enumerate(spans):
        for part in (0, 1):
            core_copies[half, part].wait_recv()
        sums[1, span] = added(in_ref[away * 2 + core, span], land_core[away, span])
        copy = remote(
            sums.at[1, span], land_low.at[span], low_sem.at[0, half], low_sem.at[1, half], mate
        )
        copy.start()
        low_copies.append(copy)
        sums[0, span] = added(in_ref[low * 2 + core, span], land_core[low, span])
    yield
    for half, span in enumerate(spans):
        low_copies[half].wait_recv()
        pair[span] = added(sums[0, span], land_low[span])
        if half == 1:
            for other in range(4):

                @pl.when(jnp.logical_not(at_home & (shard == other)))
                def take():
                    remote(
                        land_out.at[other],
                        land_out.at[other],
                        out_send.at[other],
                        out_recv.at[other],
                        mate,
                    ).wait_recv()

            total = land_out[0].astype(F32)
            for other in range(1, 4):
                total = total + land_out[other].astype(F32)
            pair[OUT_PART * PART : (OUT_PART + 1) * PART] = total.astype(BF16)
        copy = remote(
            pair.at[span], land_high.at[span], high_sem.at[0, half], high_sem.at[1, half], far
        )
        copy.start()
        high_copies.append(copy)
        yield
    for half, span in enumerate(spans):
        high_copies[half].wait_recv()
        own[span] = added(pair[span], land_high[span])
        yield
    for copy in list(core_copies.values()) + low_copies + high_copies:
        copy.wait_send()
    for column in range(4):

        @pl.when(jnp.logical_not(at_home & (x == column)))
        def gone():
            out_copy(column).wait_send()


FOLD_STEPS = 7


def fold_scratch(rows):
    block = (rows, LANES)
    return [
        pltpu.VMEM((2,) + block, BF16),
        pltpu.VMEM((2,) + block, BF16),
        pltpu.VMEM(block, BF16),
        pltpu.VMEM(block, BF16),
        pltpu.VMEM(block, BF16),
        pltpu.VMEM((4, PART, LANES), BF16),
        pltpu.SemaphoreType.DMA((2, 2, 2)),
        pltpu.SemaphoreType.DMA((2, 2)),
        pltpu.SemaphoreType.DMA((2, 2)),
        pltpu.SemaphoreType.DMA((4,)),
        pltpu.SemaphoreType.DMA((4,)),
    ]


def sum_kernel(in_ref, quarter_ref, all_ref, own, local_sem, send_sem, recv_sem, *scratch):
    grid = Grid()
    fold_barrier(grid)
    fold = fold_steps(grid, in_ref, quarter_ref, own, scratch)
    me = grid.rank(0, 0, 0)
    half_rows = own.shape[0] // 2
    run(fold, 4)
    halves, keeps = [], []
    for half in (0, 1):
        run(fold, 1)
        span = pl.ds(half * half_rows, half_rows)
        keep = pltpu.make_async_copy(own.at[span], all_ref.at[me, span], local_sem.at[half])
        keep.start()
        keeps.append(keep)
        halves.append(gather_half(grid, half, own, all_ref, send_sem, recv_sem))
        run(halves[-1], 1)
        if half == 0:
            run(halves[0], 1)
    for step in range(GATHER_STEPS):
        for half in halves:
            run(half, 1)
    for keep in keeps:
        keep.wait()
    run(fold)


def sum_grads(addends, quarters, number):
    shards, rows, lanes = addends.shape
    return pl.pallas_call(
        sum_kernel,
        out_shape=jax.ShapeDtypeStruct((16, rows, lanes), BF16),
        in_specs=[pl.BlockSpec(memory_space=pltpu.VMEM)] * 2,
        out_specs=pl.BlockSpec(memory_space=pl.ANY),
        scratch_shapes=[
            pltpu.VMEM((rows, lanes), BF16),
            pltpu.SemaphoreType.DMA((2,)),
            pltpu.SemaphoreType.DMA((2, 20)),
            pltpu.SemaphoreType.DMA((2, 20)),
        ]
        + fold_scratch(rows),
        name="sum_grads",
        compiler_params=pltpu.CompilerParams(
            collective_id=number, has_side_effects=True, vmem_limit_bytes=40 << 20
        ),
    )(addends, quarters)


def turn_kernel(first_ref, second_ref, out_ref):
    layer = pl.program_id(0)

    @pl.when(layer == 0)
    def first():
        out_ref[0] = jnp.transpose(first_ref[...].astype(F32).reshape(-1, LANES))

    @pl.when(layer == 1)
    def second():
        out_ref[0] = jnp.transpose(second_ref[...].astype(F32).reshape(-1, LANES))


def turned_parts(gathered, first, count, turn=0):
    layers = len(gathered)

    def spec(own):
        return pl.BlockSpec(
            (16, PART, LANES),
            lambda i, j: (0, first + (jnp.where(i == own, j, own * 0) + turn) % count, 0),
        )

    return pl.pallas_call(
        turn_kernel,
        grid=(layers, count),
        out_shape=jax.ShapeDtypeStruct((layers, LANES, count * 16 * PART), F32),
        in_specs=[spec(own) for own in range(layers)],
        out_specs=pl.BlockSpec((1, LANES, 16 * PART), lambda i, j: (i, 0, j)),
        name="turned_parts",
        compiler_params=pltpu.CompilerParams(vmem_limit_bytes=24 << 20),
    )(*gathered)


def tall_kernel(down_one, down_two, out_one, out_two, down_ref, out_ref):
    layer = pl.program_id(0)

    def put(down_in, out_in):
        down_ref[0] = down_in[...].astype(F32).reshape(16 * PART, LANES)
        for x in range(4):
            for y in range(4):
                out_ref[0, pl.ds(y * HEAD + x * 16, 16)] = out_in[x * 4 + y].astype(F32)

    @pl.when(layer == 0)
    def first():
        put(down_one, out_one)

    @pl.when(layer == 1)
    def second():
        put(down_two, out_two)


def tall_parts(gathered):
    layers = len(gathered)
    width = 4 * LANES

    def step(i, j, own):
        return jnp.where(i == own, j, 0)

    return pl.pallas_call(
        tall_kernel,
        grid=(layers, 4),
        out_shape=[
            jax.ShapeDtypeStruct((layers, 16 * PART, width), F32),
            jax.ShapeDtypeStruct((layers, LANES, width), F32),
        ],
        in_specs=[
            pl.BlockSpec((16, PART, LANES), lambda i, j, own=own: (0, 7 + step(i, j, own), 0))
            for own in range(layers)
        ]
        + [
            pl.BlockSpec(
                (16, 16, LANES), lambda i, j, own=own: (0, OUT_PART * 4 + step(i, j, own), 0)
            )
            for own in range(layers)
        ],
        out_specs=[
            pl.BlockSpec((1, 16 * PART, LANES), lambda i, j: (i, 0, j)),
            pl.BlockSpec((1, LANES, LANES), lambda i, j: (i, 0, j)),
        ],
        name="tall_parts",
        compiler_params=pltpu.CompilerParams(vmem_limit_bytes=24 << 20),
    )(*gathered, *gathered)


SPAN = 1024
ATTEND_WORK = 88


def sort_in(source_ref, order_ref, target_ref, count):
    def body(i, unused):
        start = order_ref[i] * BLK
        target_ref[pl.ds(pl.multiple_of(i * BLK, BLK), BLK), :] = source_ref[
            pl.ds(start, BLK), :
        ]
        return unused

    lax.fori_loop(0, count, body, 0)


def block_numbers(number_ref, first, count, axis):
    if axis == 0:
        return jnp.concatenate(
            [jnp.full((BLK, 1), number_ref[first + i], jnp.int32) for i in range(count)], 0
        )
    lane = lax.broadcasted_iota(jnp.int32, (1, count * BLK), 1) // BLK
    numbers = jnp.zeros((1, count * BLK), jnp.int32)
    for i in range(count):
        numbers = jnp.where(lane == i, number_ref[first + i], numbers)
    return numbers


def far_partner():
    slot = lax.axis_index("ctx")
    return {"ctx": slot + 1 - 2 * (slot % 2)}


def far_copy(source, target, sems):
    return pltpu.make_async_remote_copy(
        src_ref=source,
        dst_ref=target,
        send_sem=sems.at[0],
        recv_sem=sems.at[1],
        device_id=far_partner(),
        device_id_type=MESH,
    )


def attend_steps(tables, q_ref, kv_ref, context_ref, qs, kvs, logs, scratch):
    order_ref, standing_ref, number_ref, other_ref = tables
    tops, totals, sums, sems = scratch
    sort_in(kv_ref, order_ref, kvs.at[0], 32)
    copy = far_copy(kvs.at[0], kvs.at[1], sems)
    copy.start()
    sort_in(q_ref, order_ref, qs, 32)
    tiles = qs.shape[0] // TILE
    row = lax.broadcasted_iota(jnp.int32, (TILE, TILE), 0)
    column = lax.broadcasted_iota(jnp.int32, (TILE, TILE), 1)
    yield 4

    def highest(scores):
        return jnp.max(scores, 1, keepdims=True)

    def weigh(scores, top, keys):
        weights = jnp.exp(scores - top)
        return jnp.sum(weights, 1, keepdims=True), dots(weights.astype(BF16), keys, 1, 0)

    def wide(vector):
        return jnp.broadcast_to(vector, (TILE, 2 * HEAD))

    def own_tile(tile):
        rows = slice(tile * TILE, (tile + 1) * TILE)
        queries, near = qs[rows, :], kvs[0, rows, :]
        parts = [(jnp.where(column <= row, dots(queries, near, 1, 1), NEGATIVE), near)]
        for low in range(0, tile * TILE, SPAN):
            keys = kvs[0, low : min(low + SPAN, tile * TILE), :]
            parts.append((dots(queries, keys, 1, 1), keys))
        top = highest(parts[0][0])
        for scores, keys in parts[1:]:
            top = jnp.maximum(top, highest(scores))
        total, weighted = 0.0, 0.0
        for scores, keys in parts:
            more, product = weigh(scores, top, keys)
            total, weighted = total + more, weighted + product
        tops[rows, :], totals[rows, :], sums[rows, :] = wide(top), wide(total), weighted

    def other_tile(tile, numbers):
        rows = slice(tile * TILE, (tile + 1) * TILE)
        queries = qs[rows, :]
        own = block_numbers(number_ref, tile * TILE // BLK, TILE // BLK, 0)
        half = tile // 4
        keys = kvs[1, half * SPAN : (half + 1) * SPAN, :]
        parts = [(jnp.where(numbers < own, dots(queries, keys, 1, 1), NEGATIVE), keys)]
        if half:
            keys = kvs[1, :SPAN, :]
            parts.append((dots(queries, keys, 1, 1), keys))
        old = tops[rows, :][:, 0:1]
        top = old
        for scores, keys in parts:
            top = jnp.maximum(top, highest(scores))
        scale = jnp.exp(old - top)
        total, weighted = totals[rows, :][:, 0:1] * scale, sums[rows, :] * scale
        for scores, keys in parts:
            more, product = weigh(scores, top, keys)
            total, weighted = total + more, weighted + product
        sums[rows, :] = weighted / total
        logs[rows, :] = wide(top + jnp.log(total))

    for tile in range(tiles):
        own_tile(tile)
        yield tile + 1
    copy.wait_recv()
    for half in (0, 1):
        numbers = block_numbers(other_ref, half * 16, 16, 1)
        for tile in range(half * 4, half * 4 + 4):
            other_tile(tile, numbers)
            yield 4 + 4 * half
    sort_in(sums, standing_ref, context_ref, 32)
    copy.wait_send()


def attend_scratch(rows):
    return [pltpu.VMEM((rows, 2 * HEAD), F32)] * 3 + [pltpu.SemaphoreType.DMA((2,))]


def attend_back_steps(
    tables, qs, kvs, logs, pull_ref, offset_ref, query_grad_ref, pair_grad_ref, scratch
):
    order_ref, standing_ref, number_ref, other_ref = tables
    pulls, offsets, turned, query_sums, pair_sums, away, land, sems = scratch
    sort_in(pull_ref, order_ref, pulls, 32)
    sort_in(offset_ref, order_ref, offsets, 32)
    pair_sums[...] = jnp.zeros_like(pair_sums)
    tiles = qs.shape[0] // TILE
    row = lax.broadcasted_iota(jnp.int32, (TILE, TILE), 0)
    column = lax.broadcasted_iota(jnp.int32, (TILE, TILE), 1)
    lane = lax.broadcasted_iota(jnp.int32, (TILE, 2 * HEAD), 1)
    yield 4

    def tile_part(tile, half, low, count, mask):
        rows = slice(tile * TILE, (tile + 1) * TILE)
        queries, pull = qs[rows, :], pulls[rows, :]
        keys = kvs[half, low : low + count, :]
        scores = dots(keys, queries, 1, 1)
        if mask is not None:
            scores = jnp.where(mask, scores, NEGATIVE)
        probs = jnp.exp(scores - turned[tile, 0:1])
        score_grad = (probs * (dots(keys, pull, 1, 1) - turned[tile, 1:2])).astype(BF16)
        pair_sums[half, low : low + count, :] += dots(score_grad, queries, 1, 0) + dots(
            probs.astype(BF16), pull, 1, 0
        )
        return dots(score_grad, keys, 0, 0)

    def other_tile(tile, numbers):
        rows = slice(tile * TILE, (tile + 1) * TILE)
        turned[tile] = jnp.transpose(
            jnp.where(lane == 0, logs[rows, :], offsets[rows, :])
        )[:8]
        own = block_numbers(number_ref, tile * TILE // BLK, TILE // BLK, 1)
        half = tile // 4
        grads = tile_part(tile, 1, half * SPAN, SPAN, numbers < own)
        if half:
            grads = grads + tile_part(tile, 1, 0, SPAN, None)
        query_sums[rows, :] = grads

    def own_tile(tile):
        rows = slice(tile * TILE, (tile + 1) * TILE)
        grads = query_sums[rows, :] + tile_part(tile, 0, tile * TILE, TILE, row <= column)
        for low in range(0, tile * TILE, SPAN):
            grads = grads + tile_part(tile, 0, low, min(SPAN, tile * TILE - low), None)
        query_sums[rows, :] = grads

    for half in (0, 1):
        numbers = block_numbers(other_ref, half * 16, 16, 0)
        for tile in range(half * 4, half * 4 + 4):
            other_tile(tile, numbers)
            yield 4 + 4 * half
    away[...] = pair_sums[1].astype(BF16)
    copy = far_copy(away, land, sems)
    copy.start()
    for tile in range(tiles):
        own_tile(tile)
        yield tile + 1
    sort_in(query_sums, standing_ref, query_grad_ref, 32)
    copy.wait_recv()
    pair_sums[0] += land[...].astype(F32)
    sort_in(pair_sums.at[0], standing_ref, pair_grad_ref, 32)
    copy.wait_send()


def attend_back_scratch(rows):
    block = (rows, 2 * HEAD)
    return [
        pltpu.VMEM(block, BF16),
        pltpu.VMEM(block, F32),
        pltpu.VMEM((rows // TILE, 8, TILE), F32),
        pltpu.VMEM(block, F32),
        pltpu.VMEM((2,) + block, F32),
        pltpu.VMEM(block, BF16),
        pltpu.VMEM(block, BF16),
        pltpu.SemaphoreType.DMA((2,)),
    ]


def take_turns(work, total, others):
    done = 0
    ran = [0] * len(others)
    for more in work:
        done += more
        for index, (steps, count) in enumerate(others):
            wanted = min(count, 1 + done * (count - 1) // total)
            run(steps, wanted - ran[index])
            ran[index] = wanted
    for steps, count in others:
        run(steps)


def attend_kernel(*refs):
    tables, (q_ref, kv_ref) = refs[:4], refs[4:6]
    context_ref, qs, kvs, logs = refs[6:10]
    Grid().barrier([far_partner()])
    run(attend_steps(tables, q_ref, kv_ref, context_ref, qs, kvs, logs, refs[10:]))


def attend_gather_kernel(*refs):
    tables, (q_ref, kv_ref, own_ref, tall_own) = refs[:4], refs[4:8]
    context_ref, qs, kvs, logs, all_ref, tall_ref = refs[8:14]
    (send_sem, recv_sem, tall_all), refs = refs[14:17], refs[17:]
    grid = Grid()
    grid.barrier([far_partner()] + share_partners())
    all_ref[grid.rank(0, 0, 0)] = own_ref[...]
    gather = gather_steps(grid, own_ref, all_ref, send_sem, recv_sem)
    work = attend_steps(tables, q_ref, kv_ref, context_ref, qs, kvs, logs, refs[2:])
    sharing = share_steps([(tall_own, tall_all)], *refs[:2])
    take_turns(work, ATTEND_WORK, [(gather, GATHER_STEPS), (sharing, 4)])
    stack_tall(tall_all, tall_ref)


def attend(tables, queries, pairs, number, own=None, tall=None):
    rows = queries.shape[0]
    smem, vmem = pl.BlockSpec(memory_space=pltpu.SMEM), pl.BlockSpec(memory_space=pltpu.VMEM)
    given = [queries, pairs]
    shapes = [
        jax.ShapeDtypeStruct((rows, 2 * HEAD), F32),
        jax.ShapeDtypeStruct((rows, 2 * HEAD), BF16),
        jax.ShapeDtypeStruct((2, rows, 2 * HEAD), BF16),
        jax.ShapeDtypeStruct((rows, 2 * HEAD), F32),
    ]
    scratch = []
    if own is not None:
        given += [own, tall]
        shapes.append(jax.ShapeDtypeStruct((16,) + own.shape, own.dtype))
        shapes.append(jax.ShapeDtypeStruct((6 * HEAD, tall.shape[1]), BF16))
        scratch = [pltpu.SemaphoreType.DMA((2, 20)), pltpu.SemaphoreType.DMA((2, 20))]
        scratch += [pltpu.VMEM((4,) + tall.shape, BF16)] + share_sems(1)
    return pl.pallas_call(
        attend_kernel if own is None else attend_gather_kernel,
        out_shape=shapes,
        in_specs=[smem] * 4 + [vmem] * len(given),
        out_specs=[vmem] * len(shapes),
        scratch_shapes=scratch + attend_scratch(rows),
        name="attend",
        compiler_params=pltpu.CompilerParams(
            collective_id=number, has_side_effects=True, vmem_limit_bytes=48 << 20
        ),
    )(*tables, *given)


def attend_back_leave_kernel(*refs):
    tables, given, made = refs[:4], refs[4:14], refs[14:17]
    qs, kvs, logs, pull_ref, offset_ref = given[:5]
    active_ref, context_ref, tall_ref, stream_ref, bias_ref = given[5:]
    query_grad_ref, pair_grad_ref, out_ref = made
    parts, total_rows = refs[17:19]
    scatter_refs, scratch = refs[19:25], refs[25:]
    grid = Grid()
    grid.barrier([far_partner()])
    scatter = leave_steps(
        grid, active_ref, context_ref, tall_ref, stream_ref, bias_ref, out_ref, parts, total_rows,
        scatter_refs,
    )
    work = attend_back_steps(
        tables, qs, kvs, logs, pull_ref, offset_ref, query_grad_ref, pair_grad_ref, scratch
    )
    take_turns(work, ATTEND_WORK, [(scatter, SCATTER_STEPS)])


def attend_back_gather_kernel(*refs):
    tables, given, made = refs[:4], refs[4:10], refs[10:13]
    qs, kvs, logs, pull_ref, offset_ref, own_ref = given
    query_grad_ref, pair_grad_ref, all_ref = made
    local_sem, send_sem, recv_sem = refs[13:16]
    grid = Grid()
    grid.barrier([far_partner()])
    keep = pltpu.make_async_copy(own_ref, all_ref.at[grid.rank(0, 0, 0)], local_sem)
    keep.start()
    gather = gather_steps(grid, own_ref, all_ref, send_sem, recv_sem)
    work = attend_back_steps(
        tables, qs, kvs, logs, pull_ref, offset_ref, query_grad_ref, pair_grad_ref, refs[16:]
    )
    take_turns(work, ATTEND_WORK, [(gather, GATHER_STEPS)])
    keep.wait()


def attend_back(tables, given, number, leaving=None, own=None):
    rows = given[0].shape[0]
    smem, vmem = pl.BlockSpec(memory_space=pltpu.SMEM), pl.BlockSpec(memory_space=pltpu.VMEM)
    shapes = [jax.ShapeDtypeStruct((rows, 2 * HEAD), F32)] * 2
    out_specs = [vmem] * 2
    if leaving is not None:
        kernel = attend_back_leave_kernel
        given = tuple(given) + tuple(leaving)
        own_rows, width = leaving[3].shape
        shapes.append(jax.ShapeDtypeStruct((own_rows, width), BF16))
        out_specs.append(vmem)
        scratch = [
            pltpu.VMEM((16, own_rows, width), BF16),
            pltpu.VMEM((own_rows, width), F32),
        ] + scatter_scratch(own_rows, width)
    else:
        kernel = attend_back_gather_kernel
        given = tuple(given) + (own,)
        shapes.append(jax.ShapeDtypeStruct((16,) + own.shape, own.dtype))
        out_specs.append(pl.BlockSpec(memory_space=pl.ANY))
        scratch = [
            pltpu.SemaphoreType.DMA,
            pltpu.SemaphoreType.DMA((2, 20)),
            pltpu.SemaphoreType.DMA((2, 20)),
        ]
    return pl.pallas_call(
        kernel,
        out_shape=shapes,
        in_specs=[smem] * 4 + [vmem] * len(given),
        out_specs=out_specs,
        scratch_shapes=scratch + attend_back_scratch(rows),
        name="attend_back",
        compiler_params=pltpu.CompilerParams(
            collective_id=number, has_side_effects=True, vmem_limit_bytes=56 << 20
        ),
    )(*tables, *given)


def block_tables(pair_table, z):
    slots = pair_table.shape[0]
    ranks = slots // 2
    index = jnp.arange(slots, dtype=jnp.int32)

    def plane(which):
        pairs = lax.dynamic_slice_in_dim(pair_table.reshape(ranks, 2), which, 1, 1)
        numbers = jnp.concatenate([pairs, 2 * slots - 1 - pairs], 1).reshape(-1)
        standing = jnp.sum((numbers[None, :] < numbers[:, None]).astype(jnp.int32), 1)
        chosen = (standing[None, :] == index[:, None]).astype(jnp.int32)
        order = jnp.sum(chosen * index[None, :], 1)
        return numbers, (order, standing, jnp.sum(chosen * numbers[None, :], 1))

    numbers, own = plane(z)
    return numbers, own + (plane(1 - z)[1][2],)


def rotation(positions):
    freqs = 10000.0 ** (-jnp.arange(0, ROT, 2, dtype=F32) / ROT)
    angles = positions.astype(F32)[:, None] * freqs[None, :]
    rest = ((0, 0), (0, 2 * HEAD - ROT))
    return (
        jnp.pad(jnp.concatenate([jnp.cos(angles)] * 2, -1), rest, constant_values=1.0),
        jnp.pad(jnp.concatenate([jnp.sin(angles)] * 2, -1), rest),
    )


def on_device(
    hidden_in,
    cotangent,
    pair_table,
    norm_gain,
    norm_bias,
    qkv_weight,
    qkv_bias,
    out_weight,
    out_bias,
    up_weight,
    up_bias,
    down_weight,
    down_bias,
):
    layers = norm_gain.shape[0]
    slot = lax.axis_index("ctx")
    shard = lax.axis_index("fsdp")
    rank, z = slot // 2, slot % 2
    width = hidden_in.shape[2]
    quarter = width // 4

    numbers, tables = block_tables(pair_table, z)
    positions = (
        numbers[:, None] * BLK + jnp.arange(BLK, dtype=jnp.int32)[None, :]
    ).reshape(-1)
    cosines, sines = rotation(positions)

    def columns(weight, part):
        return lax.dynamic_slice_in_dim(weight, part * width + rank * HEAD, HEAD, 2)

    wide = jnp.concatenate(
        [columns(qkv_weight, 1), columns(qkv_weight, 2), columns(qkv_weight, 0)]
        + [jnp.zeros((layers, quarter, HEAD), BF16)]
        + [columns(up_weight, part) for part in range(4)],
        2,
    )
    tall = jnp.concatenate(
        [
            lax.dynamic_slice_in_dim(down_weight, rank * HEAD, HEAD, 1),
            lax.dynamic_slice_in_dim(out_weight, (rank % 4) * HEAD, HEAD, 1),
        ],
        1,
    )
    vectors = lax.all_gather(
        jnp.concatenate(
            [
                norm_gain.reshape(layers, -1),
                norm_bias.reshape(layers, -1),
                qkv_bias,
                out_bias,
                up_bias,
                down_bias,
            ],
            1,
        ),
        "fsdp",
        axis=0,
    ).astype(F32)

    scales, wide_biases, last_biases = [], [], []
    for layer in range(layers):
        vector = vectors[:, layer]
        scales.append(
            jnp.transpose(vector[:, 0:1024].reshape(4, 4, 256), (1, 0, 2)).reshape(4, width)
        )
        b_qkv = lax.dynamic_slice_in_dim(
            vector[:, 1024:1792].reshape(3, 16, HEAD), rank, 1, 1
        ).reshape(3, HEAD)
        b_up = lax.dynamic_slice_in_dim(
            vector[:, 2048:3072].reshape(4, 16, HEAD), rank, 1, 1
        ).reshape(4 * HEAD)
        wide_biases.append(
            jnp.concatenate([b_qkv[1], b_qkv[2], b_qkv[0], jnp.zeros((HEAD,), F32), b_up])[None]
        )
        last_biases.append((vector[:, 1792:2048] + vector[:, 3072:3328]).reshape(1, width))

    number = 1
    stream = hidden_in[0].astype(F32)
    saved = []
    wide_all, tall_all = [None] * layers, [None] * layers
    for layer in range(layers):
        if layer == 0:
            *made, wide_all[0] = enter(
                stream, scales[0], wide_biases[0], cosines, sines, wide[0], True, number
            )
        else:
            made = enter(
                stream, scales[layer], wide_biases[layer], cosines, sines, wide_all[layer], False,
                number,
            )
        number += 1
        normed_all, queries, pairs, active, slope = made
        if layer == 0:
            context, queries, pairs, logs, branch_all, tall_all[0] = attend(
                tables, queries, pairs, number, cotangent[0], tall[0]
            )
        else:
            context, queries, pairs, logs = attend(tables, queries, pairs, number)
        number += 1
        saved.append((stream, normed_all, queries, pairs, active, slope, context, logs))
        leaving = (active, context, tall_all[layer], stream, last_biases[layer])
        if layer < layers - 1:
            stream, wide_all[layer + 1], tall_all[layer + 1] = leave(
                *leaving, wide[layer + 1], tall[layer + 1], number
            )
            number += 1

    grad = cotangent[0].astype(F32)
    gathered = [None] * layers
    addends = quarters = folded = None
    for layer in reversed(range(layers)):
        last = layer == layers - 1
        stream, normed_all, queries, pairs, active, slope, context, logs = saved[layer]
        if last:
            pull, offsets, hidden_grad, down_grad, new_quarters, up_raw, up_bias_raw = back_enter(
                branch_all, active, context, slope, normed_all, tall_all[layer]
            )
            query_grad, pair_grad, output = attend_back(
                tables, (queries, pairs, logs, pull, offsets), number, leaving
            )
        else:
            pull, offsets, hidden_grad, down_grad, new_quarters, up_raw, up_bias_raw, folded = (
                back_enter(
                    grad, active, context, slope, normed_all, tall_all[layer], number,
                    (addends, quarters),
                )
            )
            number += 1
            query_grad, pair_grad, gathered[layer + 1] = attend_back(
                tables, (queries, pairs, logs, pull, offsets), number, None, folded
            )
        number += 1
        grad, addends = back_leave(
            (
                query_grad,
                pair_grad,
                hidden_grad,
                normed_all,
                wide_all[layer].reshape(width, 8 * HEAD),
                scales[layer],
                cosines,
                sines,
                stream,
                grad,
                up_raw,
                up_bias_raw,
                down_grad,
            ),
            stream.shape[0],
            width,
            number,
        )
        quarters = new_quarters
        number += 1

    gathered[0] = sum_grads(addends, quarters, number)
    qkv_out = turned_parts(gathered, 0, 3, 2)
    up_out = turned_parts(gathered, 3, 4)
    down_out, out_out = tall_parts(gathered)
    small = jnp.stack(
        [every[:, (OUT_PART + 1) * PART : (OUT_PART + 1) * PART + 7] for every in gathered]
    ).astype(F32)
    sums = jnp.sum(small[:, :, :5], 1)
    gain_out, shift_out, branch_out = sums[:, 0:2], sums[:, 2:4], sums[:, 4]
    qkv_bias_out = jnp.transpose(
        jnp.roll(small[:, :, 5, : 3 * HEAD].reshape(layers, 16, 3, HEAD), 1, 2), (0, 2, 1, 3)
    ).reshape(layers, -1)
    share = qkv_bias_out.shape[1] // 4
    qkv_bias_out = lax.dynamic_slice_in_dim(qkv_bias_out, shard * share, share, 1)
    up_bias_out = lax.dynamic_slice_in_dim(
        small[:, :, 6].reshape(layers, 16, 4, HEAD), shard, 1, 2
    ).reshape(layers, -1)
    return (
        output[None],
        grad[None],
        gain_out,
        shift_out,
        qkv_out,
        qkv_bias_out,
        out_out,
        branch_out,
        up_out,
        up_bias_out,
        down_out,
        branch_out,
    )


def solution(mesh):
    rows = P("fsdp", "ctx", None)
    vector, matrix = P(None, "fsdp"), P(None, "fsdp", None)
    gains = P(None, None, "fsdp")
    params = (gains, gains) + (matrix, vector) * 4
    return jax.shard_map(
        on_device,
        mesh=mesh,
        in_specs=(rows, rows, P()) + params,
        out_specs=(rows, rows) + params,
        check_vma=False,
    )
```

```python
import functools

import jax
import jax.numpy as jnp
from jax import lax
from jax.experimental import pallas as pl
from jax.experimental.pallas import tpu as pltpu
from jax.sharding import PartitionSpec as P

HEADS = 16
HEAD = 64
ROT = 16
BLK = 64
SIDE = 4
EPS = 1e-05
NEGATIVE = -1e30
MESH = pl.DeviceIdType.MESH
F32 = jnp.float32
BF16 = jnp.bfloat16
TILE = 256
KEYS = 512
PART = 64
EARLY = 9 * PART
LATE = 4 * PART
LANES = 256


def place():
    slot = lax.axis_index("ctx")
    return slot // 8, (slot // 2) % SIDE, slot % 2


def device(x, y, z):
    return {"ctx": ((x % SIDE) * SIDE + (y % SIDE)) * 2 + z}


class Grid:
    def __init__(self, meets=((1, 0), (-1, 0), (0, 1), (0, -1))):
        self.x, self.y, self.z = place()
        self.meets = meets

    def spot(self, half, dp, dq):
        dx, dy = (dp, dq) if half == 0 else (dq, dp)
        return (self.x + dx + SIDE) % SIDE, (self.y + dy + SIDE) % SIDE

    def rank(self, half, dp, dq):
        x, y = self.spot(half, dp, dq)
        return x * SIDE + y

    def device(self, half, dp, dq):
        x, y = self.spot(half, dp, dq)
        return device(x, y, self.z)

    def barrier(self, others=()):
        gate = pltpu.get_barrier_semaphore()
        partners = [self.device(0, *step) for step in self.meets]
        partners += others
        for partner in partners:
            pl.semaphore_signal(gate, inc=1, device_id=partner, device_id_type=MESH)
        pl.semaphore_wait(gate, len(partners))


LARGE = 1 << 16


def size_of(array):
    return array.size * jnp.dtype(array.dtype).itemsize


def staged_call(body, name, number, given, shapes, scratch, tables=(), direct=()):
    loads = [i for i, array in enumerate(given) if size_of(array) > LARGE]
    stores = [i for i, shape in enumerate(shapes) if size_of(shape) > LARGE and i not in direct]
    counts = (len(tables), len(given), len(shapes), len(loads), len(stores))

    def kernel(*refs):
        refs, groups = list(refs), []
        for count in counts:
            groups.append(refs[:count])
            refs = refs[count:]
        table_refs, ins, outs, staged_in, staged_out = groups
        load_sem, store_sem, *refs = refs
        pending, homes = {}, {}
        for k, i in enumerate(loads):
            pending[i] = pltpu.make_async_copy(ins[i], staged_in[k], load_sem.at[k])
            pending[i].start()
            ins[i] = staged_in[k]
        for k, i in enumerate(stores):
            homes[i], outs[i] = outs[i], staged_out[k]

        def wait(*which):
            for i in which or sorted(pending):
                if i in pending:
                    pending.pop(i).wait()

        body(wait, table_refs, ins, outs, refs)
        wait()
        copies = [
            pltpu.make_async_copy(outs[i], homes[i], store_sem.at[k]) for k, i in enumerate(stores)
        ]
        for copy in copies:
            copy.start()
        for copy in copies:
            copy.wait()

    smem, vmem, hbm = (
        pl.BlockSpec(memory_space=space) for space in (pltpu.SMEM, pltpu.VMEM, pl.ANY)
    )
    far = set(stores) | set(direct)
    params = dict(vmem_limit_bytes=60 << 20)
    if number is not None:
        params.update(collective_id=number, has_side_effects=True)
    return pl.pallas_call(
        kernel,
        out_shape=list(shapes),
        in_specs=[smem] * len(tables)
        + [hbm if i in loads else vmem for i in range(len(given))],
        out_specs=[hbm if i in far else vmem for i in range(len(shapes))],
        scratch_shapes=[pltpu.VMEM(given[i].shape, given[i].dtype) for i in loads]
        + [pltpu.VMEM(shapes[i].shape, shapes[i].dtype) for i in stores]
        + [
            pltpu.SemaphoreType.DMA((max(len(loads), 1),)),
            pltpu.SemaphoreType.DMA((max(len(stores), 1),)),
        ]
        + list(scratch),
        name=name,
        compiler_params=pltpu.CompilerParams(**params),
    )(*tables, *given)


RINGS = ((1, 0), (-1, 0), (2, 0), (0, 1), (0, -1), (0, 2))


def gather_half(grid, half, own_ref, all_ref, send_sem, recv_sem):
    rows = own_ref.shape[0]
    half_rows, quarter = rows // 2, rows // 4
    sends = []

    def view(dp, dq, low, count):
        return all_ref.at[grid.rank(half, dp, dq), pl.ds(half * half_rows + low, count)]

    def start(event, to, block, low, count, own=False):
        source = (
            own_ref.at[pl.ds(half * half_rows + low, count)]
            if own
            else view(*block, low, count)
        )
        copy = pltpu.make_async_remote_copy(
            src_ref=source,
            dst_ref=view(*block, low, count),
            send_sem=send_sem.at[half, event],
            recv_sem=recv_sem.at[half, event],
            device_id=grid.device(half, *to),
            device_id_type=MESH,
        )
        copy.start()
        sends.append(copy)

    def arrive(event, block, low, count):
        there = view(*block, low, count)
        pltpu.make_async_remote_copy(
            src_ref=there,
            dst_ref=there,
            send_sem=send_sem.at[half, event],
            recv_sem=recv_sem.at[half, event],
            device_id=grid.device(half, 1, 0),
            device_id_type=MESH,
        ).wait_recv()

    def spread(column, dp, own=False):
        start(4 + 4 * column, (0, 1), (dp, 0), 0, half_rows, own)
        start(5 + 4 * column, (0, -1), (dp, 0), 0, half_rows, own)

    start(0, (1, 0), (0, 0), 0, half_rows, True)
    start(1, (-1, 0), (0, 0), 0, half_rows, True)
    spread(0, 0, True)
    yield
    arrive(0, (-1, 0), 0, half_rows)
    start(2, (1, 0), (-1, 0), 0, quarter)
    spread(1, -1)
    arrive(1, (1, 0), 0, half_rows)
    start(3, (-1, 0), (1, 0), quarter, quarter)
    spread(2, 1)
    yield
    arrive(2, (2, 0), 0, quarter)
    arrive(3, (2, 0), quarter, quarter)
    spread(3, 2)
    yield
    steps = (0, -1, 1, 2)
    for column in range(4):
        arrive(4 + 4 * column, (steps[column], -1), 0, half_rows)
        start(6 + 4 * column, (0, 1), (steps[column], -1), 0, quarter)
        arrive(5 + 4 * column, (steps[column], 1), 0, half_rows)
        start(7 + 4 * column, (0, -1), (steps[column], 1), quarter, quarter)
        yield
    for column in range(4):
        arrive(6 + 4 * column, (steps[column], 2), 0, quarter)
        arrive(7 + 4 * column, (steps[column], 2), quarter, quarter)
        if column % 2 == 0:
            yield
    for copy in sends:
        copy.wait_send()


GATHER_STEPS = 20


def gather_steps(grid, own_ref, all_ref, send_sem, recv_sem):
    halves = [
        gather_half(grid, half, own_ref, all_ref, send_sem, recv_sem) for half in (0, 1)
    ]
    for step in range(GATHER_STEPS):
        next(halves[step % 2], None)
        if step < GATHER_STEPS - 1:
            yield


DIRECT_STEPS = 8


def direct_steps(grid, own_ref, all_ref, send_sem, recv_sem):
    half_rows = own_ref.shape[0] // 2
    sends = []

    def view(half, dp, dq):
        return all_ref.at[grid.rank(half, dp, dq), pl.ds(half * half_rows, half_rows)]

    def copy(half, event, to, block, own=False):
        source = own_ref.at[pl.ds(half * half_rows, half_rows)] if own else view(half, *block)
        return pltpu.make_async_remote_copy(
            src_ref=source,
            dst_ref=view(half, *block),
            send_sem=send_sem.at[half, event],
            recv_sem=recv_sem.at[half, event],
            device_id=grid.device(half, *to),
            device_id_type=MESH,
        )

    def start(*args):
        made = copy(*args)
        made.start()
        sends.append(made)

    steps = (1, -1, 2)
    for index, step in enumerate(steps):
        for half in (0, 1):
            start(half, index, (step, 0), (0, 0), True)
    for index, step in enumerate(steps):
        for half in (0, 1):
            start(half, 3 + index, (0, step), (0, 0), True)
    yield
    for index, step in enumerate(steps):
        for half in (0, 1):
            copy(half, index, (step, 0), (-step, 0)).wait_recv()
            for other, move in enumerate(steps):
                start(half, 6 + 3 * index + other, (0, move), (-step, 0))
            yield
    for column, place_p in enumerate((0, -1, 1, -2)):
        for other, move in enumerate(steps):
            for half in (0, 1):
                copy(half, 3 + 3 * column + other, (0, move), (place_p, -move)).wait_recv()
    for made in sends:
        made.wait_send()


def run(steps, count=None):
    while count is None or count > 0:
        if next(steps, StopIteration) is StopIteration:
            return
        count = None if count is None else count - 1


def scatter_steps(
    grid, make, part_ref, out_ref, land_half, land_full, stage, total, send_sem, recv_sem
):
    rows = part_ref.shape[1]
    half_rows, quarter = rows // 2, rows // 4
    sends = []
    steps = (2, -1, 1, 0)

    def start(half, event, source, target, to):
        copy = pltpu.make_async_remote_copy(
            src_ref=source,
            dst_ref=target,
            send_sem=send_sem.at[half, event],
            recv_sem=recv_sem.at[half, event],
            device_id=grid.device(half, *to),
            device_id_type=MESH,
        )
        copy.start()
        sends.append(copy)

    def arrive(half, event, target):
        pltpu.make_async_remote_copy(
            src_ref=target,
            dst_ref=target,
            send_sem=send_sem.at[half, event],
            recv_sem=recv_sem.at[half, event],
            device_id=grid.device(half, 1, 0),
            device_id_type=MESH,
        ).wait_recv()

    def first(half, column):
        def piece(dq, low, count):
            return part_ref.at[
                grid.rank(half, steps[column], dq), pl.ds(half * half_rows + low, count)
            ]

        return piece

    def second(half):
        return lambda dp, low, count: total.at[half, steps.index(dp), pl.ds(low, count)]

    def along(step):
        return (0, step)

    def across(step):
        return (step, 0)

    def opposite(half, column, piece, step):
        for side, low in ((0, 0), (1, quarter)):
            start(
                half,
                4 * column + side,
                piece(2, low, quarter),
                land_half.at[half, column, side],
                step(1 - 2 * side),
            )

    def neighbours(half, column, piece, step):
        for side in (0, 1):
            land = land_half.at[half, column, side]
            arrive(half, 4 * column + side, land)
            low, other = side * quarter, (1 - side) * quarter
            toward = 1 - 2 * side
            stage[half, column, side, low : low + quarter] = (
                piece(toward, low, quarter)[...].astype(F32) + land[...].astype(F32)
            ).astype(BF16)
            stage[half, column, side, other : other + quarter] = piece(toward, other, quarter)[...]
            start(
                half,
                4 * column + 2 + side,
                stage.at[half, column, side],
                land_full.at[half, column, side],
                step(toward),
            )

    def settle(half, column, own):
        for side in (0, 1):
            arrive(half, 4 * column + 2 + side, land_full.at[half, column, side])
        return (
            own[...].astype(F32)
            + land_full[half, column, 0].astype(F32)
            + land_full[half, column, 1].astype(F32)
        )

    def places(*spots):
        make([grid.rank(0, dx, dy) for dx, dy in spots])

    def on_both(step, column, direction):
        for half in (0, 1):
            step(half, column, first(half, column), direction)

    places((2, 2))
    on_both(opposite, 0, along)
    for column in (1, 2, 3):
        places((steps[column], 2), (2, steps[column]))
        on_both(opposite, column, along)
        yield
    on_both(neighbours, 0, along)
    yield
    places((-1, -1), (-1, 1))
    places((1, -1), (1, 1))
    on_both(neighbours, 1, along)
    yield
    places((0, 1), (0, -1))
    on_both(neighbours, 2, along)
    yield
    places((1, 0), (-1, 0))
    on_both(neighbours, 3, along)
    yield
    places((0, 0))
    for column in range(4):
        for half in (0, 1):
            total[half, column] = settle(
                half, column, first(half, column)(0, 0, half_rows)
            ).astype(BF16)
            if column == 0:
                opposite(half, 4, second(half), across)
            if column == 2:
                neighbours(half, 4, second(half), across)
        yield
    for half in (0, 1):
        out_ref[pl.ds(half * half_rows, half_rows)] = settle(half, 4, total.at[half, 3])
    for copy in sends:
        copy.wait_send()


SCATTER_STEPS = 12


def scatter_scratch(rows, width):
    half_rows, quarter = rows // 2, rows // 4
    return [
        pltpu.VMEM((2, 5, 2, quarter, width), BF16),
        pltpu.VMEM((2, 5, 2, half_rows, width), BF16),
        pltpu.VMEM((2, 5, 2, half_rows, width), BF16),
        pltpu.VMEM((2, 4, half_rows, width), BF16),
        pltpu.SemaphoreType.DMA((2, 20)),
        pltpu.SemaphoreType.DMA((2, 20)),
    ]


def follow(grid, gather, block, ready=None):
    def places(*spots):
        block([grid.rank(0, dx, dy) for dx, dy in spots])

    run(gather, 4)
    if ready is not None:
        ready()
    places((0, 0))
    run(gather, 2)
    places((0, 1), (0, -1))
    run(gather, 2)
    places((1, 0), (-1, 0))
    run(gather, 2)
    places((1, 1), (1, -1))
    run(gather, 2)
    places((-1, 1), (-1, -1))
    run(gather, 2)
    places((0, 2), (2, 0))
    run(gather, 2)
    places((1, 2), (-1, 2))
    places((2, 1), (2, -1))
    run(gather)
    places((2, 2))


def rows_of(ref, ranks, rows):
    return jnp.concatenate([ref[block_rows(rank, rows), :] for rank in ranks], 0)


def put_rows(ref, ranks, rows, values):
    for index, rank in enumerate(ranks):
        ref[block_rows(rank, rows), :] = values[index * rows : (index + 1) * rows]


def blocks_of(ref, ranks):
    return jnp.concatenate([ref[rank] for rank in ranks], 0)


SQRT_HALF = 0.7071067811865476
DENSITY = 0.3989422804014327


def standardize(stream):
    row_mean = jnp.mean(stream, -1, keepdims=True)
    centered = stream - row_mean
    spread = jnp.mean(centered * centered, -1, keepdims=True)
    inverse = lax.rsqrt(spread + EPS)
    return (centered * inverse, inverse)


def dots(a, b, da, db):
    return lax.dot_general(a, b, (((da,), (db,)), ((), ())), preferred_element_type=F32)


def rotate(values, cosines, sines):
    lane = lax.broadcasted_iota(jnp.int32, values.shape, 1)
    half_dims = ROT // 2
    up = pltpu.roll(values, 2 * HEAD - half_dims, 1)
    down = pltpu.roll(values, half_dims, 1)
    return values * cosines + jnp.where(lane < half_dims, -up, down) * sines


def block_rows(rank, rows):
    return pl.ds(pl.multiple_of(rank * rows, rows), rows)


def share_partners():
    shard = lax.axis_index("fsdp")
    return [{"fsdp": shard + 1 - 2 * (shard % 2)}, {"fsdp": (shard + 2) % 4}]


def share_steps(items, send_sem, recv_sem):
    shard = lax.axis_index("fsdp")
    sibling = shard + 1 - 2 * (shard % 2)
    mate = (shard + 2) % 4
    third = (sibling + 2) % 4
    sends = []

    def copy(item, source, target, event, to):
        return pltpu.make_async_remote_copy(
            src_ref=source,
            dst_ref=target,
            send_sem=send_sem.at[item, event],
            recv_sem=recv_sem.at[item, event],
            device_id={"fsdp": to},
            device_id_type=MESH,
        )

    def start(*args):
        made = copy(*args)
        made.start()
        sends.append(made)

    for item, (own, every) in enumerate(items):
        start(item, own, every.at[shard], 0, mate)
        start(item, own, every.at[shard], 1, sibling)
        every[shard] = own[...]
    yield
    for item, (own, every) in enumerate(items):
        copy(item, own, every.at[mate], 0, mate).wait_recv()
        start(item, every.at[mate], every.at[mate], 2, sibling)
        yield
        copy(item, own, every.at[sibling], 1, sibling).wait_recv()
        copy(item, own, every.at[third], 2, sibling).wait_recv()
        yield
    for made in sends:
        made.wait_send()


def share_sems(items):
    return [pltpu.SemaphoreType.DMA((items, 3)), pltpu.SemaphoreType.DMA((items, 3))]


def stack_tall(tall_all, tall_ref):
    for part in range(4):
        tall_ref[part * HEAD : (part + 1) * HEAD] = tall_all[part, :HEAD]
    tall_ref[4 * HEAD : 5 * HEAD] = jnp.zeros((HEAD, tall_ref.shape[1]), BF16)
    tall_ref[5 * HEAD :] = tall_all[place()[0], HEAD:]


def enter_body(shares, wait, tables, ins, outs, refs):
    stream_ref, scale_ref, bias_ref, cos_ref, sin_ref, given_ref = ins[:6]
    homes = outs[:5]
    (normed_ref, q_ref, kv_ref, active_ref, slope_ref), refs = refs[:5], refs[5:]
    (own, keep_sem, send_sem, recv_sem), share_refs = refs[:4], refs[4:]
    wide_ref = outs[5] if shares else given_ref
    grid = Grid()
    rows, width = stream_ref.shape
    wait(0)
    own[...] = standardize(stream_ref[...])[0].astype(BF16)
    normed_ref[grid.rank(0, 0, 0)] = own[...]
    grid.barrier(share_partners() if shares else ())
    sharing = None
    if shares:
        wait(5, 6)
        tall_all, *share_sems = share_refs
        sharing = share_steps([(given_ref, wide_ref), (ins[6], tall_all)], *share_sems)
        next(sharing)
    gather = gather_steps(grid, own, normed_ref, send_sem, recv_sem)
    run(gather, 2)
    keeps, done = [], []

    def block(ranks):
        plain = blocks_of(normed_ref, ranks).astype(F32)
        first = (plain * scale_ref[0:1] + scale_ref[2:3]).astype(BF16)
        second = (plain * scale_ref[1:2] + scale_ref[3:4]).astype(BF16)
        weight = wide_ref[...].reshape(width, 8 * HEAD)
        mixed = dots(first, weight[:, : 4 * HEAD], 1, 0) + bias_ref[:, : 4 * HEAD]
        hidden = dots(second, weight[:, 4 * HEAD :], 1, 0) + bias_ref[:, 4 * HEAD :]
        cosines, sines = rows_of(cos_ref, ranks, rows), rows_of(sin_ref, ranks, rows)
        pairs = rotate(mixed[:, : 2 * HEAD], cosines, sines)
        queries = rotate(mixed[:, 2 * HEAD :], cosines, sines) * 0.125
        put_rows(kv_ref, ranks, rows, pairs.astype(BF16))
        put_rows(q_ref, ranks, rows, queries.astype(BF16))
        share = 0.5 * (1.0 + lax.erf(hidden * SQRT_HALF))
        put_rows(active_ref, ranks, rows, (hidden * share).astype(BF16))
        slope = share + hidden * (DENSITY * jnp.exp(-0.5 * hidden * hidden))
        put_rows(slope_ref, ranks, rows, slope)
        for rank in ranks:
            place_rows, event = block_rows(rank, rows), len(done)
            done.append(rank)
            keep = pltpu.make_async_copy(
                normed_ref.at[rank], homes[0].at[rank], keep_sem.at[0, event]
            )
            keep.start()
            keeps.append(keep)
            for index, made in enumerate((q_ref, kv_ref, active_ref, slope_ref), 1):
                keep = pltpu.make_async_copy(
                    made.at[place_rows], homes[index].at[place_rows], keep_sem.at[index, event]
                )
                keep.start()
                keeps.append(keep)

    def ready():
        if shares:
            run(sharing, 2)
        wait()

    follow(grid, gather, block, ready)
    if shares:
        run(sharing)
        stack_tall(tall_all, outs[6])
    for keep in keeps:
        keep.wait()


def enter(stream, scale, bias, cosines, sines, wide, tall, number):
    rows, width = stream.shape
    total = 16 * rows
    shapes = [
        jax.ShapeDtypeStruct((16, rows, width), BF16),
        jax.ShapeDtypeStruct((total, 2 * HEAD), BF16),
        jax.ShapeDtypeStruct((total, 2 * HEAD), BF16),
        jax.ShapeDtypeStruct((total, 4 * HEAD), BF16),
        jax.ShapeDtypeStruct((total, 4 * HEAD), F32),
    ]
    scratch = [pltpu.VMEM(shape.shape, shape.dtype) for shape in shapes]
    scratch += [
        pltpu.VMEM((rows, width), BF16),
        pltpu.SemaphoreType.DMA((5, 16)),
        pltpu.SemaphoreType.DMA((2, 20)),
        pltpu.SemaphoreType.DMA((2, 20)),
    ]
    given = [stream, scale, bias, cosines, sines, wide]
    if tall is not None:
        given.append(tall)
        shapes.append(jax.ShapeDtypeStruct((4,) + wide.shape, BF16))
        shapes.append(jax.ShapeDtypeStruct((6 * HEAD, width), BF16))
        scratch += [pltpu.VMEM((4,) + tall.shape, BF16)] + share_sems(2)
    body = functools.partial(enter_body, tall is not None)
    return staged_call(body, "enter", number, given, shapes, scratch, direct=range(5))


def leave_steps(
    grid, active_ref, context_ref, tall_ref, stream_ref, bias_ref, out_ref, parts, total_rows, scratch
):
    rows = stream_ref.shape[0]

    def make(ranks):
        context = rows_of(context_ref, ranks, rows).astype(BF16)
        both = jnp.concatenate([rows_of(active_ref, ranks, rows), context], 1)
        made = dots(both, tall_ref[...], 1, 0).astype(BF16)
        for index, rank in enumerate(ranks):
            parts[rank] = made[index * rows : (index + 1) * rows]

    yield from scatter_steps(grid, make, parts, total_rows, *scratch)
    out_ref[...] = (stream_ref[...] + total_rows[...] + bias_ref[...]).astype(out_ref.dtype)


def leave_body(wait, tables, ins, outs, refs):
    given, (wide_own, tall_own) = ins[:5], ins[5:]
    out_ref, wide_ref, tall_ref = outs
    (parts, total_rows, tall_all), refs = refs[:3], refs[3:]
    grid = Grid()
    grid.barrier(share_partners())
    wait()
    sharing = share_steps([(wide_own, wide_ref), (tall_own, tall_all)], *refs[:2])
    next(sharing)
    steps = leave_steps(grid, *given, out_ref, parts, total_rows, refs[2:])
    run(steps, 5)
    run(sharing, 1)
    run(steps, 3)
    run(sharing, 2)
    run(steps)
    run(sharing)
    stack_tall(tall_all, tall_ref)


def leave(active, context, tall, stream, bias, wide_own, tall_own, number):
    rows, width = stream.shape
    shapes = [
        jax.ShapeDtypeStruct((rows, width), F32),
        jax.ShapeDtypeStruct((4,) + wide_own.shape, BF16),
        jax.ShapeDtypeStruct((6 * HEAD, width), BF16),
    ]
    scratch = [
        pltpu.VMEM((16, rows, width), BF16),
        pltpu.VMEM((rows, width), F32),
        pltpu.VMEM((4,) + tall_own.shape, BF16),
    ]
    scratch += share_sems(2) + scatter_scratch(rows, width)
    given = [active, context, tall, stream, bias, wide_own, tall_own]
    return staged_call(leave_body, "leave", number, given, shapes, scratch)


def back_enter_body(gathers, folds, wait, tables, ins, outs, refs):
    grad_ref, active_ref, context_ref, slope_ref, normed_ref, tall_ref, scale_ref = ins[:7]
    pull_ref, offset_ref, hidden_ref, early_ref, out_ref, up_ref, up_bias_ref = outs[:7]
    tall_sum, refs = refs[0], refs[1:]
    grid = Grid()
    rows = normed_ref.shape[-2]
    wait(0)
    if gathers:
        own, all_rows, send_sem, recv_sem = refs[:4]
        refs = refs[4:]
        own[...] = grad_ref[...].astype(BF16)
        all_rows[grid.rank(0, 0, 0)] = own[...]
        grid.barrier([sibling(), far_partner()] if folds else ())
        gather = gather_steps(grid, own, all_rows, send_sem, recv_sem)
        run(gather, 2)
    tall_sum[...] = jnp.zeros_like(tall_sum)
    up_ref[...] = jnp.zeros_like(up_ref)
    up_bias_ref[...] = jnp.zeros_like(up_bias_ref)

    def block(ranks):
        if gathers:
            branch = blocks_of(all_rows, ranks)
        else:
            branch = jnp.concatenate([half[rank] for rank in ranks for half in (grad_ref, ins[7])], 0)
        back = dots(branch, tall_ref[...], 1, 1)
        hidden_grad = (back[:, : 4 * HEAD] * rows_of(slope_ref, ranks, rows)).astype(BF16)
        pull = back[:, 4 * HEAD :].astype(BF16)
        put_rows(hidden_ref, ranks, rows, hidden_grad)
        put_rows(pull_ref, ranks, rows, pull)
        context = rows_of(context_ref, ranks, rows)
        offset = jnp.sum(pull.astype(F32) * context, 1, keepdims=True)
        put_rows(offset_ref, ranks, rows, jnp.broadcast_to(offset, context.shape))
        both = jnp.concatenate([rows_of(active_ref, ranks, rows), context.astype(BF16)], 1)
        ones = jnp.ones(context.shape, BF16)
        tall_sum[...] += dots(both, branch, 0, 0)
        up_ref[...] += dots(hidden_grad, blocks_of(normed_ref, ranks), 0, 0)
        up_bias_ref[...] += dots(hidden_grad, ones, 0, 0)

    if gathers:
        if folds:
            pair_ref, late_ref = ins[7:]
            folded_ref, sums_ref = outs[7:]
            wait(7, 8)
            exchanges = [
                high_steps(pair_ref, folded_ref, *refs[:2]),
                core_steps(late_ref, sums_ref, *refs[2:4]),
            ]
            for steps in exchanges:
                run(steps, 1)
        follow(grid, gather, block, wait)
        if folds:
            for steps in exchanges:
                run(steps)
    else:
        wait()

        def four(index, unused):
            block([index * 4 + i for i in range(4)])
            return unused

        lax.fori_loop(0, 4, four, 0)
    up_grad = (up_ref[...] * scale_ref[1:2] + up_bias_ref[:, 0:1] * scale_ref[3:4]).astype(BF16)
    for shard in range(4):
        early_ref[shard, : 4 * PART] = up_grad[:, shard * LANES : (shard + 1) * LANES]
        early_ref[shard, 8 * PART :] = jnp.zeros((PART, LANES), BF16)
        for lanes in range(4):
            early_ref[shard, (4 + lanes) * PART : (5 + lanes) * PART] = tall_sum[
                shard * HEAD : (shard + 1) * HEAD, lanes * LANES : (lanes + 1) * LANES
            ].astype(BF16)
            low = 5 * HEAD + shard * 16
            out_ref[shard, lanes * 16 : (lanes + 1) * 16] = tall_sum[
                low : low + 16, lanes * LANES : (lanes + 1) * LANES
            ].astype(BF16)


def back_enter(grad, active, context, slope, normed, tall, scale, number=None, folding=None):
    rows, width = normed.shape[-2:]
    total = 16 * rows
    if number is None:
        given = [grad[0], active, context, slope, normed, tall, scale, grad[1]]
    else:
        given = [grad, active, context, slope, normed, tall, scale]
    shapes = [
        jax.ShapeDtypeStruct((total, 2 * HEAD), BF16),
        jax.ShapeDtypeStruct((total, 2 * HEAD), F32),
        jax.ShapeDtypeStruct((total, 4 * HEAD), BF16),
        jax.ShapeDtypeStruct((4, EARLY, LANES), BF16),
        jax.ShapeDtypeStruct((4, PART, LANES), BF16),
        jax.ShapeDtypeStruct((4 * HEAD, width), F32),
        jax.ShapeDtypeStruct((4 * HEAD, 2 * HEAD), F32),
    ]
    scratch = [pltpu.VMEM((6 * HEAD, width), F32)]
    if number is not None:
        scratch += [
            pltpu.VMEM((rows, width), BF16),
            pltpu.VMEM((16, rows, width), BF16),
            pltpu.SemaphoreType.DMA((2, 20)),
            pltpu.SemaphoreType.DMA((2, 20)),
        ]
    if folding is not None:
        given += folding
        shapes.append(jax.ShapeDtypeStruct((EARLY, LANES), BF16))
        shapes.append(jax.ShapeDtypeStruct((2, LATE, LANES), BF16))
        scratch += swap_scratch(EARLY) + core_scratch(LATE)
    body = functools.partial(back_enter_body, number is not None, folding is not None)
    return staged_call(body, "back_enter", number, given, shapes, scratch)


def back_leave_body(wait, tables, ins, outs, refs):
    query_grad_ref, pair_grad_ref, hidden_ref, normed_ref, wide_ref, scale_ref = ins[:6]
    cos_ref, sin_ref, stream_ref, grad_ref, up_ref, up_bias_ref = ins[6:12]
    new_ref, addend_ref = outs[:2]
    (mixed, raw, raw_bias, parts, total_rows), scratch, refs = refs[:5], refs[5:11], refs[11:]
    grid = Grid()
    rows, width = stream_ref.shape
    grid.barrier([mate(), far_partner()])
    wait(0, 1, 2, 4, 6, 7)

    def make(ranks):
        cosines, sines = rows_of(cos_ref, ranks, rows), -rows_of(sin_ref, ranks, rows)
        query = rows_of(query_grad_ref, ranks, rows) * 0.125
        lane = lax.broadcasted_iota(jnp.int32, query.shape, 1)
        query = jnp.where(lane < HEAD, query, 0.0)
        pair = rows_of(pair_grad_ref, ranks, rows)
        both = jnp.concatenate(
            [rotate(pair, cosines, sines), rotate(query, cosines, sines)], 1
        ).astype(BF16)
        put_rows(mixed, ranks, rows, both)
        first = dots(both, wide_ref[:, : 4 * HEAD], 1, 1)
        second = dots(rows_of(hidden_ref, ranks, rows), wide_ref[:, 4 * HEAD :], 1, 1)
        made = (first * scale_ref[0:1] + second * scale_ref[1:2]).astype(BF16)
        for index, rank in enumerate(ranks):
            parts[rank] = made[index * rows : (index + 1) * rows]

    scatter = scatter_steps(grid, make, parts, total_rows, *scratch)
    run(scatter, 3)
    wait()
    if len(outs) == 3:
        exchanges = [low_steps(ins[12], outs[2], *refs, ins[13])]
    else:
        exchanges = [
            high_steps(ins[12], outs[2], *refs[:2]),
            high_steps(ins[13], outs[3], *refs[2:]),
        ]
    for steps in exchanges:
        run(steps, 1)
    run(scatter, 5)
    raw[...] = jnp.zeros_like(raw)
    raw_bias[...] = jnp.zeros_like(raw_bias)
    ones = jnp.ones((4 * rows, 2 * HEAD), BF16)

    def sums(index):
        span = pl.ds(index * 4 * rows, 4 * rows)
        both = mixed[span, :]
        normed_rows = normed_ref[pl.ds(index * 4, 4)].reshape(4 * rows, width)
        raw[...] += dots(both, normed_rows, 0, 0)
        raw_bias[...] += dots(both, ones, 0, 0)

    sums(0)
    run(scatter, 1)
    sums(1)
    run(scatter, 1)
    sums(2)
    run(scatter, 1)
    sums(3)

    wide_t = jnp.transpose(wide_ref[:, : 4 * HEAD].astype(F32))
    up_t = jnp.transpose(wide_ref[:, 4 * HEAD :].astype(F32))
    mixed_bias, up_bias = raw_bias[:, 0:1], up_bias_ref[:, 0:1]
    first_raw, second_raw = raw[...], up_ref[...]
    vectors = [
        jnp.sum(wide_t * first_raw, 0, keepdims=True),
        jnp.sum(up_t * second_raw, 0, keepdims=True),
        jnp.sum(wide_t * mixed_bias, 0, keepdims=True),
        jnp.sum(up_t * up_bias, 0, keepdims=True),
        jnp.sum(grad_ref[...].astype(BF16).astype(F32), 0, keepdims=True),
    ]
    first_grad = (first_raw * scale_ref[0:1] + mixed_bias * scale_ref[2:3]).astype(BF16)
    biases = [
        jnp.transpose(raw_bias[...])[0:1],
        jnp.transpose(up_bias_ref[...])[0:1],
    ]
    for shard in range(4):
        lanes = slice(shard * LANES, (shard + 1) * LANES)
        addend_ref[shard, : 3 * PART] = first_grad[: 3 * PART, lanes]
        tail = [vector[:, lanes] for vector in vectors] + biases
        tail.append(jnp.zeros((PART - len(tail), LANES), F32))
        addend_ref[shard, 3 * PART :] = jnp.concatenate(tail, 0).astype(BF16)
    run(scatter)
    for steps in exchanges:
        run(steps)
    normed, inverse = standardize(stream_ref[...])
    normed_grad = total_rows[...]
    new_ref[...] = grad_ref[...] + inverse * (
        normed_grad
        - jnp.mean(normed_grad, -1, keepdims=True)
        - normed * jnp.mean(normed_grad * normed, -1, keepdims=True)
    )


def back_leave(given, rows, width, number, low=None, high=None):
    total = 16 * rows
    shapes = [
        jax.ShapeDtypeStruct((rows, width), F32),
        jax.ShapeDtypeStruct((4, LATE, LANES), BF16),
    ]
    scratch = [
        pltpu.VMEM((total, 4 * HEAD), BF16),
        pltpu.VMEM((4 * HEAD, width), F32),
        pltpu.VMEM((4 * HEAD, 2 * HEAD), F32),
        pltpu.VMEM((16, rows, width), BF16),
        pltpu.VMEM((rows, width), F32),
    ]
    scratch += scatter_scratch(rows, width)
    if low is not None:
        given = tuple(given) + tuple(low)
        swapped = [low[0].shape[1]]
    else:
        given = tuple(given) + tuple(high)
        swapped = [array.shape[0] for array in high]
    for count in swapped:
        shapes.append(jax.ShapeDtypeStruct((count, LANES), BF16))
        scratch += swap_scratch(count)
    return staged_call(back_leave_body, "back_leave", number, given, shapes, scratch)


def sibling():
    shard = lax.axis_index("fsdp")
    return {"fsdp": shard + 1 - 2 * (shard % 2)}


def mate():
    return {"fsdp": (lax.axis_index("fsdp") + 2) % 4}


def far_partner():
    slot = lax.axis_index("ctx")
    return {"ctx": slot + 1 - 2 * (slot % 2)}


def wide_barrier(grid):
    shard = lax.axis_index("fsdp")
    at_home = grid.x == shard
    gate = pltpu.get_barrier_semaphore()
    partners = [grid.device(0, *step) for step in grid.meets]
    partners += [sibling(), mate(), far_partner()]
    for partner in partners:
        pl.semaphore_signal(gate, inc=1, device_id=partner, device_id_type=MESH)
    for other in range(4):

        @pl.when(jnp.logical_not(at_home & (shard == other)))
        def greet():
            pl.semaphore_signal(
                gate,
                inc=1,
                device_id={"ctx": (shard * SIDE + grid.y) * 2 + grid.z, "fsdp": other},
                device_id_type=MESH,
            )

    pl.semaphore_wait(gate, len(partners) + 4 - at_home.astype(jnp.int32))


def remote(source, target, send, recv, to):
    return pltpu.make_async_remote_copy(
        src_ref=source,
        dst_ref=target,
        send_sem=send,
        recv_sem=recv,
        device_id=to,
        device_id_type=MESH,
    )


def added(a, b):
    return (a.astype(F32) + b.astype(F32)).astype(BF16)


def core_steps(in_ref, sums_ref, land, sems):
    shard = lax.axis_index("fsdp")
    low, core = shard // 2, shard % 2
    copies = [
        remote(
            in_ref.at[part * 2 + 1 - core],
            land.at[part],
            sems.at[0, part],
            sems.at[1, part],
            sibling(),
        )
        for part in (0, 1)
    ]
    for copy in copies:
        copy.start()
    yield
    for copy in copies:
        copy.wait_recv()
    sums_ref[0] = added(in_ref[low * 2 + core], land[low])
    sums_ref[1] = added(in_ref[(1 - low) * 2 + core], land[1 - low])
    for copy in copies:
        copy.wait_send()


def core_scratch(rows):
    return [pltpu.VMEM((2, rows, LANES), BF16), pltpu.SemaphoreType.DMA((2, 2))]


def low_steps(sums_ref, pair_ref, land, sems, total_ref=None):
    copy = remote(sums_ref.at[1], land, sems.at[0], sems.at[1], mate())
    copy.start()
    yield
    copy.wait_recv()
    pair_ref[...] = added(sums_ref[0], land[...])
    if total_ref is not None:
        pair_ref[pair_ref.shape[0] - PART :] = total_ref[...]
    copy.wait_send()


def high_steps(pair_ref, own_ref, land, sems):
    copy = remote(pair_ref, land, sems.at[0], sems.at[1], far_partner())
    copy.start()
    yield
    copy.wait_recv()
    own_ref[...] = added(pair_ref[...], land[...])
    copy.wait_send()


def swap_scratch(rows):
    return [pltpu.VMEM((rows, LANES), BF16), pltpu.SemaphoreType.DMA((2,))]


def quarter_steps(grid, quarter_ref, total_ref, land, send_sem, recv_sem):
    x, y, z = grid.x, grid.y, grid.z
    shard = lax.axis_index("fsdp")
    at_home = x == shard

    def copy(column):
        return remote(
            quarter_ref.at[column],
            land.at[shard],
            send_sem.at[column],
            recv_sem.at[shard],
            {"ctx": (column * SIDE + y) * 2 + z, "fsdp": x},
        )

    for column in range(4):

        @pl.when(jnp.logical_not(at_home & (x == column)))
        def give():
            copy(column).start()

        @pl.when(at_home & (x == column))
        def keep():
            land[shard] = quarter_ref[column]

    yield
    for other in range(4):

        @pl.when(jnp.logical_not(at_home & (shard == other)))
        def take():
            remote(
                land.at[other], land.at[other], send_sem.at[other], recv_sem.at[other], mate()
            ).wait_recv()

    total = land[0].astype(F32)
    for other in range(1, 4):
        total = total + land[other].astype(F32)
    total_ref[...] = total.astype(BF16)
    for column in range(4):

        @pl.when(jnp.logical_not(at_home & (x == column)))
        def gone():
            copy(column).wait_send()


def quarter_scratch():
    return [
        pltpu.VMEM((4, PART, LANES), BF16),
        pltpu.SemaphoreType.DMA((4,)),
        pltpu.SemaphoreType.DMA((4,)),
    ]


def gather_sems():
    return [
        pltpu.SemaphoreType.DMA,
        pltpu.SemaphoreType.DMA((2, 20)),
        pltpu.SemaphoreType.DMA((2, 20)),
    ]


def keep_own(grid, own, every, sem):
    copy = pltpu.make_async_copy(own, every.at[grid.rank(0, 0, 0)], sem)
    copy.start()
    return copy


def sum_body(wait, tables, ins, outs, refs):
    early_ref, other_ref, late_ref = ins
    all_early, all_other, all_late = outs
    grid = Grid()
    (sums, pair, late), refs = refs[:3], refs[3:]
    core_refs, low_refs, high_refs, refs = refs[:2], refs[2:4], refs[4:6], refs[6:]
    early_sems, other_sems, late_sems = refs[:3], refs[3:6], refs[6:9]
    grid.barrier([sibling(), mate(), far_partner()])
    wait(2)
    core = core_steps(late_ref, sums, *core_refs)
    run(core, 1)
    wait()
    first = gather_steps(grid, early_ref, all_early, *early_sems[1:])
    second = gather_steps(grid, other_ref, all_other, *other_sems[1:])
    run(first, 2)
    keeps = [
        keep_own(grid, early_ref, all_early, early_sems[0]),
        keep_own(grid, other_ref, all_other, other_sems[0]),
    ]
    run(core)
    low = low_steps(sums, pair, *low_refs)
    run(low, 1)
    run(first, 4)
    run(low)
    high = high_steps(pair, late, *high_refs)
    run(high, 1)
    run(second, 2)
    run(first, 4)
    run(second, 2)
    run(high)
    keeps.append(keep_own(grid, late, all_late, late_sems[0]))
    third = gather_steps(grid, late, all_late, *late_sems[1:])
    run(third, 2)
    for unused in range(GATHER_STEPS):
        run(first, 1)
        run(second, 1)
        run(third, 1)
    run(third)
    for keep in keeps:
        keep.wait()


def sum_grads(early, other, addends, number):
    rows = addends.shape[1]
    shapes = [
        jax.ShapeDtypeStruct((16,) + early.shape, BF16),
        jax.ShapeDtypeStruct((16,) + other.shape, BF16),
        jax.ShapeDtypeStruct((16, rows, LANES), BF16),
    ]
    scratch = [
        pltpu.VMEM((2, rows, LANES), BF16),
        pltpu.VMEM((rows, LANES), BF16),
        pltpu.VMEM((rows, LANES), BF16),
    ]
    scratch += core_scratch(rows) + swap_scratch(rows) + swap_scratch(rows)
    scratch += gather_sems() + gather_sems() + gather_sems()
    given = [early, other, addends]
    return staged_call(sum_body, "sum_grads", number, given, shapes, scratch, direct=(0, 1, 2))


def turn_kernel(first_ref, second_ref, out_ref):
    layer = pl.program_id(0)
    row = lax.broadcasted_iota(jnp.int32, (LANES, LANES), 0)
    column = lax.broadcasted_iota(jnp.int32, (LANES, LANES), 1)
    unit = (row == column).astype(BF16)

    @pl.when(layer == 0)
    def first():
        out_ref[0] = dots(unit, first_ref[...].reshape(-1, LANES), 1, 1)

    @pl.when(layer == 1)
    def second():
        out_ref[0] = dots(unit, second_ref[...].reshape(-1, LANES), 1, 1)


def turned_parts(gathered, first, count, turn=0):
    layers = len(gathered)

    def spec(own):
        return pl.BlockSpec(
            (16, PART, LANES),
            lambda i, j: (0, first + (jnp.where(i == own, j, own * 0) + turn) % count, 0),
        )

    return pl.pallas_call(
        turn_kernel,
        grid=(layers, count),
        out_shape=jax.ShapeDtypeStruct((layers, LANES, count * 16 * PART), F32),
        in_specs=[spec(own) for own in range(layers)],
        out_specs=pl.BlockSpec((1, LANES, 16 * PART), lambda i, j: (i, 0, j)),
        name="turned_parts",
        compiler_params=pltpu.CompilerParams(vmem_limit_bytes=60 << 20),
    )(*gathered)


def tall_kernel(down_one, down_two, out_one, out_two, down_ref, out_ref):
    layer = pl.program_id(0)

    def put(down_in, out_in):
        down_ref[0] = down_in[...].astype(F32).reshape(16 * PART, LANES)
        for x in range(4):
            for y in range(4):
                out_ref[0, pl.ds(y * HEAD + x * 16, 16)] = out_in[x * 4 + y].astype(F32)

    @pl.when(layer == 0)
    def first():
        put(down_one, out_one)

    @pl.when(layer == 1)
    def second():
        put(down_two, out_two)


def tall_parts(gathered):
    layers = len(gathered)
    width = 4 * LANES

    def step(i, j, own):
        return jnp.where(i == own, j, 0)

    return pl.pallas_call(
        tall_kernel,
        grid=(layers, 4),
        out_shape=[
            jax.ShapeDtypeStruct((layers, 16 * PART, width), F32),
            jax.ShapeDtypeStruct((layers, LANES, width), F32),
        ],
        in_specs=[
            pl.BlockSpec((16, PART, LANES), lambda i, j, own=own: (0, 4 + step(i, j, own), 0))
            for own in range(layers)
        ]
        + [
            pl.BlockSpec(
                (16, 16, LANES), lambda i, j, own=own: (0, 32 + step(i, j, own), 0)
            )
            for own in range(layers)
        ],
        out_specs=[
            pl.BlockSpec((1, 16 * PART, LANES), lambda i, j: (i, 0, j)),
            pl.BlockSpec((1, LANES, LANES), lambda i, j: (i, 0, j)),
        ],
        name="tall_parts",
        compiler_params=pltpu.CompilerParams(vmem_limit_bytes=60 << 20),
    )(*gathered, *gathered)


SPAN = 1024
ATTEND_WORK = 88
SWAP_WORK = 32


def sort_in(source_ref, order_ref, target_ref, count):
    def body(i, unused):
        start = order_ref[i] * BLK
        target_ref[pl.ds(pl.multiple_of(i * BLK, BLK), BLK), :] = source_ref[
            pl.ds(start, BLK), :
        ]
        return unused

    lax.fori_loop(0, count, body, 0, unroll=8)


def block_numbers(number_ref, first, count, axis):
    if axis == 0:
        return jnp.concatenate(
            [jnp.full((BLK, 1), number_ref[first + i], jnp.int32) for i in range(count)], 0
        )
    lane = lax.broadcasted_iota(jnp.int32, (1, count * BLK), 1) // BLK
    numbers = jnp.zeros((1, count * BLK), jnp.int32)
    for i in range(count):
        numbers = jnp.where(lane == i, number_ref[first + i], numbers)
    return numbers


def far_copy(source, target, sems):
    return pltpu.make_async_remote_copy(
        src_ref=source,
        dst_ref=target,
        send_sem=sems.at[0],
        recv_sem=sems.at[1],
        device_id=far_partner(),
        device_id_type=MESH,
    )


def attend_steps(tables, q_ref, kv_ref, context_ref, qs, kvs, logs, scratch):
    order_ref, standing_ref, number_ref, other_order, other_ref = tables
    tops, totals, sums, far_ref, sems = scratch
    copy = far_copy(kv_ref, far_ref, sems)
    copy.start()
    sort_in(kv_ref, order_ref, kvs.at[0], 32)
    sort_in(q_ref, order_ref, qs, 32)
    tiles = qs.shape[0] // TILE
    row = lax.broadcasted_iota(jnp.int32, (TILE, TILE), 0)
    column = lax.broadcasted_iota(jnp.int32, (TILE, TILE), 1)
    yield 4

    def highest(scores):
        return jnp.max(scores, 1, keepdims=True)

    def weigh(scores, top, keys):
        weights = jnp.exp(scores - top)
        return jnp.sum(weights, 1, keepdims=True), dots(weights.astype(BF16), keys, 1, 0)

    def wide(vector):
        return jnp.broadcast_to(vector, (TILE, 2 * HEAD))

    def own_tile(tile):
        rows = slice(tile * TILE, (tile + 1) * TILE)
        queries, near = qs[rows, :], kvs[0, rows, :]
        parts = [(jnp.where(column <= row, dots(queries, near, 1, 1), NEGATIVE), near)]
        for low in range(0, tile * TILE, SPAN):
            keys = kvs[0, low : min(low + SPAN, tile * TILE), :]
            parts.append((dots(queries, keys, 1, 1), keys))
        top = highest(parts[0][0])
        for scores, keys in parts[1:]:
            top = jnp.maximum(top, highest(scores))
        total, weighted = 0.0, 0.0
        for scores, keys in parts:
            more, product = weigh(scores, top, keys)
            total, weighted = total + more, weighted + product
        tops[rows, :], totals[rows, :], sums[rows, :] = wide(top), wide(total), weighted

    def other_tile(tile, numbers):
        rows = slice(tile * TILE, (tile + 1) * TILE)
        queries = qs[rows, :]
        own = block_numbers(number_ref, tile * TILE // BLK, TILE // BLK, 0)
        half = tile // 4
        keys = kvs[1, half * SPAN : (half + 1) * SPAN, :]
        parts = [(jnp.where(numbers < own, dots(queries, keys, 1, 1), NEGATIVE), keys)]
        if half:
            keys = kvs[1, :SPAN, :]
            parts.append((dots(queries, keys, 1, 1), keys))
        old = tops[rows, :][:, 0:1]
        top = old
        for scores, keys in parts:
            top = jnp.maximum(top, highest(scores))
        scale = jnp.exp(old - top)
        total, weighted = totals[rows, :][:, 0:1] * scale, sums[rows, :] * scale
        for scores, keys in parts:
            more, product = weigh(scores, top, keys)
            total, weighted = total + more, weighted + product
        sums[rows, :] = weighted / total
        logs[rows, :] = wide(top + jnp.log(total))

    for tile in range(tiles):
        own_tile(tile)
        yield tile + 1
    for unused in range(8):
        yield SWAP_WORK // 8
    copy.wait_recv()
    sort_in(far_ref, other_order, kvs.at[1], 32)
    for half in (0, 1):
        numbers = block_numbers(other_ref, half * 16, 16, 1)
        for tile in range(half * 4, half * 4 + 4):
            other_tile(tile, numbers)
            yield 4 + 4 * half
    sort_in(sums, standing_ref, context_ref, 32)
    copy.wait_send()


def attend_scratch(rows):
    return [pltpu.VMEM((rows, 2 * HEAD), F32)] * 3 + [
        pltpu.VMEM((rows, 2 * HEAD), BF16),
        pltpu.SemaphoreType.DMA((2,)),
    ]


def attend_back_steps(
    tables, qs, kvs, logs, pull_ref, offset_ref, query_grad_ref, pair_grad_ref, scratch
):
    order_ref, standing_ref, number_ref, unused, other_ref = tables
    pulls, offsets, turned, query_sums, pair_sums, away, land, sems = scratch
    sort_in(pull_ref, order_ref, pulls, 32)
    sort_in(offset_ref, order_ref, offsets, 32)
    pair_sums[...] = jnp.zeros_like(pair_sums)
    tiles = qs.shape[0] // TILE
    row = lax.broadcasted_iota(jnp.int32, (TILE, TILE), 0)
    column = lax.broadcasted_iota(jnp.int32, (TILE, TILE), 1)
    lane = lax.broadcasted_iota(jnp.int32, (TILE, 2 * HEAD), 1)
    yield 4

    def tile_part(tile, half, low, count, mask):
        rows = slice(tile * TILE, (tile + 1) * TILE)
        queries, pull = qs[rows, :], pulls[rows, :]
        keys = kvs[half, low : low + count, :]
        scores = dots(keys, queries, 1, 1)
        if mask is not None:
            scores = jnp.where(mask, scores, NEGATIVE)
        probs = jnp.exp(scores - turned[tile, 0:1])
        score_grad = (probs * (dots(keys, pull, 1, 1) - turned[tile, 1:2])).astype(BF16)
        pair_sums[half, low : low + count, :] += dots(score_grad, queries, 1, 0) + dots(
            probs.astype(BF16), pull, 1, 0
        )
        return dots(score_grad, keys, 0, 0)

    def masked_tile(tile, numbers):
        rows = slice(tile * TILE, (tile + 1) * TILE)
        turned[tile] = jnp.transpose(
            jnp.where(lane == 0, logs[rows, :], offsets[rows, :])
        )[:8]
        own = block_numbers(number_ref, tile * TILE // BLK, TILE // BLK, 1)
        query_sums[rows, :] = tile_part(tile, 1, tile // 4 * SPAN, SPAN, numbers < own)

    def send(half):
        span = pl.ds(half * SPAN, SPAN)
        away[span] = pair_sums[1, span].astype(BF16)
        copy = far_copy(away.at[span], land.at[span], sems.at[half])
        copy.start()
        return copy

    def own_tile(tile):
        rows = slice(tile * TILE, (tile + 1) * TILE)
        query_sums[rows, :] += tile_part(tile, 0, tile * TILE, TILE, row <= column)
        yield 1
        for low in range(0, tile * TILE, SPAN):
            count = min(SPAN, tile * TILE - low)
            query_sums[rows, :] += tile_part(tile, 0, low, count, None)
            yield count // TILE

    copies = []
    for half in (1, 0):
        numbers = block_numbers(other_ref, half * 16, 16, 0)
        for tile in range(half * 4, half * 4 + 4):
            masked_tile(tile, numbers)
            yield 4
        if half == 0:
            for tile in range(4, 8):
                rows = slice(tile * TILE, (tile + 1) * TILE)
                query_sums[rows, :] += tile_part(tile, 1, 0, SPAN, None)
                yield 4
        copies.append(send(half))
    for tile in range(tiles):
        yield from own_tile(tile)
    sort_in(query_sums, standing_ref, query_grad_ref, 32)
    for copy in copies:
        copy.wait_recv()
    pair_sums[0] += land[...].astype(F32)
    sort_in(pair_sums.at[0], standing_ref, pair_grad_ref, 32)
    for copy in copies:
        copy.wait_send()


def attend_back_scratch(rows):
    block = (rows, 2 * HEAD)
    return [
        pltpu.VMEM(block, BF16),
        pltpu.VMEM(block, F32),
        pltpu.VMEM((rows // TILE, 8, TILE), F32),
        pltpu.VMEM(block, F32),
        pltpu.VMEM((2,) + block, F32),
        pltpu.VMEM(block, BF16),
        pltpu.VMEM(block, BF16),
        pltpu.SemaphoreType.DMA((2, 2)),
    ]


def take_turns(work, total, others):
    done = 0
    ran = [first for steps, count, first, early, part in others]
    for steps, count, first, early, part in others:
        run(steps, first)
    for more in work:
        done += more
        for index, (steps, count, first, early, part) in enumerate(others):
            wanted = early + min(int(done * (count - early) / (total * part)), count - early)
            run(steps, wanted - ran[index])
            ran[index] = wanted
    for steps, *unused in others:
        run(steps)


def attend_body(wait, tables, ins, outs, refs):
    q_ref, kv_ref, own_ref = ins
    gather_refs, scratch = refs[:3], refs[3:]
    grid = Grid()
    grid.barrier([far_partner()])
    wait()
    keep = keep_own(grid, own_ref, outs[4], gather_refs[0])
    gather = gather_steps(grid, own_ref, outs[4], *gather_refs[1:])
    work = attend_steps(tables, q_ref, kv_ref, *outs[:4], scratch)
    take_turns(work, ATTEND_WORK + SWAP_WORK, [(gather, GATHER_STEPS, 2, 6, 0.9)])
    keep.wait()


def attend(tables, queries, pairs, number, own):
    rows = queries.shape[0]
    shapes = [
        jax.ShapeDtypeStruct((rows, 2 * HEAD), F32),
        jax.ShapeDtypeStruct((rows, 2 * HEAD), BF16),
        jax.ShapeDtypeStruct((2, rows, 2 * HEAD), BF16),
        jax.ShapeDtypeStruct((rows, 2 * HEAD), F32),
        jax.ShapeDtypeStruct((16,) + own.shape, own.dtype),
    ]
    given, scratch = [queries, pairs, own], gather_sems() + attend_scratch(rows)
    return staged_call(attend_body, "attend", number, given, shapes, scratch, tables, direct=(4,))


def attend_back_leave_body(wait, tables, ins, outs, refs):
    in_ref, quarter_ref = ins[5:7]
    query_grad_ref, pair_grad_ref, sums_ref, total_ref, out_ref = outs
    (parts, total_rows), scatter_refs, refs = refs[:2], refs[2:8], refs[8:]
    core_refs, quarter_refs, scratch = refs[:2], refs[2:5], refs[5:]
    grid = Grid()
    wide_barrier(grid)
    wait()
    scatter = leave_steps(grid, *ins[7:], out_ref, parts, total_rows, scatter_refs)
    core = core_steps(in_ref, sums_ref, *core_refs)
    quarters = quarter_steps(grid, quarter_ref, total_ref, *quarter_refs)
    work = attend_back_steps(tables, *ins[:5], query_grad_ref, pair_grad_ref, scratch)
    others = [
        (core, 1, 1, 1, 1.0),
        (quarters, 1, 1, 1, 1.0),
        (scatter, SCATTER_STEPS, 1, 1, 1.0),
    ]
    take_turns(work, ATTEND_WORK, others)


def attend_back_gather_body(wait, tables, ins, outs, refs):
    in_ref, quarter_ref, folded_ref, late_ref = ins[5:]
    query_grad_ref, pair_grad_ref, pair_ref, late_pair, all_ref = outs
    gather_refs, core_refs, quarter_refs, refs = refs[:3], refs[3:5], refs[5:8], refs[8:]
    (sums, total), early_refs, late_refs, scratch = refs[:2], refs[2:4], refs[4:6], refs[6:]
    grid = Grid(RINGS)
    wide_barrier(grid)
    wait()
    keep = keep_own(grid, folded_ref, all_ref, gather_refs[0])
    gather = direct_steps(grid, folded_ref, all_ref, *gather_refs[1:])
    quarters = quarter_steps(grid, quarter_ref, total, *quarter_refs)
    late = low_steps(late_ref, late_pair, *late_refs)

    def early_steps():
        core = core_steps(in_ref, sums, *core_refs)
        next(core)
        yield
        run(core)
        run(quarters)
        yield from low_steps(sums, pair_ref, *early_refs, total)

    work = attend_back_steps(tables, *ins[:5], query_grad_ref, pair_grad_ref, scratch)
    others = [
        (gather, DIRECT_STEPS - 1, 1, 1, 0.35),
        (quarters, 1, 1, 1, 1.0),
        (early_steps(), 2, 1, 1, 0.5),
        (late, 1, 1, 1, 1.0),
    ]
    take_turns(work, ATTEND_WORK, others)
    keep.wait()


def attend_back(tables, given, folding, number, leaving=None, gathering=None):
    rows = given[0].shape[0]
    shapes = [jax.ShapeDtypeStruct((rows, 2 * HEAD), F32)] * 2
    if leaving is not None:
        body, direct = attend_back_leave_body, ()
        given = tuple(given) + tuple(folding) + tuple(leaving)
        own_rows, width = leaving[3].shape
        shapes += [
            jax.ShapeDtypeStruct((2, EARLY, LANES), BF16),
            jax.ShapeDtypeStruct((PART, LANES), BF16),
            jax.ShapeDtypeStruct((own_rows, width), BF16),
        ]
        scratch = [
            pltpu.VMEM((16, own_rows, width), BF16),
            pltpu.VMEM((own_rows, width), F32),
        ] + scatter_scratch(own_rows, width)
        scratch += core_scratch(EARLY) + quarter_scratch()
    else:
        body, direct = attend_back_gather_body, (4,)
        given = tuple(given) + tuple(folding) + tuple(gathering)
        own = gathering[0]
        shapes += [
            jax.ShapeDtypeStruct((EARLY, LANES), BF16),
            jax.ShapeDtypeStruct((LATE, LANES), BF16),
            jax.ShapeDtypeStruct((16,) + own.shape, own.dtype),
        ]
        scratch = gather_sems() + core_scratch(EARLY) + quarter_scratch()
        scratch += [pltpu.VMEM((2, EARLY, LANES), BF16), pltpu.VMEM((PART, LANES), BF16)]
        scratch += swap_scratch(EARLY) + swap_scratch(LATE)
    scratch = scratch + attend_back_scratch(rows)
    return staged_call(body, "attend_back", number, given, shapes, scratch, tables, direct)


def block_tables(pair_table, z):
    slots = pair_table.shape[0]
    ranks = slots // 2
    index = jnp.arange(slots, dtype=jnp.int32)

    def plane(which):
        pairs = lax.dynamic_slice_in_dim(pair_table.reshape(ranks, 2), which, 1, 1)
        numbers = jnp.concatenate([pairs, 2 * slots - 1 - pairs], 1).reshape(-1)
        standing = jnp.sum((numbers[None, :] < numbers[:, None]).astype(jnp.int32), 1)
        chosen = (standing[None, :] == index[:, None]).astype(jnp.int32)
        order = jnp.sum(chosen * index[None, :], 1)
        return numbers, (order, standing, jnp.sum(chosen * numbers[None, :], 1))

    numbers, own = plane(z)
    other = plane(1 - z)[1]
    return numbers, own + (other[0], other[2])


def rotation(positions):
    freqs = 10000.0 ** (-jnp.arange(0, ROT, 2, dtype=F32) / ROT)
    angles = positions.astype(F32)[:, None] * freqs[None, :]
    rest = ((0, 0), (0, 2 * HEAD - ROT))
    return (
        jnp.pad(jnp.concatenate([jnp.cos(angles)] * 2, -1), rest, constant_values=1.0),
        jnp.pad(jnp.concatenate([jnp.sin(angles)] * 2, -1), rest),
    )


def on_device(
    hidden_in,
    cotangent,
    pair_table,
    norm_gain,
    norm_bias,
    qkv_weight,
    qkv_bias,
    out_weight,
    out_bias,
    up_weight,
    up_bias,
    down_weight,
    down_bias,
):
    layers = norm_gain.shape[0]
    slot = lax.axis_index("ctx")
    shard = lax.axis_index("fsdp")
    rank, z = slot // 2, slot % 2
    width = hidden_in.shape[2]
    quarter = width // 4

    numbers, tables = block_tables(pair_table, z)
    positions = (
        numbers[:, None] * BLK + jnp.arange(BLK, dtype=jnp.int32)[None, :]
    ).reshape(-1)
    cosines, sines = rotation(positions)

    def columns(weight, part):
        return lax.dynamic_slice_in_dim(weight, part * width + rank * HEAD, HEAD, 2)

    wide = jnp.concatenate(
        [columns(qkv_weight, 1), columns(qkv_weight, 2), columns(qkv_weight, 0)]
        + [jnp.zeros((layers, quarter, HEAD), BF16)]
        + [columns(up_weight, part) for part in range(4)],
        2,
    )
    tall = jnp.concatenate(
        [
            lax.dynamic_slice_in_dim(down_weight, rank * HEAD, HEAD, 1),
            lax.dynamic_slice_in_dim(out_weight, (rank % 4) * HEAD, HEAD, 1),
        ],
        1,
    )
    vectors = lax.all_gather(
        jnp.concatenate(
            [
                norm_gain.reshape(layers, -1),
                norm_bias.reshape(layers, -1),
                qkv_bias,
                out_bias,
                up_bias,
                down_bias,
            ],
            1,
        ),
        "fsdp",
        axis=0,
    ).astype(F32)

    scales, wide_biases, last_biases = [], [], []
    for layer in range(layers):
        vector = vectors[:, layer]
        scales.append(
            jnp.transpose(vector[:, 0:1024].reshape(4, 4, 256), (1, 0, 2)).reshape(4, width)
        )
        b_qkv = lax.dynamic_slice_in_dim(
            vector[:, 1024:1792].reshape(3, 16, HEAD), rank, 1, 1
        ).reshape(3, HEAD)
        b_up = lax.dynamic_slice_in_dim(
            vector[:, 2048:3072].reshape(4, 16, HEAD), rank, 1, 1
        ).reshape(4 * HEAD)
        wide_biases.append(
            jnp.concatenate([b_qkv[1], b_qkv[2], b_qkv[0], jnp.zeros((HEAD,), F32), b_up])[None]
        )
        last_biases.append((vector[:, 1792:2048] + vector[:, 3072:3328]).reshape(1, width))

    number = 1
    stream = hidden_in[0].astype(F32)
    saved = []
    wide_all, tall_all = [None] * layers, [None] * layers
    branch_all = []
    for layer in range(layers):
        if layer == 0:
            *made, wide_all[0], tall_all[0] = enter(
                stream, scales[0], wide_biases[0], cosines, sines, wide[0], tall[0], number
            )
        else:
            made = enter(
                stream, scales[layer], wide_biases[layer], cosines, sines, wide_all[layer], None,
                number,
            )
        number += 1
        normed_all, queries, pairs, active, slope = made
        half_rows = stream.shape[0] // layers
        own = cotangent[0, layer * half_rows : (layer + 1) * half_rows]
        context, queries, pairs, logs, branch = attend(tables, queries, pairs, number, own)
        branch_all.append(branch)
        number += 1
        saved.append((stream, normed_all, queries, pairs, active, slope, context, logs))
        leaving = (active, context, tall_all[layer], stream, last_biases[layer])
        if layer < layers - 1:
            stream, wide_all[layer + 1], tall_all[layer + 1] = leave(
                *leaving, wide[layer + 1], tall[layer + 1], number
            )
            number += 1

    grad = cotangent[0].astype(F32)
    early, late = [None] * layers, [None] * layers
    exchanged = None
    for layer in reversed(range(layers)):
        last = layer == layers - 1
        stream, normed_all, queries, pairs, active, slope, context, logs = saved[layer]
        if last:
            pull, offsets, hidden_grad, early_addends, quarters, up_raw, up_bias_raw = back_enter(
                branch_all, active, context, slope, normed_all, tall_all[layer], scales[layer]
            )
            query_grad, pair_grad, early_sums, out_total, output = attend_back(
                tables, (queries, pairs, logs, pull, offsets), (early_addends, quarters), number,
                leaving=leaving,
            )
            exchanges = dict(low=(early_sums, out_total))
        else:
            (
                pull, offsets, hidden_grad, early_addends, quarters, up_raw, up_bias_raw,
                folded, late_sums,
            ) = back_enter(
                grad, active, context, slope, normed_all, tall_all[layer], scales[layer], number,
                exchanged,
            )
            number += 1
            query_grad, pair_grad, early_pair, late_pair, early[layer + 1] = attend_back(
                tables, (queries, pairs, logs, pull, offsets), (early_addends, quarters), number,
                gathering=(folded, late_sums),
            )
            exchanges = dict(high=(early_pair, late_pair))
        number += 1
        grad, addends, *exchanged = back_leave(
            (
                query_grad,
                pair_grad,
                hidden_grad,
                normed_all,
                wide_all[layer].reshape(width, 8 * HEAD),
                scales[layer],
                cosines,
                sines,
                stream,
                grad,
                up_raw,
                up_bias_raw,
            ),
            stream.shape[0],
            width,
            number,
            **exchanges,
        )
        if last:
            exchanged = [exchanged[0], addends]
        number += 1

    early[0], late[1], late[0] = sum_grads(exchanged[0], exchanged[1], addends, number)
    qkv_out = turned_parts(late, 0, 3, 2)
    up_out = turned_parts(early, 0, 4)
    down_out, out_out = tall_parts(early)
    small = jnp.stack(
        [every[:, 3 * PART : 3 * PART + 7] for every in late]
    ).astype(F32)
    sums = jnp.sum(small[:, :, :5], 1)
    gain_out, shift_out, branch_out = sums[:, 0:2], sums[:, 2:4], sums[:, 4]
    qkv_bias_out = jnp.transpose(
        jnp.roll(small[:, :, 5, : 3 * HEAD].reshape(layers, 16, 3, HEAD), 1, 2), (0, 2, 1, 3)
    ).reshape(layers, -1)
    share = qkv_bias_out.shape[1] // 4
    qkv_bias_out = lax.dynamic_slice_in_dim(qkv_bias_out, shard * share, share, 1)
    up_bias_out = lax.dynamic_slice_in_dim(
        small[:, :, 6].reshape(layers, 16, 4, HEAD), shard, 1, 2
    ).reshape(layers, -1)
    return (
        output[None],
        grad[None],
        gain_out,
        shift_out,
        qkv_out,
        qkv_bias_out,
        out_out,
        branch_out,
        up_out,
        up_bias_out,
        down_out,
        branch_out,
    )


def solution(mesh):
    rows = P("fsdp", "ctx", None)
    vector, matrix = P(None, "fsdp"), P(None, "fsdp", None)
    gains = P(None, None, "fsdp")
    params = (gains, gains) + (matrix, vector) * 4
    return jax.shard_map(
        on_device,
        mesh=mesh,
        in_specs=(rows, rows, P()) + params,
        out_specs=(rows, rows) + params,
        check_vma=False,
    )
```

```python
import functools

import jax
import jax.numpy as jnp
from jax import lax
from jax.experimental import pallas as pl
from jax.experimental.pallas import tpu as pltpu
from jax.sharding import PartitionSpec as P

HEADS = 16
HEAD = 64
ROT = 16
BLK = 64
SIDE = 4
EPS = 1e-05
NEGATIVE = -1e30
MESH = pl.DeviceIdType.MESH
F32 = jnp.float32
BF16 = jnp.bfloat16
TILE = 256
KEYS = 512
PART = 64
EARLY = 9 * PART
LATE = 4 * PART
LANES = 256


def place():
    slot = lax.axis_index("ctx")
    return slot // 8, (slot // 2) % SIDE, slot % 2


class Grid:
    def __init__(self, meets=((1, 0), (-1, 0), (0, 1), (0, -1))):
        self.x, self.y, self.z = place()
        self.meets = meets
        self.ranks, self.slots = {}, {}
        for dx in range(SIDE):
            for dy in range(SIDE):
                rank = ((self.x + dx) % SIDE) * SIDE + (self.y + dy) % SIDE
                self.ranks[dx, dy] = rank
                self.slots[dx, dy] = rank * 2 + self.z

    def spot(self, half, dp, dq):
        dx, dy = (dp, dq) if half == 0 else (dq, dp)
        return dx % SIDE, dy % SIDE

    def rank(self, half, dp, dq):
        return self.ranks[self.spot(half, dp, dq)]

    def device(self, half, dp, dq):
        return {"ctx": self.slots[self.spot(half, dp, dq)]}

    def barrier(self, others=()):
        gate = pltpu.get_barrier_semaphore()
        partners = [self.device(0, *step) for step in self.meets]
        partners += others
        for partner in partners:
            pl.semaphore_signal(gate, inc=1, device_id=partner, device_id_type=MESH)
        pl.semaphore_wait(gate, len(partners))


LARGE = 1 << 16


def size_of(array):
    return array.size * jnp.dtype(array.dtype).itemsize


PIECES = 4


class Waits:
    def __init__(self):
        self.loads, self.stores, self.started = {}, {}, []

    def __call__(self, *which):
        for i in which or sorted(self.loads):
            for copy in self.loads.pop(i, ()):
                if copy is not None:
                    copy.wait()

    def piece(self, k, *which):
        for i in which:
            if i in self.loads:
                copies = self.loads[i]
                if copies[k] is not None:
                    copies[k].wait()
                    copies[k] = None

    def flush(self, *which):
        for i in which or sorted(self.stores):
            if i in self.stores:
                copy = self.stores.pop(i)
                copy.start()
                self.started.append(copy)

    def finish(self):
        self()
        self.flush()
        for copy in self.started:
            copy.wait()


def staged_call(
    body, name, number, given, shapes, scratch, tables=(), direct=(), parted=()
):
    loads = [i for i, array in enumerate(given) if size_of(array) > LARGE]
    stores = [i for i, shape in enumerate(shapes) if size_of(shape) > LARGE and i not in direct]
    counts = (len(tables), len(given), len(shapes), len(loads), len(stores))

    def kernel(*refs):
        refs, groups = list(refs), []
        for count in counts:
            groups.append(refs[:count])
            refs = refs[count:]
        table_refs, ins, outs, staged_in, staged_out = groups
        load_sem, store_sem, *refs = refs
        wait = Waits()
        for k, i in enumerate(loads):
            if i not in parted:
                copy = pltpu.make_async_copy(ins[i], staged_in[k], load_sem.at[k, 0])
                copy.start()
                wait.loads[i] = [copy]
        for piece in range(PIECES):
            for k, i in enumerate(loads):
                if i in parted:
                    count = given[i].shape[0] // PIECES
                    span = pl.ds(piece * count, count)
                    copy = pltpu.make_async_copy(
                        ins[i].at[span], staged_in[k].at[span], load_sem.at[k, piece]
                    )
                    copy.start()
                    wait.loads.setdefault(i, []).append(copy)
        for k, i in enumerate(loads):
            ins[i] = staged_in[k]
        for k, i in enumerate(stores):
            wait.stores[i] = pltpu.make_async_copy(staged_out[k], outs[i], store_sem.at[k])
            outs[i] = staged_out[k]
        body(wait, table_refs, ins, outs, refs)
        wait.finish()

    smem, vmem, hbm = (
        pl.BlockSpec(memory_space=space) for space in (pltpu.SMEM, pltpu.VMEM, pl.ANY)
    )
    far = set(stores) | set(direct)
    params = dict(vmem_limit_bytes=60 << 20)
    if number is not None:
        params.update(collective_id=number, has_side_effects=True)
    return pl.pallas_call(
        kernel,
        out_shape=list(shapes),
        in_specs=[smem] * len(tables)
        + [hbm if i in loads else vmem for i in range(len(given))],
        out_specs=[hbm if i in far else vmem for i in range(len(shapes))],
        scratch_shapes=[pltpu.VMEM(given[i].shape, given[i].dtype) for i in loads]
        + [pltpu.VMEM(shapes[i].shape, shapes[i].dtype) for i in stores]
        + [
            pltpu.SemaphoreType.DMA((max(len(loads), 1), PIECES)),
            pltpu.SemaphoreType.DMA((max(len(stores), 1),)),
        ]
        + list(scratch),
        name=name,
        compiler_params=pltpu.CompilerParams(**params),
    )(*tables, *given)


RINGS = ((1, 0), (-1, 0), (2, 0), (0, 1), (0, -1), (0, 2))


def gather_half(grid, half, own_ref, all_ref, send_sem, recv_sem):
    rows = own_ref.shape[0]
    half_rows, quarter = rows // 2, rows // 4
    sends = []

    def view(dp, dq, low, count):
        return all_ref.at[grid.rank(half, dp, dq), pl.ds(half * half_rows + low, count)]

    def start(event, to, block, low, count, own=False):
        source = (
            own_ref.at[pl.ds(half * half_rows + low, count)]
            if own
            else view(*block, low, count)
        )
        copy = pltpu.make_async_remote_copy(
            src_ref=source,
            dst_ref=view(*block, low, count),
            send_sem=send_sem.at[half, event],
            recv_sem=recv_sem.at[half, event],
            device_id=grid.device(half, *to),
            device_id_type=MESH,
        )
        copy.start()
        sends.append(copy)

    def arrive(event, block, low, count):
        there = view(*block, low, count)
        pltpu.make_async_remote_copy(
            src_ref=there,
            dst_ref=there,
            send_sem=send_sem.at[half, event],
            recv_sem=recv_sem.at[half, event],
            device_id=grid.device(half, 1, 0),
            device_id_type=MESH,
        ).wait_recv()

    def spread(column, dp, own=False):
        start(4 + 4 * column, (0, 1), (dp, 0), 0, half_rows, own)
        start(5 + 4 * column, (0, -1), (dp, 0), 0, half_rows, own)

    start(0, (1, 0), (0, 0), 0, half_rows, True)
    start(1, (-1, 0), (0, 0), 0, half_rows, True)
    spread(0, 0, True)
    yield
    arrive(0, (-1, 0), 0, half_rows)
    start(2, (1, 0), (-1, 0), 0, quarter)
    spread(1, -1)
    arrive(1, (1, 0), 0, half_rows)
    start(3, (-1, 0), (1, 0), quarter, quarter)
    spread(2, 1)
    yield
    arrive(2, (2, 0), 0, quarter)
    arrive(3, (2, 0), quarter, quarter)
    spread(3, 2)
    yield
    steps = (0, -1, 1, 2)
    for column in range(4):
        arrive(4 + 4 * column, (steps[column], -1), 0, half_rows)
        start(6 + 4 * column, (0, 1), (steps[column], -1), 0, quarter)
        arrive(5 + 4 * column, (steps[column], 1), 0, half_rows)
        start(7 + 4 * column, (0, -1), (steps[column], 1), quarter, quarter)
        yield
    for column in range(4):
        arrive(6 + 4 * column, (steps[column], 2), 0, quarter)
        arrive(7 + 4 * column, (steps[column], 2), quarter, quarter)
        if column % 2 == 0:
            yield
    for copy in sends:
        copy.wait_send()


GATHER_STEPS = 20


def gather_steps(grid, own_ref, all_ref, send_sem, recv_sem):
    halves = [
        gather_half(grid, half, own_ref, all_ref, send_sem, recv_sem) for half in (0, 1)
    ]
    for step in range(GATHER_STEPS):
        next(halves[step % 2], None)
        if step < GATHER_STEPS - 1:
            yield


DIRECT_STEPS = 8


def direct_steps(grid, own_ref, all_ref, send_sem, recv_sem):
    half_rows = own_ref.shape[0] // 2
    sends = []

    def view(half, dp, dq):
        return all_ref.at[grid.rank(half, dp, dq), pl.ds(half * half_rows, half_rows)]

    def copy(half, event, to, block, own=False):
        source = own_ref.at[pl.ds(half * half_rows, half_rows)] if own else view(half, *block)
        return pltpu.make_async_remote_copy(
            src_ref=source,
            dst_ref=view(half, *block),
            send_sem=send_sem.at[half, event],
            recv_sem=recv_sem.at[half, event],
            device_id=grid.device(half, *to),
            device_id_type=MESH,
        )

    def start(*args):
        made = copy(*args)
        made.start()
        sends.append(made)

    steps = (1, -1, 2)
    for index, step in enumerate(steps):
        for half in (0, 1):
            start(half, index, (step, 0), (0, 0), True)
    for index, step in enumerate(steps):
        for half in (0, 1):
            start(half, 3 + index, (0, step), (0, 0), True)
    yield
    for index, step in enumerate(steps):
        for half in (0, 1):
            copy(half, index, (step, 0), (-step, 0)).wait_recv()
            for other, move in enumerate(steps):
                start(half, 6 + 3 * index + other, (0, move), (-step, 0))
            yield
    for column, place_p in enumerate((0, -1, 1, -2)):
        for other, move in enumerate(steps):
            for half in (0, 1):
                copy(half, 3 + 3 * column + other, (0, move), (place_p, -move)).wait_recv()
    for made in sends:
        made.wait_send()


def run(steps, count=None):
    while count is None or count > 0:
        if next(steps, StopIteration) is StopIteration:
            return
        count = None if count is None else count - 1


def scatter_steps(
    grid, make, part_ref, out_ref, land_half, land_full, stage, total, send_sem, recv_sem
):
    rows = part_ref.shape[1]
    half_rows, quarter = rows // 2, rows // 4
    sends = []
    steps = (2, -1, 1, 0)

    def start(half, event, source, target, to):
        copy = pltpu.make_async_remote_copy(
            src_ref=source,
            dst_ref=target,
            send_sem=send_sem.at[half, event],
            recv_sem=recv_sem.at[half, event],
            device_id=grid.device(half, *to),
            device_id_type=MESH,
        )
        copy.start()
        sends.append(copy)

    def arrive(half, event, target):
        pltpu.make_async_remote_copy(
            src_ref=target,
            dst_ref=target,
            send_sem=send_sem.at[half, event],
            recv_sem=recv_sem.at[half, event],
            device_id=grid.device(half, 1, 0),
            device_id_type=MESH,
        ).wait_recv()

    def first(half, column):
        def piece(dq, low, count):
            return part_ref.at[
                grid.rank(half, steps[column], dq), pl.ds(half * half_rows + low, count)
            ]

        return piece

    def second(half):
        return lambda dp, low, count: total.at[half, steps.index(dp), pl.ds(low, count)]

    def along(step):
        return (0, step)

    def across(step):
        return (step, 0)

    def opposite(half, column, piece, step):
        for side, low in ((0, 0), (1, quarter)):
            start(
                half,
                4 * column + side,
                piece(2, low, quarter),
                land_half.at[half, column, side],
                step(1 - 2 * side),
            )

    def neighbours(half, column, piece, step):
        for side in (0, 1):
            land = land_half.at[half, column, side]
            arrive(half, 4 * column + side, land)
            low, other = side * quarter, (1 - side) * quarter
            toward = 1 - 2 * side
            stage[half, column, side, low : low + quarter] = (
                piece(toward, low, quarter)[...].astype(F32) + land[...].astype(F32)
            ).astype(BF16)
            stage[half, column, side, other : other + quarter] = piece(toward, other, quarter)[...]
            start(
                half,
                4 * column + 2 + side,
                stage.at[half, column, side],
                land_full.at[half, column, side],
                step(toward),
            )

    def settle(half, column, own):
        for side in (0, 1):
            arrive(half, 4 * column + 2 + side, land_full.at[half, column, side])
        return (
            own[...].astype(F32)
            + land_full[half, column, 0].astype(F32)
            + land_full[half, column, 1].astype(F32)
        )

    def places(*spots):
        make([grid.rank(0, dx, dy) for dx, dy in spots])

    def on_both(step, column, direction):
        for half in (0, 1):
            step(half, column, first(half, column), direction)

    places((2, 2))
    on_both(opposite, 0, along)
    for column in (1, 2, 3):
        places((steps[column], 2), (2, steps[column]))
        on_both(opposite, column, along)
        yield
    on_both(neighbours, 0, along)
    yield
    places((-1, -1), (-1, 1))
    places((1, -1), (1, 1))
    on_both(neighbours, 1, along)
    yield
    places((0, 1), (0, -1))
    on_both(neighbours, 2, along)
    yield
    places((1, 0), (-1, 0))
    on_both(neighbours, 3, along)
    yield
    places((0, 0))
    for column in range(4):
        for half in (0, 1):
            total[half, column] = settle(
                half, column, first(half, column)(0, 0, half_rows)
            ).astype(BF16)
            if column == 0:
                opposite(half, 4, second(half), across)
            if column == 2:
                neighbours(half, 4, second(half), across)
        yield
    for half in (0, 1):
        out_ref[pl.ds(half * half_rows, half_rows)] = settle(half, 4, total.at[half, 3])
    for copy in sends:
        copy.wait_send()


SCATTER_STEPS = 12


def scatter_scratch(rows, width):
    half_rows, quarter = rows // 2, rows // 4
    return [
        pltpu.VMEM((2, 5, 2, quarter, width), BF16),
        pltpu.VMEM((2, 5, 2, half_rows, width), BF16),
        pltpu.VMEM((2, 5, 2, half_rows, width), BF16),
        pltpu.VMEM((2, 4, half_rows, width), BF16),
        pltpu.SemaphoreType.DMA((2, 20)),
        pltpu.SemaphoreType.DMA((2, 20)),
    ]


def follow(grid, gather, block, ready=None):
    def places(*spots):
        block([grid.rank(0, dx, dy) for dx, dy in spots])

    run(gather, 4)
    if ready is not None:
        ready()
    places((0, 0))
    run(gather, 2)
    places((0, 1), (0, -1))
    run(gather, 2)
    places((1, 0), (-1, 0))
    run(gather, 2)
    places((1, 1), (1, -1))
    run(gather, 2)
    places((-1, 1), (-1, -1))
    run(gather, 2)
    places((0, 2), (2, 0))
    run(gather, 2)
    places((1, 2), (-1, 2))
    places((2, 1), (2, -1))
    run(gather)
    places((2, 2))


def rows_of(ref, ranks, rows):
    return jnp.concatenate([ref[block_rows(rank, rows), :] for rank in ranks], 0)


def put_rows(ref, ranks, rows, values):
    for index, rank in enumerate(ranks):
        ref[block_rows(rank, rows), :] = values[index * rows : (index + 1) * rows]


def blocks_of(ref, ranks):
    return jnp.concatenate([ref[rank] for rank in ranks], 0)


SQRT_HALF = 0.7071067811865476
DENSITY = 0.3989422804014327


def standardize(stream):
    row_mean = jnp.mean(stream, -1, keepdims=True)
    centered = stream - row_mean
    spread = jnp.mean(centered * centered, -1, keepdims=True)
    inverse = lax.rsqrt(spread + EPS)
    return (centered * inverse, inverse)


def dots(a, b, da, db):
    return lax.dot_general(a, b, (((da,), (db,)), ((), ())), preferred_element_type=F32)


def rotate(values, cosines, sines):
    lane = lax.broadcasted_iota(jnp.int32, values.shape, 1)
    half_dims = ROT // 2
    up = pltpu.roll(values, 2 * HEAD - half_dims, 1)
    down = pltpu.roll(values, half_dims, 1)
    return values * cosines + jnp.where(lane < half_dims, -up, down) * sines


def block_rows(rank, rows):
    return pl.ds(pl.multiple_of(rank * rows, rows), rows)


def share_partners():
    shard = lax.axis_index("fsdp")
    return [{"fsdp": shard + 1 - 2 * (shard % 2)}, {"fsdp": (shard + 2) % 4}]


def share_steps(items, send_sem, recv_sem):
    shard = lax.axis_index("fsdp")
    sibling = shard + 1 - 2 * (shard % 2)
    mate = (shard + 2) % 4
    third = (sibling + 2) % 4
    sends = []

    def copy(item, source, target, event, to):
        return pltpu.make_async_remote_copy(
            src_ref=source,
            dst_ref=target,
            send_sem=send_sem.at[item, event],
            recv_sem=recv_sem.at[item, event],
            device_id={"fsdp": to},
            device_id_type=MESH,
        )

    def start(*args):
        made = copy(*args)
        made.start()
        sends.append(made)

    for item, (own, every) in enumerate(items):
        start(item, own, every.at[shard], 0, mate)
        start(item, own, every.at[shard], 1, sibling)
        every[shard] = own[...]
    yield
    for item, (own, every) in enumerate(items):
        copy(item, own, every.at[mate], 0, mate).wait_recv()
        start(item, every.at[mate], every.at[mate], 2, sibling)
        yield
        copy(item, own, every.at[sibling], 1, sibling).wait_recv()
        copy(item, own, every.at[third], 2, sibling).wait_recv()
        yield
    for made in sends:
        made.wait_send()


def share_sems(items):
    return [pltpu.SemaphoreType.DMA((items, 3)), pltpu.SemaphoreType.DMA((items, 3))]


def stack_tall(tall_all, tall_ref):
    for part in range(4):
        tall_ref[part * HEAD : (part + 1) * HEAD] = tall_all[part, :HEAD]
    tall_ref[4 * HEAD : 5 * HEAD] = jnp.zeros((HEAD, tall_ref.shape[1]), BF16)
    tall_ref[5 * HEAD :] = tall_all[place()[0], HEAD:]


def enter_phase(grid, stream_ref, given, wide_ref, made, own, sems, ready):
    scale_ref, bias_ref, cos_ref, sin_ref = given
    normed_ref, active_ref, slope_ref, q_ref, kv_ref = made
    rows, width = stream_ref.shape
    own[...] = standardize(stream_ref[...])[0].astype(BF16)
    normed_ref[grid.rank(0, 0, 0)] = own[...]
    yield
    gather = gather_steps(grid, own, normed_ref, *sems)
    run(gather, 2)

    def block(ranks):
        plain = blocks_of(normed_ref, ranks).astype(F32)
        first = (plain * scale_ref[0:1] + scale_ref[2:3]).astype(BF16)
        second = (plain * scale_ref[1:2] + scale_ref[3:4]).astype(BF16)
        weight = wide_ref[...].reshape(width, 8 * HEAD)
        mixed = dots(first, weight[:, : 4 * HEAD], 1, 0) + bias_ref[:, : 4 * HEAD]
        hidden = dots(second, weight[:, 4 * HEAD :], 1, 0) + bias_ref[:, 4 * HEAD :]
        cosines, sines = rows_of(cos_ref, ranks, rows), rows_of(sin_ref, ranks, rows)
        pairs = rotate(mixed[:, : 2 * HEAD], cosines, sines)
        queries = rotate(mixed[:, 2 * HEAD :], cosines, sines) * 0.125
        put_rows(kv_ref, ranks, rows, pairs.astype(BF16))
        put_rows(q_ref, ranks, rows, queries.astype(BF16))
        share = 0.5 * (1.0 + lax.erf(hidden * SQRT_HALF))
        put_rows(active_ref, ranks, rows, (hidden * share).astype(BF16))
        slope = share + hidden * (DENSITY * jnp.exp(-0.5 * hidden * hidden))
        put_rows(slope_ref, ranks, rows, slope)

    follow(grid, gather, block, ready)


def leave_steps(
    grid, active_ref, context_ref, tall_ref, stream_ref, bias_ref, out_ref, parts, total_rows, scratch
):
    rows = stream_ref.shape[0]

    def make(ranks):
        context = rows_of(context_ref, ranks, rows).astype(BF16)
        both = jnp.concatenate([rows_of(active_ref, ranks, rows), context], 1)
        made = dots(both, tall_ref[...], 1, 0).astype(BF16)
        for index, rank in enumerate(ranks):
            parts[rank] = made[index * rows : (index + 1) * rows]

    yield from scatter_steps(grid, make, parts, total_rows, *scratch)
    out_ref[...] = (stream_ref[...] + total_rows[...] + bias_ref[...]).astype(out_ref.dtype)


def forward_body(wait, tables, ins, outs, refs):
    stream_ref, scale_one, bias_one, cos_ref, sin_ref, wide_one, tall_one = ins[:7]
    halves, (last_bias, wide_two, tall_two, scale_two, bias_two) = ins[7:9], ins[9:]
    layer_outs, branches = (outs[:7], outs[7:14]), outs[14:16]
    wide_refs, tall_refs, second_ref = (outs[16], outs[18]), (outs[17], outs[19]), outs[20]
    (own_one, own_two), refs = refs[:2], refs[2:]
    queries, refs = (refs[:2], refs[2:4]), refs[4:]
    enter_sems, refs = (refs[:2], refs[2:4]), refs[4:]
    branch_sems, refs = (refs[:3], refs[3:6]), refs[6:]
    share_refs, refs = (refs[:3], refs[3:6]), refs[6:]
    (parts, total_rows), scatter_refs, refs = refs[:2], refs[2:8], refs[8:]
    attend_refs = (refs[:5], refs[:3] + refs[5:7])
    grid = Grid()

    def attend_phase(layer):
        normed, active, slope, context, qs, kvs, logs = layer_outs[layer]
        half, all_ref, sems = halves[layer], branches[layer], branch_sems[layer]
        keep = keep_own(grid, half, all_ref, sems[0])
        gather = gather_steps(grid, half, all_ref, *sems[1:])
        work = attend_steps(
            tables, *queries[layer], context, qs, kvs, logs, attend_refs[layer]
        )
        take_turns(work, ATTEND_WORK + SWAP_WORK, [(gather, GATHER_STEPS, 2, 6, 0.9)])
        return keep

    def sharing(layer, wide_own, tall_own):
        tall_all, *sems = share_refs[layer]
        return share_steps([(wide_own, wide_refs[layer]), (tall_own, tall_all)], *sems)

    wait(0)
    enter = enter_phase(
        grid, stream_ref, (scale_one, bias_one, cos_ref, sin_ref), wide_refs[0],
        (*layer_outs[0][:3], *queries[0]), own_one, enter_sems[0],
        lambda: (run(shared, 2), wait()),
    )
    run(enter, 1)
    grid.barrier([far_partner()] + share_partners())
    wait(5, 6)
    shared = sharing(0, wide_one, tall_one)
    run(shared, 1)
    run(enter)
    run(shared)
    stack_tall(share_refs[0][0], tall_refs[0])
    wait.flush(0, 1, 2, 16, 17)
    keeps = [attend_phase(0)]
    wait.flush(3, 4, 5, 6)
    shared = sharing(1, wide_two, tall_two)
    run(shared, 1)
    leave = leave_steps(
        grid, layer_outs[0][1], layer_outs[0][3], tall_refs[0], stream_ref, last_bias, second_ref,
        parts, total_rows, scatter_refs,
    )
    run(leave, 5)
    run(shared, 1)
    run(leave, 3)
    run(shared, 2)
    run(leave)

    enter = enter_phase(
        grid, second_ref, (scale_two, bias_two, cos_ref, sin_ref), wide_refs[1],
        (*layer_outs[1][:3], *queries[1]), own_two, enter_sems[1], lambda: run(shared),
    )
    run(enter, 1)
    wait.flush(20)
    run(enter)
    stack_tall(share_refs[1][0], tall_refs[1])
    wait.flush(7, 8, 9, 18, 19)
    keeps.append(attend_phase(1))
    for keep in keeps:
        keep.wait()


def forward(tables, stream, scales, biases, cosines, sines, wide, tall, cotangent, last_bias, number):
    rows, width = stream.shape
    total = 16 * rows
    layers = wide.shape[0]
    half = rows // layers
    shapes = [
        jax.ShapeDtypeStruct((16, rows, width), BF16),
        jax.ShapeDtypeStruct((total, 4 * HEAD), BF16),
        jax.ShapeDtypeStruct((total, 4 * HEAD), F32),
        jax.ShapeDtypeStruct((total, 2 * HEAD), F32),
        jax.ShapeDtypeStruct((total, 2 * HEAD), BF16),
        jax.ShapeDtypeStruct((2, total, 2 * HEAD), BF16),
        jax.ShapeDtypeStruct((total, 2 * HEAD), F32),
    ] * layers
    shapes += [jax.ShapeDtypeStruct((16, half, width), BF16)] * layers
    shapes += [
        jax.ShapeDtypeStruct((4,) + wide.shape[1:], BF16),
        jax.ShapeDtypeStruct((6 * HEAD, width), BF16),
    ] * layers
    shapes.append(jax.ShapeDtypeStruct((rows, width), F32))
    swap = [pltpu.VMEM((total, 2 * HEAD), BF16), pltpu.SemaphoreType.DMA((2,))]
    scratch = [pltpu.VMEM((rows, width), BF16)] * 2
    scratch += [pltpu.VMEM((total, 2 * HEAD), BF16)] * 4
    scratch += [pltpu.SemaphoreType.DMA((2, 20))] * 4
    scratch += gather_sems() + gather_sems()
    scratch += ([pltpu.VMEM((4,) + tall.shape[1:], BF16)] + share_sems(2)) * 2
    scratch += [pltpu.VMEM((16, rows, width), BF16), pltpu.VMEM((rows, width), F32)]
    scratch += scatter_scratch(rows, width)
    scratch += [pltpu.VMEM((total, 2 * HEAD), F32)] * 3 + swap + swap
    given = [stream, scales[0], biases[0], cosines, sines, wide[0], tall[0]]
    given += [cotangent[layer * half : (layer + 1) * half] for layer in range(layers)]
    given += [last_bias, wide[1], tall[1], scales[1], biases[1]]
    made = staged_call(
        forward_body, "forward", number, given, shapes, scratch, tables, direct=(14, 15)
    )
    return (made[:7], made[7:14]), made[14:16], (made[16], made[18]), (made[17], made[19]), made[20]


def back_enter_phase(grid, wait, ins, outs, tall_sum, gather_refs=None, beside=()):
    grad_ref, active_ref, context_ref, slope_ref, normed_ref, tall_ref, scale_ref = ins[:7]
    pull_ref, offset_ref, hidden_ref, early_ref, out_ref, up_ref, up_bias_ref = outs
    gathers = gather_refs is not None
    rows = normed_ref.shape[-2]
    if gathers:
        own, all_rows, send_sem, recv_sem = gather_refs
        gather = gather_steps(grid, own, all_rows, send_sem, recv_sem)
        run(gather, 2)
        for steps in beside:
            run(steps, 1)
    tall_sum[...] = jnp.zeros_like(tall_sum)
    up_ref[...] = jnp.zeros_like(up_ref)
    up_bias_ref[...] = jnp.zeros_like(up_bias_ref)

    def block(ranks):
        if gathers:
            branch = blocks_of(all_rows, ranks)
        else:
            branch = jnp.concatenate([half[rank] for rank in ranks for half in (grad_ref, ins[7])], 0)
        back = dots(branch, tall_ref[...], 1, 1)
        hidden_grad = (back[:, : 4 * HEAD] * rows_of(slope_ref, ranks, rows)).astype(BF16)
        pull = back[:, 4 * HEAD :].astype(BF16)
        put_rows(hidden_ref, ranks, rows, hidden_grad)
        put_rows(pull_ref, ranks, rows, pull)
        context = rows_of(context_ref, ranks, rows)
        offset = jnp.sum(pull.astype(F32) * context, 1, keepdims=True)
        put_rows(offset_ref, ranks, rows, jnp.broadcast_to(offset, context.shape))
        both = jnp.concatenate([rows_of(active_ref, ranks, rows), context.astype(BF16)], 1)
        ones = jnp.ones(context.shape, BF16)
        tall_sum[...] += dots(both, branch, 0, 0)
        up_ref[...] += dots(hidden_grad, blocks_of(normed_ref, ranks), 0, 0)
        up_bias_ref[...] += dots(hidden_grad, ones, 0, 0)

    if gathers:
        follow(grid, gather, block, lambda: wait(*range(1, 7)))
    else:
        wait(5)
        for piece in range(PIECES):
            wait.piece(piece, 0, 1, 2, 3, 4, 7)
            block([piece * 4 + i for i in range(4)])
    up_grad = (up_ref[...] * scale_ref[1:2] + up_bias_ref[:, 0:1] * scale_ref[3:4]).astype(BF16)
    for shard in range(4):
        early_ref[shard, : 4 * PART] = up_grad[:, shard * LANES : (shard + 1) * LANES]
        early_ref[shard, 8 * PART :] = jnp.zeros((PART, LANES), BF16)
        for lanes in range(4):
            early_ref[shard, (4 + lanes) * PART : (5 + lanes) * PART] = tall_sum[
                shard * HEAD : (shard + 1) * HEAD, lanes * LANES : (lanes + 1) * LANES
            ].astype(BF16)
            low = 5 * HEAD + shard * 16
            out_ref[shard, lanes * 16 : (lanes + 1) * 16] = tall_sum[
                low : low + 16, lanes * LANES : (lanes + 1) * LANES
            ].astype(BF16)


def back_enter_shapes(rows, width):
    total = 16 * rows
    return [
        jax.ShapeDtypeStruct((total, 4 * HEAD), BF16),
        jax.ShapeDtypeStruct((4 * HEAD, width), F32),
        jax.ShapeDtypeStruct((4 * HEAD, 2 * HEAD), F32),
    ], [
        pltpu.VMEM((total, 2 * HEAD), BF16),
        pltpu.VMEM((total, 2 * HEAD), F32),
        pltpu.VMEM((4, EARLY, LANES), BF16),
        pltpu.VMEM((4, PART, LANES), BF16),
        pltpu.VMEM((6 * HEAD, width), F32),
    ]


def back_leave_phase(grid, wait, ins, outs, refs, exchanges, after=None):
    query_grad_ref, pair_grad_ref, hidden_ref, normed_ref, wide_ref, scale_ref = ins[:6]
    cos_ref, sin_ref, stream_ref, grad_ref, up_ref, up_bias_ref = ins[6:]
    new_ref, addend_ref = outs
    (mixed, raw, raw_bias, parts, total_rows), scratch = refs[:5], refs[5:]
    rows, width = stream_ref.shape
    wait(0, 1, 2, 4, 6, 7)

    def make(ranks):
        cosines, sines = rows_of(cos_ref, ranks, rows), -rows_of(sin_ref, ranks, rows)
        query = rows_of(query_grad_ref, ranks, rows) * 0.125
        lane = lax.broadcasted_iota(jnp.int32, query.shape, 1)
        query = jnp.where(lane < HEAD, query, 0.0)
        pair = rows_of(pair_grad_ref, ranks, rows)
        both = jnp.concatenate(
            [rotate(pair, cosines, sines), rotate(query, cosines, sines)], 1
        ).astype(BF16)
        put_rows(mixed, ranks, rows, both)
        first = dots(both, wide_ref[:, : 4 * HEAD], 1, 1)
        second = dots(rows_of(hidden_ref, ranks, rows), wide_ref[:, 4 * HEAD :], 1, 1)
        made = (first * scale_ref[0:1] + second * scale_ref[1:2]).astype(BF16)
        for index, rank in enumerate(ranks):
            parts[rank] = made[index * rows : (index + 1) * rows]

    scatter = scatter_steps(grid, make, parts, total_rows, *scratch)
    run(scatter, 3)
    wait()
    for steps in exchanges:
        run(steps, 1)
    run(scatter, 5)
    raw[...] = jnp.zeros_like(raw)
    raw_bias[...] = jnp.zeros_like(raw_bias)
    ones = jnp.ones((4 * rows, 2 * HEAD), BF16)

    def sums(index):
        span = pl.ds(index * 4 * rows, 4 * rows)
        both = mixed[span, :]
        normed_rows = normed_ref[pl.ds(index * 4, 4)].reshape(4 * rows, width)
        raw[...] += dots(both, normed_rows, 0, 0)
        raw_bias[...] += dots(both, ones, 0, 0)

    sums(0)
    run(scatter, 1)
    sums(1)
    run(scatter, 1)
    sums(2)
    run(scatter, 1)
    sums(3)

    wide_t = jnp.transpose(wide_ref[:, : 4 * HEAD].astype(F32))
    up_t = jnp.transpose(wide_ref[:, 4 * HEAD :].astype(F32))
    mixed_bias, up_bias = raw_bias[:, 0:1], up_bias_ref[:, 0:1]
    first_raw, second_raw = raw[...], up_ref[...]
    vectors = [
        jnp.sum(wide_t * first_raw, 0, keepdims=True),
        jnp.sum(up_t * second_raw, 0, keepdims=True),
        jnp.sum(wide_t * mixed_bias, 0, keepdims=True),
        jnp.sum(up_t * up_bias, 0, keepdims=True),
        jnp.sum(grad_ref[...].astype(BF16).astype(F32), 0, keepdims=True),
    ]
    first_grad = (first_raw * scale_ref[0:1] + mixed_bias * scale_ref[2:3]).astype(BF16)
    biases = [
        jnp.transpose(raw_bias[...])[0:1],
        jnp.transpose(up_bias_ref[...])[0:1],
    ]
    for shard in range(4):
        lanes = slice(shard * LANES, (shard + 1) * LANES)
        addend_ref[shard, : 3 * PART] = first_grad[: 3 * PART, lanes]
        tail = [vector[:, lanes] for vector in vectors] + biases
        tail.append(jnp.zeros((PART - len(tail), LANES), F32))
        addend_ref[shard, 3 * PART :] = jnp.concatenate(tail, 0).astype(BF16)
    run(scatter)
    for steps in exchanges:
        run(steps)
    if after is not None:
        after()
    normed, inverse = standardize(stream_ref[...])
    normed_grad = total_rows[...]
    new_ref[...] = grad_ref[...] + inverse * (
        normed_grad
        - jnp.mean(normed_grad, -1, keepdims=True)
        - normed * jnp.mean(normed_grad * normed, -1, keepdims=True)
    )


def back_leave_scratch(rows, width):
    total = 16 * rows
    return [
        pltpu.VMEM((total, 4 * HEAD), BF16),
        pltpu.VMEM((4 * HEAD, width), F32),
        pltpu.VMEM((4 * HEAD, 2 * HEAD), F32),
        pltpu.VMEM((16, rows, width), BF16),
        pltpu.VMEM((rows, width), F32),
    ] + scatter_scratch(rows, width)


def back_leave_body(wait, tables, ins, outs, refs):
    grid = Grid()
    grid.barrier([mate()])
    exchanges = [low_steps(ins[12], outs[2], *refs[11:], ins[13])]
    back_leave_phase(grid, wait, ins[:12], outs[:2], refs[:11], exchanges)


def back_leave(given, rows, width, number, sums, total):
    shapes = [
        jax.ShapeDtypeStruct((rows, width), F32),
        jax.ShapeDtypeStruct((4, LATE, LANES), BF16),
        jax.ShapeDtypeStruct((EARLY, LANES), BF16),
    ]
    scratch = back_leave_scratch(rows, width) + swap_scratch(EARLY)
    given = tuple(given) + (sums, total)
    return staged_call(back_leave_body, "back_leave", number, given, shapes, scratch)


def sibling():
    shard = lax.axis_index("fsdp")
    return {"fsdp": shard + 1 - 2 * (shard % 2)}


def mate():
    return {"fsdp": (lax.axis_index("fsdp") + 2) % 4}


def far_partner():
    slot = lax.axis_index("ctx")
    return {"ctx": slot + 1 - 2 * (slot % 2)}


def wide_barrier(grid):
    shard = lax.axis_index("fsdp")
    at_home = grid.x == shard
    gate = pltpu.get_barrier_semaphore()
    partners = [grid.device(0, *step) for step in grid.meets]
    partners += [sibling(), mate(), far_partner()]
    for partner in partners:
        pl.semaphore_signal(gate, inc=1, device_id=partner, device_id_type=MESH)
    for other in range(4):

        @pl.when(jnp.logical_not(at_home & (shard == other)))
        def greet():
            pl.semaphore_signal(
                gate,
                inc=1,
                device_id={"ctx": (shard * SIDE + grid.y) * 2 + grid.z, "fsdp": other},
                device_id_type=MESH,
            )

    pl.semaphore_wait(gate, len(partners) + 4 - at_home.astype(jnp.int32))


def remote(source, target, send, recv, to):
    return pltpu.make_async_remote_copy(
        src_ref=source,
        dst_ref=target,
        send_sem=send,
        recv_sem=recv,
        device_id=to,
        device_id_type=MESH,
    )


def added(a, b):
    return (a.astype(F32) + b.astype(F32)).astype(BF16)


def core_steps(in_ref, sums_ref, land, sems):
    shard = lax.axis_index("fsdp")
    low, core = shard // 2, shard % 2
    copies = [
        remote(
            in_ref.at[part * 2 + 1 - core],
            land.at[part],
            sems.at[0, part],
            sems.at[1, part],
            sibling(),
        )
        for part in (0, 1)
    ]
    for copy in copies:
        copy.start()
    yield
    for copy in copies:
        copy.wait_recv()
    sums_ref[0] = added(in_ref[low * 2 + core], land[low])
    sums_ref[1] = added(in_ref[(1 - low) * 2 + core], land[1 - low])
    for copy in copies:
        copy.wait_send()


def core_scratch(rows):
    return [pltpu.VMEM((2, rows, LANES), BF16), pltpu.SemaphoreType.DMA((2, 2))]


def low_steps(sums_ref, pair_ref, land, sems, total_ref=None):
    copy = remote(sums_ref.at[1], land, sems.at[0], sems.at[1], mate())
    copy.start()
    yield
    copy.wait_recv()
    pair_ref[...] = added(sums_ref[0], land[...])
    if total_ref is not None:
        pair_ref[pair_ref.shape[0] - PART :] = total_ref[...]
    copy.wait_send()


def high_steps(pair_ref, own_ref, land, sems):
    copy = remote(pair_ref, land, sems.at[0], sems.at[1], far_partner())
    copy.start()
    yield
    copy.wait_recv()
    own_ref[...] = added(pair_ref[...], land[...])
    copy.wait_send()


def swap_scratch(rows):
    return [pltpu.VMEM((rows, LANES), BF16), pltpu.SemaphoreType.DMA((2,))]


def quarter_steps(grid, quarter_ref, total_ref, land, send_sem, recv_sem):
    x, y, z = grid.x, grid.y, grid.z
    shard = lax.axis_index("fsdp")
    at_home = x == shard

    def copy(column):
        return remote(
            quarter_ref.at[column],
            land.at[shard],
            send_sem.at[column],
            recv_sem.at[shard],
            {"ctx": (column * SIDE + y) * 2 + z, "fsdp": x},
        )

    for column in range(4):

        @pl.when(jnp.logical_not(at_home & (x == column)))
        def give():
            copy(column).start()

        @pl.when(at_home & (x == column))
        def keep():
            land[shard] = quarter_ref[column]

    yield
    for other in range(4):

        @pl.when(jnp.logical_not(at_home & (shard == other)))
        def take():
            remote(
                land.at[other], land.at[other], send_sem.at[other], recv_sem.at[other], mate()
            ).wait_recv()

    total = land[0].astype(F32)
    for other in range(1, 4):
        total = total + land[other].astype(F32)
    total_ref[...] = total.astype(BF16)
    for column in range(4):

        @pl.when(jnp.logical_not(at_home & (x == column)))
        def gone():
            copy(column).wait_send()


def quarter_scratch():
    return [
        pltpu.VMEM((4, PART, LANES), BF16),
        pltpu.SemaphoreType.DMA((4,)),
        pltpu.SemaphoreType.DMA((4,)),
    ]


def gather_sems():
    return [
        pltpu.SemaphoreType.DMA,
        pltpu.SemaphoreType.DMA((2, 20)),
        pltpu.SemaphoreType.DMA((2, 20)),
    ]


def keep_own(grid, own, every, sem):
    copy = pltpu.make_async_copy(own, every.at[grid.rank(0, 0, 0)], sem)
    copy.start()
    return copy


def last_body(wait, tables, ins, outs, refs):
    new_ref, all_early, all_other, all_late = outs
    leave_refs, refs = refs[:11], refs[11:]
    (late_addends, early, other, sums, pair, late), refs = refs[:6], refs[6:]
    early_swap, other_swap, refs = refs[:2], refs[2:4], refs[4:]
    core_refs, low_refs, high_refs, refs = refs[:2], refs[2:4], refs[4:6], refs[6:]
    early_sems, other_sems, late_sems = refs[:3], refs[3:6], refs[6:9]
    grid = Grid()
    grid.barrier([sibling(), mate(), far_partner()])
    exchanges = [high_steps(ins[12], early, *early_swap), high_steps(ins[13], other, *other_swap)]
    first = gather_steps(grid, early, all_early, *early_sems[1:])
    second = gather_steps(grid, other, all_other, *other_sems[1:])
    keeps = []

    def start():
        for steps in exchanges:
            run(steps)
        run(first, 2)
        keeps.append(keep_own(grid, early, all_early, early_sems[0]))
        keeps.append(keep_own(grid, other, all_other, other_sems[0]))

    back_leave_phase(
        grid, wait, ins[:12], (new_ref, late_addends), leave_refs, exchanges, start
    )
    wait.flush()
    core = core_steps(late_addends, sums, *core_refs)
    run(core, 1)
    run(first, 2)
    run(core)
    low = low_steps(sums, pair, *low_refs)
    run(low, 1)
    run(first, 4)
    run(low)
    high = high_steps(pair, late, *high_refs)
    run(high, 1)
    run(second, 2)
    run(first, 4)
    run(second, 2)
    run(high)
    keeps.append(keep_own(grid, late, all_late, late_sems[0]))
    third = gather_steps(grid, late, all_late, *late_sems[1:])
    run(third, 2)
    for unused in range(GATHER_STEPS):
        run(first, 1)
        run(second, 1)
        run(third, 1)
    run(third)
    for keep in keeps:
        keep.wait()


def back_leave_last(given, rows, width, number, early, other):
    shapes = [
        jax.ShapeDtypeStruct((rows, width), F32),
        jax.ShapeDtypeStruct((16,) + early.shape, BF16),
        jax.ShapeDtypeStruct((16,) + other.shape, BF16),
        jax.ShapeDtypeStruct((16, LATE, LANES), BF16),
    ]
    scratch = back_leave_scratch(rows, width)
    scratch += [
        pltpu.VMEM((4, LATE, LANES), BF16),
        pltpu.VMEM(early.shape, BF16),
        pltpu.VMEM(other.shape, BF16),
        pltpu.VMEM((2, LATE, LANES), BF16),
        pltpu.VMEM((LATE, LANES), BF16),
        pltpu.VMEM((LATE, LANES), BF16),
    ]
    scratch += swap_scratch(early.shape[0]) + swap_scratch(other.shape[0])
    scratch += core_scratch(LATE) + swap_scratch(LATE) + swap_scratch(LATE)
    scratch += gather_sems() + gather_sems() + gather_sems()
    given = tuple(given) + (early, other)
    return staged_call(
        last_body, "back_leave_last", number, given, shapes, scratch, direct=(1, 2, 3)
    )


def turn_kernel(first_ref, second_ref, out_ref):
    layer = pl.program_id(0)
    row = lax.broadcasted_iota(jnp.int32, (LANES, LANES), 0)
    column = lax.broadcasted_iota(jnp.int32, (LANES, LANES), 1)
    unit = (row == column).astype(BF16)

    @pl.when(layer == 0)
    def first():
        out_ref[0] = dots(unit, first_ref[...].reshape(-1, LANES), 1, 1)

    @pl.when(layer == 1)
    def second():
        out_ref[0] = dots(unit, second_ref[...].reshape(-1, LANES), 1, 1)


def turned_parts(gathered, first, count, turn=0):
    layers = len(gathered)

    def spec(own):
        return pl.BlockSpec(
            (16, PART, LANES),
            lambda i, j: (0, first + (jnp.where(i == own, j, own * 0) + turn) % count, 0),
        )

    return pl.pallas_call(
        turn_kernel,
        grid=(layers, count),
        out_shape=jax.ShapeDtypeStruct((layers, LANES, count * 16 * PART), F32),
        in_specs=[spec(own) for own in range(layers)],
        out_specs=pl.BlockSpec((1, LANES, 16 * PART), lambda i, j: (i, 0, j)),
        name="turned_parts",
        compiler_params=pltpu.CompilerParams(vmem_limit_bytes=60 << 20),
    )(*gathered)


def tall_kernel(down_one, down_two, out_one, out_two, down_ref, out_ref):
    layer = pl.program_id(0)

    def put(down_in, out_in):
        down_ref[0] = down_in[...].astype(F32).reshape(16 * PART, LANES)
        for x in range(4):
            for y in range(4):
                out_ref[0, pl.ds(y * HEAD + x * 16, 16)] = out_in[x * 4 + y].astype(F32)

    @pl.when(layer == 0)
    def first():
        put(down_one, out_one)

    @pl.when(layer == 1)
    def second():
        put(down_two, out_two)


def tall_parts(gathered):
    layers = len(gathered)
    width = 4 * LANES

    def step(i, j, own):
        return jnp.where(i == own, j, 0)

    return pl.pallas_call(
        tall_kernel,
        grid=(layers, 4),
        out_shape=[
            jax.ShapeDtypeStruct((layers, 16 * PART, width), F32),
            jax.ShapeDtypeStruct((layers, LANES, width), F32),
        ],
        in_specs=[
            pl.BlockSpec((16, PART, LANES), lambda i, j, own=own: (0, 4 + step(i, j, own), 0))
            for own in range(layers)
        ]
        + [
            pl.BlockSpec(
                (16, 16, LANES), lambda i, j, own=own: (0, 32 + step(i, j, own), 0)
            )
            for own in range(layers)
        ],
        out_specs=[
            pl.BlockSpec((1, 16 * PART, LANES), lambda i, j: (i, 0, j)),
            pl.BlockSpec((1, LANES, LANES), lambda i, j: (i, 0, j)),
        ],
        name="tall_parts",
        compiler_params=pltpu.CompilerParams(vmem_limit_bytes=60 << 20),
    )(*gathered, *gathered)


SPAN = 1024
ATTEND_WORK = 88
SWAP_WORK = 32


def sort_in(source_ref, order_ref, target_ref, count):
    def body(i, unused):
        start = order_ref[i] * BLK
        target_ref[pl.ds(pl.multiple_of(i * BLK, BLK), BLK), :] = source_ref[
            pl.ds(start, BLK), :
        ]
        return unused

    lax.fori_loop(0, count, body, 0, unroll=8)


def block_numbers(number_ref, first, count, axis):
    if axis == 0:
        return jnp.concatenate(
            [jnp.full((BLK, 1), number_ref[first + i], jnp.int32) for i in range(count)], 0
        )
    lane = lax.broadcasted_iota(jnp.int32, (1, count * BLK), 1) // BLK
    numbers = jnp.zeros((1, count * BLK), jnp.int32)
    for i in range(count):
        numbers = jnp.where(lane == i, number_ref[first + i], numbers)
    return numbers


def far_copy(source, target, sems):
    return pltpu.make_async_remote_copy(
        src_ref=source,
        dst_ref=target,
        send_sem=sems.at[0],
        recv_sem=sems.at[1],
        device_id=far_partner(),
        device_id_type=MESH,
    )


def attend_steps(tables, q_ref, kv_ref, context_ref, qs, kvs, logs, scratch):
    order_ref, standing_ref, number_ref, other_order, other_ref = tables
    tops, totals, sums, far_ref, sems = scratch
    copy = far_copy(kv_ref, far_ref, sems)
    copy.start()
    sort_in(kv_ref, order_ref, kvs.at[0], 32)
    sort_in(q_ref, order_ref, qs, 32)
    tiles = qs.shape[0] // TILE
    row = lax.broadcasted_iota(jnp.int32, (TILE, TILE), 0)
    column = lax.broadcasted_iota(jnp.int32, (TILE, TILE), 1)
    yield 4

    def highest(scores):
        return jnp.max(scores, 1, keepdims=True)

    def weigh(scores, top, keys):
        weights = jnp.exp(scores - top)
        return jnp.sum(weights, 1, keepdims=True), dots(weights.astype(BF16), keys, 1, 0)

    def wide(vector):
        return jnp.broadcast_to(vector, (TILE, 2 * HEAD))

    def own_tile(tile):
        rows = slice(tile * TILE, (tile + 1) * TILE)
        queries, near = qs[rows, :], kvs[0, rows, :]
        parts = [(jnp.where(column <= row, dots(queries, near, 1, 1), NEGATIVE), near)]
        for low in range(0, tile * TILE, SPAN):
            keys = kvs[0, low : min(low + SPAN, tile * TILE), :]
            parts.append((dots(queries, keys, 1, 1), keys))
        top = highest(parts[0][0])
        for scores, keys in parts[1:]:
            top = jnp.maximum(top, highest(scores))
        total, weighted = 0.0, 0.0
        for scores, keys in parts:
            more, product = weigh(scores, top, keys)
            total, weighted = total + more, weighted + product
        tops[rows, :], totals[rows, :], sums[rows, :] = wide(top), wide(total), weighted

    def other_tile(tile, numbers):
        rows = slice(tile * TILE, (tile + 1) * TILE)
        queries = qs[rows, :]
        own = block_numbers(number_ref, tile * TILE // BLK, TILE // BLK, 0)
        half = tile // 4
        keys = kvs[1, half * SPAN : (half + 1) * SPAN, :]
        parts = [(jnp.where(numbers < own, dots(queries, keys, 1, 1), NEGATIVE), keys)]
        if half:
            keys = kvs[1, :SPAN, :]
            parts.append((dots(queries, keys, 1, 1), keys))
        old = tops[rows, :][:, 0:1]
        top = old
        for scores, keys in parts:
            top = jnp.maximum(top, highest(scores))
        scale = jnp.exp(old - top)
        total, weighted = totals[rows, :][:, 0:1] * scale, sums[rows, :] * scale
        for scores, keys in parts:
            more, product = weigh(scores, top, keys)
            total, weighted = total + more, weighted + product
        sums[rows, :] = weighted / total
        logs[rows, :] = wide(top + jnp.log(total))

    for tile in range(tiles):
        own_tile(tile)
        yield tile + 1
    for unused in range(8):
        yield SWAP_WORK // 8
    copy.wait_recv()
    sort_in(far_ref, other_order, kvs.at[1], 32)
    for half in (0, 1):
        numbers = block_numbers(other_ref, half * 16, 16, 1)
        for tile in range(half * 4, half * 4 + 4):
            other_tile(tile, numbers)
            yield 4 + 4 * half
    sort_in(sums, standing_ref, context_ref, 32)
    copy.wait_send()


def attend_back_steps(
    tables, qs, kvs, logs, pull_ref, offset_ref, query_grad_ref, pair_grad_ref, scratch
):
    order_ref, standing_ref, number_ref, unused, other_ref = tables
    pulls, offsets, turned, query_sums, pair_sums, away, land, sems = scratch
    sort_in(pull_ref, order_ref, pulls, 32)
    sort_in(offset_ref, order_ref, offsets, 32)
    pair_sums[...] = jnp.zeros_like(pair_sums)
    tiles = qs.shape[0] // TILE
    row = lax.broadcasted_iota(jnp.int32, (TILE, TILE), 0)
    column = lax.broadcasted_iota(jnp.int32, (TILE, TILE), 1)
    lane = lax.broadcasted_iota(jnp.int32, (TILE, 2 * HEAD), 1)
    yield 4

    def tile_part(tile, half, low, count, mask):
        rows = slice(tile * TILE, (tile + 1) * TILE)
        queries, pull = qs[rows, :], pulls[rows, :]
        keys = kvs[half, low : low + count, :]
        scores = dots(keys, queries, 1, 1)
        if mask is not None:
            scores = jnp.where(mask, scores, NEGATIVE)
        probs = jnp.exp(scores - turned[tile, 0:1])
        score_grad = (probs * (dots(keys, pull, 1, 1) - turned[tile, 1:2])).astype(BF16)
        pair_sums[half, low : low + count, :] += dots(score_grad, queries, 1, 0) + dots(
            probs.astype(BF16), pull, 1, 0
        )
        return dots(score_grad, keys, 0, 0)

    def masked_tile(tile, numbers):
        rows = slice(tile * TILE, (tile + 1) * TILE)
        turned[tile] = jnp.transpose(
            jnp.where(lane == 0, logs[rows, :], offsets[rows, :])
        )[:8]
        own = block_numbers(number_ref, tile * TILE // BLK, TILE // BLK, 1)
        query_sums[rows, :] = tile_part(tile, 1, tile // 4 * SPAN, SPAN, numbers < own)

    def send(half):
        span = pl.ds(half * SPAN, SPAN)
        away[span] = pair_sums[1, span].astype(BF16)
        copy = far_copy(away.at[span], land.at[span], sems.at[half])
        copy.start()
        return copy

    def own_tile(tile):
        rows = slice(tile * TILE, (tile + 1) * TILE)
        query_sums[rows, :] += tile_part(tile, 0, tile * TILE, TILE, row <= column)
        yield 1
        for low in range(0, tile * TILE, SPAN):
            count = min(SPAN, tile * TILE - low)
            query_sums[rows, :] += tile_part(tile, 0, low, count, None)
            yield count // TILE

    copies = []
    for half in (1, 0):
        numbers = block_numbers(other_ref, half * 16, 16, 0)
        for tile in range(half * 4, half * 4 + 4):
            masked_tile(tile, numbers)
            yield 4
        if half == 0:
            for tile in range(4, 8):
                rows = slice(tile * TILE, (tile + 1) * TILE)
                query_sums[rows, :] += tile_part(tile, 1, 0, SPAN, None)
                yield 4
        copies.append(send(half))
    for tile in range(tiles):
        yield from own_tile(tile)
    sort_in(query_sums, standing_ref, query_grad_ref, 32)
    for copy in copies:
        copy.wait_recv()
    pair_sums[0] += land[...].astype(F32)
    sort_in(pair_sums.at[0], standing_ref, pair_grad_ref, 32)
    for copy in copies:
        copy.wait_send()


def attend_back_scratch(rows):
    block = (rows, 2 * HEAD)
    return [
        pltpu.VMEM(block, BF16),
        pltpu.VMEM(block, F32),
        pltpu.VMEM((rows // TILE, 8, TILE), F32),
        pltpu.VMEM(block, F32),
        pltpu.VMEM((2,) + block, F32),
        pltpu.VMEM(block, BF16),
        pltpu.VMEM(block, BF16),
        pltpu.SemaphoreType.DMA((2, 2)),
    ]


def take_turns(work, total, others):
    done = 0
    ran = [first for steps, count, first, early, part in others]
    for steps, count, first, early, part in others:
        run(steps, first)
    for more in work:
        done += more
        for index, (steps, count, first, early, part) in enumerate(others):
            wanted = early + min(int(done * (count - early) / (total * part)), count - early)
            run(steps, wanted - ran[index])
            ran[index] = wanted
    for steps, *unused in others:
        run(steps)


def back_last_body(wait, tables, ins, outs, refs):
    hidden_ref, up_ref, up_bias_ref, query_grad_ref, pair_grad_ref, sums_ref, total_ref, out_ref = outs
    (pull, offset, early, quarter, tall_sum), refs = refs[:5], refs[5:]
    (parts, total_rows), scatter_refs, refs = refs[:2], refs[2:8], refs[8:]
    core_refs, quarter_refs, scratch = refs[:2], refs[2:5], refs[5:]
    grid = Grid()
    wide_barrier(grid)
    made = [pull, offset, hidden_ref, early, quarter, up_ref, up_bias_ref]
    back_enter_phase(grid, wait, ins[:8], made, tall_sum)
    wait.flush(0, 1, 2)
    wait()
    leaving = [ins[1], ins[2], ins[5], ins[11], ins[12]]
    scatter = leave_steps(grid, *leaving, out_ref, parts, total_rows, scatter_refs)
    core = core_steps(early, sums_ref, *core_refs)
    quarters = quarter_steps(grid, quarter, total_ref, *quarter_refs)
    work = attend_back_steps(
        tables, *ins[8:11], pull, offset, query_grad_ref, pair_grad_ref, scratch
    )
    others = [
        (core, 1, 1, 1, 1.0),
        (quarters, 1, 1, 1, 1.0),
        (scatter, SCATTER_STEPS, 1, 1, 1.0),
    ]
    take_turns(work, ATTEND_WORK, others)


def back_last(tables, branch, given, attention, stream, bias, number):
    rows, width = stream.shape
    shapes, scratch = back_enter_shapes(rows, width)
    total = 16 * rows
    shapes = shapes + [jax.ShapeDtypeStruct((total, 2 * HEAD), F32)] * 2
    shapes += [
        jax.ShapeDtypeStruct((2, EARLY, LANES), BF16),
        jax.ShapeDtypeStruct((PART, LANES), BF16),
        jax.ShapeDtypeStruct((rows, width), BF16),
    ]
    scratch = scratch + [
        pltpu.VMEM((16, rows, width), BF16),
        pltpu.VMEM((rows, width), F32),
    ]
    scratch += scatter_scratch(rows, width) + core_scratch(EARLY) + quarter_scratch()
    scratch += attend_back_scratch(total)
    given = [branch[0], *given, branch[1], *attention, stream, bias]
    return staged_call(
        back_last_body, "back_last", number, given, shapes, scratch, tables,
        parted=(0, 1, 2, 3, 4, 7),
    )


def back_first_body(wait, tables, ins, outs, refs):
    (
        hidden_ref, up_ref, up_bias_ref, query_grad_ref, pair_grad_ref, pair_ref, late_pair, all_ref
    ) = outs
    (pull, offset, early, quarter, tall_sum), refs = refs[:5], refs[5:]
    (own, all_rows, *row_sems), refs = refs[:4], refs[4:]
    (folded, late_sums, sums, total), refs = refs[:4], refs[4:]
    high_refs, late_core_refs, refs = refs[:2], refs[2:4], refs[4:]
    gather_refs, core_refs, quarter_refs, refs = refs[:3], refs[3:5], refs[5:8], refs[8:]
    early_refs, late_refs, scratch = refs[:2], refs[2:4], refs[4:]
    grid = Grid()
    wait(0)
    own[...] = ins[0][...].astype(BF16)
    all_rows[grid.rank(0, 0, 0)] = own[...]
    wide_barrier(grid)
    wait(7, 8)
    beside = [
        high_steps(ins[7], folded, *high_refs),
        core_steps(ins[8], late_sums, *late_core_refs),
    ]
    made = [pull, offset, hidden_ref, early, quarter, up_ref, up_bias_ref]
    back_enter_phase(grid, wait, ins[:7], made, tall_sum, (own, all_rows, *row_sems), beside)
    wait.flush(0, 1, 2)
    for steps in beside:
        run(steps)
    keep = keep_own(grid, folded, all_ref, gather_refs[0])
    gather = gather_steps(grid, folded, all_ref, *gather_refs[1:])
    run(gather, 2)
    wait()
    quarters = quarter_steps(grid, quarter, total, *quarter_refs)
    late = low_steps(late_sums, late_pair, *late_refs)

    def early_steps():
        core = core_steps(early, sums, *core_refs)
        next(core)
        yield
        run(core)
        run(quarters)
        yield from low_steps(sums, pair_ref, *early_refs, total)

    work = attend_back_steps(
        tables, *ins[9:12], pull, offset, query_grad_ref, pair_grad_ref, scratch
    )
    others = [
        (gather, GATHER_STEPS - 2, 0, 5, 0.9),
        (quarters, 1, 1, 1, 1.0),
        (early_steps(), 2, 1, 1, 0.5),
        (late, 1, 1, 1, 1.0),
    ]
    take_turns(work, ATTEND_WORK, others)
    keep.wait()


def back_first(tables, grad, given, exchanged, attention, number):
    rows, width = grad.shape
    shapes, scratch = back_enter_shapes(rows, width)
    total = 16 * rows
    shapes = shapes + [jax.ShapeDtypeStruct((total, 2 * HEAD), F32)] * 2
    shapes += [
        jax.ShapeDtypeStruct((EARLY, LANES), BF16),
        jax.ShapeDtypeStruct((LATE, LANES), BF16),
        jax.ShapeDtypeStruct((16, EARLY, LANES), BF16),
    ]
    scratch = scratch + [
        pltpu.VMEM((rows, width), BF16),
        pltpu.VMEM((16, rows, width), BF16),
        pltpu.SemaphoreType.DMA((2, 20)),
        pltpu.SemaphoreType.DMA((2, 20)),
        pltpu.VMEM((EARLY, LANES), BF16),
        pltpu.VMEM((2, LATE, LANES), BF16),
        pltpu.VMEM((2, EARLY, LANES), BF16),
        pltpu.VMEM((PART, LANES), BF16),
    ]
    scratch += swap_scratch(EARLY) + core_scratch(LATE) + gather_sems()
    scratch += core_scratch(EARLY) + quarter_scratch()
    scratch += swap_scratch(EARLY) + swap_scratch(LATE) + attend_back_scratch(total)
    given = [grad, *given, *exchanged, *attention]
    return staged_call(
        back_first_body, "back_first", number, given, shapes, scratch, tables, direct=(7,)
    )


def block_tables(pair_table, z):
    slots = pair_table.shape[0]
    ranks = slots // 2
    index = jnp.arange(slots, dtype=jnp.int32)

    def plane(which):
        pairs = lax.dynamic_slice_in_dim(pair_table.reshape(ranks, 2), which, 1, 1)
        numbers = jnp.concatenate([pairs, 2 * slots - 1 - pairs], 1).reshape(-1)
        standing = jnp.sum((numbers[None, :] < numbers[:, None]).astype(jnp.int32), 1)
        chosen = (standing[None, :] == index[:, None]).astype(jnp.int32)
        order = jnp.sum(chosen * index[None, :], 1)
        return numbers, (order, standing, jnp.sum(chosen * numbers[None, :], 1))

    numbers, own = plane(z)
    other = plane(1 - z)[1]
    return numbers, own + (other[0], other[2])


def rotation(positions):
    freqs = 10000.0 ** (-jnp.arange(0, ROT, 2, dtype=F32) / ROT)
    angles = positions.astype(F32)[:, None] * freqs[None, :]
    rest = ((0, 0), (0, 2 * HEAD - ROT))
    return (
        jnp.pad(jnp.concatenate([jnp.cos(angles)] * 2, -1), rest, constant_values=1.0),
        jnp.pad(jnp.concatenate([jnp.sin(angles)] * 2, -1), rest),
    )


def on_device(
    hidden_in,
    cotangent,
    pair_table,
    norm_gain,
    norm_bias,
    qkv_weight,
    qkv_bias,
    out_weight,
    out_bias,
    up_weight,
    up_bias,
    down_weight,
    down_bias,
):
    layers = norm_gain.shape[0]
    slot = lax.axis_index("ctx")
    shard = lax.axis_index("fsdp")
    rank, z = slot // 2, slot % 2
    width = hidden_in.shape[2]
    quarter = width // 4

    numbers, tables = block_tables(pair_table, z)
    positions = (
        numbers[:, None] * BLK + jnp.arange(BLK, dtype=jnp.int32)[None, :]
    ).reshape(-1)
    cosines, sines = rotation(positions)

    def columns(weight, part):
        return lax.dynamic_slice_in_dim(weight, part * width + rank * HEAD, HEAD, 2)

    wide = jnp.concatenate(
        [columns(qkv_weight, 1), columns(qkv_weight, 2), columns(qkv_weight, 0)]
        + [jnp.zeros((layers, quarter, HEAD), BF16)]
        + [columns(up_weight, part) for part in range(4)],
        2,
    )
    tall = jnp.concatenate(
        [
            lax.dynamic_slice_in_dim(down_weight, rank * HEAD, HEAD, 1),
            lax.dynamic_slice_in_dim(out_weight, (rank % 4) * HEAD, HEAD, 1),
        ],
        1,
    )
    vectors = lax.all_gather(
        jnp.concatenate(
            [
                norm_gain.reshape(layers, -1),
                norm_bias.reshape(layers, -1),
                qkv_bias,
                out_bias,
                up_bias,
                down_bias,
            ],
            1,
        ),
        "fsdp",
        axis=0,
    ).astype(F32)

    scales, wide_biases, last_biases = [], [], []
    for layer in range(layers):
        vector = vectors[:, layer]
        scales.append(
            jnp.transpose(vector[:, 0:1024].reshape(4, 4, 256), (1, 0, 2)).reshape(4, width)
        )
        b_qkv = lax.dynamic_slice_in_dim(
            vector[:, 1024:1792].reshape(3, 16, HEAD), rank, 1, 1
        ).reshape(3, HEAD)
        b_up = lax.dynamic_slice_in_dim(
            vector[:, 2048:3072].reshape(4, 16, HEAD), rank, 1, 1
        ).reshape(4 * HEAD)
        wide_biases.append(
            jnp.concatenate([b_qkv[1], b_qkv[2], b_qkv[0], jnp.zeros((HEAD,), F32), b_up])[None]
        )
        last_biases.append((vector[:, 1792:2048] + vector[:, 3072:3328]).reshape(1, width))

    stream = hidden_in[0].astype(F32)
    saved, branch_all, wide_all, tall_all, second = forward(
        tables, stream, scales, wide_biases, cosines, sines, wide, tall, cotangent[0],
        last_biases[0], 1,
    )
    streams, number = (stream, second), 2

    grad = cotangent[0].astype(F32)
    early, late = [None] * layers, [None] * layers
    exchanged = None
    for layer in reversed(range(layers)):
        last = layer == layers - 1
        normed_all, active, slope, context, queries, pairs, logs = saved[layer]
        stream = streams[layer]
        given = (active, context, slope, normed_all, tall_all[layer], scales[layer])
        attention = (queries, pairs, logs)
        if last:
            (
                hidden_grad, up_raw, up_bias_raw, query_grad, pair_grad, early_sums, out_total, output
            ) = back_last(tables, branch_all, given, attention, stream, last_biases[layer], number)
            exchanges = (early_sums, out_total)
        else:
            (
                hidden_grad, up_raw, up_bias_raw, query_grad, pair_grad, early_pair, late_pair,
                early[layer + 1],
            ) = back_first(tables, grad, given, exchanged, attention, number)
            exchanges = (early_pair, late_pair)
        number += 1
        given = (
            query_grad,
            pair_grad,
            hidden_grad,
            normed_all,
            wide_all[layer].reshape(width, 8 * HEAD),
            scales[layer],
            cosines,
            sines,
            stream,
            grad,
            up_raw,
            up_bias_raw,
        )
        if last:
            grad, addends, early_pair = back_leave(given, *stream.shape, number, *exchanges)
            exchanged = (early_pair, addends)
        else:
            grad, early[0], late[1], late[0] = back_leave_last(
                given, *stream.shape, number, *exchanges
            )
        number += 1

    qkv_out = turned_parts(late, 0, 3, 2)
    up_out = turned_parts(early, 0, 4)
    down_out, out_out = tall_parts(early)
    small = jnp.stack(
        [every[:, 3 * PART : 3 * PART + 7] for every in late]
    ).astype(F32)
    sums = jnp.sum(small[:, :, :5], 1)
    gain_out, shift_out, branch_out = sums[:, 0:2], sums[:, 2:4], sums[:, 4]
    qkv_bias_out = jnp.transpose(
        jnp.roll(small[:, :, 5, : 3 * HEAD].reshape(layers, 16, 3, HEAD), 1, 2), (0, 2, 1, 3)
    ).reshape(layers, -1)
    share = qkv_bias_out.shape[1] // 4
    qkv_bias_out = lax.dynamic_slice_in_dim(qkv_bias_out, shard * share, share, 1)
    up_bias_out = lax.dynamic_slice_in_dim(
        small[:, :, 6].reshape(layers, 16, 4, HEAD), shard, 1, 2
    ).reshape(layers, -1)
    return (
        output[None],
        grad[None],
        gain_out,
        shift_out,
        qkv_out,
        qkv_bias_out,
        out_out,
        branch_out,
        up_out,
        up_bias_out,
        down_out,
        branch_out,
    )


def solution(mesh):
    rows = P("fsdp", "ctx", None)
    vector, matrix = P(None, "fsdp"), P(None, "fsdp", None)
    gains = P(None, None, "fsdp")
    params = (gains, gains) + (matrix, vector) * 4
    return jax.shard_map(
        on_device,
        mesh=mesh,
        in_specs=(rows, rows, P()) + params,
        out_specs=(rows, rows) + params,
        check_vma=False,
    )
```

```python
import functools

import jax
import jax.numpy as jnp
from jax import lax
from jax.experimental import pallas as pl
from jax.experimental.pallas import tpu as pltpu
from jax.sharding import PartitionSpec as P

HEADS = 16
HEAD = 64
ROT = 16
BLK = 64
SIDE = 4
EPS = 1e-05
NEGATIVE = -1e30
MESH = pl.DeviceIdType.MESH
F32 = jnp.float32
BF16 = jnp.bfloat16
TILE = 256
KEYS = 512
PART = 64
EARLY = 9 * PART
LATE = 3 * PART
LANES = 256


def place():
    slot = lax.axis_index("ctx")
    return slot // 8, (slot // 2) % SIDE, slot % 2


class Grid:
    def __init__(self, meets=((1, 0), (-1, 0), (0, 1), (0, -1))):
        self.x, self.y, self.z = place()
        self.meets = meets
        self.ranks, self.slots = {}, {}
        for dx in range(SIDE):
            for dy in range(SIDE):
                rank = ((self.x + dx) % SIDE) * SIDE + (self.y + dy) % SIDE
                self.ranks[dx, dy] = rank
                self.slots[dx, dy] = rank * 2 + self.z

    def spot(self, half, dp, dq):
        dx, dy = (dp, dq) if half == 0 else (dq, dp)
        return dx % SIDE, dy % SIDE

    def rank(self, half, dp, dq):
        return self.ranks[self.spot(half, dp, dq)]

    def device(self, half, dp, dq):
        return {"ctx": self.slots[self.spot(half, dp, dq)]}

    def barrier(self, others=()):
        gate = pltpu.get_barrier_semaphore()
        partners = [self.device(0, *step) for step in self.meets]
        partners += others
        for partner in partners:
            pl.semaphore_signal(gate, inc=1, device_id=partner, device_id_type=MESH)
        pl.semaphore_wait(gate, len(partners))


LARGE = 1 << 16


def size_of(array):
    return array.size * jnp.dtype(array.dtype).itemsize


PIECES = 4


class Waits:
    def __init__(self):
        self.loads, self.stores, self.started = {}, {}, []

    def __call__(self, *which):
        for i in which or sorted(self.loads):
            for copy in self.loads.pop(i, ()):
                if copy is not None:
                    copy.wait()

    def piece(self, k, *which):
        for i in which:
            if i in self.loads:
                copies = self.loads[i]
                if copies[k] is not None:
                    copies[k].wait()
                    copies[k] = None

    def flush(self, *which):
        for i in which or sorted(self.stores):
            if i in self.stores:
                copy = self.stores.pop(i)
                copy.start()
                self.started.append(copy)

    def finish(self):
        self()
        self.flush()
        for copy in self.started:
            copy.wait()


def staged_call(
    body, name, number, given, shapes, scratch, tables=(), direct=(), parted=(), raw=()
):
    loads = [i for i, array in enumerate(given) if size_of(array) > LARGE and i not in raw]
    stores = [i for i, shape in enumerate(shapes) if size_of(shape) > LARGE and i not in direct]
    counts = (len(tables), len(given), len(shapes), len(loads), len(stores))

    def kernel(*refs):
        refs, groups = list(refs), []
        for count in counts:
            groups.append(refs[:count])
            refs = refs[count:]
        table_refs, ins, outs, staged_in, staged_out = groups
        load_sem, store_sem, *refs = refs
        wait = Waits()
        for k, i in enumerate(loads):
            if i not in parted:
                copy = pltpu.make_async_copy(ins[i], staged_in[k], load_sem.at[k, 0])
                copy.start()
                wait.loads[i] = [copy]
        for piece in range(PIECES):
            for k, i in enumerate(loads):
                if i in parted:
                    count = given[i].shape[0] // PIECES
                    span = pl.ds(piece * count, count)
                    copy = pltpu.make_async_copy(
                        ins[i].at[span], staged_in[k].at[span], load_sem.at[k, piece]
                    )
                    copy.start()
                    wait.loads.setdefault(i, []).append(copy)
        for k, i in enumerate(loads):
            ins[i] = staged_in[k]
        for k, i in enumerate(stores):
            wait.stores[i] = pltpu.make_async_copy(staged_out[k], outs[i], store_sem.at[k])
            outs[i] = staged_out[k]
        body(wait, table_refs, ins, outs, refs)
        wait.finish()

    smem, vmem, hbm = (
        pl.BlockSpec(memory_space=space) for space in (pltpu.SMEM, pltpu.VMEM, pl.ANY)
    )
    far = set(stores) | set(direct)
    params = dict(vmem_limit_bytes=60 << 20)
    if number is not None:
        params.update(collective_id=number, has_side_effects=True)
    return pl.pallas_call(
        kernel,
        out_shape=list(shapes),
        in_specs=[smem] * len(tables)
        + [hbm if i in loads or i in raw else vmem for i in range(len(given))],
        out_specs=[hbm if i in far else vmem for i in range(len(shapes))],
        scratch_shapes=[pltpu.VMEM(given[i].shape, given[i].dtype) for i in loads]
        + [pltpu.VMEM(shapes[i].shape, shapes[i].dtype) for i in stores]
        + [
            pltpu.SemaphoreType.DMA((max(len(loads), 1), PIECES)),
            pltpu.SemaphoreType.DMA((max(len(stores), 1),)),
        ]
        + list(scratch),
        name=name,
        compiler_params=pltpu.CompilerParams(**params),
    )(*tables, *given)


RINGS = ((1, 0), (-1, 0), (2, 0), (0, 1), (0, -1), (0, 2))


def gather_half(grid, half, own_ref, all_ref, send_sem, recv_sem):
    rows = own_ref.shape[0]
    half_rows, quarter = rows // 2, rows // 4
    sends = []

    def view(dp, dq, low, count):
        return all_ref.at[grid.rank(half, dp, dq), pl.ds(half * half_rows + low, count)]

    def start(event, to, block, low, count, own=False):
        source = (
            own_ref.at[pl.ds(half * half_rows + low, count)]
            if own
            else view(*block, low, count)
        )
        copy = pltpu.make_async_remote_copy(
            src_ref=source,
            dst_ref=view(*block, low, count),
            send_sem=send_sem.at[half, event],
            recv_sem=recv_sem.at[half, event],
            device_id=grid.device(half, *to),
            device_id_type=MESH,
        )
        copy.start()
        sends.append(copy)

    def arrive(event, block, low, count):
        there = view(*block, low, count)
        pltpu.make_async_remote_copy(
            src_ref=there,
            dst_ref=there,
            send_sem=send_sem.at[half, event],
            recv_sem=recv_sem.at[half, event],
            device_id=grid.device(half, 1, 0),
            device_id_type=MESH,
        ).wait_recv()

    def spread(column, dp, own=False):
        start(4 + 4 * column, (0, 1), (dp, 0), 0, half_rows, own)
        start(5 + 4 * column, (0, -1), (dp, 0), 0, half_rows, own)

    start(0, (1, 0), (0, 0), 0, half_rows, True)
    start(1, (-1, 0), (0, 0), 0, half_rows, True)
    spread(0, 0, True)
    yield
    arrive(0, (-1, 0), 0, half_rows)
    start(2, (1, 0), (-1, 0), 0, quarter)
    spread(1, -1)
    arrive(1, (1, 0), 0, half_rows)
    start(3, (-1, 0), (1, 0), quarter, quarter)
    spread(2, 1)
    yield
    arrive(2, (2, 0), 0, quarter)
    arrive(3, (2, 0), quarter, quarter)
    spread(3, 2)
    yield
    steps = (0, -1, 1, 2)
    for column in range(4):
        arrive(4 + 4 * column, (steps[column], -1), 0, half_rows)
        start(6 + 4 * column, (0, 1), (steps[column], -1), 0, quarter)
        arrive(5 + 4 * column, (steps[column], 1), 0, half_rows)
        start(7 + 4 * column, (0, -1), (steps[column], 1), quarter, quarter)
        yield
    for column in range(4):
        arrive(6 + 4 * column, (steps[column], 2), 0, quarter)
        arrive(7 + 4 * column, (steps[column], 2), quarter, quarter)
        if column % 2 == 0:
            yield
    for copy in sends:
        copy.wait_send()


GATHER_STEPS = 20


def gather_steps(grid, own_ref, all_ref, send_sem, recv_sem):
    halves = [
        gather_half(grid, half, own_ref, all_ref, send_sem, recv_sem) for half in (0, 1)
    ]
    for step in range(GATHER_STEPS):
        next(halves[step % 2], None)
        if step < GATHER_STEPS - 1:
            yield


DIRECT_STEPS = 8


def direct_steps(grid, own_ref, all_ref, send_sem, recv_sem):
    half_rows = own_ref.shape[0] // 2
    sends = []

    def view(half, dp, dq):
        return all_ref.at[grid.rank(half, dp, dq), pl.ds(half * half_rows, half_rows)]

    def copy(half, event, to, block, own=False):
        source = own_ref.at[pl.ds(half * half_rows, half_rows)] if own else view(half, *block)
        return pltpu.make_async_remote_copy(
            src_ref=source,
            dst_ref=view(half, *block),
            send_sem=send_sem.at[half, event],
            recv_sem=recv_sem.at[half, event],
            device_id=grid.device(half, *to),
            device_id_type=MESH,
        )

    def start(*args):
        made = copy(*args)
        made.start()
        sends.append(made)

    steps = (1, -1, 2)
    for index, step in enumerate(steps):
        for half in (0, 1):
            start(half, index, (step, 0), (0, 0), True)
    for index, step in enumerate(steps):
        for half in (0, 1):
            start(half, 3 + index, (0, step), (0, 0), True)
    yield
    for index, step in enumerate(steps):
        for half in (0, 1):
            copy(half, index, (step, 0), (-step, 0)).wait_recv()
            for other, move in enumerate(steps):
                start(half, 6 + 3 * index + other, (0, move), (-step, 0))
            yield
    for column, place_p in enumerate((0, -1, 1, -2)):
        for other, move in enumerate(steps):
            for half in (0, 1):
                copy(half, 3 + 3 * column + other, (0, move), (place_p, -move)).wait_recv()
    for made in sends:
        made.wait_send()


def run(steps, count=None):
    while count is None or count > 0:
        if next(steps, StopIteration) is StopIteration:
            return
        count = None if count is None else count - 1


def scatter_steps(
    grid, make, part_ref, out_ref, land_half, land_full, stage, total, send_sem, recv_sem
):
    rows = part_ref.shape[1]
    half_rows, quarter = rows // 2, rows // 4
    sends = []
    steps = (2, -1, 1, 0)

    def start(half, event, source, target, to):
        copy = pltpu.make_async_remote_copy(
            src_ref=source,
            dst_ref=target,
            send_sem=send_sem.at[half, event],
            recv_sem=recv_sem.at[half, event],
            device_id=grid.device(half, *to),
            device_id_type=MESH,
        )
        copy.start()
        sends.append(copy)

    def arrive(half, event, target):
        pltpu.make_async_remote_copy(
            src_ref=target,
            dst_ref=target,
            send_sem=send_sem.at[half, event],
            recv_sem=recv_sem.at[half, event],
            device_id=grid.device(half, 1, 0),
            device_id_type=MESH,
        ).wait_recv()

    def first(half, column):
        def piece(dq, low, count):
            return part_ref.at[
                grid.rank(half, steps[column], dq), pl.ds(half * half_rows + low, count)
            ]

        return piece

    def second(half):
        return lambda dp, low, count: total.at[half, steps.index(dp), pl.ds(low, count)]

    def along(step):
        return (0, step)

    def across(step):
        return (step, 0)

    def opposite(half, column, piece, step):
        for side, low in ((0, 0), (1, quarter)):
            start(
                half,
                4 * column + side,
                piece(2, low, quarter),
                land_half.at[half, column, side],
                step(1 - 2 * side),
            )

    def neighbours(half, column, piece, step):
        for side in (0, 1):
            land = land_half.at[half, column, side]
            arrive(half, 4 * column + side, land)
            low, other = side * quarter, (1 - side) * quarter
            toward = 1 - 2 * side
            stage[half, column, side, low : low + quarter] = (
                piece(toward, low, quarter)[...].astype(F32) + land[...].astype(F32)
            ).astype(BF16)
            stage[half, column, side, other : other + quarter] = piece(toward, other, quarter)[...]
            start(
                half,
                4 * column + 2 + side,
                stage.at[half, column, side],
                land_full.at[half, column, side],
                step(toward),
            )

    def settle(half, column, own):
        for side in (0, 1):
            arrive(half, 4 * column + 2 + side, land_full.at[half, column, side])
        return (
            own[...].astype(F32)
            + land_full[half, column, 0].astype(F32)
            + land_full[half, column, 1].astype(F32)
        )

    def places(*spots):
        make([grid.rank(0, dx, dy) for dx, dy in spots])

    def on_both(step, column, direction):
        for half in (0, 1):
            step(half, column, first(half, column), direction)

    places((2, 2))
    on_both(opposite, 0, along)
    for column in (1, 2, 3):
        places((steps[column], 2), (2, steps[column]))
        on_both(opposite, column, along)
        yield
    on_both(neighbours, 0, along)
    yield
    places((-1, -1), (-1, 1))
    places((1, -1), (1, 1))
    on_both(neighbours, 1, along)
    yield
    places((0, 1), (0, -1))
    on_both(neighbours, 2, along)
    yield
    places((1, 0), (-1, 0))
    on_both(neighbours, 3, along)
    yield
    places((0, 0))
    for column in range(4):
        for half in (0, 1):
            total[half, column] = settle(
                half, column, first(half, column)(0, 0, half_rows)
            ).astype(BF16)
            if column == 0:
                opposite(half, 4, second(half), across)
            if column == 2:
                neighbours(half, 4, second(half), across)
        yield
    for half in (0, 1):
        out_ref[pl.ds(half * half_rows, half_rows)] = settle(half, 4, total.at[half, 3])
    for copy in sends:
        copy.wait_send()


SCATTER_STEPS = 12


def scatter_scratch(rows, width):
    half_rows, quarter = rows // 2, rows // 4
    return [
        pltpu.VMEM((2, 5, 2, quarter, width), BF16),
        pltpu.VMEM((2, 5, 2, half_rows, width), BF16),
        pltpu.VMEM((2, 5, 2, half_rows, width), BF16),
        pltpu.VMEM((2, 4, half_rows, width), BF16),
        pltpu.SemaphoreType.DMA((2, 20)),
        pltpu.SemaphoreType.DMA((2, 20)),
    ]


def follow(grid, gather, block, ready=None):
    def places(*spots):
        block([grid.rank(0, dx, dy) for dx, dy in spots])

    run(gather, 4)
    if ready is not None:
        ready()
    places((0, 0))
    run(gather, 2)
    places((0, 1), (0, -1))
    run(gather, 2)
    places((1, 0), (-1, 0))
    run(gather, 2)
    places((1, 1), (1, -1))
    run(gather, 2)
    places((-1, 1), (-1, -1))
    run(gather, 2)
    places((0, 2), (2, 0))
    run(gather, 2)
    places((1, 2), (-1, 2))
    places((2, 1), (2, -1))
    run(gather)
    places((2, 2))


def rows_of(ref, ranks, rows):
    return jnp.concatenate([ref[block_rows(rank, rows), :] for rank in ranks], 0)


def put_rows(ref, ranks, rows, values):
    for index, rank in enumerate(ranks):
        ref[block_rows(rank, rows), :] = values[index * rows : (index + 1) * rows]


def blocks_of(ref, ranks):
    return jnp.concatenate([ref[rank] for rank in ranks], 0)


SQRT_HALF = 0.7071067811865476
DENSITY = 0.3989422804014327


def standardize(stream):
    row_mean = jnp.mean(stream, -1, keepdims=True)
    centered = stream - row_mean
    spread = jnp.mean(centered * centered, -1, keepdims=True)
    inverse = lax.rsqrt(spread + EPS)
    return (centered * inverse, inverse)


def dots(a, b, da, db):
    return lax.dot_general(a, b, (((da,), (db,)), ((), ())), preferred_element_type=F32)


def rotate(values, cosines, sines):
    lane = lax.broadcasted_iota(jnp.int32, values.shape, 1)
    half_dims = ROT // 2
    up = pltpu.roll(values, 2 * HEAD - half_dims, 1)
    down = pltpu.roll(values, half_dims, 1)
    return values * cosines + jnp.where(lane < half_dims, -up, down) * sines


def block_rows(rank, rows):
    return pl.ds(pl.multiple_of(rank * rows, rows), rows)


def share_partners():
    shard = lax.axis_index("fsdp")
    return [{"fsdp": shard + 1 - 2 * (shard % 2)}, {"fsdp": (shard + 2) % 4}]


def share_steps(items, send_sem, recv_sem):
    shard = lax.axis_index("fsdp")
    sibling = shard + 1 - 2 * (shard % 2)
    mate = (shard + 2) % 4
    third = (sibling + 2) % 4
    sends = []

    def copy(item, source, target, event, to):
        return pltpu.make_async_remote_copy(
            src_ref=source,
            dst_ref=target,
            send_sem=send_sem.at[item, event],
            recv_sem=recv_sem.at[item, event],
            device_id={"fsdp": to},
            device_id_type=MESH,
        )

    def start(*args):
        made = copy(*args)
        made.start()
        sends.append(made)

    for item, (own, every) in enumerate(items):
        start(item, own, every.at[shard], 0, mate)
        start(item, own, every.at[shard], 1, sibling)
        every[shard] = own[...]
    yield
    for item, (own, every) in enumerate(items):
        copy(item, own, every.at[mate], 0, mate).wait_recv()
        start(item, every.at[mate], every.at[mate], 2, sibling)
        yield
        copy(item, own, every.at[sibling], 1, sibling).wait_recv()
        copy(item, own, every.at[third], 2, sibling).wait_recv()
        yield
    for made in sends:
        made.wait_send()


def share_sems(items):
    return [pltpu.SemaphoreType.DMA((items, 3)), pltpu.SemaphoreType.DMA((items, 3))]


def stack_tall(tall_all, tall_ref):
    for part in range(4):
        tall_ref[part * HEAD : (part + 1) * HEAD] = tall_all[part, :HEAD]
    tall_ref[4 * HEAD : 5 * HEAD] = jnp.zeros((HEAD, tall_ref.shape[1]), BF16)
    tall_ref[5 * HEAD :] = tall_all[place()[0], HEAD:]


def enter_phase(grid, stream_ref, given, wide_ref, made, own, sems, ready):
    scale_ref, bias_ref, cos_ref, sin_ref = given
    normed_ref, active_ref, slope_ref, q_ref, kv_ref = made
    rows, width = stream_ref.shape
    own[...] = standardize(stream_ref[...].astype(F32))[0].astype(BF16)
    normed_ref[grid.rank(0, 0, 0)] = own[...]
    yield
    gather = gather_steps(grid, own, normed_ref, *sems)
    run(gather, 2)

    def block(ranks):
        plain = blocks_of(normed_ref, ranks).astype(F32)
        first = (plain * scale_ref[0:1] + scale_ref[2:3]).astype(BF16)
        second = (plain * scale_ref[1:2] + scale_ref[3:4]).astype(BF16)
        weight = wide_ref[...].reshape(width, 8 * HEAD)
        mixed = dots(first, weight[:, : 4 * HEAD], 1, 0) + bias_ref[:, : 4 * HEAD]
        hidden = dots(second, weight[:, 4 * HEAD :], 1, 0) + bias_ref[:, 4 * HEAD :]
        cosines, sines = rows_of(cos_ref, ranks, rows), rows_of(sin_ref, ranks, rows)
        pairs = rotate(mixed[:, : 2 * HEAD], cosines, sines)
        queries = rotate(mixed[:, 2 * HEAD :], cosines, sines) * 0.125
        put_rows(kv_ref, ranks, rows, pairs.astype(BF16))
        put_rows(q_ref, ranks, rows, queries.astype(BF16))
        share = 0.5 * (1.0 + lax.erf(hidden * SQRT_HALF))
        put_rows(active_ref, ranks, rows, (hidden * share).astype(BF16))
        slope = share + hidden * (DENSITY * jnp.exp(-0.5 * hidden * hidden))
        put_rows(slope_ref, ranks, rows, slope)

    follow(grid, gather, block, ready)


def leave_steps(
    grid, active_ref, context_ref, tall_ref, stream_ref, bias_ref, out_ref, parts, total_rows, scratch
):
    rows = stream_ref.shape[0]

    def make(ranks):
        context = rows_of(context_ref, ranks, rows).astype(BF16)
        both = jnp.concatenate([rows_of(active_ref, ranks, rows), context], 1)
        made = dots(both, tall_ref[...], 1, 0).astype(BF16)
        for index, rank in enumerate(ranks):
            parts[rank] = made[index * rows : (index + 1) * rows]

    yield from scatter_steps(grid, make, parts, total_rows, *scratch)
    stream = stream_ref[...].astype(F32)
    out_ref[...] = (stream + total_rows[...] + bias_ref[...]).astype(out_ref.dtype)


VECTOR_ROWS = 16


def unpack(grid, vectors, scale_ref, bias_ref, last_ref):
    lane = lax.broadcasted_iota(jnp.int32, (8, 2 * HEAD), 1)

    def of_rank(rows):
        row = rows[0]
        for index in range(1, 4):
            row = jnp.where(grid.x == index, rows[index], row)
        row = jnp.broadcast_to(row, (8, LANES))
        half = jnp.where(grid.y < 2, row[:, : 2 * HEAD], row[:, 2 * HEAD :])
        rolled = pltpu.roll(half, HEAD, 1)
        odd = grid.y % 2 == 1
        return jnp.where(odd, rolled, half), jnp.where(odd, half, rolled)

    def beside(low, high):
        return jnp.where(lane < HEAD, low[0], high[1])

    def shard_rows(first, count):
        return [vector[first + i : first + i + 1] for vector in vectors for i in range(count)]

    scale_ref[...] = jnp.concatenate([vector[:4] for vector in vectors], 1)
    last_ref[...] = jnp.concatenate([vector[7:8] + vector[12:13] for vector in vectors], 1)
    mixed = shard_rows(4, 3)
    q, k, v = (of_rank(mixed[4 * part : 4 * part + 4]) for part in range(3))
    up = [of_rank([vector[8 + i : 9 + i] for i in range(4)]) for vector in vectors]
    tiles = [
        beside(k, v),
        jnp.where(lane < HEAD, q[0], 0.0),
        beside(up[0], up[1]),
        beside(up[2], up[3]),
    ]
    bias_ref[...] = jnp.concatenate(tiles, 1)[0:1]


def forward_body(wait, tables, ins, outs, refs):
    stream_ref, cos_ref, sin_ref, wide_one, wide_two, branch_ref, down_ref, out_ref = ins[:8]
    vector_refs = ins[8:]
    scales, lasts = outs[21:23], outs[23:25]
    layer_outs, branches = (outs[:7], outs[7:14]), outs[14:16]
    wide_refs, tall_refs, second_ref = (outs[16], outs[18]), (outs[17], outs[19]), outs[20]
    (own_one, own_two), refs = refs[:2], refs[2:]
    queries, refs = (refs[:2], refs[2:4]), refs[4:]
    enter_sems, refs = (refs[:2], refs[2:4]), refs[4:]
    branch_sems, refs = (refs[:3], refs[3:6]), refs[6:]
    share_refs, refs = (refs[:3], refs[3:6]), refs[6:]
    (parts, total_rows), scatter_refs, refs = refs[:2], refs[2:8], refs[8:]
    attend_refs, refs = (refs[:5], refs[:3] + refs[5:7]), refs[7:]
    vector_ref, vector_all, biases, refs = refs[0], refs[1], refs[2:4], refs[4:]
    talls, tall_sem = refs[:2], refs[2]
    grid = Grid()
    tall_copies = []
    for layer in range(2):
        for index, (source, first) in enumerate(
            ((down_ref, grid.rank(0, 0, 0)), (out_ref, grid.y))
        ):
            copy = pltpu.make_async_copy(
                source.at[layer, block_rows(first, HEAD)],
                talls[layer].at[pl.ds(index * HEAD, HEAD)],
                tall_sem.at[layer, index],
            )
            copy.start()
            tall_copies.append(copy)
    for layer in range(2):
        gain, shift, qkv, out, up, down = (
            ref[layer].astype(F32) if len(ref.shape) == 3 else ref[layer : layer + 1].astype(F32)
            for ref in vector_refs
        )
        rows = [gain, shift]
        rows += [qkv[:, i * LANES : (i + 1) * LANES] for i in range(3)] + [out]
        rows += [up[:, i * LANES : (i + 1) * LANES] for i in range(4)] + [down]
        rows.append(jnp.zeros((VECTOR_ROWS - 13, LANES), F32))
        vector_ref[layer] = jnp.concatenate(rows, 0).astype(BF16)

    def attend_phase(layer):
        normed, active, slope, context, qs, kvs, logs = layer_outs[layer]
        all_ref, sems = branches[layer], branch_sems[layer]
        count = branch_ref.shape[0] // 2
        half = branch_ref.at[pl.ds(layer * count, count)]
        keep = keep_own(grid, half, all_ref, sems[0])
        gather = gather_steps(grid, half, all_ref, *sems[1:])
        work = attend_steps(
            tables, *queries[layer], context, qs, kvs, logs, attend_refs[layer]
        )
        take_turns(work, ATTEND_WORK + SWAP_WORK, [(gather, GATHER_STEPS, 2, 6, 0.9)])
        return keep

    def sharing(layer, *items):
        tall_all, *sems = share_refs[layer]
        wide_own, tall_own = items[-2:]
        items = items[:-2] + ((wide_own, wide_refs[layer]), (tall_own, tall_all))
        return share_steps(items, *sems)

    def ready():
        run(shared, 4)
        for layer in range(2):
            vectors = [vector_all[shard, layer].astype(F32) for shard in range(4)]
            unpack(grid, vectors, scales[layer], biases[layer], lasts[layer])
        wait()

    wait(0)
    enter = enter_phase(
        grid, stream_ref, (scales[0], biases[0], cos_ref, sin_ref), wide_refs[0],
        (*layer_outs[0][:3], *queries[0]), own_one, enter_sems[0], ready,
    )
    run(enter, 1)
    grid.barrier([far_partner()] + share_partners())
    wait(3)
    for copy in tall_copies:
        copy.wait()
    shared = sharing(0, (vector_ref, vector_all), wide_one, talls[0])
    run(shared, 1)
    run(enter)
    run(shared)
    stack_tall(share_refs[0][0], tall_refs[0])
    wait.flush(0, 1, 2, 16, 17)
    keeps = [attend_phase(0)]
    wait.flush(3, 4, 5, 6)
    shared = sharing(1, wide_two, talls[1])
    run(shared, 1)
    leave = leave_steps(
        grid, layer_outs[0][1], layer_outs[0][3], tall_refs[0], stream_ref, lasts[0], second_ref,
        parts, total_rows, scatter_refs,
    )
    run(leave, 5)
    run(shared, 1)
    run(leave, 3)
    run(shared, 2)
    run(leave)

    enter = enter_phase(
        grid, second_ref, (scales[1], biases[1], cos_ref, sin_ref), wide_refs[1],
        (*layer_outs[1][:3], *queries[1]), own_two, enter_sems[1], lambda: run(shared),
    )
    run(enter, 1)
    wait.flush(20)
    run(enter)
    stack_tall(share_refs[1][0], tall_refs[1])
    wait.flush(7, 8, 9, 18, 19)
    keeps.append(attend_phase(1))
    for keep in keeps:
        keep.wait()


def forward(tables, stream, vectors, cosines, sines, wide, down, out, cotangent, number):
    rows, width = stream.shape
    total = 16 * rows
    layers = wide.shape[0]
    half = rows // layers
    shapes = [
        jax.ShapeDtypeStruct((16, rows, width), BF16),
        jax.ShapeDtypeStruct((total, 4 * HEAD), BF16),
        jax.ShapeDtypeStruct((total, 4 * HEAD), F32),
        jax.ShapeDtypeStruct((total, 2 * HEAD), F32),
        jax.ShapeDtypeStruct((total, 2 * HEAD), BF16),
        jax.ShapeDtypeStruct((2, total, 2 * HEAD), BF16),
        jax.ShapeDtypeStruct((total, 2 * HEAD), F32),
    ] * layers
    shapes += [jax.ShapeDtypeStruct((16, half, width), BF16)] * layers
    shapes += [
        jax.ShapeDtypeStruct((4,) + wide.shape[1:], BF16),
        jax.ShapeDtypeStruct((6 * HEAD, width), BF16),
    ] * layers
    shapes.append(jax.ShapeDtypeStruct((rows, width), F32))
    shapes += [jax.ShapeDtypeStruct((4, width), F32)] * layers
    shapes += [jax.ShapeDtypeStruct((1, width), F32)] * layers
    swap = [pltpu.VMEM((total, 2 * HEAD), BF16), pltpu.SemaphoreType.DMA((2,))]
    scratch = [pltpu.VMEM((rows, width), BF16)] * 2
    scratch += [pltpu.VMEM((total, 2 * HEAD), BF16)] * 4
    scratch += [pltpu.SemaphoreType.DMA((2, 20))] * 4
    scratch += gather_sems() + gather_sems()
    tall = pltpu.VMEM((2 * HEAD, width), BF16)
    scratch += ([pltpu.VMEM((4, 2 * HEAD, width), BF16)] + share_sems(3)) * 2
    scratch += [pltpu.VMEM((16, rows, width), BF16), pltpu.VMEM((rows, width), F32)]
    scratch += scatter_scratch(rows, width)
    scratch += [pltpu.VMEM((total, 2 * HEAD), F32)] * 3 + swap + swap
    packed = (layers, VECTOR_ROWS, LANES)
    scratch += [pltpu.VMEM(packed, BF16), pltpu.VMEM((4,) + packed, BF16)]
    scratch += [pltpu.VMEM((1, 8 * HEAD), F32)] * layers
    scratch += [tall] * layers + [pltpu.SemaphoreType.DMA((layers, 2))]
    given = [stream, cosines, sines, wide[0], wide[1], cotangent, down, out, *vectors]
    made = staged_call(
        forward_body, "forward", number, given, shapes, scratch, tables, direct=(14, 15), raw=(6, 7)
    )
    saved, weights = (made[:7], made[7:14]), ((made[16], made[18]), (made[17], made[19]))
    return saved, made[14:16], *weights, made[20], made[21:23], made[23:25]


def back_enter_phase(
    grid, wait, ins, outs, tall_sum, gather_refs=None, beside=(), between=None
):
    grad_ref, active_ref, context_ref, slope_ref, normed_ref, tall_ref, scale_ref = ins[:7]
    pull_ref, offset_ref, hidden_ref, early_ref, out_ref, up_ref, up_bias_ref = outs
    gathers = gather_refs is not None
    rows = normed_ref.shape[-2]
    if gathers:
        own, all_rows, send_sem, recv_sem = gather_refs
        gather = gather_steps(grid, own, all_rows, send_sem, recv_sem)
        run(gather, 2)
        for steps in beside:
            run(steps, 1)
    tall_sum[...] = jnp.zeros_like(tall_sum)
    up_ref[...] = jnp.zeros_like(up_ref)
    up_bias_ref[...] = jnp.zeros_like(up_bias_ref)

    def block(ranks):
        if gathers:
            branch = blocks_of(all_rows, ranks)
        else:
            branch = jnp.concatenate([half[rank] for rank in ranks for half in (grad_ref, ins[7])], 0)
        back = dots(branch, tall_ref[...], 1, 1)
        hidden_grad = (back[:, : 4 * HEAD] * rows_of(slope_ref, ranks, rows)).astype(BF16)
        pull = back[:, 4 * HEAD :].astype(BF16)
        put_rows(hidden_ref, ranks, rows, hidden_grad)
        put_rows(pull_ref, ranks, rows, pull)
        context = rows_of(context_ref, ranks, rows)
        offset = jnp.sum(pull.astype(F32) * context, 1, keepdims=True)
        put_rows(offset_ref, ranks, rows, jnp.broadcast_to(offset, context.shape))
        both = jnp.concatenate([rows_of(active_ref, ranks, rows), context.astype(BF16)], 1)
        ones = jnp.ones(context.shape, BF16)
        tall_sum[...] += dots(both, branch, 0, 0)
        up_ref[...] += dots(hidden_grad, blocks_of(normed_ref, ranks), 0, 0)
        up_bias_ref[...] += dots(hidden_grad, ones, 0, 0)

    if gathers:
        follow(grid, gather, block, lambda: wait(*range(1, 7)))
    else:
        wait(5)
        for piece in range(PIECES):
            wait.piece(piece, 0, 1, 2, 3, 4, 7)
            block([piece * 4 + i for i in range(4)])
            between()
    up_grad = (up_ref[...] * scale_ref[1:2] + up_bias_ref[:, 0:1] * scale_ref[3:4]).astype(BF16)
    for shard in range(4):
        early_ref[shard, : 4 * PART] = up_grad[:, shard * LANES : (shard + 1) * LANES]
        early_ref[shard, 8 * PART :] = jnp.zeros((PART, LANES), BF16)
        for lanes in range(4):
            early_ref[shard, (4 + lanes) * PART : (5 + lanes) * PART] = tall_sum[
                shard * HEAD : (shard + 1) * HEAD, lanes * LANES : (lanes + 1) * LANES
            ].astype(BF16)
            low = 5 * HEAD + shard * 16
            out_ref[shard, lanes * 16 : (lanes + 1) * 16] = tall_sum[
                low : low + 16, lanes * LANES : (lanes + 1) * LANES
            ].astype(BF16)


def back_enter_shapes(rows, width):
    total = 16 * rows
    return [
        jax.ShapeDtypeStruct((total, 4 * HEAD), BF16),
        jax.ShapeDtypeStruct((4 * HEAD, width), F32),
        jax.ShapeDtypeStruct((4 * HEAD, 2 * HEAD), F32),
    ], [
        pltpu.VMEM((total, 2 * HEAD), BF16),
        pltpu.VMEM((total, 2 * HEAD), F32),
        pltpu.VMEM((4, EARLY, LANES), BF16),
        pltpu.VMEM((4, PART, LANES), BF16),
        pltpu.VMEM((6 * HEAD, width), F32),
    ]


def back_leave_phase(grid, wait, ins, outs, refs, exchanges, other_vectors=None, after=None):
    query_grad_ref, pair_grad_ref, hidden_ref, normed_ref, wide_ref, scale_ref = ins[:6]
    cos_ref, sin_ref, stream_ref, grad_ref, up_ref, up_bias_ref = ins[6:]
    new_ref, addend_ref, *vector_ref = outs
    vector_ref = vector_ref[0] if vector_ref else None
    (mixed, raw, raw_bias, parts, total_rows), scratch = refs[:5], refs[5:]
    rows, width = stream_ref.shape
    wait(0, 1, 2, 4, 6, 7)

    def make(ranks):
        cosines, sines = rows_of(cos_ref, ranks, rows), -rows_of(sin_ref, ranks, rows)
        query = rows_of(query_grad_ref, ranks, rows) * 0.125
        lane = lax.broadcasted_iota(jnp.int32, query.shape, 1)
        query = jnp.where(lane < HEAD, query, 0.0)
        pair = rows_of(pair_grad_ref, ranks, rows)
        both = jnp.concatenate(
            [rotate(pair, cosines, sines), rotate(query, cosines, sines)], 1
        ).astype(BF16)
        put_rows(mixed, ranks, rows, both)
        first = dots(both, wide_ref[:, : 4 * HEAD], 1, 1)
        second = dots(rows_of(hidden_ref, ranks, rows), wide_ref[:, 4 * HEAD :], 1, 1)
        made = (first * scale_ref[0:1] + second * scale_ref[1:2]).astype(BF16)
        for index, rank in enumerate(ranks):
            parts[rank] = made[index * rows : (index + 1) * rows]

    scatter = scatter_steps(grid, make, parts, total_rows, *scratch)
    run(scatter, 3)
    wait()
    for steps in exchanges:
        run(steps, 1)
    run(scatter, 5)
    raw[...] = jnp.zeros_like(raw)
    raw_bias[...] = jnp.zeros_like(raw_bias)
    ones = jnp.ones((4 * rows, 2 * HEAD), BF16)

    def sums(index):
        span = pl.ds(index * 4 * rows, 4 * rows)
        both = mixed[span, :]
        normed_rows = normed_ref[pl.ds(index * 4, 4)].reshape(4 * rows, width)
        raw[...] += dots(both, normed_rows, 0, 0)
        raw_bias[...] += dots(both, ones, 0, 0)

    sums(0)
    run(scatter, 1)
    sums(1)
    run(scatter, 1)
    sums(2)
    run(scatter, 1)
    sums(3)

    wide_t = jnp.transpose(wide_ref[:, : 4 * HEAD].astype(F32))
    up_t = jnp.transpose(wide_ref[:, 4 * HEAD :].astype(F32))
    mixed_bias, up_bias = raw_bias[:, 0:1], up_bias_ref[:, 0:1]
    first_raw, second_raw = raw[...], up_ref[...]
    vectors = [
        jnp.sum(wide_t * first_raw, 0, keepdims=True),
        jnp.sum(up_t * second_raw, 0, keepdims=True),
        jnp.sum(wide_t * mixed_bias, 0, keepdims=True),
        jnp.sum(up_t * up_bias, 0, keepdims=True),
        jnp.sum(grad_ref[...].astype(BF16).astype(F32), 0, keepdims=True),
    ]
    first_grad = (first_raw * scale_ref[0:1] + mixed_bias * scale_ref[2:3]).astype(BF16)
    biases = [
        jnp.transpose(raw_bias[...])[0:1],
        jnp.transpose(up_bias_ref[...])[0:1],
    ]
    for shard in range(4):
        lanes = slice(shard * LANES, (shard + 1) * LANES)
        addend_ref[shard, : 3 * PART] = first_grad[: 3 * PART, lanes]
        tail = [vector[:, lanes] for vector in vectors] + biases
        tail.append(jnp.zeros((VECTOR_ROWS - len(tail), LANES), F32))
        tail = jnp.concatenate(tail, 0).astype(BF16)
        if other_vectors is None:
            vector_ref[shard] = tail
        else:
            addend_ref[shard, LATE : LATE + 16] = tail
            addend_ref[shard, LATE + 16 : LATE + 32] = other_vectors[shard]
            addend_ref[shard, LATE + 32 :] = jnp.zeros((PART - 32, LANES), BF16)
    run(scatter)
    for steps in exchanges:
        run(steps)
    if after is not None:
        after()
    normed, inverse = standardize(stream_ref[...].astype(F32))
    normed_grad = total_rows[...]
    new_ref[...] = grad_ref[...].astype(F32) + inverse * (
        normed_grad
        - jnp.mean(normed_grad, -1, keepdims=True)
        - normed * jnp.mean(normed_grad * normed, -1, keepdims=True)
    )


def back_leave_scratch(rows, width):
    total = 16 * rows
    return [
        pltpu.VMEM((total, 4 * HEAD), BF16),
        pltpu.VMEM((4 * HEAD, width), F32),
        pltpu.VMEM((4 * HEAD, 2 * HEAD), F32),
        pltpu.VMEM((16, rows, width), BF16),
        pltpu.VMEM((rows, width), F32),
    ] + scatter_scratch(rows, width)


def back_leave_body(wait, tables, ins, outs, refs):
    grid = Grid()
    grid.barrier([mate()])
    exchanges = [low_steps(ins[12], outs[3], *refs[11:], ins[13])]
    back_leave_phase(grid, wait, ins[:12], outs[:3], refs[:11], exchanges)


def back_leave(given, rows, width, number, sums, total):
    shapes = [
        jax.ShapeDtypeStruct((rows, width), F32),
        jax.ShapeDtypeStruct((4, LATE, LANES), BF16),
        jax.ShapeDtypeStruct((4, VECTOR_ROWS, LANES), BF16),
        jax.ShapeDtypeStruct((EARLY, LANES), BF16),
    ]
    scratch = back_leave_scratch(rows, width) + swap_scratch(EARLY)
    given = tuple(given) + (sums, total)
    return staged_call(back_leave_body, "back_leave", number, given, shapes, scratch)


def sibling():
    shard = lax.axis_index("fsdp")
    return {"fsdp": shard + 1 - 2 * (shard % 2)}


def mate():
    return {"fsdp": (lax.axis_index("fsdp") + 2) % 4}


def far_partner():
    slot = lax.axis_index("ctx")
    return {"ctx": slot + 1 - 2 * (slot % 2)}


def wide_barrier(grid):
    shard = lax.axis_index("fsdp")
    at_home = grid.x == shard
    gate = pltpu.get_barrier_semaphore()
    partners = [grid.device(0, *step) for step in grid.meets]
    partners += [sibling(), mate(), far_partner()]
    for partner in partners:
        pl.semaphore_signal(gate, inc=1, device_id=partner, device_id_type=MESH)
    for other in range(4):

        @pl.when(jnp.logical_not(at_home & (shard == other)))
        def greet():
            pl.semaphore_signal(
                gate,
                inc=1,
                device_id={"ctx": (shard * SIDE + grid.y) * 2 + grid.z, "fsdp": other},
                device_id_type=MESH,
            )

    pl.semaphore_wait(gate, len(partners) + 4 - at_home.astype(jnp.int32))


def remote(source, target, send, recv, to):
    return pltpu.make_async_remote_copy(
        src_ref=source,
        dst_ref=target,
        send_sem=send,
        recv_sem=recv,
        device_id=to,
        device_id_type=MESH,
    )


def added(a, b):
    return (a.astype(F32) + b.astype(F32)).astype(BF16)


def core_steps(in_ref, sums_ref, land, sems):
    shard = lax.axis_index("fsdp")
    low, core = shard // 2, shard % 2
    copies = [
        remote(
            in_ref.at[part * 2 + 1 - core],
            land.at[part],
            sems.at[0, part],
            sems.at[1, part],
            sibling(),
        )
        for part in (0, 1)
    ]
    for copy in copies:
        copy.start()
    yield
    for copy in copies:
        copy.wait_recv()
    sums_ref[0] = added(in_ref[low * 2 + core], land[low])
    sums_ref[1] = added(in_ref[(1 - low) * 2 + core], land[1 - low])
    for copy in copies:
        copy.wait_send()


def core_scratch(rows):
    return [pltpu.VMEM((2, rows, LANES), BF16), pltpu.SemaphoreType.DMA((2, 2))]


def low_steps(sums_ref, pair_ref, land, sems, total_ref=None):
    copy = remote(sums_ref.at[1], land, sems.at[0], sems.at[1], mate())
    copy.start()
    yield
    copy.wait_recv()
    pair_ref[...] = added(sums_ref[0], land[...])
    if total_ref is not None:
        pair_ref[pair_ref.shape[0] - PART :] = total_ref[...]
    copy.wait_send()


def high_steps(pair_ref, own_ref, land, sems):
    copy = remote(pair_ref, land, sems.at[0], sems.at[1], far_partner())
    copy.start()
    yield
    copy.wait_recv()
    own_ref[...] = added(pair_ref[...], land[...])
    copy.wait_send()


def swap_scratch(rows):
    return [pltpu.VMEM((rows, LANES), BF16), pltpu.SemaphoreType.DMA((2,))]


def quarter_steps(grid, quarter_ref, total_ref, land, send_sem, recv_sem):
    x, y, z = grid.x, grid.y, grid.z
    shard = lax.axis_index("fsdp")
    at_home = x == shard

    def copy(column):
        return remote(
            quarter_ref.at[column],
            land.at[shard],
            send_sem.at[column],
            recv_sem.at[shard],
            {"ctx": (column * SIDE + y) * 2 + z, "fsdp": x},
        )

    for column in range(4):

        @pl.when(jnp.logical_not(at_home & (x == column)))
        def give():
            copy(column).start()

        @pl.when(at_home & (x == column))
        def keep():
            land[shard] = quarter_ref[column]

    yield
    for other in range(4):

        @pl.when(jnp.logical_not(at_home & (shard == other)))
        def take():
            remote(
                land.at[other], land.at[other], send_sem.at[other], recv_sem.at[other], mate()
            ).wait_recv()

    total = land[0].astype(F32)
    for other in range(1, 4):
        total = total + land[other].astype(F32)
    total_ref[...] = total.astype(BF16)
    for column in range(4):

        @pl.when(jnp.logical_not(at_home & (x == column)))
        def gone():
            copy(column).wait_send()


def quarter_scratch():
    return [
        pltpu.VMEM((4, PART, LANES), BF16),
        pltpu.SemaphoreType.DMA((4,)),
        pltpu.SemaphoreType.DMA((4,)),
    ]


def gather_sems():
    return [
        pltpu.SemaphoreType.DMA,
        pltpu.SemaphoreType.DMA((2, 20)),
        pltpu.SemaphoreType.DMA((2, 20)),
    ]


def keep_own(grid, own, every, sem):
    copy = pltpu.make_async_copy(own, every.at[grid.rank(0, 0, 0)], sem)
    copy.start()
    return copy


def last_body(wait, tables, ins, outs, refs):
    new_ref, all_early, all_other, all_late = outs
    leave_refs, refs = refs[:11], refs[11:]
    (late_addends, early, other, sums, pair, late), refs = refs[:6], refs[6:]
    early_swap, other_swap, refs = refs[:2], refs[2:4], refs[4:]
    core_refs, low_refs, high_refs, refs = refs[:2], refs[2:4], refs[4:6], refs[6:]
    early_sems, other_sems, late_sems = refs[:3], refs[3:6], refs[6:9]
    grid = Grid()
    grid.barrier([sibling(), mate(), far_partner()])
    exchanges = [high_steps(ins[12], early, *early_swap), high_steps(ins[13], other, *other_swap)]
    first = gather_steps(grid, early, all_early, *early_sems[1:])
    second = gather_steps(grid, other, all_other, *other_sems[1:])
    keeps = []

    def start():
        for steps in exchanges:
            run(steps)
        run(first, 2)
        keeps.append(keep_own(grid, early, all_early, early_sems[0]))
        keeps.append(keep_own(grid, other, all_other, other_sems[0]))

    back_leave_phase(
        grid, wait, ins[:12], (new_ref, late_addends), leave_refs, exchanges, ins[14], start
    )
    wait.flush()
    core = core_steps(late_addends, sums, *core_refs)
    run(core, 1)
    run(first, 2)
    run(core)
    low = low_steps(sums, pair, *low_refs)
    run(low, 1)
    run(first, 4)
    run(low)
    high = high_steps(pair, late, *high_refs)
    run(high, 1)
    run(second, 2)
    run(first, 4)
    run(second, 2)
    run(high)
    keeps.append(keep_own(grid, late, all_late, late_sems[0]))
    third = gather_steps(grid, late, all_late, *late_sems[1:])
    run(third, 2)
    for unused in range(GATHER_STEPS):
        run(first, 1)
        run(second, 1)
        run(third, 1)
    run(third)
    for keep in keeps:
        keep.wait()


def back_leave_last(given, rows, width, number, early, other, vectors):
    count = LATE + PART
    shapes = [
        jax.ShapeDtypeStruct((rows, width), F32),
        jax.ShapeDtypeStruct((16,) + early.shape, BF16),
        jax.ShapeDtypeStruct((16,) + other.shape, BF16),
        jax.ShapeDtypeStruct((16, count, LANES), BF16),
    ]
    scratch = back_leave_scratch(rows, width)
    scratch += [
        pltpu.VMEM((4, count, LANES), BF16),
        pltpu.VMEM(early.shape, BF16),
        pltpu.VMEM(other.shape, BF16),
        pltpu.VMEM((2, count, LANES), BF16),
        pltpu.VMEM((count, LANES), BF16),
        pltpu.VMEM((count, LANES), BF16),
    ]
    scratch += swap_scratch(early.shape[0]) + swap_scratch(other.shape[0])
    scratch += core_scratch(count) + swap_scratch(count) + swap_scratch(count)
    scratch += gather_sems() + gather_sems() + gather_sems()
    given = tuple(given) + (early, other, vectors)
    return staged_call(
        last_body, "back_leave_last", number, given, shapes, scratch, direct=(1, 2, 3)
    )


def format_kernel(layers, *refs):
    early, late, passing = refs[:layers], refs[layers : 2 * layers], refs[2 * layers : 2 * layers + 2]
    refs = refs[2 * layers + 2 :]
    (qkv_out, out_out, up_out, down_out), passed, refs = refs[:4], refs[4:6], refs[6:]
    early_in, late_in, qkv, out, up, down, *held, load_sem, store_sem, pass_sem = refs
    loads, stores = {}, []

    def store(source, target, layer, event):
        copy = pltpu.make_async_copy(source, target, store_sem.at[layer, event])
        copy.start()
        stores.append(copy)

    passes = []
    for index in range(2):
        copy = pltpu.make_async_copy(passing[index], held[index], pass_sem.at[0, index])
        copy.start()
        passes.append(copy)
    for layer in range(layers):
        for part in range(9 + 3):
            source, target, first = (
                (early[layer], early_in, part) if part < 9 else (late[layer], late_in, part - 9)
            )
            span = pl.ds(first * PART, PART)
            loads[layer, part] = pltpu.make_async_copy(
                source.at[:, span], target.at[layer, :, span], load_sem.at[layer, part]
            )
            loads[layer, part].start()
    row = lax.broadcasted_iota(jnp.int32, (LANES, LANES), 0)
    column = lax.broadcasted_iota(jnp.int32, (LANES, LANES), 1)
    unit = (row == column).astype(BF16)
    wide = 16 * PART

    def rows(ref, layer, part):
        return ref[layer, :, part * PART : (part + 1) * PART].reshape(wide, LANES)

    for index in range(2):
        passes[index].wait()
        copy = pltpu.make_async_copy(held[index], passed[index], pass_sem.at[1, index])
        copy.start()
        stores.append(copy)
    for layer in range(layers):
        for part in range(4):
            loads[layer, part].wait()
            up[layer, part] = dots(unit, rows(early_in, layer, part), 1, 1)
            target = up_out.at[layer, :, pl.ds(part * wide, wide)]
            store(up.at[layer, part], target, layer, part)
        for part in range(4):
            loads[layer, 4 + part].wait()
            lanes = slice(part * LANES, (part + 1) * LANES)
            down[layer, :, lanes] = rows(early_in, layer, 4 + part).astype(F32)
        store(down.at[layer], down_out.at[layer], layer, 4)
        loads[layer, 8].wait()
        for part in range(4):
            lanes = slice(part * LANES, (part + 1) * LANES)
            low = 8 * PART + part * 16
            for x in range(4):
                for y in range(4):
                    first = y * HEAD + x * 16
                    out[layer, first : first + 16, lanes] = early_in[
                        layer, x * 4 + y, low : low + 16
                    ].astype(F32)
        store(out.at[layer], out_out.at[layer], layer, 5)
        for part, place_of in enumerate((1, 2, 0)):
            loads[layer, 9 + part].wait()
            qkv[layer, part] = dots(unit, rows(late_in, layer, part), 1, 1)
            target = qkv_out.at[layer, :, pl.ds(place_of * wide, wide)]
            store(qkv.at[layer, part], target, layer, 6 + part)
    for copy in stores:
        copy.wait()


def format_grads(early, late, passing):
    layers = len(early)
    width = 4 * LANES
    hbm = pl.BlockSpec(memory_space=pl.ANY)
    shapes = [
        jax.ShapeDtypeStruct((layers, LANES, 3 * width), F32),
        jax.ShapeDtypeStruct((layers, LANES, width), F32),
        jax.ShapeDtypeStruct((layers, LANES, 4 * width), F32),
        jax.ShapeDtypeStruct((layers, width, width), F32),
    ]
    shapes += [jax.ShapeDtypeStruct(array.shape, array.dtype) for array in passing]
    return pl.pallas_call(
        functools.partial(format_kernel, layers),
        out_shape=shapes,
        in_specs=[hbm] * (2 * layers + 2),
        out_specs=[hbm] * 6,
        scratch_shapes=[
            pltpu.VMEM((layers, 16, EARLY, LANES), BF16),
            pltpu.VMEM((layers, 16, LATE, LANES), BF16),
            pltpu.VMEM((layers, 3, LANES, width), F32),
            pltpu.VMEM((layers, LANES, width), F32),
            pltpu.VMEM((layers, 4, LANES, width), F32),
            pltpu.VMEM((layers, width, width), F32),
        ]
        + [pltpu.VMEM(array.shape, array.dtype) for array in passing]
        + [
            pltpu.SemaphoreType.DMA((layers, 12)),
            pltpu.SemaphoreType.DMA((layers, 9)),
            pltpu.SemaphoreType.DMA((2, 2)),
        ],
        name="format_grads",
        compiler_params=pltpu.CompilerParams(vmem_limit_bytes=60 << 20),
    )(*early, *late, *passing)


SPAN = 1024
ATTEND_WORK = 88
SWAP_WORK = 32


def sort_in(source_ref, order_ref, target_ref, count):
    def body(i, unused):
        start = order_ref[i] * BLK
        target_ref[pl.ds(pl.multiple_of(i * BLK, BLK), BLK), :] = source_ref[
            pl.ds(start, BLK), :
        ]
        return unused

    lax.fori_loop(0, count, body, 0, unroll=8)


def block_numbers(number_ref, first, count, axis):
    if axis == 0:
        return jnp.concatenate(
            [jnp.full((BLK, 1), number_ref[first + i], jnp.int32) for i in range(count)], 0
        )
    lane = lax.broadcasted_iota(jnp.int32, (1, count * BLK), 1) // BLK
    numbers = jnp.zeros((1, count * BLK), jnp.int32)
    for i in range(count):
        numbers = jnp.where(lane == i, number_ref[first + i], numbers)
    return numbers


def far_copy(source, target, sems):
    return pltpu.make_async_remote_copy(
        src_ref=source,
        dst_ref=target,
        send_sem=sems.at[0],
        recv_sem=sems.at[1],
        device_id=far_partner(),
        device_id_type=MESH,
    )


def attend_steps(tables, q_ref, kv_ref, context_ref, qs, kvs, logs, scratch):
    order_ref, standing_ref, number_ref, other_order, other_ref = tables
    tops, totals, sums, far_ref, sems = scratch
    copy = far_copy(kv_ref, far_ref, sems)
    copy.start()
    sort_in(kv_ref, order_ref, kvs.at[0], 32)
    sort_in(q_ref, order_ref, qs, 32)
    tiles = qs.shape[0] // TILE
    row = lax.broadcasted_iota(jnp.int32, (TILE, TILE), 0)
    column = lax.broadcasted_iota(jnp.int32, (TILE, TILE), 1)
    yield 4

    def highest(scores):
        return jnp.max(scores, 1, keepdims=True)

    def weigh(scores, top, keys):
        weights = jnp.exp(scores - top)
        return jnp.sum(weights, 1, keepdims=True), dots(weights.astype(BF16), keys, 1, 0)

    def wide(vector):
        return jnp.broadcast_to(vector, (TILE, 2 * HEAD))

    def own_tile(tile):
        rows = slice(tile * TILE, (tile + 1) * TILE)
        queries, near = qs[rows, :], kvs[0, rows, :]
        parts = [(jnp.where(column <= row, dots(queries, near, 1, 1), NEGATIVE), near)]
        for low in range(0, tile * TILE, SPAN):
            keys = kvs[0, low : min(low + SPAN, tile * TILE), :]
            parts.append((dots(queries, keys, 1, 1), keys))
        top = highest(parts[0][0])
        for scores, keys in parts[1:]:
            top = jnp.maximum(top, highest(scores))
        total, weighted = 0.0, 0.0
        for scores, keys in parts:
            more, product = weigh(scores, top, keys)
            total, weighted = total + more, weighted + product
        tops[rows, :], totals[rows, :], sums[rows, :] = wide(top), wide(total), weighted

    def other_tile(tile, numbers):
        rows = slice(tile * TILE, (tile + 1) * TILE)
        queries = qs[rows, :]
        own = block_numbers(number_ref, tile * TILE // BLK, TILE // BLK, 0)
        half = tile // 4
        keys = kvs[1, half * SPAN : (half + 1) * SPAN, :]
        parts = [(jnp.where(numbers < own, dots(queries, keys, 1, 1), NEGATIVE), keys)]
        if half:
            keys = kvs[1, :SPAN, :]
            parts.append((dots(queries, keys, 1, 1), keys))
        old = tops[rows, :][:, 0:1]
        top = old
        for scores, keys in parts:
            top = jnp.maximum(top, highest(scores))
        scale = jnp.exp(old - top)
        total, weighted = totals[rows, :][:, 0:1] * scale, sums[rows, :] * scale
        for scores, keys in parts:
            more, product = weigh(scores, top, keys)
            total, weighted = total + more, weighted + product
        sums[rows, :] = weighted / total
        logs[rows, :] = wide(top + jnp.log(total))

    for tile in range(tiles):
        own_tile(tile)
        yield tile + 1
    for unused in range(8):
        yield SWAP_WORK // 8
    copy.wait_recv()
    sort_in(far_ref, other_order, kvs.at[1], 32)
    for half in (0, 1):
        numbers = block_numbers(other_ref, half * 16, 16, 1)
        for tile in range(half * 4, half * 4 + 4):
            other_tile(tile, numbers)
            yield 4 + 4 * half
    sort_in(sums, standing_ref, context_ref, 32)
    copy.wait_send()


def attend_back_steps(
    tables, qs, kvs, logs, pull_ref, offset_ref, query_grad_ref, pair_grad_ref, scratch
):
    order_ref, standing_ref, number_ref, unused, other_ref = tables
    pulls, offsets, turned, query_sums, pair_sums, away, land, sems = scratch
    sort_in(pull_ref, order_ref, pulls, 32)
    sort_in(offset_ref, order_ref, offsets, 32)
    pair_sums[...] = jnp.zeros_like(pair_sums)
    tiles = qs.shape[0] // TILE
    row = lax.broadcasted_iota(jnp.int32, (TILE, TILE), 0)
    column = lax.broadcasted_iota(jnp.int32, (TILE, TILE), 1)
    lane = lax.broadcasted_iota(jnp.int32, (TILE, 2 * HEAD), 1)
    yield 4

    def tile_part(tile, half, low, count, mask):
        rows = slice(tile * TILE, (tile + 1) * TILE)
        queries, pull = qs[rows, :], pulls[rows, :]
        keys = kvs[half, low : low + count, :]
        scores = dots(keys, queries, 1, 1)
        if mask is not None:
            scores = jnp.where(mask, scores, NEGATIVE)
        probs = jnp.exp(scores - turned[tile, 0:1])
        score_grad = (probs * (dots(keys, pull, 1, 1) - turned[tile, 1:2])).astype(BF16)
        pair_sums[half, low : low + count, :] += dots(score_grad, queries, 1, 0) + dots(
            probs.astype(BF16), pull, 1, 0
        )
        return dots(score_grad, keys, 0, 0)

    def masked_tile(tile, numbers):
        rows = slice(tile * TILE, (tile + 1) * TILE)
        turned[tile] = jnp.transpose(
            jnp.where(lane == 0, logs[rows, :], offsets[rows, :])
        )[:8]
        own = block_numbers(number_ref, tile * TILE // BLK, TILE // BLK, 1)
        query_sums[rows, :] = tile_part(tile, 1, tile // 4 * SPAN, SPAN, numbers < own)

    def send(half):
        span = pl.ds(half * SPAN, SPAN)
        away[span] = pair_sums[1, span].astype(BF16)
        copy = far_copy(away.at[span], land.at[span], sems.at[half])
        copy.start()
        return copy

    def own_tile(tile):
        rows = slice(tile * TILE, (tile + 1) * TILE)
        query_sums[rows, :] += tile_part(tile, 0, tile * TILE, TILE, row <= column)
        yield 1
        for low in range(0, tile * TILE, SPAN):
            count = min(SPAN, tile * TILE - low)
            query_sums[rows, :] += tile_part(tile, 0, low, count, None)
            yield count // TILE

    copies = []
    for half in (1, 0):
        numbers = block_numbers(other_ref, half * 16, 16, 0)
        for tile in range(half * 4, half * 4 + 4):
            masked_tile(tile, numbers)
            yield 4
        if half == 0:
            for tile in range(4, 8):
                rows = slice(tile * TILE, (tile + 1) * TILE)
                query_sums[rows, :] += tile_part(tile, 1, 0, SPAN, None)
                yield 4
        copies.append(send(half))
    for tile in range(tiles):
        yield from own_tile(tile)
    sort_in(query_sums, standing_ref, query_grad_ref, 32)
    for copy in copies:
        copy.wait_recv()
    pair_sums[0] += land[...].astype(F32)
    sort_in(pair_sums.at[0], standing_ref, pair_grad_ref, 32)
    for copy in copies:
        copy.wait_send()


def attend_back_scratch(rows):
    block = (rows, 2 * HEAD)
    return [
        pltpu.VMEM(block, BF16),
        pltpu.VMEM(block, F32),
        pltpu.VMEM((rows // TILE, 8, TILE), F32),
        pltpu.VMEM(block, F32),
        pltpu.VMEM((2,) + block, F32),
        pltpu.VMEM(block, BF16),
        pltpu.VMEM(block, BF16),
        pltpu.SemaphoreType.DMA((2, 2)),
    ]


def take_turns(work, total, others):
    done = 0
    ran = [first for steps, count, first, early, part in others]
    for steps, count, first, early, part in others:
        run(steps, first)
    for more in work:
        done += more
        for index, (steps, count, first, early, part) in enumerate(others):
            wanted = early + min(int(done * (count - early) / (total * part)), count - early)
            run(steps, wanted - ran[index])
            ran[index] = wanted
    for steps, *unused in others:
        run(steps)


def back_last_body(wait, tables, ins, outs, refs):
    hidden_ref, up_ref, up_bias_ref, query_grad_ref, pair_grad_ref, sums_ref, total_ref, out_ref = outs
    (pull, offset, early, quarter, tall_sum), refs = refs[:5], refs[5:]
    (parts, total_rows), scatter_refs, refs = refs[:2], refs[2:8], refs[8:]
    core_refs, quarter_refs, scratch = refs[:2], refs[2:5], refs[5:]
    grid = Grid()
    wide_barrier(grid)
    made = [pull, offset, hidden_ref, early, quarter, up_ref, up_bias_ref]
    leaving = [ins[1], ins[2], ins[5], ins[11], ins[12]]
    scatter = leave_steps(grid, *leaving, out_ref, parts, total_rows, scatter_refs)
    wait(1, 2, 5, 11)
    run(scatter, 1)
    back_enter_phase(grid, wait, ins[:8], made, tall_sum, between=lambda: run(scatter, 1))
    wait.flush(0, 1, 2)
    wait()
    core = core_steps(early, sums_ref, *core_refs)
    quarters = quarter_steps(grid, quarter, total_ref, *quarter_refs)
    work = attend_back_steps(
        tables, *ins[8:11], pull, offset, query_grad_ref, pair_grad_ref, scratch
    )
    others = [
        (core, 1, 1, 1, 1.0),
        (quarters, 1, 1, 1, 1.0),
        (scatter, SCATTER_STEPS - 1 - PIECES, 0, 0, 0.9),
    ]
    take_turns(work, ATTEND_WORK, others)


def back_last(tables, branch, given, attention, stream, bias, number):
    rows, width = stream.shape
    shapes, scratch = back_enter_shapes(rows, width)
    total = 16 * rows
    shapes = shapes + [jax.ShapeDtypeStruct((total, 2 * HEAD), F32)] * 2
    shapes += [
        jax.ShapeDtypeStruct((2, EARLY, LANES), BF16),
        jax.ShapeDtypeStruct((PART, LANES), BF16),
        jax.ShapeDtypeStruct((rows, width), BF16),
    ]
    scratch = scratch + [
        pltpu.VMEM((16, rows, width), BF16),
        pltpu.VMEM((rows, width), F32),
    ]
    scratch += scatter_scratch(rows, width) + core_scratch(EARLY) + quarter_scratch()
    scratch += attend_back_scratch(total)
    given = [branch[0], *given, branch[1], *attention, stream, bias]
    return staged_call(
        back_last_body, "back_last", number, given, shapes, scratch, tables,
        parted=(0, 1, 2, 3, 4, 7),
    )


def back_first_body(wait, tables, ins, outs, refs):
    (
        hidden_ref, up_ref, up_bias_ref, query_grad_ref, pair_grad_ref, pair_ref, late_pair, all_ref
    ) = outs
    (pull, offset, early, quarter, tall_sum), refs = refs[:5], refs[5:]
    (own, all_rows, *row_sems), refs = refs[:4], refs[4:]
    (folded, late_sums, sums, total), refs = refs[:4], refs[4:]
    high_refs, late_core_refs, refs = refs[:2], refs[2:4], refs[4:]
    gather_refs, core_refs, quarter_refs, refs = refs[:3], refs[3:5], refs[5:8], refs[8:]
    early_refs, late_refs, scratch = refs[:2], refs[2:4], refs[4:]
    grid = Grid()
    wait(0)
    own[...] = ins[0][...].astype(BF16)
    all_rows[grid.rank(0, 0, 0)] = own[...]
    wide_barrier(grid)
    wait(7, 8)
    beside = [
        high_steps(ins[7], folded, *high_refs),
        core_steps(ins[8], late_sums, *late_core_refs),
    ]
    made = [pull, offset, hidden_ref, early, quarter, up_ref, up_bias_ref]
    back_enter_phase(grid, wait, ins[:7], made, tall_sum, (own, all_rows, *row_sems), beside)
    wait.flush(0, 1, 2)
    for steps in beside:
        run(steps)
    keep = keep_own(grid, folded, all_ref, gather_refs[0])
    gather = gather_steps(grid, folded, all_ref, *gather_refs[1:])
    run(gather, 2)
    wait()
    quarters = quarter_steps(grid, quarter, total, *quarter_refs)
    late = low_steps(late_sums, late_pair, *late_refs)

    def early_steps():
        core = core_steps(early, sums, *core_refs)
        next(core)
        yield
        run(core)
        run(quarters)
        yield from low_steps(sums, pair_ref, *early_refs, total)

    work = attend_back_steps(
        tables, *ins[9:12], pull, offset, query_grad_ref, pair_grad_ref, scratch
    )
    others = [
        (gather, GATHER_STEPS - 2, 0, 5, 0.9),
        (quarters, 1, 1, 1, 1.0),
        (early_steps(), 2, 1, 1, 0.5),
        (late, 1, 1, 1, 1.0),
    ]
    take_turns(work, ATTEND_WORK, others)
    keep.wait()


def back_first(tables, grad, given, exchanged, attention, number):
    rows, width = grad.shape
    shapes, scratch = back_enter_shapes(rows, width)
    total = 16 * rows
    shapes = shapes + [jax.ShapeDtypeStruct((total, 2 * HEAD), F32)] * 2
    shapes += [
        jax.ShapeDtypeStruct((EARLY, LANES), BF16),
        jax.ShapeDtypeStruct((LATE, LANES), BF16),
        jax.ShapeDtypeStruct((16, EARLY, LANES), BF16),
    ]
    scratch = scratch + [
        pltpu.VMEM((rows, width), BF16),
        pltpu.VMEM((16, rows, width), BF16),
        pltpu.SemaphoreType.DMA((2, 20)),
        pltpu.SemaphoreType.DMA((2, 20)),
        pltpu.VMEM((EARLY, LANES), BF16),
        pltpu.VMEM((2, LATE, LANES), BF16),
        pltpu.VMEM((2, EARLY, LANES), BF16),
        pltpu.VMEM((PART, LANES), BF16),
    ]
    scratch += swap_scratch(EARLY) + core_scratch(LATE) + gather_sems()
    scratch += core_scratch(EARLY) + quarter_scratch()
    scratch += swap_scratch(EARLY) + swap_scratch(LATE) + attend_back_scratch(total)
    given = [grad, *given, *exchanged, *attention]
    return staged_call(
        back_first_body, "back_first", number, given, shapes, scratch, tables, direct=(7,)
    )


def block_tables(pair_table, z):
    slots = pair_table.shape[0]
    ranks = slots // 2
    index = jnp.arange(slots, dtype=jnp.int32)

    def plane(which):
        pairs = lax.dynamic_slice_in_dim(pair_table.reshape(ranks, 2), which, 1, 1)
        numbers = jnp.concatenate([pairs, 2 * slots - 1 - pairs], 1).reshape(-1)
        standing = jnp.sum((numbers[None, :] < numbers[:, None]).astype(jnp.int32), 1)
        chosen = (standing[None, :] == index[:, None]).astype(jnp.int32)
        order = jnp.sum(chosen * index[None, :], 1)
        return numbers, (order, standing, jnp.sum(chosen * numbers[None, :], 1))

    numbers, own = plane(z)
    other = plane(1 - z)[1]
    return numbers, own + (other[0], other[2])


def rotation(positions):
    freqs = 10000.0 ** (-jnp.arange(0, ROT, 2, dtype=F32) / ROT)
    angles = positions.astype(F32)[:, None] * freqs[None, :]
    rest = ((0, 0), (0, 2 * HEAD - ROT))
    return (
        jnp.pad(jnp.concatenate([jnp.cos(angles)] * 2, -1), rest, constant_values=1.0),
        jnp.pad(jnp.concatenate([jnp.sin(angles)] * 2, -1), rest),
    )


def on_device(
    hidden_in,
    cotangent,
    pair_table,
    norm_gain,
    norm_bias,
    qkv_weight,
    qkv_bias,
    out_weight,
    out_bias,
    up_weight,
    up_bias,
    down_weight,
    down_bias,
):
    layers = norm_gain.shape[0]
    slot = lax.axis_index("ctx")
    shard = lax.axis_index("fsdp")
    rank, z = slot // 2, slot % 2
    width = hidden_in.shape[2]
    quarter = width // 4

    numbers, tables = block_tables(pair_table, z)
    positions = (
        numbers[:, None] * BLK + jnp.arange(BLK, dtype=jnp.int32)[None, :]
    ).reshape(-1)
    cosines, sines = rotation(positions)

    def columns(weight, part):
        return lax.dynamic_slice_in_dim(weight, part * width + rank * HEAD, HEAD, 2)

    wide = jnp.concatenate(
        [columns(qkv_weight, 1), columns(qkv_weight, 2), columns(qkv_weight, 0)]
        + [jnp.zeros((layers, quarter, HEAD), BF16)]
        + [columns(up_weight, part) for part in range(4)],
        2,
    )
    vectors = (norm_gain, norm_bias, qkv_bias, out_bias, up_bias, down_bias)
    stream = hidden_in[0]
    saved, branch_all, wide_all, tall_all, second, scales, last_biases = forward(
        tables, stream, vectors, cosines, sines, wide, down_weight, out_weight, cotangent[0], 1
    )
    streams, number = (stream, second), 2

    grad = cotangent[0]
    early, late = [None] * layers, [None] * layers
    exchanged = None
    for layer in reversed(range(layers)):
        last = layer == layers - 1
        normed_all, active, slope, context, queries, pairs, logs = saved[layer]
        stream = streams[layer]
        given = (active, context, slope, normed_all, tall_all[layer], scales[layer])
        attention = (queries, pairs, logs)
        if last:
            (
                hidden_grad, up_raw, up_bias_raw, query_grad, pair_grad, early_sums, out_total, output
            ) = back_last(tables, branch_all, given, attention, stream, last_biases[layer], number)
            exchanges = (early_sums, out_total)
        else:
            (
                hidden_grad, up_raw, up_bias_raw, query_grad, pair_grad, early_pair, late_pair,
                early[layer + 1],
            ) = back_first(tables, grad, given, exchanged, attention, number)
            exchanges = (early_pair, late_pair)
        number += 1
        given = (
            query_grad,
            pair_grad,
            hidden_grad,
            normed_all,
            wide_all[layer].reshape(width, 8 * HEAD),
            scales[layer],
            cosines,
            sines,
            stream,
            grad,
            up_raw,
            up_bias_raw,
        )
        if last:
            grad, addends, vector_rows, early_pair = back_leave(
                given, *stream.shape, number, *exchanges
            )
            exchanged = (early_pair, addends)
        else:
            grad, early[0], late[1], late[0] = back_leave_last(
                given, *stream.shape, number, *exchanges, vector_rows
            )
        number += 1

    qkv_out, out_out, up_out, down_out, output, grad = format_grads(early, late, (output, grad))
    small = jnp.stack(
        [late[0][:, LATE + 16 * layer : LATE + 16 * layer + 7] for layer in range(layers)]
    ).astype(F32)
    sums = jnp.sum(small[:, :, :5], 1)
    gain_out, shift_out, branch_out = sums[:, 0:2], sums[:, 2:4], sums[:, 4]
    qkv_bias_out = jnp.transpose(
        jnp.roll(small[:, :, 5, : 3 * HEAD].reshape(layers, 16, 3, HEAD), 1, 2), (0, 2, 1, 3)
    ).reshape(layers, -1)
    share = qkv_bias_out.shape[1] // 4
    qkv_bias_out = lax.dynamic_slice_in_dim(qkv_bias_out, shard * share, share, 1)
    up_bias_out = lax.dynamic_slice_in_dim(
        small[:, :, 6].reshape(layers, 16, 4, HEAD), shard, 1, 2
    ).reshape(layers, -1)
    return (
        output[None],
        grad[None],
        gain_out,
        shift_out,
        qkv_out,
        qkv_bias_out,
        out_out,
        branch_out,
        up_out,
        up_bias_out,
        down_out,
        branch_out,
    )


def solution(mesh):
    rows = P("fsdp", "ctx", None)
    vector, matrix = P(None, "fsdp"), P(None, "fsdp", None)
    gains = P(None, None, "fsdp")
    params = (gains, gains) + (matrix, vector) * 4
    return jax.shard_map(
        on_device,
        mesh=mesh,
        in_specs=(rows, rows, P()) + params,
        out_specs=(rows, rows) + params,
        check_vma=False,
    )
```

```python
import functools

import jax
import jax.numpy as jnp
from jax import lax
from jax.experimental import pallas as pl
from jax.experimental.pallas import tpu as pltpu
from jax.sharding import PartitionSpec as P

HEADS = 16
HEAD = 64
ROT = 16
BLK = 64
SIDE = 4
EPS = 1e-05
NEGATIVE = -1e30
MESH = pl.DeviceIdType.MESH
F32 = jnp.float32
BF16 = jnp.bfloat16
TILE = 256
KEYS = 512
PART = 64
EARLY = 9 * PART
LATE = 3 * PART
LANES = 256


def place():
    slot = lax.axis_index("ctx")
    return slot // 8, (slot // 2) % SIDE, slot % 2


class Grid:
    def __init__(self, meets=((1, 0), (-1, 0), (0, 1), (0, -1))):
        self.x, self.y, self.z = place()
        self.meets = meets
        self.ranks, self.slots = {}, {}
        for dx in range(SIDE):
            for dy in range(SIDE):
                rank = ((self.x + dx) % SIDE) * SIDE + (self.y + dy) % SIDE
                self.ranks[dx, dy] = rank
                self.slots[dx, dy] = rank * 2 + self.z

    def spot(self, half, dp, dq):
        dx, dy = (dp, dq) if half == 0 else (dq, dp)
        return dx % SIDE, dy % SIDE

    def rank(self, half, dp, dq):
        return self.ranks[self.spot(half, dp, dq)]

    def device(self, half, dp, dq):
        return {"ctx": self.slots[self.spot(half, dp, dq)]}

    def barrier(self, others=()):
        gate = pltpu.get_barrier_semaphore()
        partners = [self.device(0, *step) for step in self.meets]
        partners += others
        for partner in partners:
            pl.semaphore_signal(gate, inc=1, device_id=partner, device_id_type=MESH)
        pl.semaphore_wait(gate, len(partners))


LARGE = 1 << 16


def size_of(array):
    return array.size * jnp.dtype(array.dtype).itemsize


PIECES = 4


class Waits:
    def __init__(self):
        self.loads, self.stores, self.started = {}, {}, []

    def __call__(self, *which):
        for i in which or sorted(self.loads):
            for copy in self.loads.pop(i, ()):
                if copy is not None:
                    copy.wait()

    def piece(self, k, *which):
        for i in which:
            if i in self.loads:
                copies = self.loads[i]
                if copies[k] is not None:
                    copies[k].wait()
                    copies[k] = None

    def flush(self, *which):
        for i in which or sorted(self.stores):
            if i in self.stores:
                copy = self.stores.pop(i)
                copy.start()
                self.started.append(copy)

    def finish(self):
        self()
        self.flush()
        for copy in self.started:
            copy.wait()


def staged_call(
    body, name, number, given, shapes, scratch, tables=(), direct=(), parted=(), raw=()
):
    loads = [i for i, array in enumerate(given) if size_of(array) > LARGE and i not in raw]
    stores = [i for i, shape in enumerate(shapes) if size_of(shape) > LARGE and i not in direct]
    counts = (len(tables), len(given), len(shapes), len(loads), len(stores))

    def kernel(*refs):
        refs, groups = list(refs), []
        for count in counts:
            groups.append(refs[:count])
            refs = refs[count:]
        table_refs, ins, outs, staged_in, staged_out = groups
        load_sem, store_sem, *refs = refs
        wait = Waits()
        for k, i in enumerate(loads):
            if i not in parted:
                copy = pltpu.make_async_copy(ins[i], staged_in[k], load_sem.at[k, 0])
                copy.start()
                wait.loads[i] = [copy]
        for piece in range(PIECES):
            for k, i in enumerate(loads):
                if i in parted:
                    count = given[i].shape[0] // PIECES
                    span = pl.ds(piece * count, count)
                    copy = pltpu.make_async_copy(
                        ins[i].at[span], staged_in[k].at[span], load_sem.at[k, piece]
                    )
                    copy.start()
                    wait.loads.setdefault(i, []).append(copy)
        for k, i in enumerate(loads):
            ins[i] = staged_in[k]
        for k, i in enumerate(stores):
            wait.stores[i] = pltpu.make_async_copy(staged_out[k], outs[i], store_sem.at[k])
            outs[i] = staged_out[k]
        body(wait, table_refs, ins, outs, refs)
        wait.finish()

    smem, vmem, hbm = (
        pl.BlockSpec(memory_space=space) for space in (pltpu.SMEM, pltpu.VMEM, pl.ANY)
    )
    far = set(stores) | set(direct)
    params = dict(vmem_limit_bytes=60 << 20)
    if number is not None:
        params.update(collective_id=number, has_side_effects=True)
    return pl.pallas_call(
        kernel,
        out_shape=list(shapes),
        in_specs=[smem] * len(tables)
        + [hbm if i in loads or i in raw else vmem for i in range(len(given))],
        out_specs=[hbm if i in far else vmem for i in range(len(shapes))],
        scratch_shapes=[pltpu.VMEM(given[i].shape, given[i].dtype) for i in loads]
        + [pltpu.VMEM(shapes[i].shape, shapes[i].dtype) for i in stores]
        + [
            pltpu.SemaphoreType.DMA((max(len(loads), 1), PIECES)),
            pltpu.SemaphoreType.DMA((max(len(stores), 1),)),
        ]
        + list(scratch),
        name=name,
        compiler_params=pltpu.CompilerParams(**params),
    )(*tables, *given)


RINGS = ((1, 0), (-1, 0), (2, 0), (0, 1), (0, -1), (0, 2))


def gather_half(grid, half, own_ref, all_ref, send_sem, recv_sem):
    rows = own_ref.shape[0]
    half_rows, quarter = rows // 2, rows // 4
    sends = []

    def view(dp, dq, low, count):
        return all_ref.at[grid.rank(half, dp, dq), pl.ds(half * half_rows + low, count)]

    def start(event, to, block, low, count, own=False):
        source = (
            own_ref.at[pl.ds(half * half_rows + low, count)]
            if own
            else view(*block, low, count)
        )
        copy = pltpu.make_async_remote_copy(
            src_ref=source,
            dst_ref=view(*block, low, count),
            send_sem=send_sem.at[half, event],
            recv_sem=recv_sem.at[half, event],
            device_id=grid.device(half, *to),
            device_id_type=MESH,
        )
        copy.start()
        sends.append(copy)

    def arrive(event, block, low, count):
        there = view(*block, low, count)
        pltpu.make_async_remote_copy(
            src_ref=there,
            dst_ref=there,
            send_sem=send_sem.at[half, event],
            recv_sem=recv_sem.at[half, event],
            device_id=grid.device(half, 1, 0),
            device_id_type=MESH,
        ).wait_recv()

    def spread(column, dp, own=False):
        start(4 + 4 * column, (0, 1), (dp, 0), 0, half_rows, own)
        start(5 + 4 * column, (0, -1), (dp, 0), 0, half_rows, own)

    start(0, (1, 0), (0, 0), 0, half_rows, True)
    start(1, (-1, 0), (0, 0), 0, half_rows, True)
    spread(0, 0, True)
    yield
    arrive(0, (-1, 0), 0, half_rows)
    start(2, (1, 0), (-1, 0), 0, quarter)
    spread(1, -1)
    arrive(1, (1, 0), 0, half_rows)
    start(3, (-1, 0), (1, 0), quarter, quarter)
    spread(2, 1)
    yield
    arrive(2, (2, 0), 0, quarter)
    arrive(3, (2, 0), quarter, quarter)
    spread(3, 2)
    yield
    steps = (0, -1, 1, 2)
    for column in range(4):
        arrive(4 + 4 * column, (steps[column], -1), 0, half_rows)
        start(6 + 4 * column, (0, 1), (steps[column], -1), 0, quarter)
        arrive(5 + 4 * column, (steps[column], 1), 0, half_rows)
        start(7 + 4 * column, (0, -1), (steps[column], 1), quarter, quarter)
        yield
    for column in range(4):
        arrive(6 + 4 * column, (steps[column], 2), 0, quarter)
        arrive(7 + 4 * column, (steps[column], 2), quarter, quarter)
        if column % 2 == 0:
            yield
    for copy in sends:
        copy.wait_send()


GATHER_STEPS = 20


def gather_steps(grid, own_ref, all_ref, send_sem, recv_sem):
    halves = [
        gather_half(grid, half, own_ref, all_ref, send_sem, recv_sem) for half in (0, 1)
    ]
    for step in range(GATHER_STEPS):
        next(halves[step % 2], None)
        if step < GATHER_STEPS - 1:
            yield


DIRECT_STEPS = 8


def direct_steps(grid, own_ref, all_ref, send_sem, recv_sem):
    half_rows = own_ref.shape[0] // 2
    sends = []

    def view(half, dp, dq):
        return all_ref.at[grid.rank(half, dp, dq), pl.ds(half * half_rows, half_rows)]

    def copy(half, event, to, block, own=False):
        source = own_ref.at[pl.ds(half * half_rows, half_rows)] if own else view(half, *block)
        return pltpu.make_async_remote_copy(
            src_ref=source,
            dst_ref=view(half, *block),
            send_sem=send_sem.at[half, event],
            recv_sem=recv_sem.at[half, event],
            device_id=grid.device(half, *to),
            device_id_type=MESH,
        )

    def start(*args):
        made = copy(*args)
        made.start()
        sends.append(made)

    steps = (1, -1, 2)
    for index, step in enumerate(steps):
        for half in (0, 1):
            start(half, index, (step, 0), (0, 0), True)
    for index, step in enumerate(steps):
        for half in (0, 1):
            start(half, 3 + index, (0, step), (0, 0), True)
    yield
    for index, step in enumerate(steps):
        for half in (0, 1):
            copy(half, index, (step, 0), (-step, 0)).wait_recv()
            for other, move in enumerate(steps):
                start(half, 6 + 3 * index + other, (0, move), (-step, 0))
            yield
    for column, place_p in enumerate((0, -1, 1, -2)):
        for other, move in enumerate(steps):
            for half in (0, 1):
                copy(half, 3 + 3 * column + other, (0, move), (place_p, -move)).wait_recv()
    for made in sends:
        made.wait_send()


def run(steps, count=None):
    while count is None or count > 0:
        if next(steps, StopIteration) is StopIteration:
            return
        count = None if count is None else count - 1


def scatter_steps(
    grid, make, part_ref, out_ref, land_half, land_full, stage, total, send_sem, recv_sem
):
    rows = part_ref.shape[1]
    half_rows, quarter = rows // 2, rows // 4
    sends = []
    steps = (2, -1, 1, 0)

    def start(half, event, source, target, to):
        copy = pltpu.make_async_remote_copy(
            src_ref=source,
            dst_ref=target,
            send_sem=send_sem.at[half, event],
            recv_sem=recv_sem.at[half, event],
            device_id=grid.device(half, *to),
            device_id_type=MESH,
        )
        copy.start()
        sends.append(copy)

    def arrive(half, event, target):
        pltpu.make_async_remote_copy(
            src_ref=target,
            dst_ref=target,
            send_sem=send_sem.at[half, event],
            recv_sem=recv_sem.at[half, event],
            device_id=grid.device(half, 1, 0),
            device_id_type=MESH,
        ).wait_recv()

    def first(half, column):
        def piece(dq, low, count):
            return part_ref.at[
                grid.rank(half, steps[column], dq), pl.ds(half * half_rows + low, count)
            ]

        return piece

    def second(half):
        return lambda dp, low, count: total.at[half, steps.index(dp), pl.ds(low, count)]

    def along(step):
        return (0, step)

    def across(step):
        return (step, 0)

    def opposite(half, column, piece, step):
        for side, low in ((0, 0), (1, quarter)):
            start(
                half,
                4 * column + side,
                piece(2, low, quarter),
                land_half.at[half, column, side],
                step(1 - 2 * side),
            )

    def neighbours(half, column, piece, step):
        for side in (0, 1):
            land = land_half.at[half, column, side]
            arrive(half, 4 * column + side, land)
            low, other = side * quarter, (1 - side) * quarter
            toward = 1 - 2 * side
            stage[half, column, side, low : low + quarter] = (
                piece(toward, low, quarter)[...].astype(F32) + land[...].astype(F32)
            ).astype(BF16)
            stage[half, column, side, other : other + quarter] = piece(toward, other, quarter)[...]
            start(
                half,
                4 * column + 2 + side,
                stage.at[half, column, side],
                land_full.at[half, column, side],
                step(toward),
            )

    def settle(half, column, own):
        for side in (0, 1):
            arrive(half, 4 * column + 2 + side, land_full.at[half, column, side])
        return (
            own[...].astype(F32)
            + land_full[half, column, 0].astype(F32)
            + land_full[half, column, 1].astype(F32)
        )

    def places(*spots):
        make([grid.rank(0, dx, dy) for dx, dy in spots])

    def on_both(step, column, direction):
        for half in (0, 1):
            step(half, column, first(half, column), direction)

    places((2, 2))
    on_both(opposite, 0, along)
    for column in (1, 2, 3):
        places((steps[column], 2), (2, steps[column]))
        on_both(opposite, column, along)
        yield
    on_both(neighbours, 0, along)
    yield
    places((-1, -1), (-1, 1))
    places((1, -1), (1, 1))
    on_both(neighbours, 1, along)
    yield
    places((0, 1), (0, -1))
    on_both(neighbours, 2, along)
    yield
    places((1, 0), (-1, 0))
    on_both(neighbours, 3, along)
    yield
    places((0, 0))
    for column in range(4):
        for half in (0, 1):
            total[half, column] = settle(
                half, column, first(half, column)(0, 0, half_rows)
            ).astype(BF16)
            if column == 0:
                opposite(half, 4, second(half), across)
            if column == 2:
                neighbours(half, 4, second(half), across)
        yield
    for half in (0, 1):
        out_ref[pl.ds(half * half_rows, half_rows)] = settle(half, 4, total.at[half, 3])
    for copy in sends:
        copy.wait_send()


SCATTER_STEPS = 12


def scatter_scratch(rows, width):
    half_rows, quarter = rows // 2, rows // 4
    return [
        pltpu.VMEM((2, 5, 2, quarter, width), BF16),
        pltpu.VMEM((2, 5, 2, half_rows, width), BF16),
        pltpu.VMEM((2, 5, 2, half_rows, width), BF16),
        pltpu.VMEM((2, 4, half_rows, width), BF16),
        pltpu.SemaphoreType.DMA((2, 20)),
        pltpu.SemaphoreType.DMA((2, 20)),
    ]


def follow(grid, gather, block, ready=None, last=None):
    def places(*spots):
        block([grid.rank(0, dx, dy) for dx, dy in spots])

    run(gather, 4)
    if ready is not None:
        ready()
    places((0, 0))
    run(gather, 2)
    places((0, 1), (0, -1))
    run(gather, 2)
    places((1, 0), (-1, 0))
    run(gather, 2)
    places((1, 1), (1, -1))
    run(gather, 2)
    places((-1, 1), (-1, -1))
    run(gather, 2)
    places((0, 2), (2, 0))
    run(gather, 2)
    if last is not None:
        last()
    places((1, 2), (-1, 2))
    places((2, 1), (2, -1))
    run(gather)
    places((2, 2))


def rows_of(ref, ranks, rows):
    return jnp.concatenate([ref[block_rows(rank, rows), :] for rank in ranks], 0)


def put_rows(ref, ranks, rows, values):
    for index, rank in enumerate(ranks):
        ref[block_rows(rank, rows), :] = values[index * rows : (index + 1) * rows]


def blocks_of(ref, ranks):
    return jnp.concatenate([ref[rank] for rank in ranks], 0)


SQRT_HALF = 0.7071067811865476
DENSITY = 0.3989422804014327


def standardize(stream):
    row_mean = jnp.mean(stream, -1, keepdims=True)
    centered = stream - row_mean
    spread = jnp.mean(centered * centered, -1, keepdims=True)
    inverse = lax.rsqrt(spread + EPS)
    return (centered * inverse, inverse)


def dots(a, b, da, db):
    return lax.dot_general(a, b, (((da,), (db,)), ((), ())), preferred_element_type=F32)


def rotate(values, cosines, sines):
    lane = lax.broadcasted_iota(jnp.int32, values.shape, 1)
    half_dims = ROT // 2
    up = pltpu.roll(values, 2 * HEAD - half_dims, 1)
    down = pltpu.roll(values, half_dims, 1)
    return values * cosines + jnp.where(lane < half_dims, -up, down) * sines


def block_rows(rank, rows):
    return pl.ds(pl.multiple_of(rank * rows, rows), rows)


def share_partners():
    shard = lax.axis_index("fsdp")
    return [{"fsdp": shard + 1 - 2 * (shard % 2)}, {"fsdp": (shard + 2) % 4}]


def share_steps(items, send_sem, recv_sem):
    shard = lax.axis_index("fsdp")
    sibling = shard + 1 - 2 * (shard % 2)
    mate = (shard + 2) % 4
    third = (sibling + 2) % 4
    sends = []

    def copy(item, source, target, event, to):
        return pltpu.make_async_remote_copy(
            src_ref=source,
            dst_ref=target,
            send_sem=send_sem.at[item, event],
            recv_sem=recv_sem.at[item, event],
            device_id={"fsdp": to},
            device_id_type=MESH,
        )

    def start(*args):
        made = copy(*args)
        made.start()
        sends.append(made)

    for item, (own, every) in enumerate(items):
        start(item, own, every.at[shard], 0, mate)
        start(item, own, every.at[shard], 1, sibling)
        every[shard] = own[...]
    yield
    for item, (own, every) in enumerate(items):
        copy(item, own, every.at[mate], 0, mate).wait_recv()
        start(item, every.at[mate], every.at[mate], 2, sibling)
        yield
        copy(item, own, every.at[sibling], 1, sibling).wait_recv()
        copy(item, own, every.at[third], 2, sibling).wait_recv()
        yield
    for made in sends:
        made.wait_send()


def share_sems(items):
    return [pltpu.SemaphoreType.DMA((items, 3)), pltpu.SemaphoreType.DMA((items, 3))]


def stack_tall(tall_all, tall_ref):
    for part in range(4):
        tall_ref[part * HEAD : (part + 1) * HEAD] = tall_all[part, :HEAD]
    tall_ref[4 * HEAD : 5 * HEAD] = jnp.zeros((HEAD, tall_ref.shape[1]), BF16)
    tall_ref[5 * HEAD :] = tall_all[place()[0], HEAD:]


def enter_phase(grid, stream_ref, given, wide_ref, made, own, sems, ready, swap, last):
    scale_ref, bias_ref, cos_ref, sin_ref = given
    normed_ref, active_ref, slope_ref, q_ref, kv_ref = made
    rows, width = stream_ref.shape
    own[...] = standardize(stream_ref[...].astype(F32))[0].astype(BF16)
    normed_ref[grid.rank(0, 0, 0)] = own[...]
    yield
    gather = gather_steps(grid, own, normed_ref, *sems)
    run(gather, 2)

    def block(ranks):
        plain = blocks_of(normed_ref, ranks).astype(F32)
        first = (plain * scale_ref[0:1] + scale_ref[2:3]).astype(BF16)
        second = (plain * scale_ref[1:2] + scale_ref[3:4]).astype(BF16)
        weight = wide_ref[...].reshape(width, 8 * HEAD)
        mixed = dots(first, weight[:, : 4 * HEAD], 1, 0) + bias_ref[:, : 4 * HEAD]
        hidden = dots(second, weight[:, 4 * HEAD :], 1, 0) + bias_ref[:, 4 * HEAD :]
        cosines, sines = rows_of(cos_ref, ranks, rows), rows_of(sin_ref, ranks, rows)
        pairs = rotate(mixed[:, : 2 * HEAD], cosines, sines)
        queries = rotate(mixed[:, 2 * HEAD :], cosines, sines) * 0.125
        put_rows(kv_ref, ranks, rows, pairs.astype(BF16))
        put_rows(q_ref, ranks, rows, queries.astype(BF16))
        share = 0.5 * (1.0 + lax.erf(hidden * SQRT_HALF))
        put_rows(active_ref, ranks, rows, (hidden * share).astype(BF16))
        slope = share + hidden * (DENSITY * jnp.exp(-0.5 * hidden * hidden))
        put_rows(slope_ref, ranks, rows, slope)
        swap(ranks)

    follow(grid, gather, block, ready, last)


def leave_steps(
    grid, active_ref, context_ref, tall_ref, stream_ref, bias_ref, out_ref, parts, total_rows, scratch
):
    rows = stream_ref.shape[0]

    def make(ranks):
        context = rows_of(context_ref, ranks, rows).astype(BF16)
        both = jnp.concatenate([rows_of(active_ref, ranks, rows), context], 1)
        made = dots(both, tall_ref[...], 1, 0).astype(BF16)
        for index, rank in enumerate(ranks):
            parts[rank] = made[index * rows : (index + 1) * rows]

    yield from scatter_steps(grid, make, parts, total_rows, *scratch)
    stream = stream_ref[...].astype(F32)
    out_ref[...] = (stream + total_rows[...] + bias_ref[...]).astype(out_ref.dtype)


VECTOR_ROWS = 16


def unpack(grid, vectors, scale_ref, bias_ref, last_ref):
    lane = lax.broadcasted_iota(jnp.int32, (8, 2 * HEAD), 1)

    def of_rank(rows):
        row = rows[0]
        for index in range(1, 4):
            row = jnp.where(grid.x == index, rows[index], row)
        row = jnp.broadcast_to(row, (8, LANES))
        half = jnp.where(grid.y < 2, row[:, : 2 * HEAD], row[:, 2 * HEAD :])
        rolled = pltpu.roll(half, HEAD, 1)
        odd = grid.y % 2 == 1
        return jnp.where(odd, rolled, half), jnp.where(odd, half, rolled)

    def beside(low, high):
        return jnp.where(lane < HEAD, low[0], high[1])

    def shard_rows(first, count):
        return [vector[first + i : first + i + 1] for vector in vectors for i in range(count)]

    scale_ref[...] = jnp.concatenate([vector[:4] for vector in vectors], 1)
    last_ref[...] = jnp.concatenate([vector[7:8] + vector[12:13] for vector in vectors], 1)
    mixed = shard_rows(4, 3)
    q, k, v = (of_rank(mixed[4 * part : 4 * part + 4]) for part in range(3))
    up = [of_rank([vector[8 + i : 9 + i] for i in range(4)]) for vector in vectors]
    tiles = [
        beside(k, v),
        jnp.where(lane < HEAD, q[0], 0.0),
        beside(up[0], up[1]),
        beside(up[2], up[3]),
    ]
    bias_ref[...] = jnp.concatenate(tiles, 1)[0:1]


def forward_body(wait, tables, ins, outs, refs):
    stream_ref, cos_ref, sin_ref, wide_one, wide_two, branch_ref, down_ref, out_ref = ins[:8]
    vector_refs = ins[8:]
    scales, lasts = outs[21:23], outs[23:25]
    layer_outs, branches = (outs[:7], outs[7:14]), outs[14:16]
    wide_refs, tall_refs, second_ref = (outs[16], outs[18]), (outs[17], outs[19]), outs[20]
    (own_one, own_two), refs = refs[:2], refs[2:]
    queries, refs = (refs[:2], refs[2:4]), refs[4:]
    enter_sems, refs = (refs[:2], refs[2:4]), refs[4:]
    branch_sems, refs = (refs[:3], refs[3:6]), refs[6:]
    share_refs, refs = (refs[:3], refs[3:6]), refs[6:]
    (parts, total_rows), scatter_refs, refs = refs[:2], refs[2:8], refs[8:]
    attend_refs, swap_sems, refs = (refs[:4], refs[:3] + refs[5:6]), (refs[4], refs[6]), refs[7:]
    swaps = ([], [])
    vector_ref, vector_all, biases, refs = refs[0], refs[1], refs[2:4], refs[4:]
    talls, tall_sem = refs[:2], refs[2]
    grid = Grid()
    tall_copies = []
    for layer in range(2):
        for index, (source, first) in enumerate(
            ((down_ref, grid.rank(0, 0, 0)), (out_ref, grid.y))
        ):
            copy = pltpu.make_async_copy(
                source.at[layer, block_rows(first, HEAD)],
                talls[layer].at[pl.ds(index * HEAD, HEAD)],
                tall_sem.at[layer, index],
            )
            copy.start()
            tall_copies.append(copy)
    for layer in range(2):
        gain, shift, qkv, out, up, down = (
            ref[layer].astype(F32) if len(ref.shape) == 3 else ref[layer : layer + 1].astype(F32)
            for ref in vector_refs
        )
        rows = [gain, shift]
        rows += [qkv[:, i * LANES : (i + 1) * LANES] for i in range(3)] + [out]
        rows += [up[:, i * LANES : (i + 1) * LANES] for i in range(4)] + [down]
        rows.append(jnp.zeros((VECTOR_ROWS - 13, LANES), F32))
        vector_ref[layer] = jnp.concatenate(rows, 0).astype(BF16)

    keeps, gathers = [], []

    def start_half(layer):
        all_ref, sems = branches[layer], branch_sems[layer]
        count = branch_ref.shape[0] // 2
        half = branch_ref.at[pl.ds(layer * count, count)]
        keeps.append(keep_own(grid, half, all_ref, sems[0]))
        gathers.append(gather_steps(grid, half, all_ref, *sems[1:]))
        run(gathers[layer], 2)

    def attend_phase(layer):
        normed, active, slope, context, qs, kvs, logs = layer_outs[layer]
        work = attend_steps(
            tables, *queries[layer], context, qs, kvs, logs, attend_refs[layer], swaps[layer]
        )
        take_turns(work, ATTEND_WORK, [(gathers[layer], GATHER_STEPS - 2, 0, 2, 1.0)])

    def swap(layer, ranks):
        for rank in ranks:
            span, sem = block_rows(rank, stream_ref.shape[0]), swap_sems[layer]
            event = len(swaps[layer])
            copy = remote(
                queries[layer][1].at[span],
                attend_refs[layer][3].at[span],
                sem.at[0, event],
                sem.at[1, event],
                far_partner(),
            )
            copy.start()
            swaps[layer].append(copy)

    def sharing(layer, *items):
        tall_all, *sems = share_refs[layer]
        wide_own, tall_own = items[-2:]
        items = items[:-2] + ((wide_own, wide_refs[layer]), (tall_own, tall_all))
        return share_steps(items, *sems)

    def ready():
        run(shared, 4)
        for layer in range(2):
            vectors = [vector_all[shard, layer].astype(F32) for shard in range(4)]
            unpack(grid, vectors, scales[layer], biases[layer], lasts[layer])
        wait()

    wait(0)
    enter = enter_phase(
        grid, stream_ref, (scales[0], biases[0], cos_ref, sin_ref), wide_refs[0],
        (*layer_outs[0][:3], *queries[0]), own_one, enter_sems[0], ready,
        functools.partial(swap, 0), functools.partial(start_half, 0),
    )
    run(enter, 1)
    grid.barrier([far_partner()] + share_partners())
    wait(3)
    for copy in tall_copies:
        copy.wait()
    shared = sharing(0, (vector_ref, vector_all), wide_one, talls[0])
    run(shared, 1)
    run(enter)
    run(shared)
    stack_tall(share_refs[0][0], tall_refs[0])
    wait.flush(0, 1, 2, 16, 17)
    attend_phase(0)
    wait.flush(3, 4, 5, 6)
    shared = sharing(1, wide_two, talls[1])
    run(shared, 1)
    leave = leave_steps(
        grid, layer_outs[0][1], layer_outs[0][3], tall_refs[0], stream_ref, lasts[0], second_ref,
        parts, total_rows, scatter_refs,
    )
    run(leave, 5)
    run(shared, 1)
    run(leave, 3)
    run(shared, 2)
    run(leave)

    enter = enter_phase(
        grid, second_ref, (scales[1], biases[1], cos_ref, sin_ref), wide_refs[1],
        (*layer_outs[1][:3], *queries[1]), own_two, enter_sems[1], lambda: run(shared),
        functools.partial(swap, 1), functools.partial(start_half, 1),
    )
    run(enter, 1)
    wait.flush(20)
    run(enter)
    stack_tall(share_refs[1][0], tall_refs[1])
    wait.flush(7, 8, 9, 18, 19)
    attend_phase(1)
    for keep in keeps:
        keep.wait()


def forward(tables, stream, vectors, cosines, sines, wide, down, out, cotangent, number):
    rows, width = stream.shape
    total = 16 * rows
    layers = wide.shape[0]
    half = rows // layers
    shapes = [
        jax.ShapeDtypeStruct((16, rows, width), BF16),
        jax.ShapeDtypeStruct((total, 4 * HEAD), BF16),
        jax.ShapeDtypeStruct((total, 4 * HEAD), F32),
        jax.ShapeDtypeStruct((total, 2 * HEAD), F32),
        jax.ShapeDtypeStruct((total, 2 * HEAD), BF16),
        jax.ShapeDtypeStruct((2, total, 2 * HEAD), BF16),
        jax.ShapeDtypeStruct((total, 2 * HEAD), F32),
    ] * layers
    shapes += [jax.ShapeDtypeStruct((16, half, width), BF16)] * layers
    shapes += [
        jax.ShapeDtypeStruct((4,) + wide.shape[1:], BF16),
        jax.ShapeDtypeStruct((6 * HEAD, width), BF16),
    ] * layers
    shapes.append(jax.ShapeDtypeStruct((rows, width), F32))
    shapes += [jax.ShapeDtypeStruct((4, width), F32)] * layers
    shapes += [jax.ShapeDtypeStruct((1, width), F32)] * layers
    swap = [pltpu.VMEM((total, 2 * HEAD), BF16), pltpu.SemaphoreType.DMA((2, 16))]
    scratch = [pltpu.VMEM((rows, width), BF16)] * 2
    scratch += [pltpu.VMEM((total, 2 * HEAD), BF16)] * 4
    scratch += [pltpu.SemaphoreType.DMA((2, 20))] * 4
    scratch += gather_sems() + gather_sems()
    tall = pltpu.VMEM((2 * HEAD, width), BF16)
    scratch += ([pltpu.VMEM((4, 2 * HEAD, width), BF16)] + share_sems(3)) * 2
    scratch += [pltpu.VMEM((16, rows, width), BF16), pltpu.VMEM((rows, width), F32)]
    scratch += scatter_scratch(rows, width)
    scratch += [pltpu.VMEM((total, 2 * HEAD), F32)] * 3 + swap + swap
    packed = (layers, VECTOR_ROWS, LANES)
    scratch += [pltpu.VMEM(packed, BF16), pltpu.VMEM((4,) + packed, BF16)]
    scratch += [pltpu.VMEM((1, 8 * HEAD), F32)] * layers
    scratch += [tall] * layers + [pltpu.SemaphoreType.DMA((layers, 2))]
    given = [stream, cosines, sines, wide[0], wide[1], cotangent, down, out, *vectors]
    made = staged_call(
        forward_body, "forward", number, given, shapes, scratch, tables, direct=(14, 15), raw=(6, 7)
    )
    saved, weights = (made[:7], made[7:14]), ((made[16], made[18]), (made[17], made[19]))
    return saved, made[14:16], *weights, made[20], made[21:23], made[23:25]


def back_enter_phase(
    grid, wait, ins, outs, tall_sum, gather_refs=None, beside=(), between=None, last=None
):
    grad_ref, active_ref, context_ref, slope_ref, normed_ref, tall_ref, scale_ref = ins[:7]
    pull_ref, offset_ref, hidden_ref, early_ref, out_ref, up_ref, up_bias_ref = outs
    gathers = gather_refs is not None
    rows = normed_ref.shape[-2]
    if gathers:
        own, all_rows, send_sem, recv_sem = gather_refs
        gather = gather_steps(grid, own, all_rows, send_sem, recv_sem)
        run(gather, 2)
        for steps in beside:
            run(steps, 1)
    tall_sum[...] = jnp.zeros_like(tall_sum)
    up_ref[...] = jnp.zeros_like(up_ref)
    up_bias_ref[...] = jnp.zeros_like(up_bias_ref)

    def block(ranks):
        if gathers:
            branch = blocks_of(all_rows, ranks)
        else:
            branch = jnp.concatenate([half[rank] for rank in ranks for half in (grad_ref, ins[7])], 0)
        back = dots(branch, tall_ref[...], 1, 1)
        hidden_grad = (back[:, : 4 * HEAD] * rows_of(slope_ref, ranks, rows)).astype(BF16)
        pull = back[:, 4 * HEAD :].astype(BF16)
        put_rows(hidden_ref, ranks, rows, hidden_grad)
        put_rows(pull_ref, ranks, rows, pull)
        context = rows_of(context_ref, ranks, rows)
        offset = jnp.sum(pull.astype(F32) * context, 1, keepdims=True)
        put_rows(offset_ref, ranks, rows, jnp.broadcast_to(offset, context.shape))
        both = jnp.concatenate([rows_of(active_ref, ranks, rows), context.astype(BF16)], 1)
        ones = jnp.ones(context.shape, BF16)
        tall_sum[...] += dots(both, branch, 0, 0)
        up_ref[...] += dots(hidden_grad, blocks_of(normed_ref, ranks), 0, 0)
        up_bias_ref[...] += dots(hidden_grad, ones, 0, 0)

    if gathers:
        follow(grid, gather, block, lambda: wait(*range(1, 7)), last)
    else:
        wait(5)
        for piece in range(PIECES):
            wait.piece(piece, 0, 1, 2, 3, 4, 7)
            block([piece * 4 + i for i in range(4)])
            between()
    up_grad = (up_ref[...] * scale_ref[1:2] + up_bias_ref[:, 0:1] * scale_ref[3:4]).astype(BF16)
    for shard in range(4):
        early_ref[shard, : 4 * PART] = up_grad[:, shard * LANES : (shard + 1) * LANES]
        early_ref[shard, 8 * PART :] = jnp.zeros((PART, LANES), BF16)
        for lanes in range(4):
            early_ref[shard, (4 + lanes) * PART : (5 + lanes) * PART] = tall_sum[
                shard * HEAD : (shard + 1) * HEAD, lanes * LANES : (lanes + 1) * LANES
            ].astype(BF16)
            low = 5 * HEAD + shard * 16
            out_ref[shard, lanes * 16 : (lanes + 1) * 16] = tall_sum[
                low : low + 16, lanes * LANES : (lanes + 1) * LANES
            ].astype(BF16)


def back_enter_shapes(rows, width):
    total = 16 * rows
    return [
        jax.ShapeDtypeStruct((total, 4 * HEAD), BF16),
        jax.ShapeDtypeStruct((4 * HEAD, width), F32),
        jax.ShapeDtypeStruct((4 * HEAD, 2 * HEAD), F32),
    ], [
        pltpu.VMEM((total, 2 * HEAD), BF16),
        pltpu.VMEM((total, 2 * HEAD), F32),
        pltpu.VMEM((4, EARLY, LANES), BF16),
        pltpu.VMEM((4, PART, LANES), BF16),
        pltpu.VMEM((6 * HEAD, width), F32),
    ]


def back_leave_phase(grid, wait, ins, outs, refs, exchanges, other_vectors=None, after=None):
    query_grad_ref, pair_grad_ref, hidden_ref, normed_ref, wide_ref, scale_ref = ins[:6]
    cos_ref, sin_ref, stream_ref, grad_ref, up_ref, up_bias_ref = ins[6:]
    new_ref, addend_ref, *vector_ref = outs
    vector_ref = vector_ref[0] if vector_ref else None
    (mixed, raw, raw_bias, parts, total_rows), scratch = refs[:5], refs[5:]
    rows, width = stream_ref.shape
    wait(0, 1, 2, 4, 6, 7)

    def make(ranks):
        cosines, sines = rows_of(cos_ref, ranks, rows), -rows_of(sin_ref, ranks, rows)
        query = rows_of(query_grad_ref, ranks, rows) * 0.125
        lane = lax.broadcasted_iota(jnp.int32, query.shape, 1)
        query = jnp.where(lane < HEAD, query, 0.0)
        pair = rows_of(pair_grad_ref, ranks, rows)
        both = jnp.concatenate(
            [rotate(pair, cosines, sines), rotate(query, cosines, sines)], 1
        ).astype(BF16)
        put_rows(mixed, ranks, rows, both)
        first = dots(both, wide_ref[:, : 4 * HEAD], 1, 1)
        second = dots(rows_of(hidden_ref, ranks, rows), wide_ref[:, 4 * HEAD :], 1, 1)
        made = (first * scale_ref[0:1] + second * scale_ref[1:2]).astype(BF16)
        for index, rank in enumerate(ranks):
            parts[rank] = made[index * rows : (index + 1) * rows]

    scatter = scatter_steps(grid, make, parts, total_rows, *scratch)
    run(scatter, 3)
    wait()
    for steps in exchanges:
        run(steps, 1)
    run(scatter, 5)
    raw[...] = jnp.zeros_like(raw)
    raw_bias[...] = jnp.zeros_like(raw_bias)
    ones = jnp.ones((4 * rows, 2 * HEAD), BF16)

    def sums(index):
        span = pl.ds(index * 4 * rows, 4 * rows)
        both = mixed[span, :]
        normed_rows = normed_ref[pl.ds(index * 4, 4)].reshape(4 * rows, width)
        raw[...] += dots(both, normed_rows, 0, 0)
        raw_bias[...] += dots(both, ones, 0, 0)

    sums(0)
    run(scatter, 1)
    sums(1)
    run(scatter, 1)
    sums(2)
    run(scatter, 1)
    sums(3)

    wide_t = jnp.transpose(wide_ref[:, : 4 * HEAD].astype(F32))
    up_t = jnp.transpose(wide_ref[:, 4 * HEAD :].astype(F32))
    mixed_bias, up_bias = raw_bias[:, 0:1], up_bias_ref[:, 0:1]
    first_raw, second_raw = raw[...], up_ref[...]
    vectors = [
        jnp.sum(wide_t * first_raw, 0, keepdims=True),
        jnp.sum(up_t * second_raw, 0, keepdims=True),
        jnp.sum(wide_t * mixed_bias, 0, keepdims=True),
        jnp.sum(up_t * up_bias, 0, keepdims=True),
        jnp.sum(grad_ref[...].astype(BF16).astype(F32), 0, keepdims=True),
    ]
    first_grad = (first_raw * scale_ref[0:1] + mixed_bias * scale_ref[2:3]).astype(BF16)
    biases = [
        jnp.transpose(raw_bias[...])[0:1],
        jnp.transpose(up_bias_ref[...])[0:1],
    ]
    for shard in range(4):
        lanes = slice(shard * LANES, (shard + 1) * LANES)
        addend_ref[shard, : 3 * PART] = first_grad[: 3 * PART, lanes]
        tail = [vector[:, lanes] for vector in vectors] + biases
        tail.append(jnp.zeros((VECTOR_ROWS - len(tail), LANES), F32))
        tail = jnp.concatenate(tail, 0).astype(BF16)
        if other_vectors is None:
            vector_ref[shard] = tail
        else:
            addend_ref[shard, LATE : LATE + 16] = tail
            addend_ref[shard, LATE + 16 : LATE + 32] = other_vectors[shard]
            addend_ref[shard, LATE + 32 :] = jnp.zeros((PART - 32, LANES), BF16)
    run(scatter)
    for steps in exchanges:
        run(steps)
    if after is not None:
        after()
    normed, inverse = standardize(stream_ref[...].astype(F32))
    normed_grad = total_rows[...]
    new_ref[...] = grad_ref[...].astype(F32) + inverse * (
        normed_grad
        - jnp.mean(normed_grad, -1, keepdims=True)
        - normed * jnp.mean(normed_grad * normed, -1, keepdims=True)
    )


def back_leave_scratch(rows, width):
    total = 16 * rows
    return [
        pltpu.VMEM((total, 4 * HEAD), BF16),
        pltpu.VMEM((4 * HEAD, width), F32),
        pltpu.VMEM((4 * HEAD, 2 * HEAD), F32),
        pltpu.VMEM((16, rows, width), BF16),
        pltpu.VMEM((rows, width), F32),
    ] + scatter_scratch(rows, width)


def back_leave_body(wait, tables, ins, outs, refs):
    grid = Grid()
    grid.barrier([mate()])
    exchanges = [low_steps(ins[12], outs[3], *refs[11:], ins[13])]
    back_leave_phase(grid, wait, ins[:12], outs[:3], refs[:11], exchanges)


def back_leave(given, rows, width, number, sums, total):
    shapes = [
        jax.ShapeDtypeStruct((rows, width), F32),
        jax.ShapeDtypeStruct((4, LATE, LANES), BF16),
        jax.ShapeDtypeStruct((4, VECTOR_ROWS, LANES), BF16),
        jax.ShapeDtypeStruct((EARLY, LANES), BF16),
    ]
    scratch = back_leave_scratch(rows, width) + swap_scratch(EARLY)
    given = tuple(given) + (sums, total)
    return staged_call(back_leave_body, "back_leave", number, given, shapes, scratch)


def sibling():
    shard = lax.axis_index("fsdp")
    return {"fsdp": shard + 1 - 2 * (shard % 2)}


def mate():
    return {"fsdp": (lax.axis_index("fsdp") + 2) % 4}


def far_partner():
    slot = lax.axis_index("ctx")
    return {"ctx": slot + 1 - 2 * (slot % 2)}


def wide_barrier(grid):
    shard = lax.axis_index("fsdp")
    at_home = grid.x == shard
    gate = pltpu.get_barrier_semaphore()
    partners = [grid.device(0, *step) for step in grid.meets]
    partners += [sibling(), mate(), far_partner()]
    for partner in partners:
        pl.semaphore_signal(gate, inc=1, device_id=partner, device_id_type=MESH)
    for other in range(4):

        @pl.when(jnp.logical_not(at_home & (shard == other)))
        def greet():
            pl.semaphore_signal(
                gate,
                inc=1,
                device_id={"ctx": (shard * SIDE + grid.y) * 2 + grid.z, "fsdp": other},
                device_id_type=MESH,
            )

    pl.semaphore_wait(gate, len(partners) + 4 - at_home.astype(jnp.int32))


def remote(source, target, send, recv, to):
    return pltpu.make_async_remote_copy(
        src_ref=source,
        dst_ref=target,
        send_sem=send,
        recv_sem=recv,
        device_id=to,
        device_id_type=MESH,
    )


def added(a, b):
    return (a.astype(F32) + b.astype(F32)).astype(BF16)


def core_steps(in_ref, sums_ref, land, sems):
    shard = lax.axis_index("fsdp")
    low, core = shard // 2, shard % 2
    copies = [
        remote(
            in_ref.at[part * 2 + 1 - core],
            land.at[part],
            sems.at[0, part],
            sems.at[1, part],
            sibling(),
        )
        for part in (0, 1)
    ]
    for copy in copies:
        copy.start()
    yield
    for copy in copies:
        copy.wait_recv()
    sums_ref[0] = added(in_ref[low * 2 + core], land[low])
    sums_ref[1] = added(in_ref[(1 - low) * 2 + core], land[1 - low])
    for copy in copies:
        copy.wait_send()


def core_scratch(rows):
    return [pltpu.VMEM((2, rows, LANES), BF16), pltpu.SemaphoreType.DMA((2, 2))]


def low_steps(sums_ref, pair_ref, land, sems, total_ref=None):
    copy = remote(sums_ref.at[1], land, sems.at[0], sems.at[1], mate())
    copy.start()
    yield
    copy.wait_recv()
    pair_ref[...] = added(sums_ref[0], land[...])
    if total_ref is not None:
        pair_ref[pair_ref.shape[0] - PART :] = total_ref[...]
    copy.wait_send()


def high_steps(pair_ref, own_ref, land, sems):
    copy = remote(pair_ref, land, sems.at[0], sems.at[1], far_partner())
    copy.start()
    yield
    copy.wait_recv()
    own_ref[...] = added(pair_ref[...], land[...])
    copy.wait_send()


def swap_scratch(rows):
    return [pltpu.VMEM((rows, LANES), BF16), pltpu.SemaphoreType.DMA((2,))]


def quarter_steps(grid, quarter_ref, total_ref, land, send_sem, recv_sem):
    x, y, z = grid.x, grid.y, grid.z
    shard = lax.axis_index("fsdp")
    at_home = x == shard

    def copy(column):
        return remote(
            quarter_ref.at[column],
            land.at[shard],
            send_sem.at[column],
            recv_sem.at[shard],
            {"ctx": (column * SIDE + y) * 2 + z, "fsdp": x},
        )

    for column in range(4):

        @pl.when(jnp.logical_not(at_home & (x == column)))
        def give():
            copy(column).start()

        @pl.when(at_home & (x == column))
        def keep():
            land[shard] = quarter_ref[column]

    yield
    for other in range(4):

        @pl.when(jnp.logical_not(at_home & (shard == other)))
        def take():
            remote(
                land.at[other], land.at[other], send_sem.at[other], recv_sem.at[other], mate()
            ).wait_recv()

    total = land[0].astype(F32)
    for other in range(1, 4):
        total = total + land[other].astype(F32)
    total_ref[...] = total.astype(BF16)
    for column in range(4):

        @pl.when(jnp.logical_not(at_home & (x == column)))
        def gone():
            copy(column).wait_send()


def quarter_scratch():
    return [
        pltpu.VMEM((4, PART, LANES), BF16),
        pltpu.SemaphoreType.DMA((4,)),
        pltpu.SemaphoreType.DMA((4,)),
    ]


def gather_sems():
    return [
        pltpu.SemaphoreType.DMA,
        pltpu.SemaphoreType.DMA((2, 20)),
        pltpu.SemaphoreType.DMA((2, 20)),
    ]


def keep_own(grid, own, every, sem):
    copy = pltpu.make_async_copy(own, every.at[grid.rank(0, 0, 0)], sem)
    copy.start()
    return copy


def last_body(wait, tables, ins, outs, refs):
    new_ref, all_early, all_other, all_late = outs
    leave_refs, refs = refs[:11], refs[11:]
    (late_addends, early, other, sums, pair, late), refs = refs[:6], refs[6:]
    early_swap, other_swap, refs = refs[:2], refs[2:4], refs[4:]
    core_refs, low_refs, high_refs, refs = refs[:2], refs[2:4], refs[4:6], refs[6:]
    early_sems, other_sems, late_sems = refs[:3], refs[3:6], refs[6:9]
    grid = Grid()
    grid.barrier([sibling(), mate(), far_partner()])
    exchanges = [high_steps(ins[12], early, *early_swap), high_steps(ins[13], other, *other_swap)]
    first = gather_steps(grid, early, all_early, *early_sems[1:])
    second = gather_steps(grid, other, all_other, *other_sems[1:])
    keeps = []

    def start():
        for steps in exchanges:
            run(steps)
        run(first, 2)
        run(second, 2)
        keeps.append(keep_own(grid, early, all_early, early_sems[0]))
        keeps.append(keep_own(grid, other, all_other, other_sems[0]))

    back_leave_phase(
        grid, wait, ins[:12], (new_ref, late_addends), leave_refs, exchanges, ins[14], start
    )
    wait.flush()
    core = core_steps(late_addends, sums, *core_refs)
    run(core, 1)
    run(first, 2)
    run(second, 2)
    run(core)
    low = low_steps(sums, pair, *low_refs)
    run(low, 1)
    run(first, 2)
    run(second, 2)
    run(first, 2)
    run(low)
    high = high_steps(pair, late, *high_refs)
    run(high, 1)
    run(second, 2)
    run(first, 4)
    run(high)
    keeps.append(keep_own(grid, late, all_late, late_sems[0]))
    third = gather_steps(grid, late, all_late, *late_sems[1:])
    run(third, 2)
    for unused in range(GATHER_STEPS):
        run(first, 1)
        run(second, 1)
        run(third, 1)
    run(third)
    for keep in keeps:
        keep.wait()


def back_leave_last(given, rows, width, number, early, other, vectors):
    count = LATE + PART
    shapes = [
        jax.ShapeDtypeStruct((rows, width), F32),
        jax.ShapeDtypeStruct((16,) + early.shape, BF16),
        jax.ShapeDtypeStruct((16,) + other.shape, BF16),
        jax.ShapeDtypeStruct((16, count, LANES), BF16),
    ]
    scratch = back_leave_scratch(rows, width)
    scratch += [
        pltpu.VMEM((4, count, LANES), BF16),
        pltpu.VMEM(early.shape, BF16),
        pltpu.VMEM(other.shape, BF16),
        pltpu.VMEM((2, count, LANES), BF16),
        pltpu.VMEM((count, LANES), BF16),
        pltpu.VMEM((count, LANES), BF16),
    ]
    scratch += swap_scratch(early.shape[0]) + swap_scratch(other.shape[0])
    scratch += core_scratch(count) + swap_scratch(count) + swap_scratch(count)
    scratch += gather_sems() + gather_sems() + gather_sems()
    given = tuple(given) + (early, other, vectors)
    return staged_call(
        last_body, "back_leave_last", number, given, shapes, scratch, direct=(1, 2, 3)
    )


def format_kernel(layers, *refs):
    early, late, passing = refs[:layers], refs[layers : 2 * layers], refs[2 * layers : 2 * layers + 2]
    refs = refs[2 * layers + 2 :]
    (qkv_out, out_out, up_out, down_out), passed, refs = refs[:4], refs[4:6], refs[6:]
    early_in, late_in, qkv, out, up, down, *held, load_sem, store_sem, pass_sem = refs
    loads, stores = {}, []

    def store(source, target, layer, event):
        copy = pltpu.make_async_copy(source, target, store_sem.at[layer, event])
        copy.start()
        stores.append(copy)

    passes = []
    for index in range(2):
        copy = pltpu.make_async_copy(passing[index], held[index], pass_sem.at[0, index])
        copy.start()
        passes.append(copy)
    for layer in range(layers):
        for part in range(9 + 3):
            source, target, first = (
                (early[layer], early_in, part) if part < 9 else (late[layer], late_in, part - 9)
            )
            span = pl.ds(first * PART, PART)
            loads[layer, part] = pltpu.make_async_copy(
                source.at[:, span], target.at[layer, :, span], load_sem.at[layer, part]
            )
            loads[layer, part].start()
    row = lax.broadcasted_iota(jnp.int32, (LANES, LANES), 0)
    column = lax.broadcasted_iota(jnp.int32, (LANES, LANES), 1)
    unit = (row == column).astype(BF16)
    wide = 16 * PART

    def rows(ref, layer, part):
        return ref[layer, :, part * PART : (part + 1) * PART].reshape(wide, LANES)

    for index in range(2):
        passes[index].wait()
        copy = pltpu.make_async_copy(held[index], passed[index], pass_sem.at[1, index])
        copy.start()
        stores.append(copy)
    for layer in range(layers):
        for part in range(4):
            loads[layer, part].wait()
            up[layer, part] = dots(unit, rows(early_in, layer, part), 1, 1)
            target = up_out.at[layer, :, pl.ds(part * wide, wide)]
            store(up.at[layer, part], target, layer, part)
        for part in range(4):
            loads[layer, 4 + part].wait()
            lanes = slice(part * LANES, (part + 1) * LANES)
            down[layer, :, lanes] = rows(early_in, layer, 4 + part).astype(F32)
        store(down.at[layer], down_out.at[layer], layer, 4)
        loads[layer, 8].wait()
        for part in range(4):
            lanes = slice(part * LANES, (part + 1) * LANES)
            low = 8 * PART + part * 16
            for x in range(4):
                for y in range(4):
                    first = y * HEAD + x * 16
                    out[layer, first : first + 16, lanes] = early_in[
                        layer, x * 4 + y, low : low + 16
                    ].astype(F32)
        store(out.at[layer], out_out.at[layer], layer, 5)
        for part, place_of in enumerate((1, 2, 0)):
            loads[layer, 9 + part].wait()
            qkv[layer, part] = dots(unit, rows(late_in, layer, part), 1, 1)
            target = qkv_out.at[layer, :, pl.ds(place_of * wide, wide)]
            store(qkv.at[layer, part], target, layer, 6 + part)
    for copy in stores:
        copy.wait()


def format_grads(early, late, passing):
    layers = len(early)
    width = 4 * LANES
    hbm = pl.BlockSpec(memory_space=pl.ANY)
    shapes = [
        jax.ShapeDtypeStruct((layers, LANES, 3 * width), F32),
        jax.ShapeDtypeStruct((layers, LANES, width), F32),
        jax.ShapeDtypeStruct((layers, LANES, 4 * width), F32),
        jax.ShapeDtypeStruct((layers, width, width), F32),
    ]
    shapes += [jax.ShapeDtypeStruct(array.shape, array.dtype) for array in passing]
    return pl.pallas_call(
        functools.partial(format_kernel, layers),
        out_shape=shapes,
        in_specs=[hbm] * (2 * layers + 2),
        out_specs=[hbm] * 6,
        scratch_shapes=[
            pltpu.VMEM((layers, 16, EARLY, LANES), BF16),
            pltpu.VMEM((layers, 16, LATE, LANES), BF16),
            pltpu.VMEM((layers, 3, LANES, width), F32),
            pltpu.VMEM((layers, LANES, width), F32),
            pltpu.VMEM((layers, 4, LANES, width), F32),
            pltpu.VMEM((layers, width, width), F32),
        ]
        + [pltpu.VMEM(array.shape, array.dtype) for array in passing]
        + [
            pltpu.SemaphoreType.DMA((layers, 12)),
            pltpu.SemaphoreType.DMA((layers, 9)),
            pltpu.SemaphoreType.DMA((2, 2)),
        ],
        name="format_grads",
        compiler_params=pltpu.CompilerParams(vmem_limit_bytes=60 << 20),
    )(*early, *late, *passing)


SPAN = 1024
ATTEND_WORK = 88


def sort_in(source_ref, order_ref, target_ref, count):
    def body(i, unused):
        start = order_ref[i] * BLK
        target_ref[pl.ds(pl.multiple_of(i * BLK, BLK), BLK), :] = source_ref[
            pl.ds(start, BLK), :
        ]
        return unused

    lax.fori_loop(0, count, body, 0, unroll=8)


def block_numbers(number_ref, first, count, axis):
    if axis == 0:
        return jnp.concatenate(
            [jnp.full((BLK, 1), number_ref[first + i], jnp.int32) for i in range(count)], 0
        )
    lane = lax.broadcasted_iota(jnp.int32, (1, count * BLK), 1) // BLK
    numbers = jnp.zeros((1, count * BLK), jnp.int32)
    for i in range(count):
        numbers = jnp.where(lane == i, number_ref[first + i], numbers)
    return numbers


def far_copy(source, target, sems):
    return pltpu.make_async_remote_copy(
        src_ref=source,
        dst_ref=target,
        send_sem=sems.at[0],
        recv_sem=sems.at[1],
        device_id=far_partner(),
        device_id_type=MESH,
    )


def attend_steps(tables, q_ref, kv_ref, context_ref, qs, kvs, logs, scratch, swaps):
    order_ref, standing_ref, number_ref, other_order, other_ref = tables
    tops, totals, sums, far_ref = scratch
    sort_in(kv_ref, order_ref, kvs.at[0], 32)
    sort_in(q_ref, order_ref, qs, 32)
    tiles = qs.shape[0] // TILE
    row = lax.broadcasted_iota(jnp.int32, (TILE, TILE), 0)
    column = lax.broadcasted_iota(jnp.int32, (TILE, TILE), 1)
    yield 4

    def highest(scores):
        return jnp.max(scores, 1, keepdims=True)

    def weigh(scores, top, keys):
        weights = jnp.exp(scores - top)
        return jnp.sum(weights, 1, keepdims=True), dots(weights.astype(BF16), keys, 1, 0)

    def wide(vector):
        return jnp.broadcast_to(vector, (TILE, 2 * HEAD))

    def own_tile(tile):
        rows = slice(tile * TILE, (tile + 1) * TILE)
        queries, near = qs[rows, :], kvs[0, rows, :]
        parts = [(jnp.where(column <= row, dots(queries, near, 1, 1), NEGATIVE), near)]
        for low in range(0, tile * TILE, SPAN):
            keys = kvs[0, low : min(low + SPAN, tile * TILE), :]
            parts.append((dots(queries, keys, 1, 1), keys))
        top = highest(parts[0][0])
        for scores, keys in parts[1:]:
            top = jnp.maximum(top, highest(scores))
        total, weighted = 0.0, 0.0
        for scores, keys in parts:
            more, product = weigh(scores, top, keys)
            total, weighted = total + more, weighted + product
        tops[rows, :], totals[rows, :], sums[rows, :] = wide(top), wide(total), weighted

    def other_tile(tile, numbers):
        rows = slice(tile * TILE, (tile + 1) * TILE)
        queries = qs[rows, :]
        own = block_numbers(number_ref, tile * TILE // BLK, TILE // BLK, 0)
        half = tile // 4
        keys = kvs[1, half * SPAN : (half + 1) * SPAN, :]
        parts = [(jnp.where(numbers < own, dots(queries, keys, 1, 1), NEGATIVE), keys)]
        if half:
            keys = kvs[1, :SPAN, :]
            parts.append((dots(queries, keys, 1, 1), keys))
        old = tops[rows, :][:, 0:1]
        top = old
        for scores, keys in parts:
            top = jnp.maximum(top, highest(scores))
        scale = jnp.exp(old - top)
        total, weighted = totals[rows, :][:, 0:1] * scale, sums[rows, :] * scale
        for scores, keys in parts:
            more, product = weigh(scores, top, keys)
            total, weighted = total + more, weighted + product
        sums[rows, :] = weighted / total
        logs[rows, :] = wide(top + jnp.log(total))

    for tile in range(tiles):
        own_tile(tile)
        yield tile + 1
    for copy in swaps:
        copy.wait_recv()
    yield 0
    sort_in(far_ref, other_order, kvs.at[1], 32)
    yield 0
    for half in (0, 1):
        numbers = block_numbers(other_ref, half * 16, 16, 1)
        for tile in range(half * 4, half * 4 + 4):
            other_tile(tile, numbers)
            yield 4 + 4 * half
    sort_in(sums, standing_ref, context_ref, 32)
    for copy in swaps:
        copy.wait_send()


def attend_back_steps(
    tables, qs, kvs, logs, pull_ref, offset_ref, query_grad_ref, pair_grad_ref, scratch
):
    order_ref, standing_ref, number_ref, unused, other_ref = tables
    pulls, offsets, turned, query_sums, pair_sums, away, land, sems = scratch
    sort_in(pull_ref, order_ref, pulls, 32)
    yield 1
    sort_in(offset_ref, order_ref, offsets, 32)
    yield 1
    pair_sums[...] = jnp.zeros_like(pair_sums)
    tiles = qs.shape[0] // TILE
    row = lax.broadcasted_iota(jnp.int32, (TILE, TILE), 0)
    column = lax.broadcasted_iota(jnp.int32, (TILE, TILE), 1)
    lane = lax.broadcasted_iota(jnp.int32, (TILE, 2 * HEAD), 1)
    yield 2

    def tile_part(tile, half, low, count, mask):
        rows = slice(tile * TILE, (tile + 1) * TILE)
        queries, pull = qs[rows, :], pulls[rows, :]
        keys = kvs[half, low : low + count, :]
        scores = dots(keys, queries, 1, 1)
        if mask is not None:
            scores = jnp.where(mask, scores, NEGATIVE)
        probs = jnp.exp(scores - turned[tile, 0:1])
        score_grad = (probs * (dots(keys, pull, 1, 1) - turned[tile, 1:2])).astype(BF16)
        pair_sums[half, low : low + count, :] += dots(score_grad, queries, 1, 0) + dots(
            probs.astype(BF16), pull, 1, 0
        )
        return dots(score_grad, keys, 0, 0)

    def masked_tile(tile, numbers):
        rows = slice(tile * TILE, (tile + 1) * TILE)
        turned[tile] = jnp.transpose(
            jnp.where(lane == 0, logs[rows, :], offsets[rows, :])
        )[:8]
        own = block_numbers(number_ref, tile * TILE // BLK, TILE // BLK, 1)
        query_sums[rows, :] = tile_part(tile, 1, tile // 4 * SPAN, SPAN, numbers < own)

    def send(half):
        span = pl.ds(half * SPAN, SPAN)
        away[span] = pair_sums[1, span].astype(BF16)
        copy = far_copy(away.at[span], land.at[span], sems.at[half])
        copy.start()
        return copy

    def own_tile(tile):
        rows = slice(tile * TILE, (tile + 1) * TILE)
        query_sums[rows, :] += tile_part(tile, 0, tile * TILE, TILE, row <= column)
        yield 1
        for low in range(0, tile * TILE, SPAN):
            count = min(SPAN, tile * TILE - low)
            query_sums[rows, :] += tile_part(tile, 0, low, count, None)
            yield count // TILE

    copies = []
    for half in (1, 0):
        numbers = block_numbers(other_ref, half * 16, 16, 0)
        for tile in range(half * 4, half * 4 + 4):
            masked_tile(tile, numbers)
            yield 4
        if half == 0:
            for tile in range(4, 8):
                rows = slice(tile * TILE, (tile + 1) * TILE)
                query_sums[rows, :] += tile_part(tile, 1, 0, SPAN, None)
                yield 4
        copies.append(send(half))
    for tile in range(tiles):
        yield from own_tile(tile)
    sort_in(query_sums, standing_ref, query_grad_ref, 32)
    for copy in copies:
        copy.wait_recv()
    pair_sums[0] += land[...].astype(F32)
    sort_in(pair_sums.at[0], standing_ref, pair_grad_ref, 32)
    for copy in copies:
        copy.wait_send()


def attend_back_scratch(rows):
    block = (rows, 2 * HEAD)
    return [
        pltpu.VMEM(block, BF16),
        pltpu.VMEM(block, F32),
        pltpu.VMEM((rows // TILE, 8, TILE), F32),
        pltpu.VMEM(block, F32),
        pltpu.VMEM((2,) + block, F32),
        pltpu.VMEM(block, BF16),
        pltpu.VMEM(block, BF16),
        pltpu.SemaphoreType.DMA((2, 2)),
    ]


def take_turns(work, total, others):
    done = 0
    ran = [first for steps, count, first, early, part in others]
    for steps, count, first, early, part in others:
        run(steps, first)
    for more in work:
        done += more
        for index, (steps, count, first, early, part) in enumerate(others):
            wanted = early + min(int(done * (count - early) / (total * part)), count - early)
            run(steps, wanted - ran[index])
            ran[index] = wanted
    for steps, *unused in others:
        run(steps)


def back_last_body(wait, tables, ins, outs, refs):
    hidden_ref, up_ref, up_bias_ref, query_grad_ref, pair_grad_ref, sums_ref, total_ref, out_ref = outs
    (pull, offset, early, quarter, tall_sum), refs = refs[:5], refs[5:]
    (parts, total_rows), scatter_refs, refs = refs[:2], refs[2:8], refs[8:]
    core_refs, quarter_refs, scratch = refs[:2], refs[2:5], refs[5:]
    grid = Grid()
    wide_barrier(grid)
    made = [pull, offset, hidden_ref, early, quarter, up_ref, up_bias_ref]
    leaving = [ins[1], ins[2], ins[5], ins[11], ins[12]]
    scatter = leave_steps(grid, *leaving, out_ref, parts, total_rows, scatter_refs)
    wait(1, 2, 5, 11)
    run(scatter, 1)
    back_enter_phase(grid, wait, ins[:8], made, tall_sum, between=lambda: run(scatter, 1))
    wait.flush(0, 1, 2)
    wait()
    core = core_steps(early, sums_ref, *core_refs)
    quarters = quarter_steps(grid, quarter, total_ref, *quarter_refs)
    work = attend_back_steps(
        tables, *ins[8:11], pull, offset, query_grad_ref, pair_grad_ref, scratch
    )
    others = [
        (core, 1, 1, 1, 1.0),
        (quarters, 1, 1, 1, 1.0),
        (scatter, SCATTER_STEPS - 1 - PIECES, 0, 0, 0.9),
    ]
    take_turns(work, ATTEND_WORK, others)


def back_last(tables, branch, given, attention, stream, bias, number):
    rows, width = stream.shape
    shapes, scratch = back_enter_shapes(rows, width)
    total = 16 * rows
    shapes = shapes + [jax.ShapeDtypeStruct((total, 2 * HEAD), F32)] * 2
    shapes += [
        jax.ShapeDtypeStruct((2, EARLY, LANES), BF16),
        jax.ShapeDtypeStruct((PART, LANES), BF16),
        jax.ShapeDtypeStruct((rows, width), BF16),
    ]
    scratch = scratch + [
        pltpu.VMEM((16, rows, width), BF16),
        pltpu.VMEM((rows, width), F32),
    ]
    scratch += scatter_scratch(rows, width) + core_scratch(EARLY) + quarter_scratch()
    scratch += attend_back_scratch(total)
    given = [branch[0], *given, branch[1], *attention, stream, bias]
    return staged_call(
        back_last_body, "back_last", number, given, shapes, scratch, tables,
        parted=(0, 1, 2, 3, 4, 7),
    )


def back_first_body(wait, tables, ins, outs, refs):
    (
        hidden_ref, up_ref, up_bias_ref, query_grad_ref, pair_grad_ref, pair_ref, late_pair, all_ref
    ) = outs
    (pull, offset, early, quarter, tall_sum), refs = refs[:5], refs[5:]
    (own, all_rows, *row_sems), refs = refs[:4], refs[4:]
    (folded, late_sums, sums, total), refs = refs[:4], refs[4:]
    high_refs, late_core_refs, refs = refs[:2], refs[2:4], refs[4:]
    gather_refs, core_refs, quarter_refs, refs = refs[:3], refs[3:5], refs[5:8], refs[8:]
    early_refs, late_refs, scratch = refs[:2], refs[2:4], refs[4:]
    grid = Grid()
    wait(0)
    own[...] = ins[0][...].astype(BF16)
    all_rows[grid.rank(0, 0, 0)] = own[...]
    wide_barrier(grid)
    wait(7, 8)
    beside = [
        high_steps(ins[7], folded, *high_refs),
        core_steps(ins[8], late_sums, *late_core_refs),
    ]
    made = [pull, offset, hidden_ref, early, quarter, up_ref, up_bias_ref]
    keeps = []
    gather = gather_steps(grid, folded, all_ref, *gather_refs[1:])

    def start():
        run(beside[0])
        keeps.append(keep_own(grid, folded, all_ref, gather_refs[0]))
        run(gather, 2)

    row_refs = (own, all_rows, *row_sems)
    back_enter_phase(grid, wait, ins[:7], made, tall_sum, row_refs, beside, last=start)
    wait.flush(0, 1, 2)
    run(beside[1])
    run(gather, 2)
    wait()
    quarters = quarter_steps(grid, quarter, total, *quarter_refs)
    late = low_steps(late_sums, late_pair, *late_refs)

    def early_steps():
        core = core_steps(early, sums, *core_refs)
        next(core)
        yield
        run(core)
        run(quarters)
        yield from low_steps(sums, pair_ref, *early_refs, total)

    work = attend_back_steps(
        tables, *ins[9:12], pull, offset, query_grad_ref, pair_grad_ref, scratch
    )
    others = [
        (gather, GATHER_STEPS - 4, 0, 3, 0.9),
        (quarters, 1, 1, 1, 1.0),
        (early_steps(), 2, 1, 1, 0.5),
        (late, 1, 1, 1, 1.0),
    ]
    take_turns(work, ATTEND_WORK, others)
    for keep in keeps:
        keep.wait()


def back_first(tables, grad, given, exchanged, attention, number):
    rows, width = grad.shape
    shapes, scratch = back_enter_shapes(rows, width)
    total = 16 * rows
    shapes = shapes + [jax.ShapeDtypeStruct((total, 2 * HEAD), F32)] * 2
    shapes += [
        jax.ShapeDtypeStruct((EARLY, LANES), BF16),
        jax.ShapeDtypeStruct((LATE, LANES), BF16),
        jax.ShapeDtypeStruct((16, EARLY, LANES), BF16),
    ]
    scratch = scratch + [
        pltpu.VMEM((rows, width), BF16),
        pltpu.VMEM((16, rows, width), BF16),
        pltpu.SemaphoreType.DMA((2, 20)),
        pltpu.SemaphoreType.DMA((2, 20)),
        pltpu.VMEM((EARLY, LANES), BF16),
        pltpu.VMEM((2, LATE, LANES), BF16),
        pltpu.VMEM((2, EARLY, LANES), BF16),
        pltpu.VMEM((PART, LANES), BF16),
    ]
    scratch += swap_scratch(EARLY) + core_scratch(LATE) + gather_sems()
    scratch += core_scratch(EARLY) + quarter_scratch()
    scratch += swap_scratch(EARLY) + swap_scratch(LATE) + attend_back_scratch(total)
    given = [grad, *given, *exchanged, *attention]
    return staged_call(
        back_first_body, "back_first", number, given, shapes, scratch, tables, direct=(7,)
    )


def block_tables(pair_table, z):
    slots = pair_table.shape[0]
    ranks = slots // 2
    index = jnp.arange(slots, dtype=jnp.int32)

    def plane(which):
        pairs = lax.dynamic_slice_in_dim(pair_table.reshape(ranks, 2), which, 1, 1)
        numbers = jnp.concatenate([pairs, 2 * slots - 1 - pairs], 1).reshape(-1)
        standing = jnp.sum((numbers[None, :] < numbers[:, None]).astype(jnp.int32), 1)
        chosen = (standing[None, :] == index[:, None]).astype(jnp.int32)
        order = jnp.sum(chosen * index[None, :], 1)
        return numbers, (order, standing, jnp.sum(chosen * numbers[None, :], 1))

    numbers, own = plane(z)
    other = plane(1 - z)[1]
    return numbers, own + (other[0], other[2])


def rotation(positions):
    freqs = 10000.0 ** (-jnp.arange(0, ROT, 2, dtype=F32) / ROT)
    angles = positions.astype(F32)[:, None] * freqs[None, :]
    rest = ((0, 0), (0, 2 * HEAD - ROT))
    return (
        jnp.pad(jnp.concatenate([jnp.cos(angles)] * 2, -1), rest, constant_values=1.0),
        jnp.pad(jnp.concatenate([jnp.sin(angles)] * 2, -1), rest),
    )


def on_device(
    hidden_in,
    cotangent,
    pair_table,
    norm_gain,
    norm_bias,
    qkv_weight,
    qkv_bias,
    out_weight,
    out_bias,
    up_weight,
    up_bias,
    down_weight,
    down_bias,
):
    layers = norm_gain.shape[0]
    slot = lax.axis_index("ctx")
    shard = lax.axis_index("fsdp")
    rank, z = slot // 2, slot % 2
    width = hidden_in.shape[2]
    quarter = width // 4

    numbers, tables = block_tables(pair_table, z)
    positions = (
        numbers[:, None] * BLK + jnp.arange(BLK, dtype=jnp.int32)[None, :]
    ).reshape(-1)
    cosines, sines = rotation(positions)

    def columns(weight, part):
        return lax.dynamic_slice_in_dim(weight, part * width + rank * HEAD, HEAD, 2)

    wide = jnp.concatenate(
        [columns(qkv_weight, 1), columns(qkv_weight, 2), columns(qkv_weight, 0)]
        + [jnp.zeros((layers, quarter, HEAD), BF16)]
        + [columns(up_weight, part) for part in range(4)],
        2,
    )
    vectors = (norm_gain, norm_bias, qkv_bias, out_bias, up_bias, down_bias)
    stream = hidden_in[0]
    saved, branch_all, wide_all, tall_all, second, scales, last_biases = forward(
        tables, stream, vectors, cosines, sines, wide, down_weight, out_weight, cotangent[0], 1
    )
    streams, number = (stream, second), 2

    grad = cotangent[0]
    early, late = [None] * layers, [None] * layers
    exchanged = None
    for layer in reversed(range(layers)):
        last = layer == layers - 1
        normed_all, active, slope, context, queries, pairs, logs = saved[layer]
        stream = streams[layer]
        given = (active, context, slope, normed_all, tall_all[layer], scales[layer])
        attention = (queries, pairs, logs)
        if last:
            (
                hidden_grad, up_raw, up_bias_raw, query_grad, pair_grad, early_sums, out_total, output
            ) = back_last(tables, branch_all, given, attention, stream, last_biases[layer], number)
            exchanges = (early_sums, out_total)
        else:
            (
                hidden_grad, up_raw, up_bias_raw, query_grad, pair_grad, early_pair, late_pair,
                early[layer + 1],
            ) = back_first(tables, grad, given, exchanged, attention, number)
            exchanges = (early_pair, late_pair)
        number += 1
        given = (
            query_grad,
            pair_grad,
            hidden_grad,
            normed_all,
            wide_all[layer].reshape(width, 8 * HEAD),
            scales[layer],
            cosines,
            sines,
            stream,
            grad,
            up_raw,
            up_bias_raw,
        )
        if last:
            grad, addends, vector_rows, early_pair = back_leave(
                given, *stream.shape, number, *exchanges
            )
            exchanged = (early_pair, addends)
        else:
            grad, early[0], late[1], late[0] = back_leave_last(
                given, *stream.shape, number, *exchanges, vector_rows
            )
        number += 1

    qkv_out, out_out, up_out, down_out, output, grad = format_grads(early, late, (output, grad))
    small = jnp.stack(
        [late[0][:, LATE + 16 * layer : LATE + 16 * layer + 7] for layer in range(layers)]
    ).astype(F32)
    sums = jnp.sum(small[:, :, :5], 1)
    gain_out, shift_out, branch_out = sums[:, 0:2], sums[:, 2:4], sums[:, 4]
    qkv_bias_out = jnp.transpose(
        jnp.roll(small[:, :, 5, : 3 * HEAD].reshape(layers, 16, 3, HEAD), 1, 2), (0, 2, 1, 3)
    ).reshape(layers, -1)
    share = qkv_bias_out.shape[1] // 4
    qkv_bias_out = lax.dynamic_slice_in_dim(qkv_bias_out, shard * share, share, 1)
    up_bias_out = lax.dynamic_slice_in_dim(
        small[:, :, 6].reshape(layers, 16, 4, HEAD), shard, 1, 2
    ).reshape(layers, -1)
    return (
        output[None],
        grad[None],
        gain_out,
        shift_out,
        qkv_out,
        qkv_bias_out,
        out_out,
        branch_out,
        up_out,
        up_bias_out,
        down_out,
        branch_out,
    )


def solution(mesh):
    rows = P("fsdp", "ctx", None)
    vector, matrix = P(None, "fsdp"), P(None, "fsdp", None)
    gains = P(None, None, "fsdp")
    params = (gains, gains) + (matrix, vector) * 4
    return jax.shard_map(
        on_device,
        mesh=mesh,
        in_specs=(rows, rows, P()) + params,
        out_specs=(rows, rows) + params,
        check_vma=False,
    )
```

```python
import functools

import jax
import jax.numpy as jnp
from jax import lax
from jax.experimental import pallas as pl
from jax.experimental.pallas import tpu as pltpu
from jax.sharding import PartitionSpec as P

HEADS = 16
HEAD = 64
ROT = 16
BLK = 64
SIDE = 4
EPS = 1e-05
NEGATIVE = -1e30
MESH = pl.DeviceIdType.MESH
F32 = jnp.float32
BF16 = jnp.bfloat16
TILE = 256
KEYS = 512
PART = 64
EARLY = 9 * PART
LATE = 3 * PART
LANES = 256


def place():
    slot = lax.axis_index("ctx")
    return slot // 8, (slot // 2) % SIDE, slot % 2


class Grid:
    def __init__(self, meets=((1, 0), (-1, 0), (0, 1), (0, -1))):
        self.x, self.y, self.z = place()
        self.meets = meets
        self.ranks, self.slots = {}, {}
        for dx in range(SIDE):
            for dy in range(SIDE):
                rank = ((self.x + dx) % SIDE) * SIDE + (self.y + dy) % SIDE
                self.ranks[dx, dy] = rank
                self.slots[dx, dy] = rank * 2 + self.z

    def spot(self, half, dp, dq):
        dx, dy = (dp, dq) if half == 0 else (dq, dp)
        return dx % SIDE, dy % SIDE

    def rank(self, half, dp, dq):
        return self.ranks[self.spot(half, dp, dq)]

    def device(self, half, dp, dq):
        return {"ctx": self.slots[self.spot(half, dp, dq)]}

    def barrier(self, others=()):
        gate = pltpu.get_barrier_semaphore()
        partners = [self.device(0, *step) for step in self.meets]
        partners += others
        for partner in partners:
            pl.semaphore_signal(gate, inc=1, device_id=partner, device_id_type=MESH)
        pl.semaphore_wait(gate, len(partners))


LARGE = 1 << 16


def size_of(array):
    return array.size * jnp.dtype(array.dtype).itemsize


PIECES = 4


class Waits:
    def __init__(self):
        self.loads, self.stores, self.started = {}, {}, []

    def __call__(self, *which):
        for i in which or sorted(self.loads):
            for copy in self.loads.pop(i, ()):
                if copy is not None:
                    copy.wait()

    def piece(self, k, *which):
        for i in which:
            if i in self.loads:
                copies = self.loads[i]
                if copies[k] is not None:
                    copies[k].wait()
                    copies[k] = None

    def flush(self, *which):
        for i in which or sorted(self.stores):
            if i in self.stores:
                copy = self.stores.pop(i)
                copy.start()
                self.started.append(copy)

    def finish(self):
        self()
        self.flush()
        for copy in self.started:
            copy.wait()


def staged_call(
    body, name, number, given, shapes, scratch, tables=(), direct=(), parted=(), raw=()
):
    loads = [i for i, array in enumerate(given) if size_of(array) > LARGE and i not in raw]
    stores = [i for i, shape in enumerate(shapes) if size_of(shape) > LARGE and i not in direct]
    counts = (len(tables), len(given), len(shapes), len(loads), len(stores))

    def kernel(*refs):
        refs, groups = list(refs), []
        for count in counts:
            groups.append(refs[:count])
            refs = refs[count:]
        table_refs, ins, outs, staged_in, staged_out = groups
        load_sem, store_sem, *refs = refs
        wait = Waits()
        for k, i in enumerate(loads):
            if i not in parted:
                copy = pltpu.make_async_copy(ins[i], staged_in[k], load_sem.at[k, 0])
                copy.start()
                wait.loads[i] = [copy]
        for piece in range(PIECES):
            for k, i in enumerate(loads):
                if i in parted:
                    count = given[i].shape[0] // PIECES
                    span = pl.ds(piece * count, count)
                    copy = pltpu.make_async_copy(
                        ins[i].at[span], staged_in[k].at[span], load_sem.at[k, piece]
                    )
                    copy.start()
                    wait.loads.setdefault(i, []).append(copy)
        for k, i in enumerate(loads):
            ins[i] = staged_in[k]
        for k, i in enumerate(stores):
            wait.stores[i] = pltpu.make_async_copy(staged_out[k], outs[i], store_sem.at[k])
            outs[i] = staged_out[k]
        body(wait, table_refs, ins, outs, refs)
        wait.finish()

    smem, vmem, hbm = (
        pl.BlockSpec(memory_space=space) for space in (pltpu.SMEM, pltpu.VMEM, pl.ANY)
    )
    far = set(stores) | set(direct)
    params = dict(vmem_limit_bytes=60 << 20)
    if number is not None:
        params.update(collective_id=number, has_side_effects=True)
    return pl.pallas_call(
        kernel,
        out_shape=list(shapes),
        in_specs=[smem] * len(tables)
        + [hbm if i in loads or i in raw else vmem for i in range(len(given))],
        out_specs=[hbm if i in far else vmem for i in range(len(shapes))],
        scratch_shapes=[pltpu.VMEM(given[i].shape, given[i].dtype) for i in loads]
        + [pltpu.VMEM(shapes[i].shape, shapes[i].dtype) for i in stores]
        + [
            pltpu.SemaphoreType.DMA((max(len(loads), 1), PIECES)),
            pltpu.SemaphoreType.DMA((max(len(stores), 1),)),
        ]
        + list(scratch),
        name=name,
        compiler_params=pltpu.CompilerParams(**params),
    )(*tables, *given)


RINGS = ((1, 0), (-1, 0), (2, 0), (0, 1), (0, -1), (0, 2))


def gather_half(grid, half, own_ref, all_ref, send_sem, recv_sem):
    rows = own_ref.shape[0]
    half_rows, quarter = rows // 2, rows // 4
    sends = []

    def view(dp, dq, low, count):
        return all_ref.at[grid.rank(half, dp, dq), pl.ds(half * half_rows + low, count)]

    def start(event, to, block, low, count, own=False):
        source = (
            own_ref.at[pl.ds(half * half_rows + low, count)]
            if own
            else view(*block, low, count)
        )
        copy = pltpu.make_async_remote_copy(
            src_ref=source,
            dst_ref=view(*block, low, count),
            send_sem=send_sem.at[half, event],
            recv_sem=recv_sem.at[half, event],
            device_id=grid.device(half, *to),
            device_id_type=MESH,
        )
        copy.start()
        sends.append(copy)

    def arrive(event, block, low, count):
        there = view(*block, low, count)
        pltpu.make_async_remote_copy(
            src_ref=there,
            dst_ref=there,
            send_sem=send_sem.at[half, event],
            recv_sem=recv_sem.at[half, event],
            device_id=grid.device(half, 1, 0),
            device_id_type=MESH,
        ).wait_recv()

    def spread(column, dp, own=False):
        start(4 + 4 * column, (0, 1), (dp, 0), 0, half_rows, own)
        start(5 + 4 * column, (0, -1), (dp, 0), 0, half_rows, own)

    start(0, (1, 0), (0, 0), 0, half_rows, True)
    start(1, (-1, 0), (0, 0), 0, half_rows, True)
    spread(0, 0, True)
    yield
    arrive(0, (-1, 0), 0, half_rows)
    start(2, (1, 0), (-1, 0), 0, quarter)
    spread(1, -1)
    arrive(1, (1, 0), 0, half_rows)
    start(3, (-1, 0), (1, 0), quarter, quarter)
    spread(2, 1)
    yield
    arrive(2, (2, 0), 0, quarter)
    arrive(3, (2, 0), quarter, quarter)
    spread(3, 2)
    yield
    steps = (0, -1, 1, 2)
    for column in range(4):
        arrive(4 + 4 * column, (steps[column], -1), 0, half_rows)
        start(6 + 4 * column, (0, 1), (steps[column], -1), 0, quarter)
        arrive(5 + 4 * column, (steps[column], 1), 0, half_rows)
        start(7 + 4 * column, (0, -1), (steps[column], 1), quarter, quarter)
        yield
    for column in range(4):
        arrive(6 + 4 * column, (steps[column], 2), 0, quarter)
        arrive(7 + 4 * column, (steps[column], 2), quarter, quarter)
        if column % 2 == 0:
            yield
    for copy in sends:
        copy.wait_send()


GATHER_STEPS = 20


def gather_steps(grid, own_ref, all_ref, send_sem, recv_sem):
    halves = [
        gather_half(grid, half, own_ref, all_ref, send_sem, recv_sem) for half in (0, 1)
    ]
    for step in range(GATHER_STEPS):
        next(halves[step % 2], None)
        if step < GATHER_STEPS - 1:
            yield


DIRECT_STEPS = 8


def direct_steps(grid, own_ref, all_ref, send_sem, recv_sem):
    half_rows = own_ref.shape[0] // 2
    sends = []

    def view(half, dp, dq):
        return all_ref.at[grid.rank(half, dp, dq), pl.ds(half * half_rows, half_rows)]

    def copy(half, event, to, block, own=False):
        source = own_ref.at[pl.ds(half * half_rows, half_rows)] if own else view(half, *block)
        return pltpu.make_async_remote_copy(
            src_ref=source,
            dst_ref=view(half, *block),
            send_sem=send_sem.at[half, event],
            recv_sem=recv_sem.at[half, event],
            device_id=grid.device(half, *to),
            device_id_type=MESH,
        )

    def start(*args):
        made = copy(*args)
        made.start()
        sends.append(made)

    steps = (1, -1, 2)
    for index, step in enumerate(steps):
        for half in (0, 1):
            start(half, index, (step, 0), (0, 0), True)
    for index, step in enumerate(steps):
        for half in (0, 1):
            start(half, 3 + index, (0, step), (0, 0), True)
    yield
    for index, step in enumerate(steps):
        for half in (0, 1):
            copy(half, index, (step, 0), (-step, 0)).wait_recv()
            for other, move in enumerate(steps):
                start(half, 6 + 3 * index + other, (0, move), (-step, 0))
            yield
    for column, place_p in enumerate((0, -1, 1, -2)):
        for other, move in enumerate(steps):
            for half in (0, 1):
                copy(half, 3 + 3 * column + other, (0, move), (place_p, -move)).wait_recv()
    for made in sends:
        made.wait_send()


def run(steps, count=None):
    while count is None or count > 0:
        if next(steps, StopIteration) is StopIteration:
            return
        count = None if count is None else count - 1


def scatter_steps(
    grid, make, part_ref, out_ref, land_half, land_full, stage, total, send_sem, recv_sem
):
    rows = part_ref.shape[1]
    half_rows, quarter = rows // 2, rows // 4
    sends = []
    steps = (2, -1, 1, 0)

    def start(half, event, source, target, to):
        copy = pltpu.make_async_remote_copy(
            src_ref=source,
            dst_ref=target,
            send_sem=send_sem.at[half, event],
            recv_sem=recv_sem.at[half, event],
            device_id=grid.device(half, *to),
            device_id_type=MESH,
        )
        copy.start()
        sends.append(copy)

    def arrive(half, event, target):
        pltpu.make_async_remote_copy(
            src_ref=target,
            dst_ref=target,
            send_sem=send_sem.at[half, event],
            recv_sem=recv_sem.at[half, event],
            device_id=grid.device(half, 1, 0),
            device_id_type=MESH,
        ).wait_recv()

    def first(half, column):
        def piece(dq, low, count):
            return part_ref.at[
                grid.rank(half, steps[column], dq), pl.ds(half * half_rows + low, count)
            ]

        return piece

    def second(half):
        return lambda dp, low, count: total.at[half, steps.index(dp), pl.ds(low, count)]

    def along(step):
        return (0, step)

    def across(step):
        return (step, 0)

    def opposite(half, column, piece, step):
        for side, low in ((0, 0), (1, quarter)):
            start(
                half,
                4 * column + side,
                piece(2, low, quarter),
                land_half.at[half, column, side],
                step(1 - 2 * side),
            )

    def neighbours(half, column, piece, step):
        for side in (0, 1):
            land = land_half.at[half, column, side]
            arrive(half, 4 * column + side, land)
            low, other = side * quarter, (1 - side) * quarter
            toward = 1 - 2 * side
            stage[half, column, side, low : low + quarter] = (
                piece(toward, low, quarter)[...].astype(F32) + land[...].astype(F32)
            ).astype(BF16)
            stage[half, column, side, other : other + quarter] = piece(toward, other, quarter)[...]
            start(
                half,
                4 * column + 2 + side,
                stage.at[half, column, side],
                land_full.at[half, column, side],
                step(toward),
            )

    def settle(half, column, own):
        for side in (0, 1):
            arrive(half, 4 * column + 2 + side, land_full.at[half, column, side])
        return (
            own[...].astype(F32)
            + land_full[half, column, 0].astype(F32)
            + land_full[half, column, 1].astype(F32)
        )

    def places(*spots):
        make([grid.rank(0, dx, dy) for dx, dy in spots])

    def on_both(step, column, direction):
        for half in (0, 1):
            step(half, column, first(half, column), direction)

    places((2, 2))
    on_both(opposite, 0, along)
    for column in (1, 2, 3):
        places((steps[column], 2), (2, steps[column]))
        on_both(opposite, column, along)
        yield
    on_both(neighbours, 0, along)
    yield
    places((-1, -1), (-1, 1))
    places((1, -1), (1, 1))
    on_both(neighbours, 1, along)
    yield
    places((0, 1), (0, -1))
    on_both(neighbours, 2, along)
    yield
    places((1, 0), (-1, 0))
    on_both(neighbours, 3, along)
    yield
    places((0, 0))
    for column in range(4):
        for half in (0, 1):
            total[half, column] = settle(
                half, column, first(half, column)(0, 0, half_rows)
            ).astype(BF16)
            if column == 0:
                opposite(half, 4, second(half), across)
            if column == 2:
                neighbours(half, 4, second(half), across)
        yield
    for half in (0, 1):
        out_ref[pl.ds(half * half_rows, half_rows)] = settle(half, 4, total.at[half, 3])
    for copy in sends:
        copy.wait_send()


SCATTER_STEPS = 12


def scatter_scratch(rows, width):
    half_rows, quarter = rows // 2, rows // 4
    return [
        pltpu.VMEM((2, 5, 2, quarter, width), BF16),
        pltpu.VMEM((2, 5, 2, half_rows, width), BF16),
        pltpu.VMEM((2, 5, 2, half_rows, width), BF16),
        pltpu.VMEM((2, 4, half_rows, width), BF16),
        pltpu.SemaphoreType.DMA((2, 20)),
        pltpu.SemaphoreType.DMA((2, 20)),
    ]


def follow(grid, gather, block, ready=None, last=None):
    def places(*spots):
        block([grid.rank(0, dx, dy) for dx, dy in spots])

    run(gather, 4)
    if ready is not None:
        ready()
    places((0, 0))
    run(gather, 2)
    places((0, 1), (0, -1))
    run(gather, 2)
    places((1, 0), (-1, 0))
    run(gather, 2)
    places((1, 1), (1, -1))
    run(gather, 2)
    places((-1, 1), (-1, -1))
    run(gather, 2)
    places((0, 2), (2, 0))
    run(gather, 2)
    if last is not None:
        last()
    places((1, 2), (-1, 2))
    places((2, 1), (2, -1))
    run(gather)
    places((2, 2))


def rows_of(ref, ranks, rows):
    return jnp.concatenate([ref[block_rows(rank, rows), :] for rank in ranks], 0)


def put_rows(ref, ranks, rows, values):
    for index, rank in enumerate(ranks):
        ref[block_rows(rank, rows), :] = values[index * rows : (index + 1) * rows]


def blocks_of(ref, ranks):
    return jnp.concatenate([ref[rank] for rank in ranks], 0)


SQRT_HALF = 0.7071067811865476
DENSITY = 0.3989422804014327


def standardize(stream):
    row_mean = jnp.mean(stream, -1, keepdims=True)
    centered = stream - row_mean
    spread = jnp.mean(centered * centered, -1, keepdims=True)
    inverse = lax.rsqrt(spread + EPS)
    return (centered * inverse, inverse)


def dots(a, b, da, db):
    return lax.dot_general(a, b, (((da,), (db,)), ((), ())), preferred_element_type=F32)


def rotate(values, cosines, sines):
    lane = lax.broadcasted_iota(jnp.int32, values.shape, 1)
    half_dims = ROT // 2
    up = pltpu.roll(values, 2 * HEAD - half_dims, 1)
    down = pltpu.roll(values, half_dims, 1)
    return values * cosines + jnp.where(lane < half_dims, -up, down) * sines


def block_rows(rank, rows):
    return pl.ds(pl.multiple_of(rank * rows, rows), rows)


def share_partners():
    shard = lax.axis_index("fsdp")
    return [{"fsdp": shard + 1 - 2 * (shard % 2)}, {"fsdp": (shard + 2) % 4}]


def share_steps(items, send_sem, recv_sem):
    shard = lax.axis_index("fsdp")
    sibling = shard + 1 - 2 * (shard % 2)
    mate = (shard + 2) % 4
    third = (sibling + 2) % 4
    sends = []

    def copy(item, source, target, event, to):
        return pltpu.make_async_remote_copy(
            src_ref=source,
            dst_ref=target,
            send_sem=send_sem.at[item, event],
            recv_sem=recv_sem.at[item, event],
            device_id={"fsdp": to},
            device_id_type=MESH,
        )

    def start(*args):
        made = copy(*args)
        made.start()
        sends.append(made)

    for item, (own, every) in enumerate(items):
        start(item, own, every.at[shard], 0, mate)
        start(item, own, every.at[shard], 1, sibling)
        every[shard] = own[...]
    yield
    for item, (own, every) in enumerate(items):
        copy(item, own, every.at[mate], 0, mate).wait_recv()
        start(item, every.at[mate], every.at[mate], 2, sibling)
        yield
        copy(item, own, every.at[sibling], 1, sibling).wait_recv()
        copy(item, own, every.at[third], 2, sibling).wait_recv()
        yield
    for made in sends:
        made.wait_send()


def share_sems(items):
    return [pltpu.SemaphoreType.DMA((items, 3)), pltpu.SemaphoreType.DMA((items, 3))]


def stack_tall(tall_all, tall_ref):
    for part in range(4):
        tall_ref[part * HEAD : (part + 1) * HEAD] = tall_all[part, :HEAD]
    tall_ref[4 * HEAD : 5 * HEAD] = jnp.zeros((HEAD, tall_ref.shape[1]), BF16)
    tall_ref[5 * HEAD :] = tall_all[place()[0], HEAD:]


def enter_phase(grid, stream_ref, given, wide_ref, made, own, sems, ready, swap, last):
    scale_ref, bias_ref, cos_ref, sin_ref = given
    normed_ref, active_ref, slope_ref, q_ref, kv_ref = made
    rows, width = stream_ref.shape
    own[...] = standardize(stream_ref[...].astype(F32))[0].astype(BF16)
    normed_ref[grid.rank(0, 0, 0)] = own[...]
    yield
    gather = gather_steps(grid, own, normed_ref, *sems)
    run(gather, 2)

    def block(ranks):
        plain = blocks_of(normed_ref, ranks).astype(F32)
        first = (plain * scale_ref[0:1] + scale_ref[2:3]).astype(BF16)
        second = (plain * scale_ref[1:2] + scale_ref[3:4]).astype(BF16)
        weight = wide_ref[...].reshape(width, 8 * HEAD)
        mixed = dots(first, weight[:, : 4 * HEAD], 1, 0) + bias_ref[:, : 4 * HEAD]
        hidden = dots(second, weight[:, 4 * HEAD :], 1, 0) + bias_ref[:, 4 * HEAD :]
        cosines, sines = rows_of(cos_ref, ranks, rows), rows_of(sin_ref, ranks, rows)
        pairs = rotate(mixed[:, : 2 * HEAD], cosines, sines)
        queries = rotate(mixed[:, 2 * HEAD :], cosines, sines) * 0.125
        put_rows(kv_ref, ranks, rows, pairs.astype(BF16))
        put_rows(q_ref, ranks, rows, queries.astype(BF16))
        share = 0.5 * (1.0 + lax.erf(hidden * SQRT_HALF))
        put_rows(active_ref, ranks, rows, (hidden * share).astype(BF16))
        slope = share + hidden * (DENSITY * jnp.exp(-0.5 * hidden * hidden))
        put_rows(slope_ref, ranks, rows, slope)
        swap(ranks)

    follow(grid, gather, block, ready, last)


def leave_steps(
    grid, active_ref, context_ref, tall_ref, stream_ref, bias_ref, out_ref, parts, total_rows, scratch
):
    rows = stream_ref.shape[0]

    def make(ranks):
        context = rows_of(context_ref, ranks, rows).astype(BF16)
        both = jnp.concatenate([rows_of(active_ref, ranks, rows), context], 1)
        made = dots(both, tall_ref[...], 1, 0).astype(BF16)
        for index, rank in enumerate(ranks):
            parts[rank] = made[index * rows : (index + 1) * rows]

    yield from scatter_steps(grid, make, parts, total_rows, *scratch)
    stream = stream_ref[...].astype(F32)
    out_ref[...] = (stream + total_rows[...] + bias_ref[...]).astype(out_ref.dtype)


VECTOR_ROWS = 16


def unpack(grid, vectors, scale_ref, bias_ref, last_ref):
    lane = lax.broadcasted_iota(jnp.int32, (8, 2 * HEAD), 1)

    def of_rank(rows):
        row = rows[0]
        for index in range(1, 4):
            row = jnp.where(grid.x == index, rows[index], row)
        row = jnp.broadcast_to(row, (8, LANES))
        half = jnp.where(grid.y < 2, row[:, : 2 * HEAD], row[:, 2 * HEAD :])
        rolled = pltpu.roll(half, HEAD, 1)
        odd = grid.y % 2 == 1
        return jnp.where(odd, rolled, half), jnp.where(odd, half, rolled)

    def beside(low, high):
        return jnp.where(lane < HEAD, low[0], high[1])

    def shard_rows(first, count):
        return [vector[first + i : first + i + 1] for vector in vectors for i in range(count)]

    scale_ref[...] = jnp.concatenate([vector[:4] for vector in vectors], 1)
    last_ref[...] = jnp.concatenate([vector[7:8] + vector[12:13] for vector in vectors], 1)
    mixed = shard_rows(4, 3)
    q, k, v = (of_rank(mixed[4 * part : 4 * part + 4]) for part in range(3))
    up = [of_rank([vector[8 + i : 9 + i] for i in range(4)]) for vector in vectors]
    tiles = [
        beside(k, v),
        jnp.where(lane < HEAD, q[0], 0.0),
        beside(up[0], up[1]),
        beside(up[2], up[3]),
    ]
    bias_ref[...] = jnp.concatenate(tiles, 1)[0:1]


def forward_body(wait, tables, ins, outs, refs):
    stream_ref, cos_ref, sin_ref, wide_one, wide_two, branch_ref, down_ref, out_ref = ins[:8]
    vector_refs = ins[8:]
    scales, lasts = outs[21:23], outs[23:25]
    layer_outs, branches = (outs[:7], outs[7:14]), outs[14:16]
    wide_refs, tall_refs, second_ref = (outs[16], outs[18]), (outs[17], outs[19]), outs[20]
    (own_one, own_two), refs = refs[:2], refs[2:]
    queries, refs = (refs[:2], refs[2:4]), refs[4:]
    enter_sems, refs = (refs[:2], refs[2:4]), refs[4:]
    branch_sems, refs = (refs[:3], refs[3:6]), refs[6:]
    share_refs, refs = (refs[:3], refs[3:6]), refs[6:]
    (parts, total_rows), scatter_refs, refs = refs[:2], refs[2:8], refs[8:]
    attend_refs, swap_sems, refs = (refs[:4], refs[:3] + refs[5:6]), (refs[4], refs[6]), refs[7:]
    swaps = ([], [])
    vector_ref, vector_all, biases, refs = refs[0], refs[1], refs[2:4], refs[4:]
    talls, tall_sem = refs[:2], refs[2]
    grid = Grid()
    tall_copies = []
    for layer in range(2):
        for index, (source, first) in enumerate(
            ((down_ref, grid.rank(0, 0, 0)), (out_ref, grid.y))
        ):
            copy = pltpu.make_async_copy(
                source.at[layer, block_rows(first, HEAD)],
                talls[layer].at[pl.ds(index * HEAD, HEAD)],
                tall_sem.at[layer, index],
            )
            copy.start()
            tall_copies.append(copy)
    for layer in range(2):
        gain, shift, qkv, out, up, down = (
            ref[layer].astype(F32) if len(ref.shape) == 3 else ref[layer : layer + 1].astype(F32)
            for ref in vector_refs
        )
        rows = [gain, shift]
        rows += [qkv[:, i * LANES : (i + 1) * LANES] for i in range(3)] + [out]
        rows += [up[:, i * LANES : (i + 1) * LANES] for i in range(4)] + [down]
        rows.append(jnp.zeros((VECTOR_ROWS - 13, LANES), F32))
        vector_ref[layer] = jnp.concatenate(rows, 0).astype(BF16)

    keeps, gathers = [], []

    def start_half(layer):
        all_ref, sems = branches[layer], branch_sems[layer]
        count = branch_ref.shape[0] // 2
        half = branch_ref.at[pl.ds(layer * count, count)]
        keeps.append(keep_own(grid, half, all_ref, sems[0]))
        gathers.append(gather_steps(grid, half, all_ref, *sems[1:]))
        run(gathers[layer], 2)

    def attend_phase(layer):
        normed, active, slope, context, qs, kvs, logs = layer_outs[layer]
        work = attend_steps(
            tables, *queries[layer], context, qs, kvs, logs, attend_refs[layer], swaps[layer]
        )
        take_turns(work, ATTEND_WORK, [(gathers[layer], GATHER_STEPS - 2, 0, 2, 1.0)])

    def swap(layer, ranks):
        for rank in ranks:
            span, sem = block_rows(rank, stream_ref.shape[0]), swap_sems[layer]
            event = len(swaps[layer])
            copy = remote(
                queries[layer][1].at[span],
                attend_refs[layer][3].at[span],
                sem.at[0, event],
                sem.at[1, event],
                far_partner(),
            )
            copy.start()
            swaps[layer].append(copy)

    def sharing(layer, *items):
        tall_all, *sems = share_refs[layer]
        wide_own, tall_own = items[-2:]
        items = items[:-2] + ((wide_own, wide_refs[layer]), (tall_own, tall_all))
        return share_steps(items, *sems)

    def ready():
        run(shared, 4)
        for layer in range(2):
            vectors = [vector_all[shard, layer].astype(F32) for shard in range(4)]
            unpack(grid, vectors, scales[layer], biases[layer], lasts[layer])
        wait()

    wait(0)
    enter = enter_phase(
        grid, stream_ref, (scales[0], biases[0], cos_ref, sin_ref), wide_refs[0],
        (*layer_outs[0][:3], *queries[0]), own_one, enter_sems[0], ready,
        functools.partial(swap, 0), functools.partial(start_half, 0),
    )
    run(enter, 1)
    grid.barrier([far_partner()] + share_partners())
    wait(3)
    for copy in tall_copies:
        copy.wait()
    shared = sharing(0, (vector_ref, vector_all), wide_one, talls[0])
    run(shared, 1)
    run(enter)
    run(shared, 1)
    wait.flush(0, 1, 2, 16)
    attend_phase(0)
    run(shared)
    stack_tall(share_refs[0][0], tall_refs[0])
    wait.flush(3, 4, 5, 6, 17)
    shared = sharing(1, wide_two, talls[1])
    run(shared, 1)
    leave = leave_steps(
        grid, layer_outs[0][1], layer_outs[0][3], tall_refs[0], stream_ref, lasts[0], second_ref,
        parts, total_rows, scatter_refs,
    )
    run(leave, 5)
    run(shared, 1)
    run(leave, 3)
    run(shared, 2)
    run(leave)

    enter = enter_phase(
        grid, second_ref, (scales[1], biases[1], cos_ref, sin_ref), wide_refs[1],
        (*layer_outs[1][:3], *queries[1]), own_two, enter_sems[1], lambda: run(shared),
        functools.partial(swap, 1), functools.partial(start_half, 1),
    )
    run(enter, 1)
    wait.flush(20)
    run(enter)
    stack_tall(share_refs[1][0], tall_refs[1])
    wait.flush(7, 8, 9, 18, 19)
    attend_phase(1)
    for keep in keeps:
        keep.wait()


def forward(tables, stream, vectors, cosines, sines, wide, down, out, cotangent, number):
    rows, width = stream.shape
    total = 16 * rows
    layers = wide.shape[0]
    half = rows // layers
    shapes = [
        jax.ShapeDtypeStruct((16, rows, width), BF16),
        jax.ShapeDtypeStruct((total, 4 * HEAD), BF16),
        jax.ShapeDtypeStruct((total, 4 * HEAD), F32),
        jax.ShapeDtypeStruct((total, 2 * HEAD), F32),
        jax.ShapeDtypeStruct((total, 2 * HEAD), BF16),
        jax.ShapeDtypeStruct((2, total, 2 * HEAD), BF16),
        jax.ShapeDtypeStruct((total, 2 * HEAD), F32),
    ] * layers
    shapes += [jax.ShapeDtypeStruct((16, half, width), BF16)] * layers
    shapes += [
        jax.ShapeDtypeStruct((4,) + wide.shape[1:], BF16),
        jax.ShapeDtypeStruct((6 * HEAD, width), BF16),
    ] * layers
    shapes.append(jax.ShapeDtypeStruct((rows, width), F32))
    shapes += [jax.ShapeDtypeStruct((4, width), F32)] * layers
    shapes += [jax.ShapeDtypeStruct((1, width), F32)] * layers
    swap = [pltpu.VMEM((total, 2 * HEAD), BF16), pltpu.SemaphoreType.DMA((2, 16))]
    scratch = [pltpu.VMEM((rows, width), BF16)] * 2
    scratch += [pltpu.VMEM((total, 2 * HEAD), BF16)] * 4
    scratch += [pltpu.SemaphoreType.DMA((2, 20))] * 4
    scratch += gather_sems() + gather_sems()
    tall = pltpu.VMEM((2 * HEAD, width), BF16)
    scratch += ([pltpu.VMEM((4, 2 * HEAD, width), BF16)] + share_sems(3)) * 2
    scratch += [pltpu.VMEM((16, rows, width), BF16), pltpu.VMEM((rows, width), F32)]
    scratch += scatter_scratch(rows, width)
    scratch += [pltpu.VMEM((total, 2 * HEAD), F32)] * 3 + swap + swap
    packed = (layers, VECTOR_ROWS, LANES)
    scratch += [pltpu.VMEM(packed, BF16), pltpu.VMEM((4,) + packed, BF16)]
    scratch += [pltpu.VMEM((1, 8 * HEAD), F32)] * layers
    scratch += [tall] * layers + [pltpu.SemaphoreType.DMA((layers, 2))]
    given = [stream, cosines, sines, wide[0], wide[1], cotangent, down, out, *vectors]
    made = staged_call(
        forward_body, "forward", number, given, shapes, scratch, tables, direct=(14, 15), raw=(6, 7)
    )
    saved, weights = (made[:7], made[7:14]), ((made[16], made[18]), (made[17], made[19]))
    return saved, made[14:16], *weights, made[20], made[21:23], made[23:25]


def back_enter_phase(
    grid, wait, ins, outs, tall_sum, gather_refs=None, beside=(), between=None, last=None
):
    grad_ref, active_ref, context_ref, slope_ref, normed_ref, tall_ref, scale_ref = ins[:7]
    pull_ref, offset_ref, hidden_ref, early_ref, out_ref, up_ref, up_bias_ref = outs
    gathers = gather_refs is not None
    rows = normed_ref.shape[-2]
    if gathers:
        own, all_rows, send_sem, recv_sem = gather_refs
        gather = gather_steps(grid, own, all_rows, send_sem, recv_sem)
        run(gather, 2)
        for steps in beside:
            run(steps, 1)
    tall_sum[...] = jnp.zeros_like(tall_sum)
    up_ref[...] = jnp.zeros_like(up_ref)
    up_bias_ref[...] = jnp.zeros_like(up_bias_ref)

    def block(ranks):
        if gathers:
            branch = blocks_of(all_rows, ranks)
        else:
            branch = jnp.concatenate([half[rank] for rank in ranks for half in (grad_ref, ins[7])], 0)
        back = dots(branch, tall_ref[...], 1, 1)
        hidden_grad = (back[:, : 4 * HEAD] * rows_of(slope_ref, ranks, rows)).astype(BF16)
        pull = back[:, 4 * HEAD :].astype(BF16)
        put_rows(hidden_ref, ranks, rows, hidden_grad)
        put_rows(pull_ref, ranks, rows, pull)
        context = rows_of(context_ref, ranks, rows)
        offset = jnp.sum(pull.astype(F32) * context, 1, keepdims=True)
        put_rows(offset_ref, ranks, rows, jnp.broadcast_to(offset, context.shape))
        both = jnp.concatenate([rows_of(active_ref, ranks, rows), context.astype(BF16)], 1)
        ones = jnp.ones(context.shape, BF16)
        tall_sum[...] += dots(both, branch, 0, 0)
        up_ref[...] += dots(hidden_grad, blocks_of(normed_ref, ranks), 0, 0)
        up_bias_ref[...] += dots(hidden_grad, ones, 0, 0)

    if gathers:
        follow(grid, gather, block, lambda: wait(*range(1, 7)), last)
    else:
        wait(5)
        for piece in range(PIECES):
            wait.piece(piece, 0, 1, 2, 3, 4, 7)
            block([piece * 4 + i for i in range(4)])
            between()
    up_grad = (up_ref[...] * scale_ref[1:2] + up_bias_ref[:, 0:1] * scale_ref[3:4]).astype(BF16)
    for shard in range(4):
        early_ref[shard, : 4 * PART] = up_grad[:, shard * LANES : (shard + 1) * LANES]
        early_ref[shard, 8 * PART :] = jnp.zeros((PART, LANES), BF16)
        for lanes in range(4):
            early_ref[shard, (4 + lanes) * PART : (5 + lanes) * PART] = tall_sum[
                shard * HEAD : (shard + 1) * HEAD, lanes * LANES : (lanes + 1) * LANES
            ].astype(BF16)
            low = 5 * HEAD + shard * 16
            out_ref[shard, lanes * 16 : (lanes + 1) * 16] = tall_sum[
                low : low + 16, lanes * LANES : (lanes + 1) * LANES
            ].astype(BF16)


def back_enter_shapes(rows, width):
    total = 16 * rows
    return [
        jax.ShapeDtypeStruct((total, 4 * HEAD), BF16),
        jax.ShapeDtypeStruct((4 * HEAD, width), F32),
        jax.ShapeDtypeStruct((4 * HEAD, 2 * HEAD), F32),
    ], [
        pltpu.VMEM((total, 2 * HEAD), BF16),
        pltpu.VMEM((total, 2 * HEAD), F32),
        pltpu.VMEM((4, EARLY, LANES), BF16),
        pltpu.VMEM((4, PART, LANES), BF16),
        pltpu.VMEM((6 * HEAD, width), F32),
    ]


def back_leave_phase(grid, wait, ins, outs, refs, exchanges, other_vectors=None, after=None):
    query_grad_ref, pair_grad_ref, hidden_ref, normed_ref, wide_ref, scale_ref = ins[:6]
    cos_ref, sin_ref, stream_ref, grad_ref, up_ref, up_bias_ref = ins[6:]
    new_ref, addend_ref, *vector_ref = outs
    vector_ref = vector_ref[0] if vector_ref else None
    (mixed, raw, raw_bias, parts, total_rows), scratch = refs[:5], refs[5:]
    rows, width = stream_ref.shape
    wait(0, 1, 2, 4, 6, 7)

    def make(ranks):
        cosines, sines = rows_of(cos_ref, ranks, rows), -rows_of(sin_ref, ranks, rows)
        query = rows_of(query_grad_ref, ranks, rows) * 0.125
        lane = lax.broadcasted_iota(jnp.int32, query.shape, 1)
        query = jnp.where(lane < HEAD, query, 0.0)
        pair = rows_of(pair_grad_ref, ranks, rows)
        both = jnp.concatenate(
            [rotate(pair, cosines, sines), rotate(query, cosines, sines)], 1
        ).astype(BF16)
        put_rows(mixed, ranks, rows, both)
        first = dots(both, wide_ref[:, : 4 * HEAD], 1, 1)
        second = dots(rows_of(hidden_ref, ranks, rows), wide_ref[:, 4 * HEAD :], 1, 1)
        made = (first * scale_ref[0:1] + second * scale_ref[1:2]).astype(BF16)
        for index, rank in enumerate(ranks):
            parts[rank] = made[index * rows : (index + 1) * rows]

    scatter = scatter_steps(grid, make, parts, total_rows, *scratch)
    run(scatter, 3)
    wait()
    for steps in exchanges:
        run(steps, 1)
    run(scatter, 5)
    raw[...] = jnp.zeros_like(raw)
    raw_bias[...] = jnp.zeros_like(raw_bias)
    ones = jnp.ones((4 * rows, 2 * HEAD), BF16)

    def sums(index):
        span = pl.ds(index * 4 * rows, 4 * rows)
        both = mixed[span, :]
        normed_rows = normed_ref[pl.ds(index * 4, 4)].reshape(4 * rows, width)
        raw[...] += dots(both, normed_rows, 0, 0)
        raw_bias[...] += dots(both, ones, 0, 0)

    sums(0)
    run(scatter, 1)
    sums(1)
    run(scatter, 1)
    sums(2)
    run(scatter, 1)
    sums(3)

    wide_t = jnp.transpose(wide_ref[:, : 4 * HEAD].astype(F32))
    up_t = jnp.transpose(wide_ref[:, 4 * HEAD :].astype(F32))
    mixed_bias, up_bias = raw_bias[:, 0:1], up_bias_ref[:, 0:1]
    first_raw, second_raw = raw[...], up_ref[...]
    vectors = [
        jnp.sum(wide_t * first_raw, 0, keepdims=True),
        jnp.sum(up_t * second_raw, 0, keepdims=True),
        jnp.sum(wide_t * mixed_bias, 0, keepdims=True),
        jnp.sum(up_t * up_bias, 0, keepdims=True),
        jnp.sum(grad_ref[...].astype(BF16).astype(F32), 0, keepdims=True),
    ]
    first_grad = (first_raw * scale_ref[0:1] + mixed_bias * scale_ref[2:3]).astype(BF16)
    biases = [
        jnp.transpose(raw_bias[...])[0:1],
        jnp.transpose(up_bias_ref[...])[0:1],
    ]
    for shard in range(4):
        lanes = slice(shard * LANES, (shard + 1) * LANES)
        addend_ref[shard, : 3 * PART] = first_grad[: 3 * PART, lanes]
        tail = [vector[:, lanes] for vector in vectors] + biases
        tail.append(jnp.zeros((VECTOR_ROWS - len(tail), LANES), F32))
        tail = jnp.concatenate(tail, 0).astype(BF16)
        if other_vectors is None:
            vector_ref[shard] = tail
        else:
            addend_ref[shard, LATE : LATE + 16] = tail
            addend_ref[shard, LATE + 16 : LATE + 32] = other_vectors[shard]
            addend_ref[shard, LATE + 32 :] = jnp.zeros((PART - 32, LANES), BF16)
    run(scatter)
    for steps in exchanges:
        run(steps)
    if after is not None:
        after()
    normed, inverse = standardize(stream_ref[...].astype(F32))
    normed_grad = total_rows[...]
    new_ref[...] = grad_ref[...].astype(F32) + inverse * (
        normed_grad
        - jnp.mean(normed_grad, -1, keepdims=True)
        - normed * jnp.mean(normed_grad * normed, -1, keepdims=True)
    )


def back_leave_scratch(rows, width):
    total = 16 * rows
    return [
        pltpu.VMEM((total, 4 * HEAD), BF16),
        pltpu.VMEM((4 * HEAD, width), F32),
        pltpu.VMEM((4 * HEAD, 2 * HEAD), F32),
        pltpu.VMEM((16, rows, width), BF16),
        pltpu.VMEM((rows, width), F32),
    ] + scatter_scratch(rows, width)


def back_leave_body(wait, tables, ins, outs, refs):
    grid = Grid()
    grid.barrier([mate()])
    exchanges = [low_steps(ins[12], outs[3], *refs[11:], ins[13])]
    back_leave_phase(grid, wait, ins[:12], outs[:3], refs[:11], exchanges)


def back_leave(given, rows, width, number, sums, total):
    shapes = [
        jax.ShapeDtypeStruct((rows, width), F32),
        jax.ShapeDtypeStruct((4, LATE, LANES), BF16),
        jax.ShapeDtypeStruct((4, VECTOR_ROWS, LANES), BF16),
        jax.ShapeDtypeStruct((EARLY, LANES), BF16),
    ]
    scratch = back_leave_scratch(rows, width) + swap_scratch(EARLY)
    given = tuple(given) + (sums, total)
    return staged_call(back_leave_body, "back_leave", number, given, shapes, scratch)


def sibling():
    shard = lax.axis_index("fsdp")
    return {"fsdp": shard + 1 - 2 * (shard % 2)}


def mate():
    return {"fsdp": (lax.axis_index("fsdp") + 2) % 4}


def far_partner():
    slot = lax.axis_index("ctx")
    return {"ctx": slot + 1 - 2 * (slot % 2)}


def wide_barrier(grid):
    shard = lax.axis_index("fsdp")
    at_home = grid.x == shard
    gate = pltpu.get_barrier_semaphore()
    partners = [grid.device(0, *step) for step in grid.meets]
    partners += [sibling(), mate(), far_partner()]
    for partner in partners:
        pl.semaphore_signal(gate, inc=1, device_id=partner, device_id_type=MESH)
    for other in range(4):

        @pl.when(jnp.logical_not(at_home & (shard == other)))
        def greet():
            pl.semaphore_signal(
                gate,
                inc=1,
                device_id={"ctx": (shard * SIDE + grid.y) * 2 + grid.z, "fsdp": other},
                device_id_type=MESH,
            )

    pl.semaphore_wait(gate, len(partners) + 4 - at_home.astype(jnp.int32))


def remote(source, target, send, recv, to):
    return pltpu.make_async_remote_copy(
        src_ref=source,
        dst_ref=target,
        send_sem=send,
        recv_sem=recv,
        device_id=to,
        device_id_type=MESH,
    )


def added(a, b):
    return (a.astype(F32) + b.astype(F32)).astype(BF16)


def core_steps(in_ref, sums_ref, land, sems):
    shard = lax.axis_index("fsdp")
    low, core = shard // 2, shard % 2
    copies = [
        remote(
            in_ref.at[part * 2 + 1 - core],
            land.at[part],
            sems.at[0, part],
            sems.at[1, part],
            sibling(),
        )
        for part in (0, 1)
    ]
    for copy in copies:
        copy.start()
    yield
    for copy in copies:
        copy.wait_recv()
    sums_ref[0] = added(in_ref[low * 2 + core], land[low])
    sums_ref[1] = added(in_ref[(1 - low) * 2 + core], land[1 - low])
    for copy in copies:
        copy.wait_send()


def core_scratch(rows):
    return [pltpu.VMEM((2, rows, LANES), BF16), pltpu.SemaphoreType.DMA((2, 2))]


def low_steps(sums_ref, pair_ref, land, sems, total_ref=None):
    copy = remote(sums_ref.at[1], land, sems.at[0], sems.at[1], mate())
    copy.start()
    yield
    copy.wait_recv()
    pair_ref[...] = added(sums_ref[0], land[...])
    if total_ref is not None:
        pair_ref[pair_ref.shape[0] - PART :] = total_ref[...]
    copy.wait_send()


def high_steps(pair_ref, own_ref, land, sems):
    copy = remote(pair_ref, land, sems.at[0], sems.at[1], far_partner())
    copy.start()
    yield
    copy.wait_recv()
    own_ref[...] = added(pair_ref[...], land[...])
    copy.wait_send()


def swap_scratch(rows):
    return [pltpu.VMEM((rows, LANES), BF16), pltpu.SemaphoreType.DMA((2,))]


def quarter_steps(grid, quarter_ref, total_ref, land, send_sem, recv_sem):
    x, y, z = grid.x, grid.y, grid.z
    shard = lax.axis_index("fsdp")
    at_home = x == shard

    def copy(column):
        return remote(
            quarter_ref.at[column],
            land.at[shard],
            send_sem.at[column],
            recv_sem.at[shard],
            {"ctx": (column * SIDE + y) * 2 + z, "fsdp": x},
        )

    for column in range(4):

        @pl.when(jnp.logical_not(at_home & (x == column)))
        def give():
            copy(column).start()

        @pl.when(at_home & (x == column))
        def keep():
            land[shard] = quarter_ref[column]

    yield
    for other in range(4):

        @pl.when(jnp.logical_not(at_home & (shard == other)))
        def take():
            remote(
                land.at[other], land.at[other], send_sem.at[other], recv_sem.at[other], mate()
            ).wait_recv()

    total = land[0].astype(F32)
    for other in range(1, 4):
        total = total + land[other].astype(F32)
    total_ref[...] = total.astype(BF16)
    for column in range(4):

        @pl.when(jnp.logical_not(at_home & (x == column)))
        def gone():
            copy(column).wait_send()


def quarter_scratch():
    return [
        pltpu.VMEM((4, PART, LANES), BF16),
        pltpu.SemaphoreType.DMA((4,)),
        pltpu.SemaphoreType.DMA((4,)),
    ]


def gather_sems():
    return [
        pltpu.SemaphoreType.DMA,
        pltpu.SemaphoreType.DMA((2, 20)),
        pltpu.SemaphoreType.DMA((2, 20)),
    ]


def keep_own(grid, own, every, sem):
    copy = pltpu.make_async_copy(own, every.at[grid.rank(0, 0, 0)], sem)
    copy.start()
    return copy


def last_body(wait, tables, ins, outs, refs):
    new_ref, all_early, all_other, all_late = outs
    leave_refs, refs = refs[:11], refs[11:]
    (late_addends, early, other, sums, pair, late), refs = refs[:6], refs[6:]
    early_swap, other_swap, refs = refs[:2], refs[2:4], refs[4:]
    core_refs, low_refs, high_refs, refs = refs[:2], refs[2:4], refs[4:6], refs[6:]
    early_sems, other_sems, late_sems = refs[:3], refs[3:6], refs[6:9]
    grid = Grid()
    grid.barrier([sibling(), mate(), far_partner()])
    exchanges = [high_steps(ins[12], early, *early_swap), high_steps(ins[13], other, *other_swap)]
    first = gather_steps(grid, early, all_early, *early_sems[1:])
    second = gather_steps(grid, other, all_other, *other_sems[1:])
    keeps = []

    def start():
        for steps in exchanges:
            run(steps)
        run(first, 2)
        run(second, 2)
        keeps.append(keep_own(grid, early, all_early, early_sems[0]))
        keeps.append(keep_own(grid, other, all_other, other_sems[0]))

    back_leave_phase(
        grid, wait, ins[:12], (new_ref, late_addends), leave_refs, exchanges, ins[14], start
    )
    wait.flush()
    core = core_steps(late_addends, sums, *core_refs)
    run(core, 1)
    run(first, 2)
    run(second, 2)
    run(core)
    low = low_steps(sums, pair, *low_refs)
    run(low, 1)
    run(first, 2)
    run(second, 2)
    run(first, 2)
    run(low)
    high = high_steps(pair, late, *high_refs)
    run(high, 1)
    run(second, 2)
    run(first, 4)
    run(high)
    keeps.append(keep_own(grid, late, all_late, late_sems[0]))
    third = gather_steps(grid, late, all_late, *late_sems[1:])
    run(third, 2)
    for unused in range(GATHER_STEPS):
        run(first, 1)
        run(second, 1)
        run(third, 1)
    run(third)
    for keep in keeps:
        keep.wait()


def back_leave_last(given, rows, width, number, early, other, vectors):
    count = LATE + PART
    shapes = [
        jax.ShapeDtypeStruct((rows, width), F32),
        jax.ShapeDtypeStruct((16,) + early.shape, BF16),
        jax.ShapeDtypeStruct((16,) + other.shape, BF16),
        jax.ShapeDtypeStruct((16, count, LANES), BF16),
    ]
    scratch = back_leave_scratch(rows, width)
    scratch += [
        pltpu.VMEM((4, count, LANES), BF16),
        pltpu.VMEM(early.shape, BF16),
        pltpu.VMEM(other.shape, BF16),
        pltpu.VMEM((2, count, LANES), BF16),
        pltpu.VMEM((count, LANES), BF16),
        pltpu.VMEM((count, LANES), BF16),
    ]
    scratch += swap_scratch(early.shape[0]) + swap_scratch(other.shape[0])
    scratch += core_scratch(count) + swap_scratch(count) + swap_scratch(count)
    scratch += gather_sems() + gather_sems() + gather_sems()
    given = tuple(given) + (early, other, vectors)
    return staged_call(
        last_body, "back_leave_last", number, given, shapes, scratch, direct=(1, 2, 3)
    )


def format_kernel(layers, *refs):
    early, late, passing = refs[:layers], refs[layers : 2 * layers], refs[2 * layers : 2 * layers + 2]
    refs = refs[2 * layers + 2 :]
    (qkv_out, out_out, up_out, down_out), passed, refs = refs[:4], refs[4:6], refs[6:]
    early_in, late_in, qkv, out, up, down, *held, load_sem, store_sem, pass_sem = refs
    loads, stores = {}, []

    def store(source, target, layer, event):
        copy = pltpu.make_async_copy(source, target, store_sem.at[layer, event])
        copy.start()
        stores.append(copy)

    passes = []
    for index in range(2):
        copy = pltpu.make_async_copy(passing[index], held[index], pass_sem.at[0, index])
        copy.start()
        passes.append(copy)
    for layer in range(layers):
        for part in range(9 + 3):
            source, target, first = (
                (early[layer], early_in, part) if part < 9 else (late[layer], late_in, part - 9)
            )
            span = pl.ds(first * PART, PART)
            loads[layer, part] = pltpu.make_async_copy(
                source.at[:, span], target.at[layer, :, span], load_sem.at[layer, part]
            )
            loads[layer, part].start()
    row = lax.broadcasted_iota(jnp.int32, (LANES, LANES), 0)
    column = lax.broadcasted_iota(jnp.int32, (LANES, LANES), 1)
    unit = (row == column).astype(BF16)
    wide = 16 * PART

    def rows(ref, layer, part):
        return ref[layer, :, part * PART : (part + 1) * PART].reshape(wide, LANES)

    for index in range(2):
        passes[index].wait()
        copy = pltpu.make_async_copy(held[index], passed[index], pass_sem.at[1, index])
        copy.start()
        stores.append(copy)
    for layer in range(layers):
        for part in range(4):
            loads[layer, part].wait()
            up[layer, part] = dots(unit, rows(early_in, layer, part), 1, 1)
            target = up_out.at[layer, :, pl.ds(part * wide, wide)]
            store(up.at[layer, part], target, layer, part)
        for part in range(4):
            loads[layer, 4 + part].wait()
            lanes = slice(part * LANES, (part + 1) * LANES)
            down[layer, :, lanes] = rows(early_in, layer, 4 + part).astype(F32)
        store(down.at[layer], down_out.at[layer], layer, 4)
        loads[layer, 8].wait()
        for part in range(4):
            lanes = slice(part * LANES, (part + 1) * LANES)
            low = 8 * PART + part * 16
            for x in range(4):
                for y in range(4):
                    first = y * HEAD + x * 16
                    out[layer, first : first + 16, lanes] = early_in[
                        layer, x * 4 + y, low : low + 16
                    ].astype(F32)
        store(out.at[layer], out_out.at[layer], layer, 5)
        for part, place_of in enumerate((1, 2, 0)):
            loads[layer, 9 + part].wait()
            qkv[layer, part] = dots(unit, rows(late_in, layer, part), 1, 1)
            target = qkv_out.at[layer, :, pl.ds(place_of * wide, wide)]
            store(qkv.at[layer, part], target, layer, 6 + part)
    for copy in stores:
        copy.wait()


def format_grads(early, late, passing):
    layers = len(early)
    width = 4 * LANES
    hbm = pl.BlockSpec(memory_space=pl.ANY)
    shapes = [
        jax.ShapeDtypeStruct((layers, LANES, 3 * width), F32),
        jax.ShapeDtypeStruct((layers, LANES, width), F32),
        jax.ShapeDtypeStruct((layers, LANES, 4 * width), F32),
        jax.ShapeDtypeStruct((layers, width, width), F32),
    ]
    shapes += [jax.ShapeDtypeStruct(array.shape, array.dtype) for array in passing]
    return pl.pallas_call(
        functools.partial(format_kernel, layers),
        out_shape=shapes,
        in_specs=[hbm] * (2 * layers + 2),
        out_specs=[hbm] * 6,
        scratch_shapes=[
            pltpu.VMEM((layers, 16, EARLY, LANES), BF16),
            pltpu.VMEM((layers, 16, LATE, LANES), BF16),
            pltpu.VMEM((layers, 3, LANES, width), F32),
            pltpu.VMEM((layers, LANES, width), F32),
            pltpu.VMEM((layers, 4, LANES, width), F32),
            pltpu.VMEM((layers, width, width), F32),
        ]
        + [pltpu.VMEM(array.shape, array.dtype) for array in passing]
        + [
            pltpu.SemaphoreType.DMA((layers, 12)),
            pltpu.SemaphoreType.DMA((layers, 9)),
            pltpu.SemaphoreType.DMA((2, 2)),
        ],
        name="format_grads",
        compiler_params=pltpu.CompilerParams(vmem_limit_bytes=60 << 20),
    )(*early, *late, *passing)


SPAN = 1024
ATTEND_WORK = 88


def sort_in(source_ref, order_ref, target_ref, count):
    def body(i, unused):
        start = order_ref[i] * BLK
        target_ref[pl.ds(pl.multiple_of(i * BLK, BLK), BLK), :] = source_ref[
            pl.ds(start, BLK), :
        ]
        return unused

    lax.fori_loop(0, count, body, 0, unroll=8)


def block_numbers(number_ref, first, count, axis):
    if axis == 0:
        return jnp.concatenate(
            [jnp.full((BLK, 1), number_ref[first + i], jnp.int32) for i in range(count)], 0
        )
    lane = lax.broadcasted_iota(jnp.int32, (1, count * BLK), 1) // BLK
    numbers = jnp.zeros((1, count * BLK), jnp.int32)
    for i in range(count):
        numbers = jnp.where(lane == i, number_ref[first + i], numbers)
    return numbers


def far_copy(source, target, sems):
    return pltpu.make_async_remote_copy(
        src_ref=source,
        dst_ref=target,
        send_sem=sems.at[0],
        recv_sem=sems.at[1],
        device_id=far_partner(),
        device_id_type=MESH,
    )


def attend_steps(tables, q_ref, kv_ref, context_ref, qs, kvs, logs, scratch, swaps):
    order_ref, standing_ref, number_ref, other_order, other_ref = tables
    tops, totals, sums, far_ref = scratch
    sort_in(kv_ref, order_ref, kvs.at[0], 32)
    sort_in(q_ref, order_ref, qs, 32)
    tiles = qs.shape[0] // TILE
    row = lax.broadcasted_iota(jnp.int32, (TILE, TILE), 0)
    column = lax.broadcasted_iota(jnp.int32, (TILE, TILE), 1)
    yield 4

    def highest(scores):
        return jnp.max(scores, 1, keepdims=True)

    def weigh(scores, top, keys):
        weights = jnp.exp(scores - top)
        return jnp.sum(weights, 1, keepdims=True), dots(weights.astype(BF16), keys, 1, 0)

    def wide(vector):
        return jnp.broadcast_to(vector, (TILE, 2 * HEAD))

    def own_tile(tile):
        rows = slice(tile * TILE, (tile + 1) * TILE)
        queries, near = qs[rows, :], kvs[0, rows, :]
        parts = [(jnp.where(column <= row, dots(queries, near, 1, 1), NEGATIVE), near)]
        for low in range(0, tile * TILE, SPAN):
            keys = kvs[0, low : min(low + SPAN, tile * TILE), :]
            parts.append((dots(queries, keys, 1, 1), keys))
        top = highest(parts[0][0])
        for scores, keys in parts[1:]:
            top = jnp.maximum(top, highest(scores))
        total, weighted = 0.0, 0.0
        for scores, keys in parts:
            more, product = weigh(scores, top, keys)
            total, weighted = total + more, weighted + product
        tops[rows, :], totals[rows, :], sums[rows, :] = wide(top), wide(total), weighted

    def other_tile(tile, numbers):
        rows = slice(tile * TILE, (tile + 1) * TILE)
        queries = qs[rows, :]
        own = block_numbers(number_ref, tile * TILE // BLK, TILE // BLK, 0)
        half = tile // 4
        keys = kvs[1, half * SPAN : (half + 1) * SPAN, :]
        parts = [(jnp.where(numbers < own, dots(queries, keys, 1, 1), NEGATIVE), keys)]
        if half:
            keys = kvs[1, :SPAN, :]
            parts.append((dots(queries, keys, 1, 1), keys))
        old = tops[rows, :][:, 0:1]
        top = old
        for scores, keys in parts:
            top = jnp.maximum(top, highest(scores))
        scale = jnp.exp(old - top)
        total, weighted = totals[rows, :][:, 0:1] * scale, sums[rows, :] * scale
        for scores, keys in parts:
            more, product = weigh(scores, top, keys)
            total, weighted = total + more, weighted + product
        sums[rows, :] = weighted / total
        logs[rows, :] = wide(top + jnp.log(total))

    for tile in range(tiles):
        own_tile(tile)
        yield tile + 1
    for copy in swaps:
        copy.wait_recv()
    yield 0
    sort_in(far_ref, other_order, kvs.at[1], 32)
    yield 0
    for half in (0, 1):
        numbers = block_numbers(other_ref, half * 16, 16, 1)
        for tile in range(half * 4, half * 4 + 4):
            other_tile(tile, numbers)
            yield 4 + 4 * half
    sort_in(sums, standing_ref, context_ref, 32)
    for copy in swaps:
        copy.wait_send()


def attend_back_steps(
    tables, qs, kvs, logs, pull_ref, offset_ref, query_grad_ref, pair_grad_ref, scratch
):
    order_ref, standing_ref, number_ref, unused, other_ref = tables
    pulls, offsets, turned, query_sums, pair_sums, away, land, sems = scratch
    sort_in(pull_ref, order_ref, pulls, 32)
    yield 1
    sort_in(offset_ref, order_ref, offsets, 32)
    yield 1
    pair_sums[...] = jnp.zeros_like(pair_sums)
    tiles = qs.shape[0] // TILE
    row = lax.broadcasted_iota(jnp.int32, (TILE, TILE), 0)
    column = lax.broadcasted_iota(jnp.int32, (TILE, TILE), 1)
    lane = lax.broadcasted_iota(jnp.int32, (TILE, 2 * HEAD), 1)
    yield 2

    def tile_part(tile, half, low, count, mask):
        rows = slice(tile * TILE, (tile + 1) * TILE)
        queries, pull = qs[rows, :], pulls[rows, :]
        keys = kvs[half, low : low + count, :]
        scores = dots(keys, queries, 1, 1)
        if mask is not None:
            scores = jnp.where(mask, scores, NEGATIVE)
        probs = jnp.exp(scores - turned[tile, 0:1])
        score_grad = (probs * (dots(keys, pull, 1, 1) - turned[tile, 1:2])).astype(BF16)
        pair_sums[half, low : low + count, :] += dots(score_grad, queries, 1, 0) + dots(
            probs.astype(BF16), pull, 1, 0
        )
        return dots(score_grad, keys, 0, 0)

    def masked_tile(tile, numbers):
        rows = slice(tile * TILE, (tile + 1) * TILE)
        turned[tile] = jnp.transpose(
            jnp.where(lane == 0, logs[rows, :], offsets[rows, :])
        )[:8]
        own = block_numbers(number_ref, tile * TILE // BLK, TILE // BLK, 1)
        query_sums[rows, :] = tile_part(tile, 1, tile // 4 * SPAN, SPAN, numbers < own)

    def send(half):
        span = pl.ds(half * SPAN, SPAN)
        away[span] = pair_sums[1, span].astype(BF16)
        copy = far_copy(away.at[span], land.at[span], sems.at[half])
        copy.start()
        return copy

    def own_tile(tile):
        rows = slice(tile * TILE, (tile + 1) * TILE)
        query_sums[rows, :] += tile_part(tile, 0, tile * TILE, TILE, row <= column)
        yield 1
        for low in range(0, tile * TILE, SPAN):
            count = min(SPAN, tile * TILE - low)
            query_sums[rows, :] += tile_part(tile, 0, low, count, None)
            yield count // TILE

    copies = []
    for half in (1, 0):
        numbers = block_numbers(other_ref, half * 16, 16, 0)
        for tile in range(half * 4, half * 4 + 4):
            masked_tile(tile, numbers)
            yield 4
        if half == 0:
            for tile in range(4, 8):
                rows = slice(tile * TILE, (tile + 1) * TILE)
                query_sums[rows, :] += tile_part(tile, 1, 0, SPAN, None)
                yield 4
        copies.append(send(half))
    for tile in range(tiles):
        yield from own_tile(tile)
    sort_in(query_sums, standing_ref, query_grad_ref, 32)
    for copy in copies:
        copy.wait_recv()
    pair_sums[0] += land[...].astype(F32)
    sort_in(pair_sums.at[0], standing_ref, pair_grad_ref, 32)
    for copy in copies:
        copy.wait_send()


def attend_back_scratch(rows):
    block = (rows, 2 * HEAD)
    return [
        pltpu.VMEM(block, BF16),
        pltpu.VMEM(block, F32),
        pltpu.VMEM((rows // TILE, 8, TILE), F32),
        pltpu.VMEM(block, F32),
        pltpu.VMEM((2,) + block, F32),
        pltpu.VMEM(block, BF16),
        pltpu.VMEM(block, BF16),
        pltpu.SemaphoreType.DMA((2, 2)),
    ]


def take_turns(work, total, others):
    done = 0
    ran = [first for steps, count, first, early, part in others]
    for steps, count, first, early, part in others:
        run(steps, first)
    for more in work:
        done += more
        for index, (steps, count, first, early, part) in enumerate(others):
            wanted = early + min(int(done * (count - early) / (total * part)), count - early)
            run(steps, wanted - ran[index])
            ran[index] = wanted
    for steps, *unused in others:
        run(steps)


def back_last_body(wait, tables, ins, outs, refs):
    hidden_ref, up_ref, up_bias_ref, query_grad_ref, pair_grad_ref, sums_ref, total_ref, out_ref = outs
    (pull, offset, early, quarter, tall_sum), refs = refs[:5], refs[5:]
    (parts, total_rows), scatter_refs, refs = refs[:2], refs[2:8], refs[8:]
    core_refs, quarter_refs, scratch = refs[:2], refs[2:5], refs[5:]
    grid = Grid()
    wide_barrier(grid)
    made = [pull, offset, hidden_ref, early, quarter, up_ref, up_bias_ref]
    leaving = [ins[1], ins[2], ins[5], ins[11], ins[12]]
    scatter = leave_steps(grid, *leaving, out_ref, parts, total_rows, scatter_refs)
    wait(1, 2, 5, 11)
    run(scatter, 1)
    back_enter_phase(grid, wait, ins[:8], made, tall_sum, between=lambda: run(scatter, 1))
    wait.flush(0, 1, 2)
    wait()
    core = core_steps(early, sums_ref, *core_refs)
    quarters = quarter_steps(grid, quarter, total_ref, *quarter_refs)
    work = attend_back_steps(
        tables, *ins[8:11], pull, offset, query_grad_ref, pair_grad_ref, scratch
    )
    others = [
        (core, 1, 1, 1, 1.0),
        (quarters, 1, 1, 1, 1.0),
        (scatter, SCATTER_STEPS - 1 - PIECES, 0, 0, 0.9),
    ]
    take_turns(work, ATTEND_WORK, others)


def back_last(tables, branch, given, attention, stream, bias, number):
    rows, width = stream.shape
    shapes, scratch = back_enter_shapes(rows, width)
    total = 16 * rows
    shapes = shapes + [jax.ShapeDtypeStruct((total, 2 * HEAD), F32)] * 2
    shapes += [
        jax.ShapeDtypeStruct((2, EARLY, LANES), BF16),
        jax.ShapeDtypeStruct((PART, LANES), BF16),
        jax.ShapeDtypeStruct((rows, width), BF16),
    ]
    scratch = scratch + [
        pltpu.VMEM((16, rows, width), BF16),
        pltpu.VMEM((rows, width), F32),
    ]
    scratch += scatter_scratch(rows, width) + core_scratch(EARLY) + quarter_scratch()
    scratch += attend_back_scratch(total)
    given = [branch[0], *given, branch[1], *attention, stream, bias]
    return staged_call(
        back_last_body, "back_last", number, given, shapes, scratch, tables,
        parted=(0, 1, 2, 3, 4, 7),
    )


def back_first_body(wait, tables, ins, outs, refs):
    (
        hidden_ref, up_ref, up_bias_ref, query_grad_ref, pair_grad_ref, pair_ref, late_pair, all_ref
    ) = outs
    (pull, offset, early, quarter, tall_sum), refs = refs[:5], refs[5:]
    (own, all_rows, *row_sems), refs = refs[:4], refs[4:]
    (folded, late_sums, sums, total), refs = refs[:4], refs[4:]
    high_refs, late_core_refs, refs = refs[:2], refs[2:4], refs[4:]
    gather_refs, core_refs, quarter_refs, refs = refs[:3], refs[3:5], refs[5:8], refs[8:]
    early_refs, late_refs, scratch = refs[:2], refs[2:4], refs[4:]
    grid = Grid()
    wait(0)
    own[...] = ins[0][...].astype(BF16)
    all_rows[grid.rank(0, 0, 0)] = own[...]
    wide_barrier(grid)
    wait(7, 8)
    beside = [
        high_steps(ins[7], folded, *high_refs),
        core_steps(ins[8], late_sums, *late_core_refs),
    ]
    made = [pull, offset, hidden_ref, early, quarter, up_ref, up_bias_ref]
    keeps = []
    gather = gather_steps(grid, folded, all_ref, *gather_refs[1:])

    def start():
        run(beside[0])
        keeps.append(keep_own(grid, folded, all_ref, gather_refs[0]))
        run(gather, 2)

    row_refs = (own, all_rows, *row_sems)
    back_enter_phase(grid, wait, ins[:7], made, tall_sum, row_refs, beside, last=start)
    wait.flush(0, 1, 2)
    run(beside[1])
    run(gather, 2)
    wait()
    quarters = quarter_steps(grid, quarter, total, *quarter_refs)
    late = low_steps(late_sums, late_pair, *late_refs)

    def early_steps():
        core = core_steps(early, sums, *core_refs)
        next(core)
        yield
        run(core)
        run(quarters)
        yield from low_steps(sums, pair_ref, *early_refs, total)

    work = attend_back_steps(
        tables, *ins[9:12], pull, offset, query_grad_ref, pair_grad_ref, scratch
    )
    others = [
        (gather, GATHER_STEPS - 4, 0, 3, 0.9),
        (quarters, 1, 1, 1, 1.0),
        (early_steps(), 2, 1, 1, 0.5),
        (late, 1, 1, 1, 1.0),
    ]
    take_turns(work, ATTEND_WORK, others)
    for keep in keeps:
        keep.wait()


def back_first(tables, grad, given, exchanged, attention, number):
    rows, width = grad.shape
    shapes, scratch = back_enter_shapes(rows, width)
    total = 16 * rows
    shapes = shapes + [jax.ShapeDtypeStruct((total, 2 * HEAD), F32)] * 2
    shapes += [
        jax.ShapeDtypeStruct((EARLY, LANES), BF16),
        jax.ShapeDtypeStruct((LATE, LANES), BF16),
        jax.ShapeDtypeStruct((16, EARLY, LANES), BF16),
    ]
    scratch = scratch + [
        pltpu.VMEM((rows, width), BF16),
        pltpu.VMEM((16, rows, width), BF16),
        pltpu.SemaphoreType.DMA((2, 20)),
        pltpu.SemaphoreType.DMA((2, 20)),
        pltpu.VMEM((EARLY, LANES), BF16),
        pltpu.VMEM((2, LATE, LANES), BF16),
        pltpu.VMEM((2, EARLY, LANES), BF16),
        pltpu.VMEM((PART, LANES), BF16),
    ]
    scratch += swap_scratch(EARLY) + core_scratch(LATE) + gather_sems()
    scratch += core_scratch(EARLY) + quarter_scratch()
    scratch += swap_scratch(EARLY) + swap_scratch(LATE) + attend_back_scratch(total)
    given = [grad, *given, *exchanged, *attention]
    return staged_call(
        back_first_body, "back_first", number, given, shapes, scratch, tables, direct=(7,)
    )


def block_tables(pair_table, z):
    slots = pair_table.shape[0]
    ranks = slots // 2
    index = jnp.arange(slots, dtype=jnp.int32)

    def plane(which):
        pairs = lax.dynamic_slice_in_dim(pair_table.reshape(ranks, 2), which, 1, 1)
        numbers = jnp.concatenate([pairs, 2 * slots - 1 - pairs], 1).reshape(-1)
        standing = jnp.sum((numbers[None, :] < numbers[:, None]).astype(jnp.int32), 1)
        chosen = (standing[None, :] == index[:, None]).astype(jnp.int32)
        order = jnp.sum(chosen * index[None, :], 1)
        return numbers, (order, standing, jnp.sum(chosen * numbers[None, :], 1))

    numbers, own = plane(z)
    other = plane(1 - z)[1]
    return numbers, own + (other[0], other[2])


def rotation(positions):
    freqs = 10000.0 ** (-jnp.arange(0, ROT, 2, dtype=F32) / ROT)
    angles = positions.astype(F32)[:, None] * freqs[None, :]
    rest = ((0, 0), (0, 2 * HEAD - ROT))
    return (
        jnp.pad(jnp.concatenate([jnp.cos(angles)] * 2, -1), rest, constant_values=1.0),
        jnp.pad(jnp.concatenate([jnp.sin(angles)] * 2, -1), rest),
    )


def on_device(
    hidden_in,
    cotangent,
    pair_table,
    norm_gain,
    norm_bias,
    qkv_weight,
    qkv_bias,
    out_weight,
    out_bias,
    up_weight,
    up_bias,
    down_weight,
    down_bias,
):
    layers = norm_gain.shape[0]
    slot = lax.axis_index("ctx")
    shard = lax.axis_index("fsdp")
    rank, z = slot // 2, slot % 2
    width = hidden_in.shape[2]
    quarter = width // 4

    numbers, tables = block_tables(pair_table, z)
    positions = (
        numbers[:, None] * BLK + jnp.arange(BLK, dtype=jnp.int32)[None, :]
    ).reshape(-1)
    cosines, sines = rotation(positions)

    def columns(weight, part):
        return lax.dynamic_slice_in_dim(weight, part * width + rank * HEAD, HEAD, 2)

    wide = jnp.concatenate(
        [columns(qkv_weight, 1), columns(qkv_weight, 2), columns(qkv_weight, 0)]
        + [jnp.zeros((layers, quarter, HEAD), BF16)]
        + [columns(up_weight, part) for part in range(4)],
        2,
    )
    vectors = (norm_gain, norm_bias, qkv_bias, out_bias, up_bias, down_bias)
    stream = hidden_in[0]
    saved, branch_all, wide_all, tall_all, second, scales, last_biases = forward(
        tables, stream, vectors, cosines, sines, wide, down_weight, out_weight, cotangent[0], 1
    )
    streams, number = (stream, second), 2

    grad = cotangent[0]
    early, late = [None] * layers, [None] * layers
    exchanged = None
    for layer in reversed(range(layers)):
        last = layer == layers - 1
        normed_all, active, slope, context, queries, pairs, logs = saved[layer]
        stream = streams[layer]
        given = (active, context, slope, normed_all, tall_all[layer], scales[layer])
        attention = (queries, pairs, logs)
        if last:
            (
                hidden_grad, up_raw, up_bias_raw, query_grad, pair_grad, early_sums, out_total, output
            ) = back_last(tables, branch_all, given, attention, stream, last_biases[layer], number)
            exchanges = (early_sums, out_total)
        else:
            (
                hidden_grad, up_raw, up_bias_raw, query_grad, pair_grad, early_pair, late_pair,
                early[layer + 1],
            ) = back_first(tables, grad, given, exchanged, attention, number)
            exchanges = (early_pair, late_pair)
        number += 1
        given = (
            query_grad,
            pair_grad,
            hidden_grad,
            normed_all,
            wide_all[layer].reshape(width, 8 * HEAD),
            scales[layer],
            cosines,
            sines,
            stream,
            grad,
            up_raw,
            up_bias_raw,
        )
        if last:
            grad, addends, vector_rows, early_pair = back_leave(
                given, *stream.shape, number, *exchanges
            )
            exchanged = (early_pair, addends)
        else:
            grad, early[0], late[1], late[0] = back_leave_last(
                given, *stream.shape, number, *exchanges, vector_rows
            )
        number += 1

    qkv_out, out_out, up_out, down_out, output, grad = format_grads(early, late, (output, grad))
    small = jnp.stack(
        [late[0][:, LATE + 16 * layer : LATE + 16 * layer + 7] for layer in range(layers)]
    ).astype(F32)
    sums = jnp.sum(small[:, :, :5], 1)
    gain_out, shift_out, branch_out = sums[:, 0:2], sums[:, 2:4], sums[:, 4]
    qkv_bias_out = jnp.transpose(
        jnp.roll(small[:, :, 5, : 3 * HEAD].reshape(layers, 16, 3, HEAD), 1, 2), (0, 2, 1, 3)
    ).reshape(layers, -1)
    share = qkv_bias_out.shape[1] // 4
    qkv_bias_out = lax.dynamic_slice_in_dim(qkv_bias_out, shard * share, share, 1)
    up_bias_out = lax.dynamic_slice_in_dim(
        small[:, :, 6].reshape(layers, 16, 4, HEAD), shard, 1, 2
    ).reshape(layers, -1)
    return (
        output[None],
        grad[None],
        gain_out,
        shift_out,
        qkv_out,
        qkv_bias_out,
        out_out,
        branch_out,
        up_out,
        up_bias_out,
        down_out,
        branch_out,
    )


def solution(mesh):
    rows = P("fsdp", "ctx", None)
    vector, matrix = P(None, "fsdp"), P(None, "fsdp", None)
    gains = P(None, None, "fsdp")
    params = (gains, gains) + (matrix, vector) * 4
    return jax.shard_map(
        on_device,
        mesh=mesh,
        in_specs=(rows, rows, P()) + params,
        out_specs=(rows, rows) + params,
        check_vma=False,
    )
```
